32 devices in a mesh: items: 4 (over y, core), blk: 8 (over z, x).
Axes of the slice: x: 2, y: 2, z: 4, core: 2. Of those that a mesh axis runs over, the one named last changes fastest.
Arguments:
- hidden_in: bfloat16 [8, 1536, 1024], P('items', 'blk'), may hold values from -6 to 6
- text_states: bfloat16 [8, 64, 1024], P('items'), may hold values from -6 to 6
- frame_lengths: int32 [8], P('items'), may hold values from 768 to 1536, as said below
- text_lengths: int32 [8], P('items'), may hold values from 16 to 64, as said below
- out_grad: bfloat16 [8, 1536, 1024], P('items', 'blk'), may hold values from -6 to 6
- attn_in: bfloat16 [1024, 3072], replicated, may hold values from -0.1875 to 0.1875
- attn_in_bias: bfloat16 [2048], replicated, may hold values from -3 to 3
- attn_out: bfloat16 [1024, 1024], replicated, may hold values from -4 to 4
- attn_out_bias: bfloat16 [1024], replicated, may hold values from -2 to 2
- cross_query: bfloat16 [1024, 1024], replicated, may hold values from -0.1875 to 0.1875
- cross_query_bias: bfloat16 [1024], replicated, may hold values from -3 to 3
- cross_kv: bfloat16 [1024, 2048], replicated, may hold values from -0.1875 to 0.1875
- cross_v_bias: bfloat16 [1024], replicated, may hold values from -3 to 3
- cross_out: bfloat16 [1024, 1024], replicated, may hold values from -0.75 to 0.75
- cross_out_bias: bfloat16 [1024], replicated, may hold values from -2 to 2
- ff_up: bfloat16 [1024, 4096], replicated, may hold values from -0.1875 to 0.1875
- ff_up_bias: bfloat16 [4096], replicated, may hold values from -3 to 3
- ff_down: bfloat16 [4096, 1024], replicated, may hold values from -0.09375 to 0.09375
- ff_down_bias: bfloat16 [1024], replicated, may hold values from -2 to 2
- norm_gain: bfloat16 [3, 1024], replicated, may hold values from 0.5 to 1.5
- norm_bias: bfloat16 [3, 1024], replicated, may hold values from -2 to 2
Outputs:
- layer_output: bfloat16 [8, 1536, 1024], P('items', 'blk')
- hidden_grad: bfloat16 [8, 1536, 1024], P('items', 'blk')
- text_grad: bfloat16 [8, 64, 1024], P('items')
- attn_in_grad: float32 [1024, 3072], P('blk')
- attn_in_bias_grad: float32 [2048], P('blk')
- attn_out_grad: float32 [1024, 1024], P('blk')
- attn_out_bias_grad: float32 [1024], P('blk')
- cross_query_grad: float32 [1024, 1024], P('blk')
- cross_query_bias_grad: float32 [1024], P('blk')
- cross_kv_grad: float32 [1024, 2048], P('blk')
- cross_v_bias_grad: float32 [1024], P('blk')
- cross_out_grad: float32 [1024, 1024], P('blk')
- cross_out_bias_grad: float32 [1024], P('blk')
- ff_up_grad: float32 [1024, 4096], P('blk')
- ff_up_bias_grad: float32 [4096], P('blk')
- ff_down_grad: float32 [4096, 1024], P('blk')
- ff_down_bias_grad: float32 [1024], P('blk')
- norm_gain_grad: float32 [3, 1024], P(None, 'blk')
- norm_bias_grad: float32 [3, 1024], P(None, 'blk')
The draws below stay inside these ranges and needn't reach their ends.
Inputs may be any that keep to these rules, and one draw needn't show every extreme that they name: Frames at or after frame_lengths[b] are padding: no query sees them as keys. Among the 2 items of each index of items, one has all 1536 frames valid and another 1536 // 2. Item b attends to text states 0 to text_lengths[b] - 1. Among the 2 items of each index of items, one has all 64 and another 64 // 4.
All inputs are finite; a program needn't handle non-finite values.
Results may differ from the reference program's by a relative error of at most 0.02.
Values may be sent and summed in bfloat16 or wider, within the bound.
A program may use at most 384 MiB of HBM per device.

```python
import jax
import jax.numpy as jnp
from jax import lax

D = 1024
HEADS = 16
HEAD = 64
FF = 4096
TEXT = 64
LEN = 1536
SEQS = 2
BATCH = 8


def two_marked(key, groups, members, top_value, low_value, spread_lo):
    key_base, key_full, key_step = jax.random.split(key, 3)
    base = jax.random.randint(key_base, (groups, members), spread_lo, top_value + 1)
    full_at = jax.random.randint(key_full, (groups, 1), 0, members)
    step_by = jax.random.randint(key_step, (groups, 1), 1, members)
    half_at = (full_at + step_by) % members
    column = jnp.arange(members)[None, :]
    marked = jnp.where(column == full_at, top_value, jnp.where(column == half_at, low_value, base))
    return marked.reshape(groups * members).astype(jnp.int32)


def draw_frame_lengths(key, part):
    key = jax.random.fold_in(key, 11)
    return two_marked(key, BATCH // SEQS, SEQS, LEN, LEN // 2, LEN // 2)


def draw_text_lengths(key, part):
    key = jax.random.fold_in(key, 12)
    return two_marked(key, BATCH // SEQS, SEQS, TEXT, TEXT // 4, TEXT // 4)


def steps_of(own_key, extent, pieces, least, largest):
    def one(position, shards_of):
        steps = jax.random.uniform(jax.random.fold_in(jax.random.fold_in(own_key, 6), position), (shards_of,), jnp.float32, least / len(pieces), largest / len(pieces))
        return jnp.repeat(jnp.exp(steps), extent[position] // shards_of).reshape((-1,) + (1,) * (len(extent) - position - 1))

    level = one(*pieces[0])
    for cut in pieces[1:]:
        level = level * one(*cut)
    return level


def noise(rng, extent, width, limit, pieces=(), kind=jnp.bfloat16):
    array = width * jax.random.normal(rng, extent, jnp.float32)
    if pieces:
        array = array * steps_of(rng, extent, pieces, -0.22, 0.18)
    return jnp.clip(array, -limit, limit).astype(kind)


def setup_inputs(seed: int = 0) -> dict:
    splits = jax.random.split(jax.random.key(seed), 22)
    return {
        "hidden_in": noise(splits[0], (BATCH, LEN, D), 1.0, 6.0, ((0, 4), (1, 8))),
        "text_states": noise(splits[1], (BATCH, TEXT, D), 1.0, 6.0, ((0, 4),)),
        "frame_lengths": draw_frame_lengths(jax.random.fold_in(splits[21], 71), 0),
        "text_lengths": draw_text_lengths(jax.random.fold_in(splits[21], 71), 0),
        "out_grad": noise(splits[4], (BATCH, LEN, D), 1.0, 6.0, ((0, 4), (1, 8))),
        "attn_in": noise(splits[5], (D, 3 * D), D ** -0.5, 0.1875),
        "attn_in_bias": noise(splits[6], (2 * D,), 0.5, 3.0),
        "attn_out": noise(splits[7], (D, D), (max(1, 4 * D // LEN)) ** -0.5, 4.0),
        "attn_out_bias": noise(splits[8], (D,), 0.3, 2.0),
        "cross_query": noise(splits[9], (D, D), D ** -0.5, 0.1875),
        "cross_query_bias": noise(splits[10], (D,), 0.5, 3.0),
        "cross_kv": noise(splits[11], (D, 2 * D), D ** -0.5, 0.1875),
        "cross_v_bias": noise(splits[12], (D,), 0.5, 3.0),
        "cross_out": noise(splits[13], (D, D), (D // 16) ** -0.5, 0.75),
        "cross_out_bias": noise(splits[14], (D,), 0.3, 2.0),
        "ff_up": noise(splits[15], (D, FF), D ** -0.5, 0.1875),
        "ff_up_bias": noise(splits[16], (FF,), 0.5, 3.0),
        "ff_down": noise(splits[17], (FF, D), FF ** -0.5, 0.09375),
        "ff_down_bias": noise(splits[18], (D,), 0.3, 2.0),
        "norm_gain": jnp.clip(1.0 + 0.1 * jax.random.normal(splits[19], (3, D), jnp.float32), 0.5, 1.5).astype(jnp.bfloat16),
        "norm_bias": noise(splits[20], (3, D), 0.3, 2.0),
    }


@jax.custom_vjp
def low(v):
    return lax.optimization_barrier(v.astype(jnp.bfloat16)).astype(jnp.float32)

@jax.custom_vjp
def low_back(v):
    return v

def low_keep(v):
    return (low(v), None)

def low_pass(kept, grad):
    return (grad,)

def back_keep(v):
    return (v, None)

def back_low(kept, grad):
    return (low(grad),)
low.defvjp(low_keep, low_pass)
low_back.defvjp(back_keep, back_low)
NEG_FILL = -1e+30
HIGH = lax.Precision.HIGHEST

def layer_norm(values, gain, shift):
    centre = lax.optimization_barrier(jnp.mean(values, -1, keepdims=True))
    spread = values - centre
    variance = lax.optimization_barrier(jnp.mean(spread * spread, -1, keepdims=True))
    return spread * lax.rsqrt(variance + 1e-05) * gain + shift

def matmul(left, right):
    return jnp.dot(left, right, precision=HIGH)

def masked_softmax(scores, visible):
    scores = jnp.where(visible, scores, NEG_FILL)
    top_score = lax.optimization_barrier(jnp.max(scores, -1, keepdims=True))
    raised = jnp.where(visible, jnp.exp(scores - top_score), 0.0)
    return raised / lax.optimization_barrier(jnp.sum(raised, -1, keepdims=True))

def one_item(hidden, text, frame_count, text_count, params):
    attn_in, attn_in_bias, attn_out, attn_out_bias, cross_query, cross_query_bias, cross_kv, cross_v_bias, cross_out, cross_out_bias, ff_up, ff_up_bias, ff_down, ff_down_bias, norm_gain, norm_bias = params
    scale = HEAD ** (-0.5)
    normed = low(layer_norm(hidden, norm_gain[0], norm_bias[0]))
    projected = matmul(normed, attn_in)
    queries = low(low_back(projected[:, :D] + attn_in_bias[:D])).reshape(LEN, HEADS, HEAD)
    keys_all = low(low_back(projected[:, D:2 * D])).reshape(LEN, HEADS, HEAD)
    values_all = low(low_back(projected[:, 2 * D:] + attn_in_bias[D:])).reshape(LEN, HEADS, HEAD)
    key_pos = jnp.arange(LEN)
    block_rows = min(512, LEN)

    def attend(inputs):
        query_block, offset = inputs
        query_pos = offset + jnp.arange(block_rows)
        scores = low_back(scale * jnp.einsum('qhd,khd->hqk', query_block, keys_all, precision=HIGH))
        visible = (key_pos[None, None, :] <= query_pos[None, :, None]) & (key_pos[None, None, :] < frame_count)
        weights = low(masked_softmax(scores, visible))
        return jnp.einsum('hqk,khd->qhd', weights, values_all, precision=HIGH)
    blocks = LEN // block_rows
    attended = lax.map(jax.checkpoint(attend), (queries.reshape(blocks, block_rows, HEADS, HEAD), jnp.arange(blocks) * block_rows))
    attended = low(low_back(attended.reshape(LEN, D)))
    after_self = hidden + low_back(matmul(attended, attn_out) + attn_out_bias)
    cross_normed = low(layer_norm(after_self, norm_gain[1], norm_bias[1]))
    cross_queries = low(low_back(matmul(cross_normed, cross_query) + cross_query_bias)).reshape(LEN, HEADS, HEAD)
    text_proj = matmul(text, cross_kv)
    encoder_key_rows = low(low_back(text_proj[:, :D])).reshape(TEXT, HEADS, HEAD)
    encoder_value_rows = low(low_back(text_proj[:, D:] + cross_v_bias)).reshape(TEXT, HEADS, HEAD)
    cross_scores = low_back(scale * jnp.einsum('qhd,thd->hqt', cross_queries, encoder_key_rows, precision=HIGH))
    text_visible = jnp.arange(TEXT)[None, None, :] < text_count
    cross_attention_weights = low(masked_softmax(cross_scores, text_visible))
    cross_attended = jnp.einsum('hqt,thd->qhd', cross_attention_weights, encoder_value_rows, precision=HIGH).reshape(LEN, D)
    cross_attended = low(low_back(cross_attended))
    after_cross = after_self + low_back(matmul(cross_attended, cross_out) + cross_out_bias)
    ff_normed = low(layer_norm(after_cross, norm_gain[2], norm_bias[2]))
    pre_gelu = low_back(matmul(ff_normed, ff_up) + ff_up_bias)
    activated = low(jax.nn.gelu(pre_gelu, approximate=False))
    return after_cross + low_back(matmul(activated, ff_down) + ff_down_bias)

def reference(hidden_in, text_states, frame_lengths, text_lengths, out_grad, attn_in, attn_in_bias, attn_out, attn_out_bias, cross_query, cross_query_bias, cross_kv, cross_v_bias, cross_out, cross_out_bias, ff_up, ff_up_bias, ff_down, ff_down_bias, norm_gain, norm_bias):
    params = tuple((weight.astype(jnp.float32) for weight in (attn_in, attn_in_bias, attn_out, attn_out_bias, cross_query, cross_query_bias, cross_kv, cross_v_bias, cross_out, cross_out_bias, ff_up, ff_up_bias, ff_down, ff_down_bias, norm_gain, norm_bias)))
    zero_grads = jax.tree.map(jnp.zeros_like, params)

    def turn(totals, item):
        hidden, text, cotangent, frame_count, text_count = item

        def forward(hidden_f, text_f, weights_f):
            return one_item(hidden_f, text_f, frame_count, text_count, weights_f)
        output, pullback = jax.vjp(forward, hidden.astype(jnp.float32), text.astype(jnp.float32), params)
        hidden_g, text_g, weight_grads = pullback(cotangent.astype(jnp.float32))
        totals = jax.tree.map(jnp.add, totals, weight_grads)
        return (totals, (output.astype(jnp.bfloat16), hidden_g.astype(jnp.bfloat16), text_g.astype(jnp.bfloat16)))
    totals, outputs = lax.scan(turn, zero_grads, (hidden_in, text_states, out_grad, frame_lengths, text_lengths))
    layer_output, hidden_grad, text_grad = outputs
    return (layer_output, hidden_grad, text_grad, totals[0], totals[1], totals[2], totals[3], totals[4], totals[5], totals[6], totals[7], totals[8], totals[9], totals[10], totals[11], totals[12], totals[13], totals[14], totals[15])
```

```python
from functools import partial

import jax
import jax.numpy as jnp
from jax import lax
from jax.experimental import pallas as pl
from jax.experimental.pallas import tpu as pltpu
from jax.sharding import PartitionSpec as P

HEADS = 16


NEG_FILL = -1e30


def normalize(values, gain, shift):
    centre = jnp.mean(values, -1, keepdims=True)
    spread = values - centre
    variance = jnp.mean(spread * spread, -1, keepdims=True)
    inverse = lax.rsqrt(variance + 1e-05)
    normed = spread * inverse
    return (normed * gain + shift, normed, inverse)


def norm_back(grad, normed, inverse, gain):
    scaled = grad * gain
    first_mean = jnp.mean(scaled, -1, keepdims=True)
    second_mean = jnp.mean(scaled * normed, -1, keepdims=True)
    return (
        inverse * (scaled - first_mean - normed * second_mean),
        jnp.sum(grad * normed, (0, 1)),
        jnp.sum(grad, (0, 1)),
    )


def outer_sum(left, right):
    return jnp.einsum("sfd,sfe->de", left, right, preferred_element_type=jnp.float32)


def apply_fwd(values, weight):
    return jnp.einsum("sfd,de->sfe", values, weight, preferred_element_type=jnp.float32)


def apply_back(grad, weight):
    return jnp.einsum("sfe,de->sfd", grad, weight, preferred_element_type=jnp.float32)


def column_sum(values):
    return jnp.sum(values.astype(jnp.float32), (0, 1))


def general_device(
    hidden_in,
    text_states,
    frame_lengths,
    text_lengths,
    out_grad,
    attn_in,
    attn_in_bias,
    attn_out,
    attn_out_bias,
    cross_query,
    cross_query_bias,
    cross_kv,
    cross_v_bias,
    cross_out,
    cross_out_bias,
    ff_up,
    ff_up_bias,
    ff_down,
    ff_down_bias,
    norm_gain,
    norm_bias,
):
    seq_count, frames, width = hidden_in.shape
    head_count = HEADS
    head_size = width // head_count
    scale = head_size ** (-0.5)
    text_count = text_states.shape[1]
    axis_count = lax.axis_size("blk")
    block_index = lax.axis_index("blk")
    first_frame = block_index * frames
    last_frame = first_frame + frames - 1
    my_pos = first_frame + jnp.arange(frames, dtype=jnp.int32)
    frame_limit = frame_lengths[:, None, None, None]
    gains = norm_gain.astype(jnp.float32)
    shifts = norm_bias.astype(jnp.float32)

    def visible(key_pos, query_pos):
        return (key_pos[None, None, None, :] <= query_pos[None, None, :, None]) & (
            key_pos[None, None, None, :] < frame_limit
        )

    def heads_of(values):
        return values.reshape(values.shape[0], values.shape[1], head_count, head_size)

    residual = hidden_in.astype(jnp.float32)
    attn_full, normed_zero, inverse_zero = normalize(residual, gains[0], shifts[0])
    attn_normed = attn_full.astype(jnp.bfloat16)
    projected = apply_fwd(attn_normed, attn_in)
    query_rows = (projected[..., :width] + attn_in_bias[:width]).astype(jnp.bfloat16)
    key_rows = projected[..., width : 2 * width].astype(jnp.bfloat16)
    value_rows = (projected[..., 2 * width :] + attn_in_bias[width:]).astype(jnp.bfloat16)
    query_heads = heads_of(query_rows)

    def keep_state(state):
        return state

    start_state = (
        jnp.full((seq_count, head_count, frames), NEG_FILL, jnp.float32),
        jnp.zeros((seq_count, head_count, frames), jnp.float32),
        jnp.zeros((seq_count, head_count, frames, head_size), jnp.float32),
    )
    key_piece = lax.all_gather(key_rows, "blk", axis=1, tiled=True)
    value_piece = lax.all_gather(value_rows, "blk", axis=1, tiled=True)
    span = key_piece.shape[1]

    def forward_compute(state):
        running_max, running_sum, accumulated = state
        key_pos = jnp.arange(span, dtype=jnp.int32)
        scores = (
            jnp.einsum(
                "sfhd,sphd->shfp",
                query_heads,
                heads_of(key_piece),
                preferred_element_type=jnp.float32,
            )
            * scale
        )
        mask = visible(key_pos, my_pos)
        scores = jnp.where(mask, scores, NEG_FILL)
        new_max = jnp.maximum(running_max, jnp.max(scores, -1))
        weights = jnp.where(mask, jnp.exp(scores - new_max[..., None]), 0.0)
        running_sum = jnp.sum(weights, -1)
        accumulated = jnp.einsum(
            "shfp,sphd->shfd",
            weights.astype(jnp.bfloat16),
            heads_of(value_piece),
            preferred_element_type=jnp.float32,
        )
        return (new_max, running_sum, accumulated)

    final_state = lax.cond(jnp.int32(0) > last_frame, keep_state, forward_compute, start_state)
    final_max, final_sum, final_acc = final_state
    log_total = final_max + jnp.log(final_sum)
    attended_full = final_acc / final_sum[..., None]
    attended = (
        jnp.transpose(attended_full, (0, 2, 1, 3))
        .reshape(seq_count, frames, width)
        .astype(jnp.bfloat16)
    )
    after_self = residual + apply_fwd(attended, attn_out) + attn_out_bias
    cross_full, normed_one, inverse_one = normalize(after_self, gains[1], shifts[1])
    cross_normed = cross_full.astype(jnp.bfloat16)
    cross_queries = (apply_fwd(cross_normed, cross_query) + cross_query_bias).astype(jnp.bfloat16)
    cross_attention_heads = heads_of(cross_queries)
    text_proj = apply_fwd(text_states, cross_kv)
    encoder_key_rows = heads_of(text_proj[..., :width].astype(jnp.bfloat16))
    encoder_value_rows = heads_of((text_proj[..., width:] + cross_v_bias).astype(jnp.bfloat16))
    cross_scores = (
        jnp.einsum(
            "qybj,qzbj->qbyz",
            cross_attention_heads,
            encoder_key_rows,
            preferred_element_type=jnp.float32,
        )
        * scale
    )
    text_mask = (
        jnp.arange(text_count, dtype=jnp.int32)[None, None, None, :]
        < text_lengths[:, None, None, None]
    )
    cross_scores = jnp.where(text_mask, cross_scores, NEG_FILL)
    cross_top = jnp.max(cross_scores, -1, keepdims=True)
    cross_raised = jnp.where(text_mask, jnp.exp(cross_scores - cross_top), 0.0)
    cross_probs = cross_raised / jnp.sum(cross_raised, -1, keepdims=True)
    cross_attention_weights = cross_probs.astype(jnp.bfloat16)
    cross_attended = (
        jnp.einsum(
            "oalx,oxak->olak",
            cross_attention_weights,
            encoder_value_rows,
            preferred_element_type=jnp.float32,
        )
        .reshape(seq_count, frames, width)
        .astype(jnp.bfloat16)
    )
    after_cross = after_self + apply_fwd(cross_attended, cross_out) + cross_out_bias
    ff_full, normed_two, inverse_two = normalize(after_cross, gains[2], shifts[2])
    ff_normed = ff_full.astype(jnp.bfloat16)
    pre_gelu = apply_fwd(ff_normed, ff_up) + ff_up_bias
    activated = jax.nn.gelu(pre_gelu, approximate=False).astype(jnp.bfloat16)
    layer_output = (after_cross + apply_fwd(activated, ff_down) + ff_down_bias).astype(jnp.bfloat16)
    ff_down_grad = outer_sum(activated, out_grad)
    ff_down_bias_grad = column_sum(out_grad)
    act_grad = apply_back(out_grad, ff_down)
    gelu_value, gelu_pull = jax.vjp(partial(jax.nn.gelu, approximate=False), pre_gelu)
    before_gelu_gradient = gelu_pull(act_grad)[0].astype(jnp.bfloat16)
    ff_up_grad = outer_sum(ff_normed, before_gelu_gradient)
    ff_up_bias_grad = column_sum(before_gelu_gradient)
    back_two, gain_two, shift_two = norm_back(
        apply_back(before_gelu_gradient, ff_up), normed_two, inverse_two, gains[2]
    )
    cross_grad = out_grad.astype(jnp.float32) + back_two
    cross_grad_low = cross_grad.astype(jnp.bfloat16)
    cross_out_grad = outer_sum(cross_attended, cross_grad_low)
    cross_out_bias_grad = column_sum(cross_grad_low)
    cross_attention_gradient = heads_of(apply_back(cross_grad_low, cross_out).astype(jnp.bfloat16))
    cross_dp = jnp.einsum(
        "qybj,qzbj->qbyz",
        cross_attention_gradient,
        encoder_value_rows,
        preferred_element_type=jnp.float32,
    )
    cross_logit_gradient = (
        cross_probs * (cross_dp - jnp.sum(cross_probs * cross_dp, -1, keepdims=True))
    ).astype(jnp.bfloat16)
    text_key_grad = scale * jnp.einsum(
        "wopc,wpou->wcou",
        cross_logit_gradient,
        cross_attention_heads,
        preferred_element_type=jnp.float32,
    ).reshape(seq_count, text_count, width)
    text_value_grad = jnp.einsum(
        "wopc,wpou->wcou",
        cross_attention_weights,
        cross_attention_gradient,
        preferred_element_type=jnp.float32,
    ).reshape(seq_count, text_count, width)
    text_key_grad, text_value_grad = lax.psum((text_key_grad, text_value_grad), "blk")
    text_kv_low = jnp.concatenate([text_key_grad, text_value_grad], -1).astype(jnp.bfloat16)
    text_grad = jnp.einsum(
        "stf,df->std", text_kv_low, cross_kv, preferred_element_type=jnp.float32
    ).astype(jnp.bfloat16)
    row_share = width // axis_count
    text_slice = lax.dynamic_slice_in_dim(text_states, block_index * row_share, row_share, 2)
    cross_kv_rows = jnp.einsum(
        "std,stf->df", text_slice, text_kv_low, preferred_element_type=jnp.float32
    )
    value_slice = lax.dynamic_slice_in_dim(
        text_kv_low, width + block_index * row_share, row_share, 2
    )
    cross_v_bias_rows = column_sum(value_slice)
    cross_q_grad = (
        (
            scale
            * jnp.einsum(
                "oalx,oxak->olak",
                cross_logit_gradient,
                encoder_key_rows,
                preferred_element_type=jnp.float32,
            )
        )
        .reshape(seq_count, frames, width)
        .astype(jnp.bfloat16)
    )
    cross_query_grad = outer_sum(cross_normed, cross_q_grad)
    cross_query_bias_grad = column_sum(cross_q_grad)
    back_one, gain_one, shift_one = norm_back(
        apply_back(cross_q_grad, cross_query), normed_one, inverse_one, gains[1]
    )
    self_grad = cross_grad + back_one
    self_grad_low = self_grad.astype(jnp.bfloat16)
    attn_out_grad = outer_sum(attended, self_grad_low)
    attn_out_bias_grad = column_sum(self_grad_low)
    att_grad = apply_back(self_grad_low, attn_out).astype(jnp.bfloat16)
    att_heads = heads_of(att_grad)
    delta = jnp.sum(jnp.transpose(att_heads.astype(jnp.float32), (0, 2, 1, 3)) * attended_full, -1)
    query_zero = jnp.zeros((seq_count, frames, head_count, head_size), jnp.float32)
    query_key_piece = lax.all_gather(key_rows, "blk", axis=1, tiled=True)
    query_value_piece = lax.all_gather(value_rows, "blk", axis=1, tiled=True)
    query_span = query_key_piece.shape[1]

    def query_compute(state):
        key_pos = jnp.arange(query_span, dtype=jnp.int32)
        piece_keys = heads_of(query_key_piece)
        scores = (
            jnp.einsum(
                "sfhd,sphd->shfp", query_heads, piece_keys, preferred_element_type=jnp.float32
            )
            * scale
        )
        mask = visible(key_pos, my_pos)
        probs = jnp.where(mask, jnp.exp(scores - log_total[..., None]), 0.0)
        prob_grad = jnp.einsum(
            "sfhd,sphd->shfp",
            att_heads,
            heads_of(query_value_piece),
            preferred_element_type=jnp.float32,
        )
        score_grad = (probs * (prob_grad - delta[..., None])).astype(jnp.bfloat16)
        return scale * jnp.einsum(
            "shfp,sphd->sfhd", score_grad, piece_keys, preferred_element_type=jnp.float32
        )

    query_grad = lax.cond(jnp.int32(0) > last_frame, keep_state, query_compute, query_zero)
    total_logs, total_deltas = (
        lax.all_gather(log_total, "blk", axis=2, tiled=True),
        lax.all_gather(delta, "blk", axis=2, tiled=True),
    )
    my_keys = heads_of(key_rows)
    my_values = heads_of(value_rows)
    query_piece_rows = lax.all_gather(query_rows, "blk", axis=1, tiled=True)
    grad_piece_rows = lax.all_gather(att_grad, "blk", axis=1, tiled=True)
    key_span = query_piece_rows.shape[1]

    def key_compute(state):
        query_pos = jnp.arange(key_span, dtype=jnp.int32)
        piece_queries = heads_of(query_piece_rows)
        piece_grads = heads_of(grad_piece_rows)
        scores = (
            jnp.einsum(
                "sphd,sfhd->shpf", piece_queries, my_keys, preferred_element_type=jnp.float32
            )
            * scale
        )
        mask = visible(my_pos, query_pos)
        probs = jnp.where(mask, jnp.exp(scores - total_logs[..., None]), 0.0)
        value_acc = jnp.einsum(
            "shpf,sphd->sfhd",
            probs.astype(jnp.bfloat16),
            piece_grads,
            preferred_element_type=jnp.float32,
        )
        prob_grad = jnp.einsum(
            "sphd,sfhd->shpf", piece_grads, my_values, preferred_element_type=jnp.float32
        )
        score_grad = (probs * (prob_grad - total_deltas[..., None])).astype(jnp.bfloat16)
        key_acc = scale * jnp.einsum(
            "shpf,sphd->sfhd", score_grad, piece_queries, preferred_element_type=jnp.float32
        )
        return (key_acc, value_acc)

    key_grad, value_grad = lax.cond(
        jnp.int32(0) + key_span - 1 < first_frame, keep_state, key_compute, (query_zero, query_zero)
    )
    query_low = query_grad.reshape(seq_count, frames, width).astype(jnp.bfloat16)
    value_low = value_grad.reshape(seq_count, frames, width).astype(jnp.bfloat16)
    qkv_grad = jnp.concatenate(
        [query_low, key_grad.reshape(seq_count, frames, width).astype(jnp.bfloat16), value_low], -1
    )
    attn_in_grad = outer_sum(attn_normed, qkv_grad)
    attn_in_bias_grad = jnp.concatenate([column_sum(query_low), column_sum(value_low)])
    back_zero, gain_zero, shift_zero = norm_back(
        apply_back(qkv_grad, attn_in), normed_zero, inverse_zero, gains[0]
    )
    hidden_grad = (self_grad + back_zero).astype(jnp.bfloat16)
    gain_grads = jnp.stack([gain_zero, gain_one, gain_two])
    shift_grads = jnp.stack([shift_zero, shift_one, shift_two])
    (
        ain_rows,
        ainb_rows,
        aout_rows,
        aoutb_rows,
        cq_rows,
        cqb_rows,
        cout_rows,
        coutb_rows,
        up_rows,
        up_bias_rows,
        down_rows,
        downb_rows,
        gain_rows,
        shift_rows,
    ) = (
        lax.psum_scatter(attn_in_grad, "blk", scatter_dimension=0, tiled=True),
        lax.psum_scatter(attn_in_bias_grad, "blk", scatter_dimension=0, tiled=True),
        lax.psum_scatter(attn_out_grad, "blk", scatter_dimension=0, tiled=True),
        lax.psum_scatter(attn_out_bias_grad, "blk", scatter_dimension=0, tiled=True),
        lax.psum_scatter(cross_query_grad, "blk", scatter_dimension=0, tiled=True),
        lax.psum_scatter(cross_query_bias_grad, "blk", scatter_dimension=0, tiled=True),
        lax.psum_scatter(cross_out_grad, "blk", scatter_dimension=0, tiled=True),
        lax.psum_scatter(cross_out_bias_grad, "blk", scatter_dimension=0, tiled=True),
        lax.psum_scatter(ff_up_grad, "blk", scatter_dimension=0, tiled=True),
        lax.psum_scatter(ff_up_bias_grad, "blk", scatter_dimension=0, tiled=True),
        lax.psum_scatter(ff_down_grad, "blk", scatter_dimension=0, tiled=True),
        lax.psum_scatter(ff_down_bias_grad, "blk", scatter_dimension=0, tiled=True),
        lax.psum_scatter(gain_grads, "blk", scatter_dimension=1, tiled=True),
        lax.psum_scatter(shift_grads, "blk", scatter_dimension=1, tiled=True),
    )
    summed = (
        lax.psum(ain_rows.astype(jnp.bfloat16), "items").astype(jnp.float32),
        lax.psum(ainb_rows.astype(jnp.bfloat16), "items").astype(jnp.float32),
        lax.psum(aout_rows.astype(jnp.bfloat16), "items").astype(jnp.float32),
        lax.psum(aoutb_rows.astype(jnp.bfloat16), "items").astype(jnp.float32),
        lax.psum(cq_rows.astype(jnp.bfloat16), "items").astype(jnp.float32),
        lax.psum(cqb_rows.astype(jnp.bfloat16), "items").astype(jnp.float32),
        lax.psum(cross_kv_rows.astype(jnp.bfloat16), "items").astype(jnp.float32),
        lax.psum(cross_v_bias_rows.astype(jnp.bfloat16), "items").astype(jnp.float32),
        lax.psum(cout_rows.astype(jnp.bfloat16), "items").astype(jnp.float32),
        lax.psum(coutb_rows.astype(jnp.bfloat16), "items").astype(jnp.float32),
        lax.psum(up_rows.astype(jnp.bfloat16), "items").astype(jnp.float32),
        lax.psum(up_bias_rows.astype(jnp.bfloat16), "items").astype(jnp.float32),
        lax.psum(down_rows.astype(jnp.bfloat16), "items").astype(jnp.float32),
        lax.psum(downb_rows.astype(jnp.bfloat16), "items").astype(jnp.float32),
        lax.psum(gain_rows.astype(jnp.bfloat16), "items").astype(jnp.float32),
        lax.psum(shift_rows.astype(jnp.bfloat16), "items").astype(jnp.float32),
    )
    return (
        layer_output,
        hidden_grad,
        text_grad,
        summed[0],
        summed[1],
        summed[2],
        summed[3],
        summed[4],
        summed[5],
        summed[6],
        summed[7],
        summed[8],
        summed[9],
        summed[10],
        summed[11],
        summed[12],
        summed[13],
        summed[14],
        summed[15],
    )


LANES = 128
MESH_ID = pl.DeviceIdType.MESH
CORE_SWAP = tuple((i, i ^ 1) for i in range(4))
Y_SWAP = tuple((i, i ^ 2) for i in range(4))
X_SWAP = tuple((b, b ^ 1) for b in range(8))
VMEM_BYTES = 56 * 1024 * 1024


def z_turn(step):
    return tuple((b, (b + 2 * step) % 8) for b in range(8))


def contract(left, right, left_dim, right_dim):
    return lax.dot_general(
        left, right, (((left_dim,), (right_dim,)), ((), ())), preferred_element_type=jnp.float32
    )


def exchange_kernel(count, moves, *refs):
    sources = refs[: len(moves)]
    targets = refs[len(moves) : 2 * len(moves)]
    send_sem, recv_sem, own_sem = refs[2 * len(moves) :]
    mine = lax.axis_index("blk")
    barrier = pltpu.get_barrier_semaphore()
    for step in range(1, count):
        pl.semaphore_signal(
            barrier, inc=1, device_id={"blk": lax.rem(mine + step, count)}, device_id_type=MESH_ID
        )
    pl.semaphore_wait(barrier, count - 1)
    copies = []
    for step in range(1, count):
        peer = lax.rem(mine + step, count)
        for index, (cut, place) in enumerate(moves):
            slot = index * count + step
            copy = pltpu.make_async_remote_copy(
                src_ref=cut(sources[index], peer),
                dst_ref=place(targets[index], mine),
                send_sem=send_sem.at[slot],
                recv_sem=recv_sem.at[slot],
                device_id={"blk": peer},
                device_id_type=MESH_ID,
            )
            copy.start()
            copies.append(copy)
    for index, (cut, place) in enumerate(moves):
        copy = pltpu.make_async_copy(
            cut(sources[index], mine), place(targets[index], mine), own_sem.at[index]
        )
        copy.start()
        copies.append(copy)
    for copy in copies:
        copy.wait()


def exchange(count, identity, arrays, shapes, moves):
    outs = [jax.ShapeDtypeStruct(shape, array.dtype) for shape, array in zip(shapes, arrays)]
    return pl.pallas_call(
        partial(exchange_kernel, count, moves),
        out_shape=outs,
        in_specs=[pl.BlockSpec(memory_space=pl.ANY)] * len(arrays),
        out_specs=[pl.BlockSpec(memory_space=pl.ANY)] * len(arrays),
        scratch_shapes=[
            pltpu.SemaphoreType.DMA((len(moves) * count,)),
            pltpu.SemaphoreType.DMA((len(moves) * count,)),
            pltpu.SemaphoreType.DMA((len(moves),)),
        ],
        compiler_params=pltpu.CompilerParams(collective_id=identity, has_side_effects=True),
    )(*arrays)


def column_block(offset):
    def view(ref, index):
        return ref.at[:, :, pl.ds(pl.multiple_of(offset + index * LANES, LANES), LANES)]

    return view


def row_block(rows):
    def view(ref, index):
        return ref.at[:, pl.ds(pl.multiple_of(index * rows, rows), rows), :]

    return view


def lead_block(ref, index):
    return ref.at[index]


def whole(ref, index):
    return ref


def vector_kernel(blocks, groups, in_ref, out_ref, stage, second, send_sem, recv_sem):
    mine = lax.axis_index("blk")
    group = lax.axis_index("items")
    barrier = pltpu.get_barrier_semaphore()
    for step in range(1, blocks):
        pl.semaphore_signal(
            barrier, inc=1, device_id={"blk": lax.rem(mine + step, blocks)}, device_id_type=MESH_ID
        )
    for step in range(1, groups):
        pl.semaphore_signal(
            barrier,
            inc=1,
            device_id={"items": lax.rem(group + step, groups)},
            device_id_type=MESH_ID,
        )
    pl.semaphore_wait(barrier, blocks + groups - 2)
    copies = []
    for step in range(1, blocks):
        peer = lax.rem(mine + step, blocks)
        copy = pltpu.make_async_remote_copy(
            src_ref=in_ref.at[peer],
            dst_ref=stage.at[step],
            send_sem=send_sem.at[step],
            recv_sem=recv_sem.at[step],
            device_id={"blk": peer},
            device_id_type=MESH_ID,
        )
        copy.start()
        copies.append(copy)
    total = in_ref[mine]
    for step, copy in enumerate(copies):
        copy.wait()
        total = total + stage[step + 1]
    second[0] = total
    copies = []
    for step in range(1, groups):
        copy = pltpu.make_async_remote_copy(
            src_ref=second.at[0],
            dst_ref=second.at[step],
            send_sem=send_sem.at[blocks + step],
            recv_sem=recv_sem.at[blocks + step],
            device_id={"items": lax.rem(group + step, groups)},
            device_id_type=MESH_ID,
        )
        copy.start()
        copies.append(copy)
    for step, copy in enumerate(copies):
        copy.wait()
    out_ref[...] = (second[0] + second[1]) + (second[2] + second[3])


def vector_sum(values, blocks, groups, identity):
    _, rows, columns = values.shape
    return pl.pallas_call(
        partial(vector_kernel, blocks, groups),
        out_shape=jax.ShapeDtypeStruct((rows, columns), jnp.float32),
        in_specs=[pl.BlockSpec(memory_space=pltpu.VMEM)],
        out_specs=pl.BlockSpec(memory_space=pltpu.VMEM),
        scratch_shapes=[
            pltpu.VMEM((blocks, rows, columns), jnp.float32),
            pltpu.VMEM((groups, rows, columns), jnp.float32),
            pltpu.SemaphoreType.DMA((blocks + groups,)),
            pltpu.SemaphoreType.DMA((blocks + groups,)),
        ],
        compiler_params=pltpu.CompilerParams(collective_id=identity, has_side_effects=True),
    )(values)


def two_heads(values, low_half):
    none = jnp.zeros_like(values)
    return jnp.concatenate(
        [jnp.where(low_half, values, none), jnp.where(low_half, none, values)], 0
    )


def attend_kernel(rows, head, limit_ref, q_ref, k_ref, v_ref, o_ref, low_ref, lse_ref):
    length = q_ref.shape[1]
    limit = limit_ref[pl.program_id(0)]
    low_half = lax.broadcasted_iota(jnp.int32, (rows, 2 * head), 1) < head
    scale = jnp.bfloat16(head ** (-0.5))
    for block in range(length // rows):
        span = (block + 1) * rows
        here = slice(block * rows, span)
        queries = two_heads(q_ref[0, here, :] * scale, low_half)
        scores = contract(queries, k_ref[0, :span, :], 1, 1)
        query_pos = lax.broadcasted_iota(jnp.int32, (2 * rows, rows), 0) % rows
        key_pos = lax.broadcasted_iota(jnp.int32, (2 * rows, rows), 1)
        corner = jnp.where(key_pos <= query_pos, scores[:, span - rows :], NEG_FILL)
        scores = corner if block == 0 else jnp.concatenate([scores[:, : span - rows], corner], 1)
        if span > length // 2:
            valid = lax.broadcasted_iota(jnp.int32, (1, span), 1) < limit
            scores = scores + jnp.where(valid, 0.0, NEG_FILL)
        top = jnp.max(scores, 1, keepdims=True)
        raised = jnp.exp(scores - top)
        total = jnp.sum(raised, 1, keepdims=True)
        mixed = contract(raised.astype(jnp.bfloat16), v_ref[0, :span, :], 1, 0) / total
        mixed = jnp.where(low_half, mixed[:rows], mixed[rows:])
        o_ref[0, here, :] = mixed
        low_ref[0, here, :] = mixed.astype(jnp.bfloat16)
        log_total = top + jnp.log(total)
        lse_ref[0, here, :] = jnp.where(low_half, log_total[:rows], log_total[rows:])


def attend_back_kernel(
    rows,
    head,
    limit_ref,
    q_ref,
    k_ref,
    v_ref,
    o_ref,
    lse_ref,
    g_ref,
    dq_ref,
    dk_ref,
    dv_ref,
    dk_sum,
    dv_sum,
):
    length = q_ref.shape[1]
    limit = limit_ref[pl.program_id(0)]
    low_half = lax.broadcasted_iota(jnp.int32, (rows, 2 * head), 1) < head
    scale = head ** (-0.5)
    blocks = length // rows
    for block in reversed(range(blocks)):
        span = (block + 1) * rows
        here = slice(block * rows, span)
        queries = two_heads(q_ref[0, here, :] * jnp.bfloat16(scale), low_half)
        grads = two_heads(g_ref[0, here, :], low_half)
        logs = jnp.transpose(lse_ref[0, here, :])
        logs = jnp.concatenate([logs[0:1], logs[head : head + 1]], 1)
        products = jnp.transpose(g_ref[0, here, :].astype(jnp.float32) * o_ref[0, here, :])
        delta = jnp.concatenate(
            [
                jnp.sum(products[:head], 0, keepdims=True),
                jnp.sum(products[head:], 0, keepdims=True),
            ],
            1,
        )
        scores = contract(k_ref[0, :span, :], queries, 1, 1)
        key_pos = lax.broadcasted_iota(jnp.int32, (rows, 2 * rows), 0)
        query_pos = lax.broadcasted_iota(jnp.int32, (rows, 2 * rows), 1) % rows
        corner = jnp.where(key_pos <= query_pos, scores[span - rows :], NEG_FILL)
        scores = corner if block == 0 else jnp.concatenate([scores[: span - rows], corner], 0)
        if span > length // 2:
            valid = lax.broadcasted_iota(jnp.int32, (span, 1), 0) < limit
            scores = scores + jnp.where(valid, 0.0, NEG_FILL)
        probs = jnp.exp(scores - logs)
        prob_grads = contract(v_ref[0, :span, :], grads, 1, 1)
        score_grads = (probs * (prob_grads - delta)).astype(jnp.bfloat16)
        query_grads = scale * contract(score_grads, k_ref[0, :span, :], 0, 0)
        dq_ref[0, here, :] = jnp.where(low_half, query_grads[:rows], query_grads[rows:]).astype(
            jnp.bfloat16
        )
        value_part = contract(probs.astype(jnp.bfloat16), grads, 1, 0)
        key_part = contract(score_grads, queries, 1, 0)
        if block == blocks - 1:
            dv_sum[...] = value_part
            dk_sum[...] = key_part
        else:
            dv_sum[:span] += value_part
            dk_sum[:span] += key_part
    dk_ref[0] = dk_sum[...].astype(jnp.bfloat16)
    dv_ref[0] = dv_sum[...].astype(jnp.bfloat16)


def attention_call(kernel, limits, arrays, out_types, scratch):
    items, length, lanes = arrays[0].shape
    block = pl.BlockSpec((1, length, lanes), lambda item, *_: (item, 0, 0))
    rows = 256 if length % 256 == 0 else length
    return pl.pallas_call(
        partial(kernel, rows, lanes // 2),
        grid_spec=pltpu.PrefetchScalarGridSpec(
            num_scalar_prefetch=1,
            grid=(items,),
            in_specs=[block] * len(arrays),
            out_specs=[block] * len(out_types),
            scratch_shapes=[pltpu.VMEM((length, lanes), jnp.float32)] * scratch,
        ),
        out_shape=[jax.ShapeDtypeStruct((items, length, lanes), kind) for kind in out_types],
        compiler_params=pltpu.CompilerParams(vmem_limit_bytes=VMEM_BYTES),
    )(limits, *arrays)


def core_half(values, dim, core, parts=1):
    size = values.shape[dim]
    shape = values.shape[:dim] + (parts, 2, size // parts // 2) + values.shape[dim + 1 :]
    split = lax.dynamic_index_in_dim(values.reshape(shape), core, dim + 1, keepdims=False)
    return split.reshape(values.shape[:dim] + (size // 2,) + values.shape[dim + 1 :])


def chip_rows(values):
    return values.reshape(-1, values.shape[-1])


def add_low(*terms):
    total = terms[0].astype(jnp.float32)
    for term in terms[1:]:
        total = total + term.astype(jnp.float32)
    return total.astype(jnp.bfloat16)


def reduce_rows(partial_sum):
    items = lax.axis_index("items")
    block = lax.axis_index("blk")
    y_place = items // 2
    x_place = block % 2
    z_place = block // 2
    count, rows, columns = partial_sum.shape
    halves = partial_sum.reshape(count, 2, rows // 2, columns)
    keep = lax.dynamic_index_in_dim(halves, y_place, 1, keepdims=False)
    sent = lax.dynamic_index_in_dim(halves, 1 - y_place, 1, keepdims=False)
    total = add_low(keep, lax.ppermute(sent, "items", Y_SWAP))
    pairs = total.reshape(count // 2, 2, rows // 2, columns)
    keep = lax.dynamic_index_in_dim(pairs, x_place, 1, keepdims=False)
    sent = lax.dynamic_index_in_dim(pairs, 1 - x_place, 1, keepdims=False)
    total = add_low(keep, lax.ppermute(sent, "blk", X_SWAP))
    terms = [lax.dynamic_index_in_dim(total, z_place, 0, keepdims=False)]
    for step in range(1, 4):
        sent = lax.dynamic_index_in_dim(total, (z_place + step) % 4, 0, keepdims=False)
        terms.append(lax.ppermute(sent, "blk", z_turn(step)))
    total = add_low(*terms)
    other = lax.ppermute(total, "items", Y_SWAP)
    first = jnp.where(y_place == 0, total, other)
    second = jnp.where(y_place == 0, other, total)
    return jnp.concatenate([first, second], 0)


def join_cores(half, dim):
    core = lax.axis_index("items") % 2
    other = lax.ppermute(half, "items", CORE_SWAP)
    first = jnp.where(core == 0, half, other).astype(jnp.float32)
    second = jnp.where(core == 0, other, half).astype(jnp.float32)
    return jnp.concatenate([first, second], dim)


def weight_grad(left, right, split_left, blocks):
    core = lax.axis_index("items") % 2
    left = chip_rows(left)
    right = chip_rows(right)
    if split_left:
        left_mine = core_half(left, 1, core, blocks)
        left_sent = core_half(left, 1, 1 - core, blocks)
        right_mine, right_sent = right, right
    else:
        right_mine = core_half(right, 1, core)
        right_sent = core_half(right, 1, 1 - core)
        left_mine, left_sent = left, left
    left_got = lax.ppermute(left_sent, "items", CORE_SWAP)
    right_got = lax.ppermute(right_sent, "items", CORE_SWAP)
    left_all = jnp.concatenate([left_mine, left_got], 0)
    right_all = jnp.concatenate([right_mine, right_got], 0)
    product = contract(left_all, right_all, 0, 0).astype(jnp.bfloat16)
    rows, columns = product.shape
    total = reduce_rows(product.reshape(blocks, rows // blocks, columns))
    return join_cores(total, 0 if split_left else 1)


def fast_device(
    hidden_in,
    text_states,
    frame_lengths,
    text_lengths,
    out_grad,
    attn_in,
    attn_in_bias,
    attn_out,
    attn_out_bias,
    cross_query,
    cross_query_bias,
    cross_kv,
    cross_v_bias,
    cross_out,
    cross_out_bias,
    ff_up,
    ff_up_bias,
    ff_down,
    ff_down_bias,
    norm_gain,
    norm_bias,
):
    seq_count, frames, width = hidden_in.shape
    head_count = HEADS
    head_size = width // head_count
    scale = head_size ** (-0.5)
    text_count = text_states.shape[1]
    blocks = lax.axis_size("blk")
    groups = lax.axis_size("items")
    block_index = lax.axis_index("blk")
    length = frames * blocks
    gains = norm_gain.astype(jnp.float32)
    shifts = norm_bias.astype(jnp.float32)

    def heads_of(values):
        return values.reshape(values.shape[0], values.shape[1], head_count, head_size)

    residual = hidden_in.astype(jnp.float32)
    attn_full, normed_zero, inverse_zero = normalize(residual, gains[0], shifts[0])
    attn_normed = attn_full.astype(jnp.bfloat16)
    qkv_bias = jnp.concatenate(
        [attn_in_bias[:width], jnp.zeros((width,), attn_in_bias.dtype), attn_in_bias[width:]]
    )
    projected = (apply_fwd(attn_normed, attn_in) + qkv_bias).astype(jnp.bfloat16)
    whole_shape = (seq_count, length, LANES)
    queries, keys, values = exchange(
        blocks,
        0,
        [projected] * 3,
        [whole_shape] * 3,
        [(column_block(part * width), row_block(frames)) for part in range(3)],
    )
    mixed, mixed_low, log_total = attention_call(
        attend_kernel,
        frame_lengths,
        [queries, keys, values],
        [jnp.float32, jnp.bfloat16, jnp.float32],
        0,
    )
    frame_shape = (seq_count, frames, width)
    (attended,) = exchange(
        blocks, 1, [mixed_low], [frame_shape], [(row_block(frames), column_block(0))]
    )
    after_self = residual + apply_fwd(attended, attn_out) + attn_out_bias
    cross_full, normed_one, inverse_one = normalize(after_self, gains[1], shifts[1])
    cross_normed = cross_full.astype(jnp.bfloat16)
    cross_queries = (apply_fwd(cross_normed, cross_query) + cross_query_bias).astype(jnp.bfloat16)
    cross_attention_heads = heads_of(cross_queries)
    text_proj = apply_fwd(text_states, cross_kv)
    encoder_key_rows = heads_of(text_proj[..., :width].astype(jnp.bfloat16))
    encoder_value_rows = heads_of((text_proj[..., width:] + cross_v_bias).astype(jnp.bfloat16))
    cross_scores = (
        jnp.einsum(
            "qybj,qzbj->qbyz",
            cross_attention_heads,
            encoder_key_rows,
            preferred_element_type=jnp.float32,
        )
        * scale
    )
    text_mask = (
        jnp.arange(text_count, dtype=jnp.int32)[None, None, None, :]
        < text_lengths[:, None, None, None]
    )
    cross_scores = jnp.where(text_mask, cross_scores, NEG_FILL)
    cross_top = jnp.max(cross_scores, -1, keepdims=True)
    cross_raised = jnp.where(text_mask, jnp.exp(cross_scores - cross_top), 0.0)
    cross_probs = cross_raised / jnp.sum(cross_raised, -1, keepdims=True)
    cross_attention_weights = cross_probs.astype(jnp.bfloat16)
    cross_attended = (
        jnp.einsum(
            "oalx,oxak->olak",
            cross_attention_weights,
            encoder_value_rows,
            preferred_element_type=jnp.float32,
        )
        .reshape(seq_count, frames, width)
        .astype(jnp.bfloat16)
    )
    after_cross = after_self + apply_fwd(cross_attended, cross_out) + cross_out_bias
    ff_full, normed_two, inverse_two = normalize(after_cross, gains[2], shifts[2])
    ff_normed = ff_full.astype(jnp.bfloat16)
    pre_gelu = apply_fwd(ff_normed, ff_up) + ff_up_bias
    activated = jax.nn.gelu(pre_gelu, approximate=False).astype(jnp.bfloat16)
    layer_output = (after_cross + apply_fwd(activated, ff_down) + ff_down_bias).astype(jnp.bfloat16)
    ff_down_grad = weight_grad(activated, out_grad, True, blocks)
    ff_down_bias_grad = column_sum(out_grad)
    act_grad = apply_back(out_grad, ff_down)
    gelu_value, gelu_pull = jax.vjp(partial(jax.nn.gelu, approximate=False), pre_gelu)
    before_gelu_gradient = gelu_pull(act_grad)[0].astype(jnp.bfloat16)
    ff_up_grad = weight_grad(ff_normed, before_gelu_gradient, False, blocks)
    ff_up_bias_grad = column_sum(before_gelu_gradient)
    back_two, gain_two, shift_two = norm_back(
        apply_back(before_gelu_gradient, ff_up), normed_two, inverse_two, gains[2]
    )
    cross_grad = out_grad.astype(jnp.float32) + back_two
    cross_grad_low = cross_grad.astype(jnp.bfloat16)
    cross_out_grad = weight_grad(cross_attended, cross_grad_low, False, blocks)
    cross_out_bias_grad = column_sum(cross_grad_low)
    cross_attention_gradient = heads_of(apply_back(cross_grad_low, cross_out).astype(jnp.bfloat16))
    cross_dp = jnp.einsum(
        "qybj,qzbj->qbyz",
        cross_attention_gradient,
        encoder_value_rows,
        preferred_element_type=jnp.float32,
    )
    cross_logit_gradient = (
        cross_probs * (cross_dp - jnp.sum(cross_probs * cross_dp, -1, keepdims=True))
    ).astype(jnp.bfloat16)
    text_key_part = scale * jnp.einsum(
        "wopc,wpou->wcou",
        cross_logit_gradient,
        cross_attention_heads,
        preferred_element_type=jnp.float32,
    ).reshape(seq_count, text_count, width)
    text_value_part = jnp.einsum(
        "wopc,wpou->wcou",
        cross_attention_weights,
        cross_attention_gradient,
        preferred_element_type=jnp.float32,
    ).reshape(seq_count, text_count, width)
    cross_q_grad = (
        (
            scale
            * jnp.einsum(
                "oalx,oxak->olak",
                cross_logit_gradient,
                encoder_key_rows,
                preferred_element_type=jnp.float32,
            )
        )
        .reshape(seq_count, frames, width)
        .astype(jnp.bfloat16)
    )
    cross_query_grad = weight_grad(cross_normed, cross_q_grad, False, blocks)
    cross_query_bias_grad = column_sum(cross_q_grad)
    back_one, gain_one, shift_one = norm_back(
        apply_back(cross_q_grad, cross_query), normed_one, inverse_one, gains[1]
    )
    self_grad = cross_grad + back_one
    self_grad_low = self_grad.astype(jnp.bfloat16)
    attn_out_grad = weight_grad(attended, self_grad_low, False, blocks)
    attn_out_bias_grad = column_sum(self_grad_low)
    att_grad = apply_back(self_grad_low, attn_out).astype(jnp.bfloat16)
    text_parts_shape = (blocks, seq_count, text_count, LANES)
    mixed_grads, text_key_parts, text_value_parts = exchange(
        blocks,
        2,
        [att_grad, text_key_part.astype(jnp.bfloat16), text_value_part.astype(jnp.bfloat16)],
        [whole_shape, text_parts_shape, text_parts_shape],
        [
            (column_block(0), row_block(frames)),
            (column_block(0), lead_block),
            (column_block(0), lead_block),
        ],
    )
    query_grads, key_grads, value_grads = attention_call(
        attend_back_kernel,
        frame_lengths,
        [queries, keys, values, mixed, log_total, mixed_grads],
        [jnp.bfloat16] * 3,
        2,
    )
    text_key_sum = jnp.sum(text_key_parts.astype(jnp.float32), 0).astype(jnp.bfloat16)
    text_value_sum = jnp.sum(text_value_parts.astype(jnp.float32), 0).astype(jnp.bfloat16)
    text_shape = (seq_count, text_count, width)
    query_low, key_low, value_low, text_key_low, text_value_low = exchange(
        blocks,
        3,
        [query_grads, key_grads, value_grads, text_key_sum, text_value_sum],
        [frame_shape] * 3 + [text_shape] * 2,
        [(row_block(frames), column_block(0))] * 3 + [(whole, column_block(0))] * 2,
    )
    qkv_grad = jnp.concatenate([query_low, key_low, value_low], -1)
    attn_in_grad = weight_grad(attn_normed, qkv_grad, False, blocks)
    back_zero, gain_zero, shift_zero = norm_back(
        apply_back(qkv_grad, attn_in), normed_zero, inverse_zero, gains[0]
    )
    hidden_grad = (self_grad + back_zero).astype(jnp.bfloat16)

    text_kv_low = jnp.concatenate([text_key_low, text_value_low], -1)
    text_grad = jnp.einsum(
        "stf,df->std", text_kv_low, cross_kv, preferred_element_type=jnp.float32
    ).astype(jnp.bfloat16)
    row_share = width // blocks
    text_slice = lax.dynamic_slice_in_dim(text_states, block_index * row_share, row_share, 2)
    cross_kv_rows = jnp.einsum(
        "std,stf->df", text_slice, text_kv_low, preferred_element_type=jnp.float32
    ).astype(jnp.bfloat16)
    value_slice = lax.dynamic_slice_in_dim(text_value_low, block_index * row_share, row_share, 2)
    cross_v_bias_rows = column_sum(value_slice)
    cross_kv_rows = add_low(cross_kv_rows, lax.ppermute(cross_kv_rows, "items", CORE_SWAP))
    cross_kv_grad = cross_kv_rows.astype(jnp.float32) + lax.ppermute(
        cross_kv_rows, "items", Y_SWAP
    ).astype(jnp.float32)

    def by_block(vector):
        return vector.reshape(blocks, -1)

    own_slot = jnp.arange(blocks, dtype=jnp.int32)[:, None] == block_index
    pieces = [
        by_block(jnp.concatenate([column_sum(query_low), column_sum(value_low)])),
        by_block(attn_out_bias_grad),
        by_block(cross_query_bias_grad),
        jnp.where(own_slot, cross_v_bias_rows[None, :], 0.0),
        by_block(cross_out_bias_grad),
        by_block(ff_up_bias_grad),
        by_block(ff_down_bias_grad),
        by_block(gain_zero),
        by_block(gain_one),
        by_block(gain_two),
        by_block(shift_zero),
        by_block(shift_one),
        by_block(shift_two),
    ]
    sizes = [piece.shape[1] for piece in pieces]
    packed = jnp.concatenate(pieces, 1)
    spare = -packed.shape[1] % (8 * LANES)
    packed = jnp.pad(packed, ((0, 0), (0, spare))).reshape(blocks, 8, -1)
    summed = vector_sum(packed, blocks, groups, 4).reshape(-1)
    vectors = []
    start = 0
    for size in sizes:
        vectors.append(summed[start : start + size])
        start += size
    return (
        layer_output,
        hidden_grad,
        text_grad,
        attn_in_grad,
        vectors[0],
        attn_out_grad,
        vectors[1],
        cross_query_grad,
        vectors[2],
        cross_kv_grad,
        vectors[3],
        cross_out_grad,
        vectors[4],
        ff_up_grad,
        vectors[5],
        ff_down_grad,
        vectors[6],
        jnp.stack(vectors[7:10]),
        jnp.stack(vectors[10:13]),
    )


def solution(mesh):
    fast = mesh.shape["items"] == 4 and mesh.shape["blk"] == 8
    placed = (
        P("items", "blk", None),
        P("items", None, None),
        P("items"),
        P("items"),
        P("items", "blk", None),
        P(),
        P(),
        P(),
        P(),
        P(),
        P(),
        P(),
        P(),
        P(),
        P(),
        P(),
        P(),
        P(),
        P(),
        P(),
        P(),
    )
    return jax.shard_map(
        fast_device if fast else general_device,
        mesh=mesh,
        in_specs=placed,
        out_specs=(
            P("items", "blk", None),
            P("items", "blk", None),
            P("items", None, None),
            P("blk", None),
            P("blk"),
            P("blk", None),
            P("blk"),
            P("blk", None),
            P("blk"),
            P("blk", None),
            P("blk"),
            P("blk", None),
            P("blk"),
            P("blk", None),
            P("blk"),
            P("blk", None),
            P("blk"),
            P(None, "blk"),
            P(None, "blk"),
        ),
        check_vma=False,
    )
```

```python
from functools import partial

import jax
import jax.numpy as jnp
from jax import lax
from jax.experimental import pallas as pl
from jax.experimental.pallas import tpu as pltpu
from jax.sharding import PartitionSpec as P

HEADS = 16


NEG_FILL = -1e30


def normalize(values, gain, shift):
    centre = jnp.mean(values, -1, keepdims=True)
    spread = values - centre
    variance = jnp.mean(spread * spread, -1, keepdims=True)
    inverse = lax.rsqrt(variance + 1e-05)
    normed = spread * inverse
    return (normed * gain + shift, normed, inverse)


def norm_back(grad, normed, inverse, gain):
    scaled = grad * gain
    first_mean = jnp.mean(scaled, -1, keepdims=True)
    second_mean = jnp.mean(scaled * normed, -1, keepdims=True)
    return (
        inverse * (scaled - first_mean - normed * second_mean),
        jnp.sum(grad * normed, (0, 1)),
        jnp.sum(grad, (0, 1)),
    )


def outer_sum(left, right):
    return jnp.einsum("sfd,sfe->de", left, right, preferred_element_type=jnp.float32)


def apply_fwd(values, weight):
    return jnp.einsum("sfd,de->sfe", values, weight, preferred_element_type=jnp.float32)


def apply_back(grad, weight):
    return jnp.einsum("sfe,de->sfd", grad, weight, preferred_element_type=jnp.float32)


def column_sum(values):
    return jnp.sum(values.astype(jnp.float32), (0, 1))


def general_device(
    hidden_in,
    text_states,
    frame_lengths,
    text_lengths,
    out_grad,
    attn_in,
    attn_in_bias,
    attn_out,
    attn_out_bias,
    cross_query,
    cross_query_bias,
    cross_kv,
    cross_v_bias,
    cross_out,
    cross_out_bias,
    ff_up,
    ff_up_bias,
    ff_down,
    ff_down_bias,
    norm_gain,
    norm_bias,
):
    seq_count, frames, width = hidden_in.shape
    head_count = HEADS
    head_size = width // head_count
    scale = head_size ** (-0.5)
    text_count = text_states.shape[1]
    axis_count = lax.axis_size("blk")
    block_index = lax.axis_index("blk")
    first_frame = block_index * frames
    last_frame = first_frame + frames - 1
    my_pos = first_frame + jnp.arange(frames, dtype=jnp.int32)
    frame_limit = frame_lengths[:, None, None, None]
    gains = norm_gain.astype(jnp.float32)
    shifts = norm_bias.astype(jnp.float32)

    def visible(key_pos, query_pos):
        return (key_pos[None, None, None, :] <= query_pos[None, None, :, None]) & (
            key_pos[None, None, None, :] < frame_limit
        )

    def heads_of(values):
        return values.reshape(values.shape[0], values.shape[1], head_count, head_size)

    residual = hidden_in.astype(jnp.float32)
    attn_full, normed_zero, inverse_zero = normalize(residual, gains[0], shifts[0])
    attn_normed = attn_full.astype(jnp.bfloat16)
    projected = apply_fwd(attn_normed, attn_in)
    query_rows = (projected[..., :width] + attn_in_bias[:width]).astype(jnp.bfloat16)
    key_rows = projected[..., width : 2 * width].astype(jnp.bfloat16)
    value_rows = (projected[..., 2 * width :] + attn_in_bias[width:]).astype(jnp.bfloat16)
    query_heads = heads_of(query_rows)

    def keep_state(state):
        return state

    start_state = (
        jnp.full((seq_count, head_count, frames), NEG_FILL, jnp.float32),
        jnp.zeros((seq_count, head_count, frames), jnp.float32),
        jnp.zeros((seq_count, head_count, frames, head_size), jnp.float32),
    )
    key_piece = lax.all_gather(key_rows, "blk", axis=1, tiled=True)
    value_piece = lax.all_gather(value_rows, "blk", axis=1, tiled=True)
    span = key_piece.shape[1]

    def forward_compute(state):
        running_max, running_sum, accumulated = state
        key_pos = jnp.arange(span, dtype=jnp.int32)
        scores = (
            jnp.einsum(
                "sfhd,sphd->shfp",
                query_heads,
                heads_of(key_piece),
                preferred_element_type=jnp.float32,
            )
            * scale
        )
        mask = visible(key_pos, my_pos)
        scores = jnp.where(mask, scores, NEG_FILL)
        new_max = jnp.maximum(running_max, jnp.max(scores, -1))
        weights = jnp.where(mask, jnp.exp(scores - new_max[..., None]), 0.0)
        running_sum = jnp.sum(weights, -1)
        accumulated = jnp.einsum(
            "shfp,sphd->shfd",
            weights.astype(jnp.bfloat16),
            heads_of(value_piece),
            preferred_element_type=jnp.float32,
        )
        return (new_max, running_sum, accumulated)

    final_state = lax.cond(jnp.int32(0) > last_frame, keep_state, forward_compute, start_state)
    final_max, final_sum, final_acc = final_state
    log_total = final_max + jnp.log(final_sum)
    attended_full = final_acc / final_sum[..., None]
    attended = (
        jnp.transpose(attended_full, (0, 2, 1, 3))
        .reshape(seq_count, frames, width)
        .astype(jnp.bfloat16)
    )
    after_self = residual + apply_fwd(attended, attn_out) + attn_out_bias
    cross_full, normed_one, inverse_one = normalize(after_self, gains[1], shifts[1])
    cross_normed = cross_full.astype(jnp.bfloat16)
    cross_queries = (apply_fwd(cross_normed, cross_query) + cross_query_bias).astype(jnp.bfloat16)
    cross_attention_heads = heads_of(cross_queries)
    text_proj = apply_fwd(text_states, cross_kv)
    encoder_key_rows = heads_of(text_proj[..., :width].astype(jnp.bfloat16))
    encoder_value_rows = heads_of((text_proj[..., width:] + cross_v_bias).astype(jnp.bfloat16))
    cross_scores = (
        jnp.einsum(
            "qybj,qzbj->qbyz",
            cross_attention_heads,
            encoder_key_rows,
            preferred_element_type=jnp.float32,
        )
        * scale
    )
    text_mask = (
        jnp.arange(text_count, dtype=jnp.int32)[None, None, None, :]
        < text_lengths[:, None, None, None]
    )
    cross_scores = jnp.where(text_mask, cross_scores, NEG_FILL)
    cross_top = jnp.max(cross_scores, -1, keepdims=True)
    cross_raised = jnp.where(text_mask, jnp.exp(cross_scores - cross_top), 0.0)
    cross_probs = cross_raised / jnp.sum(cross_raised, -1, keepdims=True)
    cross_attention_weights = cross_probs.astype(jnp.bfloat16)
    cross_attended = (
        jnp.einsum(
            "oalx,oxak->olak",
            cross_attention_weights,
            encoder_value_rows,
            preferred_element_type=jnp.float32,
        )
        .reshape(seq_count, frames, width)
        .astype(jnp.bfloat16)
    )
    after_cross = after_self + apply_fwd(cross_attended, cross_out) + cross_out_bias
    ff_full, normed_two, inverse_two = normalize(after_cross, gains[2], shifts[2])
    ff_normed = ff_full.astype(jnp.bfloat16)
    pre_gelu = apply_fwd(ff_normed, ff_up) + ff_up_bias
    activated = jax.nn.gelu(pre_gelu, approximate=False).astype(jnp.bfloat16)
    layer_output = (after_cross + apply_fwd(activated, ff_down) + ff_down_bias).astype(jnp.bfloat16)
    ff_down_grad = outer_sum(activated, out_grad)
    ff_down_bias_grad = column_sum(out_grad)
    act_grad = apply_back(out_grad, ff_down)
    gelu_value, gelu_pull = jax.vjp(partial(jax.nn.gelu, approximate=False), pre_gelu)
    before_gelu_gradient = gelu_pull(act_grad)[0].astype(jnp.bfloat16)
    ff_up_grad = outer_sum(ff_normed, before_gelu_gradient)
    ff_up_bias_grad = column_sum(before_gelu_gradient)
    back_two, gain_two, shift_two = norm_back(
        apply_back(before_gelu_gradient, ff_up), normed_two, inverse_two, gains[2]
    )
    cross_grad = out_grad.astype(jnp.float32) + back_two
    cross_grad_low = cross_grad.astype(jnp.bfloat16)
    cross_out_grad = outer_sum(cross_attended, cross_grad_low)
    cross_out_bias_grad = column_sum(cross_grad_low)
    cross_attention_gradient = heads_of(apply_back(cross_grad_low, cross_out).astype(jnp.bfloat16))
    cross_dp = jnp.einsum(
        "qybj,qzbj->qbyz",
        cross_attention_gradient,
        encoder_value_rows,
        preferred_element_type=jnp.float32,
    )
    cross_logit_gradient = (
        cross_probs * (cross_dp - jnp.sum(cross_probs * cross_dp, -1, keepdims=True))
    ).astype(jnp.bfloat16)
    text_key_grad = scale * jnp.einsum(
        "wopc,wpou->wcou",
        cross_logit_gradient,
        cross_attention_heads,
        preferred_element_type=jnp.float32,
    ).reshape(seq_count, text_count, width)
    text_value_grad = jnp.einsum(
        "wopc,wpou->wcou",
        cross_attention_weights,
        cross_attention_gradient,
        preferred_element_type=jnp.float32,
    ).reshape(seq_count, text_count, width)
    text_key_grad, text_value_grad = lax.psum((text_key_grad, text_value_grad), "blk")
    text_kv_low = jnp.concatenate([text_key_grad, text_value_grad], -1).astype(jnp.bfloat16)
    text_grad = jnp.einsum(
        "stf,df->std", text_kv_low, cross_kv, preferred_element_type=jnp.float32
    ).astype(jnp.bfloat16)
    row_share = width // axis_count
    text_slice = lax.dynamic_slice_in_dim(text_states, block_index * row_share, row_share, 2)
    cross_kv_rows = jnp.einsum(
        "std,stf->df", text_slice, text_kv_low, preferred_element_type=jnp.float32
    )
    value_slice = lax.dynamic_slice_in_dim(
        text_kv_low, width + block_index * row_share, row_share, 2
    )
    cross_v_bias_rows = column_sum(value_slice)
    cross_q_grad = (
        (
            scale
            * jnp.einsum(
                "oalx,oxak->olak",
                cross_logit_gradient,
                encoder_key_rows,
                preferred_element_type=jnp.float32,
            )
        )
        .reshape(seq_count, frames, width)
        .astype(jnp.bfloat16)
    )
    cross_query_grad = outer_sum(cross_normed, cross_q_grad)
    cross_query_bias_grad = column_sum(cross_q_grad)
    back_one, gain_one, shift_one = norm_back(
        apply_back(cross_q_grad, cross_query), normed_one, inverse_one, gains[1]
    )
    self_grad = cross_grad + back_one
    self_grad_low = self_grad.astype(jnp.bfloat16)
    attn_out_grad = outer_sum(attended, self_grad_low)
    attn_out_bias_grad = column_sum(self_grad_low)
    att_grad = apply_back(self_grad_low, attn_out).astype(jnp.bfloat16)
    att_heads = heads_of(att_grad)
    delta = jnp.sum(jnp.transpose(att_heads.astype(jnp.float32), (0, 2, 1, 3)) * attended_full, -1)
    query_zero = jnp.zeros((seq_count, frames, head_count, head_size), jnp.float32)
    query_key_piece = lax.all_gather(key_rows, "blk", axis=1, tiled=True)
    query_value_piece = lax.all_gather(value_rows, "blk", axis=1, tiled=True)
    query_span = query_key_piece.shape[1]

    def query_compute(state):
        key_pos = jnp.arange(query_span, dtype=jnp.int32)
        piece_keys = heads_of(query_key_piece)
        scores = (
            jnp.einsum(
                "sfhd,sphd->shfp", query_heads, piece_keys, preferred_element_type=jnp.float32
            )
            * scale
        )
        mask = visible(key_pos, my_pos)
        probs = jnp.where(mask, jnp.exp(scores - log_total[..., None]), 0.0)
        prob_grad = jnp.einsum(
            "sfhd,sphd->shfp",
            att_heads,
            heads_of(query_value_piece),
            preferred_element_type=jnp.float32,
        )
        score_grad = (probs * (prob_grad - delta[..., None])).astype(jnp.bfloat16)
        return scale * jnp.einsum(
            "shfp,sphd->sfhd", score_grad, piece_keys, preferred_element_type=jnp.float32
        )

    query_grad = lax.cond(jnp.int32(0) > last_frame, keep_state, query_compute, query_zero)
    total_logs, total_deltas = (
        lax.all_gather(log_total, "blk", axis=2, tiled=True),
        lax.all_gather(delta, "blk", axis=2, tiled=True),
    )
    my_keys = heads_of(key_rows)
    my_values = heads_of(value_rows)
    query_piece_rows = lax.all_gather(query_rows, "blk", axis=1, tiled=True)
    grad_piece_rows = lax.all_gather(att_grad, "blk", axis=1, tiled=True)
    key_span = query_piece_rows.shape[1]

    def key_compute(state):
        query_pos = jnp.arange(key_span, dtype=jnp.int32)
        piece_queries = heads_of(query_piece_rows)
        piece_grads = heads_of(grad_piece_rows)
        scores = (
            jnp.einsum(
                "sphd,sfhd->shpf", piece_queries, my_keys, preferred_element_type=jnp.float32
            )
            * scale
        )
        mask = visible(my_pos, query_pos)
        probs = jnp.where(mask, jnp.exp(scores - total_logs[..., None]), 0.0)
        value_acc = jnp.einsum(
            "shpf,sphd->sfhd",
            probs.astype(jnp.bfloat16),
            piece_grads,
            preferred_element_type=jnp.float32,
        )
        prob_grad = jnp.einsum(
            "sphd,sfhd->shpf", piece_grads, my_values, preferred_element_type=jnp.float32
        )
        score_grad = (probs * (prob_grad - total_deltas[..., None])).astype(jnp.bfloat16)
        key_acc = scale * jnp.einsum(
            "shpf,sphd->sfhd", score_grad, piece_queries, preferred_element_type=jnp.float32
        )
        return (key_acc, value_acc)

    key_grad, value_grad = lax.cond(
        jnp.int32(0) + key_span - 1 < first_frame, keep_state, key_compute, (query_zero, query_zero)
    )
    query_low = query_grad.reshape(seq_count, frames, width).astype(jnp.bfloat16)
    value_low = value_grad.reshape(seq_count, frames, width).astype(jnp.bfloat16)
    qkv_grad = jnp.concatenate(
        [query_low, key_grad.reshape(seq_count, frames, width).astype(jnp.bfloat16), value_low], -1
    )
    attn_in_grad = outer_sum(attn_normed, qkv_grad)
    attn_in_bias_grad = jnp.concatenate([column_sum(query_low), column_sum(value_low)])
    back_zero, gain_zero, shift_zero = norm_back(
        apply_back(qkv_grad, attn_in), normed_zero, inverse_zero, gains[0]
    )
    hidden_grad = (self_grad + back_zero).astype(jnp.bfloat16)
    gain_grads = jnp.stack([gain_zero, gain_one, gain_two])
    shift_grads = jnp.stack([shift_zero, shift_one, shift_two])
    (
        ain_rows,
        ainb_rows,
        aout_rows,
        aoutb_rows,
        cq_rows,
        cqb_rows,
        cout_rows,
        coutb_rows,
        up_rows,
        up_bias_rows,
        down_rows,
        downb_rows,
        gain_rows,
        shift_rows,
    ) = (
        lax.psum_scatter(attn_in_grad, "blk", scatter_dimension=0, tiled=True),
        lax.psum_scatter(attn_in_bias_grad, "blk", scatter_dimension=0, tiled=True),
        lax.psum_scatter(attn_out_grad, "blk", scatter_dimension=0, tiled=True),
        lax.psum_scatter(attn_out_bias_grad, "blk", scatter_dimension=0, tiled=True),
        lax.psum_scatter(cross_query_grad, "blk", scatter_dimension=0, tiled=True),
        lax.psum_scatter(cross_query_bias_grad, "blk", scatter_dimension=0, tiled=True),
        lax.psum_scatter(cross_out_grad, "blk", scatter_dimension=0, tiled=True),
        lax.psum_scatter(cross_out_bias_grad, "blk", scatter_dimension=0, tiled=True),
        lax.psum_scatter(ff_up_grad, "blk", scatter_dimension=0, tiled=True),
        lax.psum_scatter(ff_up_bias_grad, "blk", scatter_dimension=0, tiled=True),
        lax.psum_scatter(ff_down_grad, "blk", scatter_dimension=0, tiled=True),
        lax.psum_scatter(ff_down_bias_grad, "blk", scatter_dimension=0, tiled=True),
        lax.psum_scatter(gain_grads, "blk", scatter_dimension=1, tiled=True),
        lax.psum_scatter(shift_grads, "blk", scatter_dimension=1, tiled=True),
    )
    summed = (
        lax.psum(ain_rows.astype(jnp.bfloat16), "items").astype(jnp.float32),
        lax.psum(ainb_rows.astype(jnp.bfloat16), "items").astype(jnp.float32),
        lax.psum(aout_rows.astype(jnp.bfloat16), "items").astype(jnp.float32),
        lax.psum(aoutb_rows.astype(jnp.bfloat16), "items").astype(jnp.float32),
        lax.psum(cq_rows.astype(jnp.bfloat16), "items").astype(jnp.float32),
        lax.psum(cqb_rows.astype(jnp.bfloat16), "items").astype(jnp.float32),
        lax.psum(cross_kv_rows.astype(jnp.bfloat16), "items").astype(jnp.float32),
        lax.psum(cross_v_bias_rows.astype(jnp.bfloat16), "items").astype(jnp.float32),
        lax.psum(cout_rows.astype(jnp.bfloat16), "items").astype(jnp.float32),
        lax.psum(coutb_rows.astype(jnp.bfloat16), "items").astype(jnp.float32),
        lax.psum(up_rows.astype(jnp.bfloat16), "items").astype(jnp.float32),
        lax.psum(up_bias_rows.astype(jnp.bfloat16), "items").astype(jnp.float32),
        lax.psum(down_rows.astype(jnp.bfloat16), "items").astype(jnp.float32),
        lax.psum(downb_rows.astype(jnp.bfloat16), "items").astype(jnp.float32),
        lax.psum(gain_rows.astype(jnp.bfloat16), "items").astype(jnp.float32),
        lax.psum(shift_rows.astype(jnp.bfloat16), "items").astype(jnp.float32),
    )
    return (
        layer_output,
        hidden_grad,
        text_grad,
        summed[0],
        summed[1],
        summed[2],
        summed[3],
        summed[4],
        summed[5],
        summed[6],
        summed[7],
        summed[8],
        summed[9],
        summed[10],
        summed[11],
        summed[12],
        summed[13],
        summed[14],
        summed[15],
    )


LANES = 128
MESH_ID = pl.DeviceIdType.MESH
CORE_SWAP = tuple((i, i ^ 1) for i in range(4))
Y_SWAP = tuple((i, i ^ 2) for i in range(4))
VMEM_BYTES = 56 * 1024 * 1024


def contract(left, right, left_dim, right_dim):
    return lax.dot_general(
        left, right, (((left_dim,), (right_dim,)), ((), ())), preferred_element_type=jnp.float32
    )


def exchange_kernel(count, moves, *refs):
    sources = refs[: len(moves)]
    targets = refs[len(moves) : 2 * len(moves)]
    send_sem, recv_sem, own_sem = refs[2 * len(moves) :]
    mine = lax.axis_index("blk")
    barrier = pltpu.get_barrier_semaphore()
    for step in range(1, count):
        pl.semaphore_signal(
            barrier, inc=1, device_id={"blk": lax.rem(mine + step, count)}, device_id_type=MESH_ID
        )
    pl.semaphore_wait(barrier, count - 1)
    copies = []
    for step in range(1, count):
        peer = lax.rem(mine + step, count)
        for index, (cut, place) in enumerate(moves):
            slot = index * count + step
            copy = pltpu.make_async_remote_copy(
                src_ref=cut(sources[index], peer),
                dst_ref=place(targets[index], mine),
                send_sem=send_sem.at[slot],
                recv_sem=recv_sem.at[slot],
                device_id={"blk": peer},
                device_id_type=MESH_ID,
            )
            copy.start()
            copies.append(copy)
    for index, (cut, place) in enumerate(moves):
        copy = pltpu.make_async_copy(
            cut(sources[index], mine), place(targets[index], mine), own_sem.at[index]
        )
        copy.start()
        copies.append(copy)
    for copy in copies:
        copy.wait()


def exchange(count, identity, arrays, shapes, moves):
    outs = [jax.ShapeDtypeStruct(shape, array.dtype) for shape, array in zip(shapes, arrays)]
    return pl.pallas_call(
        partial(exchange_kernel, count, moves),
        out_shape=outs,
        in_specs=[pl.BlockSpec(memory_space=pl.ANY)] * len(arrays),
        out_specs=[pl.BlockSpec(memory_space=pl.ANY)] * len(arrays),
        scratch_shapes=[
            pltpu.SemaphoreType.DMA((len(moves) * count,)),
            pltpu.SemaphoreType.DMA((len(moves) * count,)),
            pltpu.SemaphoreType.DMA((len(moves),)),
        ],
        compiler_params=pltpu.CompilerParams(collective_id=identity, has_side_effects=True),
    )(*arrays)


def column_block(offset):
    def view(ref, index):
        return ref.at[:, :, pl.ds(pl.multiple_of(offset + index * LANES, LANES), LANES)]

    return view


def row_block(rows):
    def view(ref, index):
        return ref.at[:, pl.ds(pl.multiple_of(index * rows, rows), rows), :]

    return view


def lead_block(ref, index):
    return ref.at[index]


def whole(ref, index):
    return ref


def vector_kernel(blocks, groups, in_ref, out_ref, stage, second, send_sem, recv_sem):
    mine = lax.axis_index("blk")
    group = lax.axis_index("items")
    barrier = pltpu.get_barrier_semaphore()
    for step in range(1, blocks):
        pl.semaphore_signal(
            barrier, inc=1, device_id={"blk": lax.rem(mine + step, blocks)}, device_id_type=MESH_ID
        )
    for step in range(1, groups):
        pl.semaphore_signal(
            barrier,
            inc=1,
            device_id={"items": lax.rem(group + step, groups)},
            device_id_type=MESH_ID,
        )
    pl.semaphore_wait(barrier, blocks + groups - 2)
    copies = []
    for step in range(1, blocks):
        peer = lax.rem(mine + step, blocks)
        copy = pltpu.make_async_remote_copy(
            src_ref=in_ref.at[peer],
            dst_ref=stage.at[step],
            send_sem=send_sem.at[step],
            recv_sem=recv_sem.at[step],
            device_id={"blk": peer},
            device_id_type=MESH_ID,
        )
        copy.start()
        copies.append(copy)
    total = in_ref[mine]
    for step, copy in enumerate(copies):
        copy.wait()
        total = total + stage[step + 1]
    second[0] = total
    copies = []
    for step in range(1, groups):
        copy = pltpu.make_async_remote_copy(
            src_ref=second.at[0],
            dst_ref=second.at[step],
            send_sem=send_sem.at[blocks + step],
            recv_sem=recv_sem.at[blocks + step],
            device_id={"items": lax.rem(group + step, groups)},
            device_id_type=MESH_ID,
        )
        copy.start()
        copies.append(copy)
    for step, copy in enumerate(copies):
        copy.wait()
    out_ref[...] = (second[0] + second[1]) + (second[2] + second[3])


def vector_sum(values, blocks, groups, identity):
    _, rows, columns = values.shape
    return pl.pallas_call(
        partial(vector_kernel, blocks, groups),
        out_shape=jax.ShapeDtypeStruct((rows, columns), jnp.float32),
        in_specs=[pl.BlockSpec(memory_space=pltpu.VMEM)],
        out_specs=pl.BlockSpec(memory_space=pltpu.VMEM),
        scratch_shapes=[
            pltpu.VMEM((blocks, rows, columns), jnp.float32),
            pltpu.VMEM((groups, rows, columns), jnp.float32),
            pltpu.SemaphoreType.DMA((blocks + groups,)),
            pltpu.SemaphoreType.DMA((blocks + groups,)),
        ],
        compiler_params=pltpu.CompilerParams(collective_id=identity, has_side_effects=True),
    )(values)


def two_heads(values, low_half):
    none = jnp.zeros_like(values)
    return jnp.concatenate(
        [jnp.where(low_half, values, none), jnp.where(low_half, none, values)], 0
    )


def attend_kernel(rows, head, limit_ref, q_ref, k_ref, v_ref, o_ref, low_ref, lse_ref):
    length = q_ref.shape[1]
    limit = limit_ref[pl.program_id(0)]
    low_half = lax.broadcasted_iota(jnp.int32, (rows, 2 * head), 1) < head
    scale = jnp.bfloat16(head ** (-0.5))
    for block in range(length // rows):
        span = (block + 1) * rows
        here = slice(block * rows, span)
        queries = two_heads(q_ref[0, here, :] * scale, low_half)
        scores = contract(queries, k_ref[0, :span, :], 1, 1)
        query_pos = lax.broadcasted_iota(jnp.int32, (2 * rows, rows), 0) % rows
        key_pos = lax.broadcasted_iota(jnp.int32, (2 * rows, rows), 1)
        corner = jnp.where(key_pos <= query_pos, scores[:, span - rows :], NEG_FILL)
        scores = corner if block == 0 else jnp.concatenate([scores[:, : span - rows], corner], 1)
        if span > length // 2:
            valid = lax.broadcasted_iota(jnp.int32, (1, span), 1) < limit
            scores = scores + jnp.where(valid, 0.0, NEG_FILL)
        top = jnp.max(scores, 1, keepdims=True)
        raised = jnp.exp(scores - top)
        total = jnp.sum(raised, 1, keepdims=True)
        mixed = contract(raised.astype(jnp.bfloat16), v_ref[0, :span, :], 1, 0) / total
        mixed = jnp.where(low_half, mixed[:rows], mixed[rows:])
        o_ref[0, here, :] = mixed
        low_ref[0, here, :] = mixed.astype(jnp.bfloat16)
        log_total = top + jnp.log(total)
        lse_ref[0, here, :] = jnp.where(low_half, log_total[:rows], log_total[rows:])


def attend_back_kernel(
    rows,
    head,
    limit_ref,
    q_ref,
    k_ref,
    v_ref,
    o_ref,
    lse_ref,
    g_ref,
    dq_ref,
    dk_ref,
    dv_ref,
    dk_sum,
    dv_sum,
):
    length = q_ref.shape[1]
    limit = limit_ref[pl.program_id(0)]
    low_half = lax.broadcasted_iota(jnp.int32, (rows, 2 * head), 1) < head
    scale = head ** (-0.5)
    blocks = length // rows
    for block in reversed(range(blocks)):
        span = (block + 1) * rows
        here = slice(block * rows, span)
        queries = two_heads(q_ref[0, here, :] * jnp.bfloat16(scale), low_half)
        grads = two_heads(g_ref[0, here, :], low_half)
        logs = jnp.transpose(lse_ref[0, here, :])
        logs = jnp.concatenate([logs[0:1], logs[head : head + 1]], 1)
        products = jnp.transpose(g_ref[0, here, :].astype(jnp.float32) * o_ref[0, here, :])
        delta = jnp.concatenate(
            [
                jnp.sum(products[:head], 0, keepdims=True),
                jnp.sum(products[head:], 0, keepdims=True),
            ],
            1,
        )
        scores = contract(k_ref[0, :span, :], queries, 1, 1)
        key_pos = lax.broadcasted_iota(jnp.int32, (rows, 2 * rows), 0)
        query_pos = lax.broadcasted_iota(jnp.int32, (rows, 2 * rows), 1) % rows
        corner = jnp.where(key_pos <= query_pos, scores[span - rows :], NEG_FILL)
        scores = corner if block == 0 else jnp.concatenate([scores[: span - rows], corner], 0)
        if span > length // 2:
            valid = lax.broadcasted_iota(jnp.int32, (span, 1), 0) < limit
            scores = scores + jnp.where(valid, 0.0, NEG_FILL)
        probs = jnp.exp(scores - logs)
        prob_grads = contract(v_ref[0, :span, :], grads, 1, 1)
        score_grads = (probs * (prob_grads - delta)).astype(jnp.bfloat16)
        query_grads = scale * contract(score_grads, k_ref[0, :span, :], 0, 0)
        dq_ref[0, here, :] = jnp.where(low_half, query_grads[:rows], query_grads[rows:]).astype(
            jnp.bfloat16
        )
        value_part = contract(probs.astype(jnp.bfloat16), grads, 1, 0)
        key_part = contract(score_grads, queries, 1, 0)
        if block == blocks - 1:
            dv_sum[...] = value_part
            dk_sum[...] = key_part
        else:
            dv_sum[:span] += value_part
            dk_sum[:span] += key_part
    dk_ref[0] = dk_sum[...].astype(jnp.bfloat16)
    dv_ref[0] = dv_sum[...].astype(jnp.bfloat16)


def attention_call(kernel, limits, arrays, out_types, scratch):
    items, length, lanes = arrays[0].shape
    block = pl.BlockSpec((1, length, lanes), lambda item, *_: (item, 0, 0))
    rows = 256 if length % 256 == 0 else length
    return pl.pallas_call(
        partial(kernel, rows, lanes // 2),
        grid_spec=pltpu.PrefetchScalarGridSpec(
            num_scalar_prefetch=1,
            grid=(items,),
            in_specs=[block] * len(arrays),
            out_specs=[block] * len(out_types),
            scratch_shapes=[pltpu.VMEM((length, lanes), jnp.float32)] * scratch,
        ),
        out_shape=[jax.ShapeDtypeStruct((items, length, lanes), kind) for kind in out_types],
        compiler_params=pltpu.CompilerParams(vmem_limit_bytes=VMEM_BYTES),
    )(limits, *arrays)


RING = 8
PIECE = 2 * LANES


def added(*terms):
    total = terms[0].astype(jnp.float32)
    for term in terms[1:]:
        total = total + term.astype(jnp.float32)
    return total.astype(jnp.bfloat16)


def reduce_kernel(plan, first_count, second_count, *refs):
    tensors = len(plan)
    grads = refs[:tensors]
    outs = refs[tensors : 2 * tensors]
    scratch = list(refs[2 * tensors :])
    (own_a, got_a, y_got, y_sum, x_got, x_sum, z_got, z_sum, y_back, a_half, a_back, a_out) = scratch[:12]
    (own_b, got_b, xb_got, xb_sum, zb_got, zb_sum, yb_got, b_half, b_back, b_out) = scratch[12:22]
    send_sem, recv_sem, load_sem, store_sem = scratch[22:]
    items = lax.axis_index("items")
    block = lax.axis_index("blk")
    y, core = items // 2, items % 2
    z, x = block // 2, block % 2
    to_core = {"items": y * 2 + (1 - core)}
    to_y = {"items": (1 - y) * 2 + core}
    to_x = {"blk": z * 2 + (1 - x)}
    z_places = [lax.rem(z + step, 4) for step in range(1, 4)]
    to_z = [{"blk": place * 2 + x} for place in z_places]
    barrier = pltpu.get_barrier_semaphore()
    for peer in [to_core, to_y, to_x] + to_z:
        pl.semaphore_signal(barrier, inc=1, device_id=peer, device_id_type=MESH_ID)
    pl.semaphore_wait(barrier, 6)

    def half_rows(place):
        return pl.ds(pl.multiple_of(place * (LANES // 2), LANES // 2), LANES // 2)

    def remote(kind, slot, source, target, peer):
        return pltpu.make_async_remote_copy(
            src_ref=source,
            dst_ref=target,
            send_sem=send_sem.at[kind, slot],
            recv_sem=recv_sem.at[kind, slot],
            device_id=peer,
            device_id_type=MESH_ID,
        )

    def source_view(tensor, local, half):
        parts = plan[tensor][2]
        column = pl.multiple_of((local // parts) * PIECE + half * LANES, LANES)
        return grads[tensor].at[:, :, local % parts, :, pl.ds(column, LANES)]

    def target_view(tensor, local, half):
        parts = plan[tensor][2]
        column = pl.multiple_of((local // parts) * PIECE + half * LANES, LANES)
        return outs[tensor].at[local % parts, :, pl.ds(column, LANES)]

    def with_tensor(piece, action):
        for tensor, (start, count, _) in enumerate(plan):

            @pl.when((piece >= start) & (piece < start + count))
            def _():
                action(tensor, piece - start)

    def begin(lane, own, got, base):
        def run(index):
            slot = lax.rem(index, RING)

            def start(tensor, local):
                pltpu.make_async_copy(
                    source_view(tensor, local, core), own.at[slot], load_sem.at[lane, slot]
                ).start()
                remote(
                    lane, slot, source_view(tensor, local, 1 - core), got.at[slot], to_core
                ).start()

            with_tensor(base + index, start)

        return run

    def joined(lane, own, got, slot):
        pltpu.make_async_copy(
            source_view(0, 0, core), own.at[slot], load_sem.at[lane, slot]
        ).wait()
        remote(lane, slot, source_view(0, 0, 1 - core), got.at[slot], to_core).wait()
        own[slot] = added(own[slot], got[slot])

    def finish(lane, kind, half, back, out, base):
        def run(index):
            slot = lax.rem(index, RING)
            remote(kind, slot, half.at[slot], back.at[slot], to_core).wait()
            out[slot, core] = half[slot].astype(jnp.float32)
            out[slot, 1 - core] = back[slot].astype(jnp.float32)

            def start(tensor, local):
                for side in range(2):
                    pltpu.make_async_copy(
                        out.at[slot, side],
                        target_view(tensor, local, side),
                        store_sem.at[lane, side, slot],
                    ).start()

            with_tensor(base + index, start)

        return run

    def close(lane, out):
        def run(index):
            slot = lax.rem(index, RING)
            for side in range(2):
                pltpu.make_async_copy(
                    out.at[slot, side], target_view(0, 0, side), store_sem.at[lane, side, slot]
                ).wait()

        return run

    def y_copy(slot):
        return remote(2, slot, own_a.at[slot, :, :, half_rows(1 - y), :], y_got.at[slot], to_y)

    def x_copy(slot):
        return remote(3, slot, y_sum.at[slot, :, 1 - x], x_got.at[slot], to_x)

    def z_copies(slot):
        return [
            remote(4 + k, slot, x_sum.at[slot, z_places[k]], z_got.at[slot, k], to_z[k])
            for k in range(3)
        ]

    def y_return(slot):
        return remote(7, slot, z_sum.at[slot], y_back.at[slot], to_y)

    def a_return(slot):
        return remote(8, slot, a_half.at[slot], a_back.at[slot], to_core)

    def a_one(index):
        slot = lax.rem(index, RING)
        joined(0, own_a, got_a, slot)
        y_copy(slot).start()

    def a_two(index):
        slot = lax.rem(index, RING)
        y_copy(slot).wait()
        y_sum[slot] = added(own_a[slot, :, :, half_rows(y), :], y_got[slot])
        x_copy(slot).start()

    def a_three(index):
        slot = lax.rem(index, RING)
        x_copy(slot).wait()
        x_sum[slot] = added(y_sum[slot, :, x], x_got[slot])
        for copy in z_copies(slot):
            copy.start()

    def a_four(index):
        slot = lax.rem(index, RING)
        for copy in z_copies(slot):
            copy.wait()
        z_sum[slot] = added(x_sum[slot, z], z_got[slot, 0], z_got[slot, 1], z_got[slot, 2])
        y_return(slot).start()

    def a_five(index):
        slot = lax.rem(index, RING)
        y_return(slot).wait()
        a_half[slot, half_rows(y), :] = z_sum[slot]
        a_half[slot, half_rows(1 - y), :] = y_back[slot]
        a_return(slot).start()

    def xb_copy(slot):
        return remote(9, slot, own_b.at[slot, :, 1 - x], xb_got.at[slot], to_x)

    def zb_copies(slot):
        return [
            remote(10 + k, slot, xb_sum.at[slot, z_places[k]], zb_got.at[slot, k], to_z[k])
            for k in range(3)
        ]

    def yb_copy(slot):
        return remote(13, slot, zb_sum.at[slot], yb_got.at[slot], to_y)

    def b_return(slot):
        return remote(14, slot, b_half.at[slot], b_back.at[slot], to_core)

    def b_one(index):
        slot = lax.rem(index, RING)
        joined(1, own_b, got_b, slot)
        xb_copy(slot).start()

    def b_two(index):
        slot = lax.rem(index, RING)
        xb_copy(slot).wait()
        xb_sum[slot] = added(own_b[slot, :, x], xb_got[slot])
        for copy in zb_copies(slot):
            copy.start()

    def b_three(index):
        slot = lax.rem(index, RING)
        for copy in zb_copies(slot):
            copy.wait()
        zb_sum[slot] = added(xb_sum[slot, z], zb_got[slot, 0], zb_got[slot, 1], zb_got[slot, 2])
        yb_copy(slot).start()

    def b_four(index):
        slot = lax.rem(index, RING)
        yb_copy(slot).wait()
        b_half[slot] = added(zb_sum[slot], yb_got[slot])
        b_return(slot).start()

    stages = [
        (0, first_count, begin(0, own_a, got_a, 0)),
        (0, second_count, begin(1, own_b, got_b, first_count)),
        (1, first_count, a_one),
        (1, second_count, b_one),
        (3, first_count, a_two),
        (3, second_count, b_two),
        (5, first_count, a_three),
        (5, second_count, b_three),
        (7, first_count, a_four),
        (7, second_count, b_four),
        (9, first_count, a_five),
        (8, second_count, finish(1, 14, b_half, b_back, b_out, first_count)),
        (10, first_count, finish(0, 8, a_half, a_back, a_out, 0)),
        (10, second_count, close(1, b_out)),
        (12, first_count, close(0, a_out)),
    ]

    def turn(time, carry):
        for lag, count, action in stages:

            @pl.when((time >= lag) & (time < lag + count))
            def _():
                action(time - lag)

        return carry

    lax.fori_loop(0, max(lag + count for lag, count, _ in stages), turn, 0)


def reduce_grads(products, blocks, identity, first_share=0.5):
    plan = []
    start = 0
    arrays = []
    shapes = []
    for product in products:
        rows, columns = product.shape
        parts = rows // blocks // LANES
        count = parts * columns // PIECE
        plan.append((start, count, parts))
        start += count
        arrays.append(product.reshape(blocks // 2, 2, parts, LANES, columns))
        shapes.append(jax.ShapeDtypeStruct((parts, LANES, columns), jnp.float32))
    first_count = int(start * first_share)

    def low(*shape):
        return pltpu.VMEM((RING,) + shape, jnp.bfloat16)

    half = LANES // 2
    first = [
        low(4, 2, LANES, LANES),
        low(4, 2, LANES, LANES),
        low(4, 2, half, LANES),
        low(4, 2, half, LANES),
        low(4, half, LANES),
        low(4, half, LANES),
        low(3, half, LANES),
        low(half, LANES),
        low(half, LANES),
        low(LANES, LANES),
        low(LANES, LANES),
        pltpu.VMEM((RING, 2, LANES, LANES), jnp.float32),
    ]
    second = [
        low(4, 2, LANES, LANES),
        low(4, 2, LANES, LANES),
        low(4, LANES, LANES),
        low(4, LANES, LANES),
        low(3, LANES, LANES),
        low(LANES, LANES),
        low(LANES, LANES),
        low(LANES, LANES),
        low(LANES, LANES),
        pltpu.VMEM((RING, 2, LANES, LANES), jnp.float32),
    ]
    outs = pl.pallas_call(
        partial(reduce_kernel, plan, first_count, start - first_count),
        out_shape=shapes,
        in_specs=[pl.BlockSpec(memory_space=pl.ANY)] * len(arrays),
        out_specs=[pl.BlockSpec(memory_space=pl.ANY)] * len(arrays),
        scratch_shapes=first
        + second
        + [
            pltpu.SemaphoreType.DMA((15, RING)),
            pltpu.SemaphoreType.DMA((15, RING)),
            pltpu.SemaphoreType.DMA((2, RING)),
            pltpu.SemaphoreType.DMA((2, 2, RING)),
        ],
        compiler_params=pltpu.CompilerParams(
            collective_id=identity, has_side_effects=True, vmem_limit_bytes=VMEM_BYTES
        ),
    )(*arrays)
    return [out.reshape(-1, out.shape[-1]) for out in outs]


def product(left, right):
    return contract(
        left.reshape(-1, left.shape[-1]), right.reshape(-1, right.shape[-1]), 0, 0
    ).astype(jnp.bfloat16)


def fast_device(
    hidden_in,
    text_states,
    frame_lengths,
    text_lengths,
    out_grad,
    attn_in,
    attn_in_bias,
    attn_out,
    attn_out_bias,
    cross_query,
    cross_query_bias,
    cross_kv,
    cross_v_bias,
    cross_out,
    cross_out_bias,
    ff_up,
    ff_up_bias,
    ff_down,
    ff_down_bias,
    norm_gain,
    norm_bias,
):
    seq_count, frames, width = hidden_in.shape
    head_count = HEADS
    head_size = width // head_count
    scale = head_size ** (-0.5)
    text_count = text_states.shape[1]
    blocks = lax.axis_size("blk")
    groups = lax.axis_size("items")
    block_index = lax.axis_index("blk")
    length = frames * blocks
    gains = norm_gain.astype(jnp.float32)
    shifts = norm_bias.astype(jnp.float32)

    def heads_of(values):
        return values.reshape(values.shape[0], values.shape[1], head_count, head_size)

    residual = hidden_in.astype(jnp.float32)
    attn_full, normed_zero, inverse_zero = normalize(residual, gains[0], shifts[0])
    attn_normed = attn_full.astype(jnp.bfloat16)
    qkv_bias = jnp.concatenate(
        [attn_in_bias[:width], jnp.zeros((width,), attn_in_bias.dtype), attn_in_bias[width:]]
    )
    projected = (apply_fwd(attn_normed, attn_in) + qkv_bias).astype(jnp.bfloat16)
    whole_shape = (seq_count, length, LANES)
    queries, keys, values = exchange(
        blocks,
        0,
        [projected] * 3,
        [whole_shape] * 3,
        [(column_block(part * width), row_block(frames)) for part in range(3)],
    )
    mixed, mixed_low, log_total = attention_call(
        attend_kernel,
        frame_lengths,
        [queries, keys, values],
        [jnp.float32, jnp.bfloat16, jnp.float32],
        0,
    )
    frame_shape = (seq_count, frames, width)
    (attended,) = exchange(
        blocks, 1, [mixed_low], [frame_shape], [(row_block(frames), column_block(0))]
    )
    after_self = residual + apply_fwd(attended, attn_out) + attn_out_bias
    cross_full, normed_one, inverse_one = normalize(after_self, gains[1], shifts[1])
    cross_normed = cross_full.astype(jnp.bfloat16)
    cross_queries = (apply_fwd(cross_normed, cross_query) + cross_query_bias).astype(jnp.bfloat16)
    cross_attention_heads = heads_of(cross_queries)
    text_proj = apply_fwd(text_states, cross_kv)
    encoder_key_rows = heads_of(text_proj[..., :width].astype(jnp.bfloat16))
    encoder_value_rows = heads_of((text_proj[..., width:] + cross_v_bias).astype(jnp.bfloat16))
    cross_scores = (
        jnp.einsum(
            "qybj,qzbj->qbyz",
            cross_attention_heads,
            encoder_key_rows,
            preferred_element_type=jnp.float32,
        )
        * scale
    )
    text_mask = (
        jnp.arange(text_count, dtype=jnp.int32)[None, None, None, :]
        < text_lengths[:, None, None, None]
    )
    cross_scores = jnp.where(text_mask, cross_scores, NEG_FILL)
    cross_top = jnp.max(cross_scores, -1, keepdims=True)
    cross_raised = jnp.where(text_mask, jnp.exp(cross_scores - cross_top), 0.0)
    cross_probs = cross_raised / jnp.sum(cross_raised, -1, keepdims=True)
    cross_attention_weights = cross_probs.astype(jnp.bfloat16)
    cross_attended = (
        jnp.einsum(
            "oalx,oxak->olak",
            cross_attention_weights,
            encoder_value_rows,
            preferred_element_type=jnp.float32,
        )
        .reshape(seq_count, frames, width)
        .astype(jnp.bfloat16)
    )
    after_cross = after_self + apply_fwd(cross_attended, cross_out) + cross_out_bias
    ff_full, normed_two, inverse_two = normalize(after_cross, gains[2], shifts[2])
    ff_normed = ff_full.astype(jnp.bfloat16)
    pre_gelu = apply_fwd(ff_normed, ff_up) + ff_up_bias
    activated = jax.nn.gelu(pre_gelu, approximate=False).astype(jnp.bfloat16)
    layer_output = (after_cross + apply_fwd(activated, ff_down) + ff_down_bias).astype(jnp.bfloat16)
    ff_down_grad = product(activated, out_grad)
    ff_down_bias_grad = column_sum(out_grad)
    act_grad = apply_back(out_grad, ff_down)
    gelu_value, gelu_pull = jax.vjp(partial(jax.nn.gelu, approximate=False), pre_gelu)
    before_gelu_gradient = gelu_pull(act_grad)[0].astype(jnp.bfloat16)
    ff_up_grad = product(ff_normed, before_gelu_gradient)
    ff_up_bias_grad = column_sum(before_gelu_gradient)
    back_two, gain_two, shift_two = norm_back(
        apply_back(before_gelu_gradient, ff_up), normed_two, inverse_two, gains[2]
    )
    cross_grad = out_grad.astype(jnp.float32) + back_two
    cross_grad_low = cross_grad.astype(jnp.bfloat16)
    cross_out_grad = product(cross_attended, cross_grad_low)
    cross_out_bias_grad = column_sum(cross_grad_low)
    cross_attention_gradient = heads_of(apply_back(cross_grad_low, cross_out).astype(jnp.bfloat16))
    cross_dp = jnp.einsum(
        "qybj,qzbj->qbyz",
        cross_attention_gradient,
        encoder_value_rows,
        preferred_element_type=jnp.float32,
    )
    cross_logit_gradient = (
        cross_probs * (cross_dp - jnp.sum(cross_probs * cross_dp, -1, keepdims=True))
    ).astype(jnp.bfloat16)
    text_key_part = scale * jnp.einsum(
        "wopc,wpou->wcou",
        cross_logit_gradient,
        cross_attention_heads,
        preferred_element_type=jnp.float32,
    ).reshape(seq_count, text_count, width)
    text_value_part = jnp.einsum(
        "wopc,wpou->wcou",
        cross_attention_weights,
        cross_attention_gradient,
        preferred_element_type=jnp.float32,
    ).reshape(seq_count, text_count, width)
    cross_q_grad = (
        (
            scale
            * jnp.einsum(
                "oalx,oxak->olak",
                cross_logit_gradient,
                encoder_key_rows,
                preferred_element_type=jnp.float32,
            )
        )
        .reshape(seq_count, frames, width)
        .astype(jnp.bfloat16)
    )
    cross_query_grad = product(cross_normed, cross_q_grad)
    cross_query_bias_grad = column_sum(cross_q_grad)
    back_one, gain_one, shift_one = norm_back(
        apply_back(cross_q_grad, cross_query), normed_one, inverse_one, gains[1]
    )
    self_grad = cross_grad + back_one
    self_grad_low = self_grad.astype(jnp.bfloat16)
    attn_out_grad = product(attended, self_grad_low)
    attn_out_bias_grad = column_sum(self_grad_low)
    att_grad = apply_back(self_grad_low, attn_out).astype(jnp.bfloat16)
    text_parts_shape = (blocks, seq_count, text_count, LANES)
    mixed_grads, text_key_parts, text_value_parts = exchange(
        blocks,
        2,
        [att_grad, text_key_part.astype(jnp.bfloat16), text_value_part.astype(jnp.bfloat16)],
        [whole_shape, text_parts_shape, text_parts_shape],
        [
            (column_block(0), row_block(frames)),
            (column_block(0), lead_block),
            (column_block(0), lead_block),
        ],
    )
    query_grads, key_grads, value_grads = attention_call(
        attend_back_kernel,
        frame_lengths,
        [queries, keys, values, mixed, log_total, mixed_grads],
        [jnp.bfloat16] * 3,
        2,
    )
    text_key_sum = jnp.sum(text_key_parts.astype(jnp.float32), 0).astype(jnp.bfloat16)
    text_value_sum = jnp.sum(text_value_parts.astype(jnp.float32), 0).astype(jnp.bfloat16)
    text_shape = (seq_count, text_count, width)
    query_low, key_low, value_low, text_key_low, text_value_low = exchange(
        blocks,
        3,
        [query_grads, key_grads, value_grads, text_key_sum, text_value_sum],
        [frame_shape] * 3 + [text_shape] * 2,
        [(row_block(frames), column_block(0))] * 3 + [(whole, column_block(0))] * 2,
    )
    qkv_grad = jnp.concatenate([query_low, key_low, value_low], -1)
    attn_in_grad = product(attn_normed, qkv_grad)
    back_zero, gain_zero, shift_zero = norm_back(
        apply_back(qkv_grad, attn_in), normed_zero, inverse_zero, gains[0]
    )
    hidden_grad = (self_grad + back_zero).astype(jnp.bfloat16)

    (
        attn_in_grad,
        attn_out_grad,
        cross_query_grad,
        cross_out_grad,
        ff_up_grad,
        ff_down_grad,
    ) = reduce_grads(
        [attn_in_grad, attn_out_grad, cross_query_grad, cross_out_grad, ff_up_grad, ff_down_grad],
        blocks,
        5,
    )
    text_kv_low = jnp.concatenate([text_key_low, text_value_low], -1)
    text_grad = jnp.einsum(
        "stf,df->std", text_kv_low, cross_kv, preferred_element_type=jnp.float32
    ).astype(jnp.bfloat16)
    row_share = width // blocks
    text_slice = lax.dynamic_slice_in_dim(text_states, block_index * row_share, row_share, 2)
    cross_kv_rows = jnp.einsum(
        "std,stf->df", text_slice, text_kv_low, preferred_element_type=jnp.float32
    ).astype(jnp.bfloat16)
    value_slice = lax.dynamic_slice_in_dim(text_value_low, block_index * row_share, row_share, 2)
    cross_v_bias_rows = column_sum(value_slice)
    cross_kv_rows = added(cross_kv_rows, lax.ppermute(cross_kv_rows, "items", CORE_SWAP))
    cross_kv_grad = cross_kv_rows.astype(jnp.float32) + lax.ppermute(
        cross_kv_rows, "items", Y_SWAP
    ).astype(jnp.float32)

    def by_block(vector):
        return vector.reshape(blocks, -1)

    own_slot = jnp.arange(blocks, dtype=jnp.int32)[:, None] == block_index
    pieces = [
        by_block(jnp.concatenate([column_sum(query_low), column_sum(value_low)])),
        by_block(attn_out_bias_grad),
        by_block(cross_query_bias_grad),
        jnp.where(own_slot, cross_v_bias_rows[None, :], 0.0),
        by_block(cross_out_bias_grad),
        by_block(ff_up_bias_grad),
        by_block(ff_down_bias_grad),
        by_block(gain_zero),
        by_block(gain_one),
        by_block(gain_two),
        by_block(shift_zero),
        by_block(shift_one),
        by_block(shift_two),
    ]
    sizes = [piece.shape[1] for piece in pieces]
    packed = jnp.concatenate(pieces, 1)
    spare = -packed.shape[1] % (8 * LANES)
    packed = jnp.pad(packed, ((0, 0), (0, spare))).reshape(blocks, 8, -1)
    summed = vector_sum(packed, blocks, groups, 4).reshape(-1)
    vectors = []
    start = 0
    for size in sizes:
        vectors.append(summed[start : start + size])
        start += size
    return (
        layer_output,
        hidden_grad,
        text_grad,
        attn_in_grad,
        vectors[0],
        attn_out_grad,
        vectors[1],
        cross_query_grad,
        vectors[2],
        cross_kv_grad,
        vectors[3],
        cross_out_grad,
        vectors[4],
        ff_up_grad,
        vectors[5],
        ff_down_grad,
        vectors[6],
        jnp.stack(vectors[7:10]),
        jnp.stack(vectors[10:13]),
    )


def solution(mesh):
    fast = mesh.shape["items"] == 4 and mesh.shape["blk"] == 8
    placed = (
        P("items", "blk", None),
        P("items", None, None),
        P("items"),
        P("items"),
        P("items", "blk", None),
        P(),
        P(),
        P(),
        P(),
        P(),
        P(),
        P(),
        P(),
        P(),
        P(),
        P(),
        P(),
        P(),
        P(),
        P(),
        P(),
    )
    return jax.shard_map(
        fast_device if fast else general_device,
        mesh=mesh,
        in_specs=placed,
        out_specs=(
            P("items", "blk", None),
            P("items", "blk", None),
            P("items", None, None),
            P("blk", None),
            P("blk"),
            P("blk", None),
            P("blk"),
            P("blk", None),
            P("blk"),
            P("blk", None),
            P("blk"),
            P("blk", None),
            P("blk"),
            P("blk", None),
            P("blk"),
            P("blk", None),
            P("blk"),
            P(None, "blk"),
            P(None, "blk"),
        ),
        check_vma=False,
    )
```

```python
from functools import partial
from typing import NamedTuple

import jax
import jax.numpy as jnp
from jax import lax
from jax.experimental import pallas as pl
from jax.experimental.pallas import tpu as pltpu
from jax.sharding import PartitionSpec as P

HEADS = 16


NEG_FILL = -1e30


def normalize(values, gain, shift):
    centre = jnp.mean(values, -1, keepdims=True)
    spread = values - centre
    variance = jnp.mean(spread * spread, -1, keepdims=True)
    inverse = lax.rsqrt(variance + 1e-05)
    normed = spread * inverse
    return (normed * gain + shift, normed, inverse)


def norm_back(grad, normed, inverse, gain):
    scaled = grad * gain
    first_mean = jnp.mean(scaled, -1, keepdims=True)
    second_mean = jnp.mean(scaled * normed, -1, keepdims=True)
    return (
        inverse * (scaled - first_mean - normed * second_mean),
        jnp.sum(grad * normed, (0, 1)),
        jnp.sum(grad, (0, 1)),
    )


def outer_sum(left, right):
    return jnp.einsum("sfd,sfe->de", left, right, preferred_element_type=jnp.float32)


def apply_fwd(values, weight):
    return jnp.einsum("sfd,de->sfe", values, weight, preferred_element_type=jnp.float32)


def apply_back(grad, weight):
    return jnp.einsum("sfe,de->sfd", grad, weight, preferred_element_type=jnp.float32)


def column_sum(values):
    return jnp.sum(values.astype(jnp.float32), (0, 1))


def general_device(
    hidden_in,
    text_states,
    frame_lengths,
    text_lengths,
    out_grad,
    attn_in,
    attn_in_bias,
    attn_out,
    attn_out_bias,
    cross_query,
    cross_query_bias,
    cross_kv,
    cross_v_bias,
    cross_out,
    cross_out_bias,
    ff_up,
    ff_up_bias,
    ff_down,
    ff_down_bias,
    norm_gain,
    norm_bias,
):
    seq_count, frames, width = hidden_in.shape
    head_count = HEADS
    head_size = width // head_count
    scale = head_size ** (-0.5)
    text_count = text_states.shape[1]
    axis_count = lax.axis_size("blk")
    block_index = lax.axis_index("blk")
    first_frame = block_index * frames
    last_frame = first_frame + frames - 1
    my_pos = first_frame + jnp.arange(frames, dtype=jnp.int32)
    frame_limit = frame_lengths[:, None, None, None]
    gains = norm_gain.astype(jnp.float32)
    shifts = norm_bias.astype(jnp.float32)

    def visible(key_pos, query_pos):
        return (key_pos[None, None, None, :] <= query_pos[None, None, :, None]) & (
            key_pos[None, None, None, :] < frame_limit
        )

    def heads_of(values):
        return values.reshape(values.shape[0], values.shape[1], head_count, head_size)

    residual = hidden_in.astype(jnp.float32)
    attn_full, normed_zero, inverse_zero = normalize(residual, gains[0], shifts[0])
    attn_normed = attn_full.astype(jnp.bfloat16)
    projected = apply_fwd(attn_normed, attn_in)
    query_rows = (projected[..., :width] + attn_in_bias[:width]).astype(jnp.bfloat16)
    key_rows = projected[..., width : 2 * width].astype(jnp.bfloat16)
    value_rows = (projected[..., 2 * width :] + attn_in_bias[width:]).astype(jnp.bfloat16)
    query_heads = heads_of(query_rows)

    def keep_state(state):
        return state

    start_state = (
        jnp.full((seq_count, head_count, frames), NEG_FILL, jnp.float32),
        jnp.zeros((seq_count, head_count, frames), jnp.float32),
        jnp.zeros((seq_count, head_count, frames, head_size), jnp.float32),
    )
    key_piece = lax.all_gather(key_rows, "blk", axis=1, tiled=True)
    value_piece = lax.all_gather(value_rows, "blk", axis=1, tiled=True)
    span = key_piece.shape[1]

    def forward_compute(state):
        running_max, running_sum, accumulated = state
        key_pos = jnp.arange(span, dtype=jnp.int32)
        scores = (
            jnp.einsum(
                "sfhd,sphd->shfp",
                query_heads,
                heads_of(key_piece),
                preferred_element_type=jnp.float32,
            )
            * scale
        )
        mask = visible(key_pos, my_pos)
        scores = jnp.where(mask, scores, NEG_FILL)
        new_max = jnp.maximum(running_max, jnp.max(scores, -1))
        weights = jnp.where(mask, jnp.exp(scores - new_max[..., None]), 0.0)
        running_sum = jnp.sum(weights, -1)
        accumulated = jnp.einsum(
            "shfp,sphd->shfd",
            weights.astype(jnp.bfloat16),
            heads_of(value_piece),
            preferred_element_type=jnp.float32,
        )
        return (new_max, running_sum, accumulated)

    final_state = lax.cond(jnp.int32(0) > last_frame, keep_state, forward_compute, start_state)
    final_max, final_sum, final_acc = final_state
    log_total = final_max + jnp.log(final_sum)
    attended_full = final_acc / final_sum[..., None]
    attended = (
        jnp.transpose(attended_full, (0, 2, 1, 3))
        .reshape(seq_count, frames, width)
        .astype(jnp.bfloat16)
    )
    after_self = residual + apply_fwd(attended, attn_out) + attn_out_bias
    cross_full, normed_one, inverse_one = normalize(after_self, gains[1], shifts[1])
    cross_normed = cross_full.astype(jnp.bfloat16)
    cross_queries = (apply_fwd(cross_normed, cross_query) + cross_query_bias).astype(jnp.bfloat16)
    cross_attention_heads = heads_of(cross_queries)
    text_proj = apply_fwd(text_states, cross_kv)
    encoder_key_rows = heads_of(text_proj[..., :width].astype(jnp.bfloat16))
    encoder_value_rows = heads_of((text_proj[..., width:] + cross_v_bias).astype(jnp.bfloat16))
    cross_scores = (
        jnp.einsum(
            "qybj,qzbj->qbyz",
            cross_attention_heads,
            encoder_key_rows,
            preferred_element_type=jnp.float32,
        )
        * scale
    )
    text_mask = (
        jnp.arange(text_count, dtype=jnp.int32)[None, None, None, :]
        < text_lengths[:, None, None, None]
    )
    cross_scores = jnp.where(text_mask, cross_scores, NEG_FILL)
    cross_top = jnp.max(cross_scores, -1, keepdims=True)
    cross_raised = jnp.where(text_mask, jnp.exp(cross_scores - cross_top), 0.0)
    cross_probs = cross_raised / jnp.sum(cross_raised, -1, keepdims=True)
    cross_attention_weights = cross_probs.astype(jnp.bfloat16)
    cross_attended = (
        jnp.einsum(
            "oalx,oxak->olak",
            cross_attention_weights,
            encoder_value_rows,
            preferred_element_type=jnp.float32,
        )
        .reshape(seq_count, frames, width)
        .astype(jnp.bfloat16)
    )
    after_cross = after_self + apply_fwd(cross_attended, cross_out) + cross_out_bias
    ff_full, normed_two, inverse_two = normalize(after_cross, gains[2], shifts[2])
    ff_normed = ff_full.astype(jnp.bfloat16)
    pre_gelu = apply_fwd(ff_normed, ff_up) + ff_up_bias
    activated = jax.nn.gelu(pre_gelu, approximate=False).astype(jnp.bfloat16)
    layer_output = (after_cross + apply_fwd(activated, ff_down) + ff_down_bias).astype(jnp.bfloat16)
    ff_down_grad = outer_sum(activated, out_grad)
    ff_down_bias_grad = column_sum(out_grad)
    act_grad = apply_back(out_grad, ff_down)
    gelu_value, gelu_pull = jax.vjp(partial(jax.nn.gelu, approximate=False), pre_gelu)
    before_gelu_gradient = gelu_pull(act_grad)[0].astype(jnp.bfloat16)
    ff_up_grad = outer_sum(ff_normed, before_gelu_gradient)
    ff_up_bias_grad = column_sum(before_gelu_gradient)
    back_two, gain_two, shift_two = norm_back(
        apply_back(before_gelu_gradient, ff_up), normed_two, inverse_two, gains[2]
    )
    cross_grad = out_grad.astype(jnp.float32) + back_two
    cross_grad_low = cross_grad.astype(jnp.bfloat16)
    cross_out_grad = outer_sum(cross_attended, cross_grad_low)
    cross_out_bias_grad = column_sum(cross_grad_low)
    cross_attention_gradient = heads_of(apply_back(cross_grad_low, cross_out).astype(jnp.bfloat16))
    cross_dp = jnp.einsum(
        "qybj,qzbj->qbyz",
        cross_attention_gradient,
        encoder_value_rows,
        preferred_element_type=jnp.float32,
    )
    cross_logit_gradient = (
        cross_probs * (cross_dp - jnp.sum(cross_probs * cross_dp, -1, keepdims=True))
    ).astype(jnp.bfloat16)
    text_key_grad = scale * jnp.einsum(
        "wopc,wpou->wcou",
        cross_logit_gradient,
        cross_attention_heads,
        preferred_element_type=jnp.float32,
    ).reshape(seq_count, text_count, width)
    text_value_grad = jnp.einsum(
        "wopc,wpou->wcou",
        cross_attention_weights,
        cross_attention_gradient,
        preferred_element_type=jnp.float32,
    ).reshape(seq_count, text_count, width)
    text_key_grad, text_value_grad = lax.psum((text_key_grad, text_value_grad), "blk")
    text_kv_low = jnp.concatenate([text_key_grad, text_value_grad], -1).astype(jnp.bfloat16)
    text_grad = jnp.einsum(
        "stf,df->std", text_kv_low, cross_kv, preferred_element_type=jnp.float32
    ).astype(jnp.bfloat16)
    row_share = width // axis_count
    text_slice = lax.dynamic_slice_in_dim(text_states, block_index * row_share, row_share, 2)
    cross_kv_rows = jnp.einsum(
        "std,stf->df", text_slice, text_kv_low, preferred_element_type=jnp.float32
    )
    value_slice = lax.dynamic_slice_in_dim(
        text_kv_low, width + block_index * row_share, row_share, 2
    )
    cross_v_bias_rows = column_sum(value_slice)
    cross_q_grad = (
        (
            scale
            * jnp.einsum(
                "oalx,oxak->olak",
                cross_logit_gradient,
                encoder_key_rows,
                preferred_element_type=jnp.float32,
            )
        )
        .reshape(seq_count, frames, width)
        .astype(jnp.bfloat16)
    )
    cross_query_grad = outer_sum(cross_normed, cross_q_grad)
    cross_query_bias_grad = column_sum(cross_q_grad)
    back_one, gain_one, shift_one = norm_back(
        apply_back(cross_q_grad, cross_query), normed_one, inverse_one, gains[1]
    )
    self_grad = cross_grad + back_one
    self_grad_low = self_grad.astype(jnp.bfloat16)
    attn_out_grad = outer_sum(attended, self_grad_low)
    attn_out_bias_grad = column_sum(self_grad_low)
    att_grad = apply_back(self_grad_low, attn_out).astype(jnp.bfloat16)
    att_heads = heads_of(att_grad)
    delta = jnp.sum(jnp.transpose(att_heads.astype(jnp.float32), (0, 2, 1, 3)) * attended_full, -1)
    query_zero = jnp.zeros((seq_count, frames, head_count, head_size), jnp.float32)
    query_key_piece = lax.all_gather(key_rows, "blk", axis=1, tiled=True)
    query_value_piece = lax.all_gather(value_rows, "blk", axis=1, tiled=True)
    query_span = query_key_piece.shape[1]

    def query_compute(state):
        key_pos = jnp.arange(query_span, dtype=jnp.int32)
        piece_keys = heads_of(query_key_piece)
        scores = (
            jnp.einsum(
                "sfhd,sphd->shfp", query_heads, piece_keys, preferred_element_type=jnp.float32
            )
            * scale
        )
        mask = visible(key_pos, my_pos)
        probs = jnp.where(mask, jnp.exp(scores - log_total[..., None]), 0.0)
        prob_grad = jnp.einsum(
            "sfhd,sphd->shfp",
            att_heads,
            heads_of(query_value_piece),
            preferred_element_type=jnp.float32,
        )
        score_grad = (probs * (prob_grad - delta[..., None])).astype(jnp.bfloat16)
        return scale * jnp.einsum(
            "shfp,sphd->sfhd", score_grad, piece_keys, preferred_element_type=jnp.float32
        )

    query_grad = lax.cond(jnp.int32(0) > last_frame, keep_state, query_compute, query_zero)
    total_logs, total_deltas = (
        lax.all_gather(log_total, "blk", axis=2, tiled=True),
        lax.all_gather(delta, "blk", axis=2, tiled=True),
    )
    my_keys = heads_of(key_rows)
    my_values = heads_of(value_rows)
    query_piece_rows = lax.all_gather(query_rows, "blk", axis=1, tiled=True)
    grad_piece_rows = lax.all_gather(att_grad, "blk", axis=1, tiled=True)
    key_span = query_piece_rows.shape[1]

    def key_compute(state):
        query_pos = jnp.arange(key_span, dtype=jnp.int32)
        piece_queries = heads_of(query_piece_rows)
        piece_grads = heads_of(grad_piece_rows)
        scores = (
            jnp.einsum(
                "sphd,sfhd->shpf", piece_queries, my_keys, preferred_element_type=jnp.float32
            )
            * scale
        )
        mask = visible(my_pos, query_pos)
        probs = jnp.where(mask, jnp.exp(scores - total_logs[..., None]), 0.0)
        value_acc = jnp.einsum(
            "shpf,sphd->sfhd",
            probs.astype(jnp.bfloat16),
            piece_grads,
            preferred_element_type=jnp.float32,
        )
        prob_grad = jnp.einsum(
            "sphd,sfhd->shpf", piece_grads, my_values, preferred_element_type=jnp.float32
        )
        score_grad = (probs * (prob_grad - total_deltas[..., None])).astype(jnp.bfloat16)
        key_acc = scale * jnp.einsum(
            "shpf,sphd->sfhd", score_grad, piece_queries, preferred_element_type=jnp.float32
        )
        return (key_acc, value_acc)

    key_grad, value_grad = lax.cond(
        jnp.int32(0) + key_span - 1 < first_frame, keep_state, key_compute, (query_zero, query_zero)
    )
    query_low = query_grad.reshape(seq_count, frames, width).astype(jnp.bfloat16)
    value_low = value_grad.reshape(seq_count, frames, width).astype(jnp.bfloat16)
    qkv_grad = jnp.concatenate(
        [query_low, key_grad.reshape(seq_count, frames, width).astype(jnp.bfloat16), value_low], -1
    )
    attn_in_grad = outer_sum(attn_normed, qkv_grad)
    attn_in_bias_grad = jnp.concatenate([column_sum(query_low), column_sum(value_low)])
    back_zero, gain_zero, shift_zero = norm_back(
        apply_back(qkv_grad, attn_in), normed_zero, inverse_zero, gains[0]
    )
    hidden_grad = (self_grad + back_zero).astype(jnp.bfloat16)
    gain_grads = jnp.stack([gain_zero, gain_one, gain_two])
    shift_grads = jnp.stack([shift_zero, shift_one, shift_two])
    (
        ain_rows,
        ainb_rows,
        aout_rows,
        aoutb_rows,
        cq_rows,
        cqb_rows,
        cout_rows,
        coutb_rows,
        up_rows,
        up_bias_rows,
        down_rows,
        downb_rows,
        gain_rows,
        shift_rows,
    ) = (
        lax.psum_scatter(attn_in_grad, "blk", scatter_dimension=0, tiled=True),
        lax.psum_scatter(attn_in_bias_grad, "blk", scatter_dimension=0, tiled=True),
        lax.psum_scatter(attn_out_grad, "blk", scatter_dimension=0, tiled=True),
        lax.psum_scatter(attn_out_bias_grad, "blk", scatter_dimension=0, tiled=True),
        lax.psum_scatter(cross_query_grad, "blk", scatter_dimension=0, tiled=True),
        lax.psum_scatter(cross_query_bias_grad, "blk", scatter_dimension=0, tiled=True),
        lax.psum_scatter(cross_out_grad, "blk", scatter_dimension=0, tiled=True),
        lax.psum_scatter(cross_out_bias_grad, "blk", scatter_dimension=0, tiled=True),
        lax.psum_scatter(ff_up_grad, "blk", scatter_dimension=0, tiled=True),
        lax.psum_scatter(ff_up_bias_grad, "blk", scatter_dimension=0, tiled=True),
        lax.psum_scatter(ff_down_grad, "blk", scatter_dimension=0, tiled=True),
        lax.psum_scatter(ff_down_bias_grad, "blk", scatter_dimension=0, tiled=True),
        lax.psum_scatter(gain_grads, "blk", scatter_dimension=1, tiled=True),
        lax.psum_scatter(shift_grads, "blk", scatter_dimension=1, tiled=True),
    )
    summed = (
        lax.psum(ain_rows.astype(jnp.bfloat16), "items").astype(jnp.float32),
        lax.psum(ainb_rows.astype(jnp.bfloat16), "items").astype(jnp.float32),
        lax.psum(aout_rows.astype(jnp.bfloat16), "items").astype(jnp.float32),
        lax.psum(aoutb_rows.astype(jnp.bfloat16), "items").astype(jnp.float32),
        lax.psum(cq_rows.astype(jnp.bfloat16), "items").astype(jnp.float32),
        lax.psum(cqb_rows.astype(jnp.bfloat16), "items").astype(jnp.float32),
        lax.psum(cross_kv_rows.astype(jnp.bfloat16), "items").astype(jnp.float32),
        lax.psum(cross_v_bias_rows.astype(jnp.bfloat16), "items").astype(jnp.float32),
        lax.psum(cout_rows.astype(jnp.bfloat16), "items").astype(jnp.float32),
        lax.psum(coutb_rows.astype(jnp.bfloat16), "items").astype(jnp.float32),
        lax.psum(up_rows.astype(jnp.bfloat16), "items").astype(jnp.float32),
        lax.psum(up_bias_rows.astype(jnp.bfloat16), "items").astype(jnp.float32),
        lax.psum(down_rows.astype(jnp.bfloat16), "items").astype(jnp.float32),
        lax.psum(downb_rows.astype(jnp.bfloat16), "items").astype(jnp.float32),
        lax.psum(gain_rows.astype(jnp.bfloat16), "items").astype(jnp.float32),
        lax.psum(shift_rows.astype(jnp.bfloat16), "items").astype(jnp.float32),
    )
    return (
        layer_output,
        hidden_grad,
        text_grad,
        summed[0],
        summed[1],
        summed[2],
        summed[3],
        summed[4],
        summed[5],
        summed[6],
        summed[7],
        summed[8],
        summed[9],
        summed[10],
        summed[11],
        summed[12],
        summed[13],
        summed[14],
        summed[15],
    )


LANES = 128
MESH_ID = pl.DeviceIdType.MESH
VMEM_BYTES = 56 * 1024 * 1024


def contract(left, right, left_dim, right_dim):
    return lax.dot_general(
        left, right, (((left_dim,), (right_dim,)), ((), ())), preferred_element_type=jnp.float32
    )


def exchange_kernel(count, moves, *refs):
    sources = refs[: len(moves)]
    targets = refs[len(moves) : 2 * len(moves)]
    mine = lax.axis_index("blk")
    barrier = pltpu.get_barrier_semaphore()
    for step in range(1, count):
        pl.semaphore_signal(
            barrier, inc=1, device_id={"blk": lax.rem(mine + step, count)}, device_id_type=MESH_ID
        )
    pl.semaphore_wait(barrier, count - 1)
    copies = exchange_copies(moves, sources, targets, refs[2 * len(moves) :], mine, count)
    for copy in copies:
        copy.start()
    for copy in copies:
        copy.wait()


def exchange_copies(moves, sources, targets, semaphores, mine, count):
    send_sem, recv_sem, own_sem = semaphores
    copies = []
    for step in range(1, count):
        peer = lax.rem(mine + step, count)
        for index, (cut, place) in enumerate(moves):
            slot = index * count + step
            copies.append(
                pltpu.make_async_remote_copy(
                    src_ref=cut(sources[index], peer),
                    dst_ref=place(targets[index], mine),
                    send_sem=send_sem.at[slot],
                    recv_sem=recv_sem.at[slot],
                    device_id={"blk": peer},
                    device_id_type=MESH_ID,
                )
            )
    for index, (cut, place) in enumerate(moves):
        copies.append(
            pltpu.make_async_copy(
                cut(sources[index], mine), place(targets[index], mine), own_sem.at[index]
            )
        )
    return copies


def exchange_semaphores(moves, count):
    return [
        pltpu.SemaphoreType.DMA((len(moves) * count,)),
        pltpu.SemaphoreType.DMA((len(moves) * count,)),
        pltpu.SemaphoreType.DMA((len(moves),)),
    ]


def exchange(count, identity, arrays, shapes, moves):
    outs = [jax.ShapeDtypeStruct(shape, array.dtype) for shape, array in zip(shapes, arrays)]
    return pl.pallas_call(
        partial(exchange_kernel, count, moves),
        out_shape=outs,
        in_specs=[pl.BlockSpec(memory_space=pl.ANY)] * len(arrays),
        out_specs=[pl.BlockSpec(memory_space=pl.ANY)] * len(arrays),
        scratch_shapes=exchange_semaphores(moves, count),
        compiler_params=pltpu.CompilerParams(collective_id=identity, has_side_effects=True),
    )(*arrays)


def column_block(offset):
    def view(ref, index):
        return ref.at[:, :, pl.ds(pl.multiple_of(offset + index * LANES, LANES), LANES)]

    return view


def row_block(rows):
    def view(ref, index):
        return ref.at[:, pl.ds(pl.multiple_of(index * rows, rows), rows), :]

    return view


def lead_block(ref, index):
    return ref.at[index]


def whole(ref, index):
    return ref


def vector_kernel(blocks, groups, in_ref, out_ref, stage, second, send_sem, recv_sem):
    mine = lax.axis_index("blk")
    group = lax.axis_index("items")
    barrier = pltpu.get_barrier_semaphore()
    for step in range(1, blocks):
        pl.semaphore_signal(
            barrier, inc=1, device_id={"blk": lax.rem(mine + step, blocks)}, device_id_type=MESH_ID
        )
    for step in range(1, groups):
        pl.semaphore_signal(
            barrier,
            inc=1,
            device_id={"items": lax.rem(group + step, groups)},
            device_id_type=MESH_ID,
        )
    pl.semaphore_wait(barrier, blocks + groups - 2)
    copies = []
    for step in range(1, blocks):
        peer = lax.rem(mine + step, blocks)
        copy = pltpu.make_async_remote_copy(
            src_ref=in_ref.at[peer],
            dst_ref=stage.at[step],
            send_sem=send_sem.at[step],
            recv_sem=recv_sem.at[step],
            device_id={"blk": peer},
            device_id_type=MESH_ID,
        )
        copy.start()
        copies.append(copy)
    total = in_ref[mine]
    for step, copy in enumerate(copies):
        copy.wait()
        total = total + stage[step + 1]
    second[0] = total
    copies = []
    for step in range(1, groups):
        copy = pltpu.make_async_remote_copy(
            src_ref=second.at[0],
            dst_ref=second.at[step],
            send_sem=send_sem.at[blocks + step],
            recv_sem=recv_sem.at[blocks + step],
            device_id={"items": lax.rem(group + step, groups)},
            device_id_type=MESH_ID,
        )
        copy.start()
        copies.append(copy)
    for step, copy in enumerate(copies):
        copy.wait()
    out_ref[...] = (second[0] + second[1]) + (second[2] + second[3])


def vector_sum(values, blocks, groups, identity):
    _, rows, columns = values.shape
    return pl.pallas_call(
        partial(vector_kernel, blocks, groups),
        out_shape=jax.ShapeDtypeStruct((rows, columns), jnp.float32),
        in_specs=[pl.BlockSpec(memory_space=pltpu.VMEM)],
        out_specs=pl.BlockSpec(memory_space=pltpu.VMEM),
        scratch_shapes=[
            pltpu.VMEM((blocks, rows, columns), jnp.float32),
            pltpu.VMEM((groups, rows, columns), jnp.float32),
            pltpu.SemaphoreType.DMA((blocks + groups,)),
            pltpu.SemaphoreType.DMA((blocks + groups,)),
        ],
        compiler_params=pltpu.CompilerParams(collective_id=identity, has_side_effects=True),
    )(values)


def two_heads(values, low_half):
    none = jnp.zeros_like(values)
    return jnp.concatenate(
        [jnp.where(low_half, values, none), jnp.where(low_half, none, values)], 0
    )


def attend_kernel(rows, head, limit_ref, q_ref, k_ref, v_ref, o_ref, low_ref, lse_ref):
    length = q_ref.shape[1]
    limit = limit_ref[pl.program_id(0)]
    low_half = lax.broadcasted_iota(jnp.int32, (rows, 2 * head), 1) < head
    scale = jnp.bfloat16(head ** (-0.5))
    for block in range(length // rows):
        span = (block + 1) * rows
        here = slice(block * rows, span)
        queries = two_heads(q_ref[0, here, :] * scale, low_half)
        scores = contract(queries, k_ref[0, :span, :], 1, 1)
        query_pos = lax.broadcasted_iota(jnp.int32, (2 * rows, rows), 0) % rows
        key_pos = lax.broadcasted_iota(jnp.int32, (2 * rows, rows), 1)
        corner = jnp.where(key_pos <= query_pos, scores[:, span - rows :], NEG_FILL)
        scores = corner if block == 0 else jnp.concatenate([scores[:, : span - rows], corner], 1)
        if span > length // 2:
            valid = lax.broadcasted_iota(jnp.int32, (1, span), 1) < limit
            scores = scores + jnp.where(valid, 0.0, NEG_FILL)
        top = jnp.max(scores, 1, keepdims=True)
        raised = jnp.exp(scores - top)
        total = jnp.sum(raised, 1, keepdims=True)
        mixed = contract(raised.astype(jnp.bfloat16), v_ref[0, :span, :], 1, 0) / total
        mixed = jnp.where(low_half, mixed[:rows], mixed[rows:])
        o_ref[0, here, :] = mixed
        low_ref[0, here, :] = mixed.astype(jnp.bfloat16)
        log_total = top + jnp.log(total)
        lse_ref[0, here, :] = jnp.where(low_half, log_total[:rows], log_total[rows:])


def attention_call(kernel, limits, arrays, out_types, scratch):
    items, length, lanes = arrays[0].shape
    block = pl.BlockSpec((1, length, lanes), lambda item, *_: (item, 0, 0))
    rows = 256 if length % 256 == 0 else length
    return pl.pallas_call(
        partial(kernel, rows, lanes // 2),
        grid_spec=pltpu.PrefetchScalarGridSpec(
            num_scalar_prefetch=1,
            grid=(items,),
            in_specs=[block] * len(arrays),
            out_specs=[block] * len(out_types),
            scratch_shapes=[pltpu.VMEM((length, lanes), jnp.float32)] * scratch,
        ),
        out_shape=[jax.ShapeDtypeStruct((items, length, lanes), kind) for kind in out_types],
        compiler_params=pltpu.CompilerParams(vmem_limit_bytes=VMEM_BYTES),
    )(limits, *arrays)


LAGS = (0, 1, 5, 11, 20, 24, 25, 27)
FLASH_TURN = 7
TEXT_TURN = 8
SEND_TURNS = (10, 13)
LAND_TURN = 32
EARLY = 32
LATE = 5
SECOND_TURN = 11
ROWS = 256


def added(*terms):
    total = terms[0].astype(jnp.float32)
    for term in terms[1:]:
        total = total + term.astype(jnp.float32)
    return total.astype(jnp.bfloat16)


class Lane(NamedTuple):
    own: object
    got: object
    one_got: object
    one_sum: object
    two_got: object
    two_sum: object
    z_got: object
    z_sum: object
    spread: object
    half: object
    back: object
    out: object
    made: object


class Slots(NamedTuple):
    mixed_grads: object
    query_grads: object
    key_grads: object
    value_grads: object
    key_sum: object
    value_sum: object
    landed: object
    turned: object
    text_parts: object
    text_sums: object
    text_low: object
    matrix: object
    matrix_got: object
    matrix_sum: object
    send_sem: object
    recv_sem: object
    load_sem: object
    store_sem: object
    out_send: object
    out_recv: object
    back_send: object
    back_recv: object
    text_send: object
    text_recv: object
    matrix_send: object
    matrix_recv: object
    save_sem: object


def lane_slots(half, rows_first):
    low = jnp.bfloat16
    one = (4, 2, half, LANES) if rows_first else (4, LANES, LANES)
    return Lane(
        own=pltpu.VMEM((8, 4, 2, LANES, LANES), low),
        got=pltpu.VMEM((4, 4, 2, LANES, LANES), low),
        one_got=pltpu.VMEM((16,) + one, low),
        one_sum=pltpu.VMEM((10,) + one, low),
        two_got=pltpu.VMEM((18, 4, half, LANES), low),
        two_sum=pltpu.VMEM((12, 4, half, LANES), low),
        z_got=pltpu.VMEM((22, 3, half, LANES), low),
        z_sum=pltpu.VMEM((8, half, LANES), low),
        spread=pltpu.VMEM((12, half, LANES), low),
        half=pltpu.VMEM((4, LANES, LANES), low),
        back=pltpu.VMEM((4, LANES, LANES), low),
        out=pltpu.VMEM((4, 2, LANES, LANES), jnp.float32),
        made=pltpu.VMEM((4, 4, 2, LANES, LANES), low),
    )


def rings(text_shape, item_shape, frame_shape, blocks):
    items, length, lanes = item_shape
    low = jnp.bfloat16
    return Slots(
        mixed_grads=pltpu.VMEM(item_shape, low),
        query_grads=pltpu.VMEM(item_shape, low),
        key_grads=pltpu.VMEM(item_shape, low),
        value_grads=pltpu.VMEM(item_shape, low),
        key_sum=pltpu.VMEM((length, lanes), jnp.float32),
        value_sum=pltpu.VMEM((length, lanes), jnp.float32),
        landed=pltpu.VMEM(frame_shape, low),
        turned=pltpu.VMEM((frame_shape[0], frame_shape[2] // 3, frame_shape[1]), low),
        text_parts=pltpu.VMEM((2, blocks) + text_shape, low),
        text_sums=pltpu.VMEM((2,) + text_shape, low),
        text_low=pltpu.VMEM(text_shape[:2] + (2 * blocks * LANES,), low),
        matrix=pltpu.VMEM((2, LANES, blocks * LANES), low),
        matrix_got=pltpu.VMEM((3, LANES, blocks * LANES), low),
        matrix_sum=pltpu.VMEM((2, LANES, blocks * LANES), low),
        send_sem=pltpu.SemaphoreType.DMA((16, 22)),
        recv_sem=pltpu.SemaphoreType.DMA((16, 22)),
        load_sem=pltpu.SemaphoreType.DMA((2, 8)),
        store_sem=pltpu.SemaphoreType.DMA((2, 2, 4)),
        out_send=pltpu.SemaphoreType.DMA((3, blocks)),
        out_recv=pltpu.SemaphoreType.DMA((3, blocks)),
        back_send=pltpu.SemaphoreType.DMA((items, 3, blocks)),
        back_recv=pltpu.SemaphoreType.DMA((items, 3, blocks)),
        text_send=pltpu.SemaphoreType.DMA((2, blocks)),
        text_recv=pltpu.SemaphoreType.DMA((2, blocks)),
        matrix_send=pltpu.SemaphoreType.DMA((3,)),
        matrix_recv=pltpu.SemaphoreType.DMA((3,)),
        save_sem=pltpu.SemaphoreType.DMA((2,)),
    )


def backward_kernel(plan, head, *refs):
    refs = list(refs)

    def take(count):
        taken = refs[:count]
        del refs[:count]
        return taken

    (limit_ref, att_grad, text_key, text_value) = take(4)
    (q_ref, k_ref, v_ref, o_ref, lse_ref, normed_ref, text_ref) = take(7)
    grads = take(len(plan) - 1)
    outs = take(len(plan))
    qkv_out, text_out, matrix_out = take(3)
    lanes_of = [Lane(*take(len(Lane._fields))) for _ in range(2)]
    own = Slots(*refs)
    items, length, lanes = q_ref.shape
    frames = att_grad.shape[1]
    width = att_grad.shape[2]
    blocks = length // frames
    group = lax.axis_index("items")
    block = lax.axis_index("blk")
    y, core = group // 2, group % 2
    z, x = block // 2, block % 2
    to_core = {"items": y * 2 + (1 - core)}
    to_y = {"items": (1 - y) * 2 + core}
    to_x = {"blk": z * 2 + (1 - x)}
    z_places = [lax.rem(z + step, 4) for step in range(1, 4)]
    to_z = [{"blk": place * 2 + x} for place in z_places]
    places = [lax.rem(block + step, blocks) for step in range(blocks)]
    barrier = pltpu.get_barrier_semaphore()
    peers = [to_core, to_y] + [{"blk": place} for place in places[1:]]
    for peer in peers:
        pl.semaphore_signal(barrier, inc=1, device_id=peer, device_id_type=MESH_ID)
    pl.semaphore_wait(barrier, len(peers))

    def at(ring, index):
        return ring.at[lax.rem(index, ring.shape[0])]

    def half_rows(place):
        return pl.ds(pl.multiple_of(place * (LANES // 2), LANES // 2), LANES // 2)

    def lane_block(offset, place):
        return pl.ds(pl.multiple_of(offset + place * LANES, LANES), LANES)

    def frame_rows(place):
        return pl.ds(pl.multiple_of(place * frames, frames), frames)

    def copy_to(peer, source, target, send, recv):
        return pltpu.make_async_remote_copy(
            src_ref=source,
            dst_ref=target,
            send_sem=send,
            recv_sem=recv,
            device_id=peer,
            device_id_type=MESH_ID,
        )

    def remote(kind, got, index, source, peer):
        slot = lax.rem(index, got.shape[0])
        return copy_to(
            peer,
            source,
            got.at[slot],
            own.send_sem.at[kind, slot],
            own.recv_sem.at[kind, slot],
        )

    def source_view(tensor, local, half):
        parts = plan[tensor][2]
        return grads[tensor].at[
            :, :, local % parts, :, lane_block(half * LANES, 2 * (local // parts))
        ]

    def target_view(tensor, local, half):
        parts = plan[tensor][2]
        return outs[tensor].at[local % parts, :, lane_block(half * LANES, 2 * (local // parts))]

    def with_tensor(piece, action):
        for tensor, (start, count, _) in enumerate(plan):

            @pl.when((piece >= start) & (piece < start + count))
            def _():
                action(tensor, piece - start)

    made_start = plan[-1][0]

    def lane_steps(number, lane, base, offset, rows_first):
        def load(index, tensor, local):
            slot = lax.rem(index, lane.own.shape[0])
            return pltpu.make_async_copy(
                source_view(tensor, local, core), lane.own.at[slot], own.load_sem.at[number, slot]
            )

        def send(kind, got, index, source, peer):
            return remote(8 * number + kind, got, index, source, peer)

        def begin(index):
            def start(tensor, local):
                if tensor < len(plan) - 1:
                    load(index, tensor, local).start()
                    send(0, lane.got, index, source_view(tensor, local, 1 - core), to_core).start()
                else:
                    columns = pl.ds(pl.multiple_of(local * 2 * LANES, LANES), 2 * LANES)
                    product = sum(
                        contract(own.turned[item], own.landed[item, :, columns], 1, 0)
                        for item in range(items)
                    )
                    product = product.reshape(4, 2, LANES, 2 * LANES).astype(jnp.bfloat16)
                    sides = (product[..., :LANES], product[..., LANES:])
                    at(lane.own, index)[...] = jnp.where(core == 0, sides[0], sides[1])
                    at(lane.made, index)[...] = jnp.where(core == 0, sides[1], sides[0])
                    send(0, lane.got, index, at(lane.made, index), to_core).start()

            with_tensor(base + index, start)

        def one_copy(index):
            if rows_first:
                source = at(lane.own, index).at[:, :, half_rows(1 - y), :]
                return send(1, lane.one_got, index, source, to_y)
            return send(1, lane.one_got, index, at(lane.own, index).at[:, 1 - x], to_x)

        def two_copy(index):
            if rows_first:
                return send(2, lane.two_got, index, at(lane.one_sum, index).at[:, 1 - x], to_x)
            source = at(lane.one_sum, index).at[:, half_rows(1 - y), :]
            return send(2, lane.two_got, index, source, to_y)

        def z_copies(index):
            slot = lax.rem(index, lane.z_got.shape[0])
            return [
                copy_to(
                    to_z[k],
                    at(lane.two_sum, index).at[z_places[k]],
                    lane.z_got.at[slot, k],
                    own.send_sem.at[8 * number + 3 + k, slot],
                    own.recv_sem.at[8 * number + 3 + k, slot],
                )
                for k in range(3)
            ]

        def spread_copy(index):
            return send(6, lane.spread, index, at(lane.z_sum, index), to_y)

        def back_copy(index):
            return send(7, lane.back, index, at(lane.half, index), to_core)

        def chip(index):
            @pl.when(base + index < made_start)
            def _():
                load(index, 0, 0).wait()

            send(0, lane.got, index, source_view(0, 0, 1 - core), to_core).wait()
            target = at(lane.own, index)
            target[...] = added(target[...], at(lane.got, index)[...])
            one_copy(index).start()

        def one(index):
            one_copy(index).wait()
            kept = at(lane.own, index)
            kept = kept[:, :, half_rows(y), :] if rows_first else kept[:, x]
            at(lane.one_sum, index)[...] = added(kept, at(lane.one_got, index)[...])
            two_copy(index).start()

        def two(index):
            two_copy(index).wait()
            kept = at(lane.one_sum, index)
            kept = kept[:, x] if rows_first else kept[:, half_rows(y), :]
            at(lane.two_sum, index)[...] = added(kept, at(lane.two_got, index)[...])
            for copy in z_copies(index):
                copy.start()

        def three(index):
            for copy in z_copies(index):
                copy.wait()
            terms = at(lane.z_got, index)
            at(lane.z_sum, index)[...] = added(
                at(lane.two_sum, index)[z], terms[0], terms[1], terms[2]
            )
            spread_copy(index).start()

        def four(index):
            spread_copy(index).wait()
            target = at(lane.half, index)
            target[half_rows(y), :] = at(lane.z_sum, index)[...]
            target[half_rows(1 - y), :] = at(lane.spread, index)[...]
            back_copy(index).start()

        def finish(index):
            back_copy(index).wait()
            slot = lax.rem(index, lane.out.shape[0])
            lane.out[slot, core] = at(lane.half, index)[...].astype(jnp.float32)
            lane.out[slot, 1 - core] = at(lane.back, index)[...].astype(jnp.float32)

            def start(tensor, local):
                for side in range(2):
                    pltpu.make_async_copy(
                        lane.out.at[slot, side],
                        target_view(tensor, local, side),
                        own.store_sem.at[number, side, slot],
                    ).start()

            with_tensor(base + index, start)

        def close(index):
            slot = lax.rem(index, lane.out.shape[0])
            for side in range(2):
                pltpu.make_async_copy(
                    lane.out.at[slot, side],
                    target_view(0, 0, side),
                    own.store_sem.at[number, side, slot],
                ).wait()

        return [
            lambda index, step=step: step(index + offset)
            for step in (begin, chip, one, two, three, four, finish, close)
        ]

    def out_copies():
        copies = []
        for step in range(1, blocks):
            ends = [
                (
                    att_grad.at[:, :, lane_block(0, places[step])],
                    own.mixed_grads.at[:, frame_rows(block), :],
                ),
                (
                    text_key.at[:, :, lane_block(0, places[step])],
                    own.text_parts.at[0, step],
                ),
                (
                    text_value.at[:, :, lane_block(0, places[step])],
                    own.text_parts.at[1, step],
                ),
            ]
            for kind, (source, target) in enumerate(ends):
                copies.append(
                    copy_to(
                        {"blk": places[step]},
                        source,
                        target,
                        own.out_send.at[kind, step],
                        own.out_recv.at[kind, step],
                    )
                )
        ends = [
            (att_grad.at[:, :, lane_block(0, block)], own.mixed_grads.at[:, frame_rows(block), :]),
            (text_key.at[:, :, lane_block(0, block)], own.text_parts.at[0, 0]),
            (text_value.at[:, :, lane_block(0, block)], own.text_parts.at[1, 0]),
        ]
        for kind, (source, target) in enumerate(ends):
            copies.append(pltpu.make_async_copy(source, target, own.out_recv.at[kind, 0]))
        return copies

    def out_start(_):
        for copy in out_copies():
            copy.start()

    def out_wait(_):
        for copy in out_copies():
            copy.wait()

    scale = head ** (-0.5)
    flash_blocks = length // ROWS

    def flash_unit(item, number):
        span = (number + 1) * ROWS
        here = slice(number * ROWS, span)
        low_half = lax.broadcasted_iota(jnp.int32, (ROWS, lanes), 1) < head
        queries = two_heads(q_ref[item, here, :] * jnp.bfloat16(scale), low_half)
        mixed_grad = own.mixed_grads[item, here, :]
        mixed_grads = two_heads(mixed_grad, low_half)
        logs = jnp.transpose(lse_ref[item, here, :])
        logs = jnp.concatenate([logs[0:1], logs[head : head + 1]], 1)
        products = jnp.transpose(mixed_grad.astype(jnp.float32) * o_ref[item, here, :])
        delta = jnp.concatenate(
            [
                jnp.sum(products[:head], 0, keepdims=True),
                jnp.sum(products[head:], 0, keepdims=True),
            ],
            1,
        )
        keys = k_ref[item, :span, :]
        scores = contract(keys, queries, 1, 1)
        key_pos = lax.broadcasted_iota(jnp.int32, (ROWS, 2 * ROWS), 0)
        query_pos = lax.broadcasted_iota(jnp.int32, (ROWS, 2 * ROWS), 1) % ROWS
        corner = jnp.where(key_pos <= query_pos, scores[span - ROWS :], NEG_FILL)
        scores = corner if number == 0 else jnp.concatenate([scores[: span - ROWS], corner], 0)
        if span > length // 2:
            valid = lax.broadcasted_iota(jnp.int32, (span, 1), 0) < limit_ref[item]
            scores = scores + jnp.where(valid, 0.0, NEG_FILL)
        probs = jnp.exp(scores - logs)
        prob_grads = contract(v_ref[item, :span, :], mixed_grads, 1, 1)
        score_grads = (probs * (prob_grads - delta)).astype(jnp.bfloat16)
        query_grads = scale * contract(score_grads, keys, 0, 0)
        own.query_grads[item, here, :] = jnp.where(
            low_half, query_grads[:ROWS], query_grads[ROWS:]
        ).astype(jnp.bfloat16)
        value_part = contract(probs.astype(jnp.bfloat16), mixed_grads, 1, 0)
        key_part = contract(score_grads, queries, 1, 0)
        if number == flash_blocks - 1:
            own.value_sum[...] = value_part
            own.key_sum[...] = key_part
        else:
            own.value_sum[:span] += value_part
            own.key_sum[:span] += key_part
        if number == flash_order[-1]:
            own.key_grads[item] = own.key_sum[...].astype(jnp.bfloat16)
            own.value_grads[item] = own.value_sum[...].astype(jnp.bfloat16)

    pairs = flash_blocks // 2
    flash_order = [flash_blocks - 1 - turn if side == 0 else turn for turn in range(pairs) for side in range(2)]

    def flash(index):
        for pair in range(pairs):

            @pl.when(lax.rem(index, pairs) == pair)
            def _():
                for number in flash_order[2 * pair : 2 * pair + 2]:
                    flash_unit(index // pairs, number)

    parts_of = (own.query_grads, own.key_grads, own.value_grads)

    def back_copy(item, part, step):
        place = lax.rem(block + step, blocks)
        return copy_to(
            {"blk": place},
            parts_of[part].at[item, frame_rows(place), :],
            own.landed.at[item, :, lane_block(part * width, block)],
            own.back_send.at[item, part, step],
            own.back_recv.at[item, part, step],
        )

    def back_own(item, part):
        return pltpu.make_async_copy(
            parts_of[part].at[item, frame_rows(block), :],
            own.landed.at[item, :, lane_block(part * width, block)],
            own.back_recv.at[item, part, 0],
        )

    def back_some(item):
        def run(index):
            @pl.when(index == 0)
            def _():
                for part in range(3):
                    back_own(item, part).start()

            for turn in range(2):

                @pl.when(lax.rem(index, 2) == turn)
                def _():
                    for part in range(turn, 1 + 2 * turn):
                        back_copy(item, part, 1 + index // 2).start()

        return run

    def save_copies():
        return [
            pltpu.make_async_copy(own.landed, qkv_out, own.save_sem.at[0]),
            pltpu.make_async_copy(own.text_low, text_out, own.save_sem.at[1]),
        ]

    def back_wait(_):
        for item in range(items):
            for part in range(3):
                back_own(item, part).wait()
                for step in range(1, blocks):
                    back_copy(item, part, step).wait()
            own.turned[item] = jnp.transpose(normed_ref[item])
        for copy in save_copies():
            copy.start()

    def text_copies():
        copies = []
        for part in range(2):
            target = own.text_low.at[:, :, lane_block(part * width, block)]
            source = own.text_sums.at[part]
            for step in range(1, blocks):
                copies.append(
                    copy_to(
                        {"blk": places[step]},
                        source,
                        target,
                        own.text_send.at[part, step],
                        own.text_recv.at[part, step],
                    )
                )
            copies.append(pltpu.make_async_copy(source, target, own.text_recv.at[part, 0]))
        return copies

    def text_sum(_):
        for part in range(2):
            own.text_sums[part] = added(*[own.text_parts[part, step] for step in range(blocks)])
        for copy in text_copies():
            copy.start()

    def matrix_copy(number):
        source = [own.matrix.at[1 - core], own.matrix_sum.at[0], own.matrix_sum.at[1]]
        return copy_to(
            [to_core, to_y, to_core][number],
            source[number],
            own.matrix_got.at[number],
            own.matrix_send.at[number],
            own.matrix_recv.at[number],
        )

    def text_product(_):
        for copy in text_copies():
            copy.wait()
        for side in range(2):
            columns = slice(side * width, (side + 1) * width)
            rows = sum(
                contract(text_ref[item], own.text_low[item, :, columns], 0, 0)
                for item in range(items)
            )
            own.matrix[side] = rows.astype(jnp.bfloat16)
        matrix_copy(0).start()

    def matrix_one(_):
        matrix_copy(0).wait()
        own.matrix_sum[0] = added(own.matrix[core], own.matrix_got[0])
        matrix_copy(1).start()

    def matrix_two(_):
        matrix_copy(1).wait()
        own.matrix_sum[1] = added(own.matrix_sum[0], own.matrix_got[1])
        matrix_copy(2).start()

    def matrix_three(_):
        matrix_copy(2).wait()
        matrix_out[core] = own.matrix_sum[1].astype(jnp.float32)
        matrix_out[1 - core] = own.matrix_got[2].astype(jnp.float32)

    stages = [(0, 1, out_start), (LAND_TURN, 1, back_wait)]
    late = plan[-1][1]
    segments = [
        (0, EARLY, 0, 0, 0),
        (1, made_start - EARLY, 0, EARLY, SECOND_TURN),
        (0, LATE, EARLY, made_start - EARLY, LAND_TURN),
        (1, late - LATE, made_start - EARLY, LATE + EARLY, LAND_TURN),
    ]
    for number, count, offset, base, turn_base in segments:
        steps = lane_steps(number, lanes_of[number], base, offset, number == 0)
        stages += [(turn_base + lag, count, step) for lag, step in zip(LAGS, steps)]
    stages += [
        (FLASH_TURN, 1, out_wait),
        (FLASH_TURN, items * pairs, flash),
        (TEXT_TURN, 1, text_sum),
        (TEXT_TURN + 6, 1, text_product),
        (TEXT_TURN + 8, 1, matrix_one),
        (TEXT_TURN + 16, 1, matrix_two),
        (TEXT_TURN + 18, 1, matrix_three),
    ]
    stages += [
        (turn, 2 * (blocks - 1), back_some(item)) for item, turn in enumerate(SEND_TURNS)
    ]

    def turn(time, carry):
        for lag, count, action in stages:

            @pl.when((time >= lag) & (time < lag + count))
            def _():
                action(time - lag)

        return carry

    lax.fori_loop(0, max(lag + count for lag, count, _ in stages), turn, 0)
    for copy in save_copies():
        copy.wait()


def backward(products, last_columns, blocks, identity, limits, sent, kept):
    plan = []
    start = 0
    arrays = []
    shapes = []
    width = sent[0].shape[2]
    for rows, columns in [product.shape for product in products] + [(width, last_columns)]:
        parts = rows // blocks // LANES
        count = parts * columns // (2 * LANES)
        plan.append((start, count, parts))
        start += count
        shapes.append(jax.ShapeDtypeStruct((parts, LANES, columns), jnp.float32))
    for product, (_, _, parts) in zip(products, plan):
        arrays.append(product.reshape(blocks // 2, 2, parts, LANES, product.shape[1]))
    items, frames, _ = sent[0].shape
    text_count = sent[1].shape[1]
    frame_shape = (items, frames, 3 * width)
    text_shape = (items, text_count, LANES)
    scratch = lane_slots(LANES // 2, True) + lane_slots(LANES // 2, False)
    scratch += rings(text_shape, kept[0].shape, frame_shape, blocks)
    far = pl.BlockSpec(memory_space=pl.ANY)
    near = pl.BlockSpec(memory_space=pltpu.VMEM)
    small = pl.BlockSpec(memory_space=pltpu.SMEM)
    outs = pl.pallas_call(
        partial(
            backward_kernel,
            plan,
            width // HEADS,
        ),
        out_shape=shapes
        + [
            jax.ShapeDtypeStruct(frame_shape, jnp.bfloat16),
            jax.ShapeDtypeStruct((items, text_count, 2 * width), jnp.bfloat16),
            jax.ShapeDtypeStruct((2, LANES, width), jnp.float32),
        ],
        in_specs=[small] + [far] * len(sent) + [near] * len(kept) + [far] * len(arrays),
        out_specs=[far] * (len(shapes) + 2) + [near],
        scratch_shapes=list(scratch),
        compiler_params=pltpu.CompilerParams(
            collective_id=identity, has_side_effects=True, vmem_limit_bytes=VMEM_BYTES
        ),
    )(limits, *sent, *kept, *arrays)
    grads = [out.reshape(-1, out.shape[-1]) for out in outs[: len(shapes)]]
    return grads, outs[len(shapes) :]


def product(left, right):
    return contract(
        left.reshape(-1, left.shape[-1]), right.reshape(-1, right.shape[-1]), 0, 0
    ).astype(jnp.bfloat16)


FF_TILE = 512


class Middle(NamedTuple):
    attn_out: object
    cross_query: object
    cross_out: object
    ff_up: object
    ff_down: object
    layer_output: object
    cross_normed: object
    cross_attended: object
    ff_normed: object
    activated: object
    pre_grad: object
    cross_grad_low: object
    cross_q_grad: object
    self_grad_low: object
    self_grad: object
    att_grad: object
    text_key: object
    text_value: object
    after: object
    normed_one: object
    normed_two: object
    forward_sum: object
    backward_sum: object
    cross_queries: object
    cross_att_grad: object
    probs: object
    load_sem: object
    save_sem: object


def row_norm(values):
    centre = jnp.mean(values, -1, keepdims=True)
    spread = values - centre
    inverse = lax.rsqrt(jnp.mean(spread * spread, -1, keepdims=True) + 1e-05)
    return spread * inverse, inverse


def row_norm_back(grad, normed, inverse, gain):
    scaled = grad * gain
    first_mean = jnp.mean(scaled, -1, keepdims=True)
    second_mean = jnp.mean(scaled * normed, -1, keepdims=True)
    return inverse * (scaled - first_mean - normed * second_mean)


def total_rows(values):
    return jnp.sum(values.astype(jnp.float32), 0, keepdims=True)


def middle_kernel(items, head, *refs):
    refs = list(refs)
    length_ref, hidden, attended, out_grad, text_keys, text_values, small, up_bias = refs[:8]
    weights = refs[8:13]
    saved = refs[13:26]
    sums, up_sums = refs[26:28]
    own = Middle(*refs[28:])
    low = jnp.bfloat16
    rows = hidden.shape[0]
    width = hidden.shape[1]
    frames = rows // items
    text_count = text_keys.shape[0] // items
    pairs = width // (2 * head)
    scale = head ** (-0.5)
    loads = [
        pltpu.make_async_copy(weight, own[number], own.load_sem.at[number])
        for number, weight in enumerate(weights)
    ]
    for load in loads:
        load.start()
    saves = [
        pltpu.make_async_copy(own[5 + number], out, own.save_sem.at[number])
        for number, out in enumerate(saved)
    ]

    def save(*names):
        for name in names:
            saves[Middle._fields.index(name) - 5].start()

    loads[0].wait()
    after_self = (
        hidden[...].astype(jnp.float32)
        + contract(attended[...], own.attn_out[...], 1, 0)
        + small[0:1, :]
    )
    own.after[...] = after_self
    normed, inverse_one = row_norm(after_self)
    own.normed_one[...] = normed
    own.cross_normed[...] = (normed * small[4:5, :] + small[6:7, :]).astype(low)
    loads[1].wait()
    own.cross_queries[...] = (
        contract(own.cross_normed[...], own.cross_query[...], 1, 0) + small[1:2, :]
    ).astype(low)
    low_half = lax.broadcasted_iota(jnp.int32, (frames, 2 * head), 1) < head

    def pair_parts(item, pair):
        return (
            slice(item * frames, (item + 1) * frames),
            slice(item * text_count, (item + 1) * text_count),
            slice(pair * 2 * head, (pair + 1) * 2 * head),
        )

    def joined(values):
        return jnp.where(low_half, values[:frames], values[frames:])

    for item in range(items):
        seen = lax.broadcasted_iota(jnp.int32, (text_count, 1), 0) < length_ref[item]
        for pair in range(pairs):
            here, texts, lanes = pair_parts(item, pair)
            queries = two_heads(own.cross_queries[here, lanes] * low(scale), low_half)
            scores = contract(text_keys[texts, lanes], queries, 1, 1)
            scores = jnp.where(seen, scores, NEG_FILL)
            raised = jnp.exp(scores - jnp.max(scores, 0, keepdims=True))
            raised = jnp.where(seen, raised, 0.0)
            probs = raised / jnp.sum(raised, 0, keepdims=True)
            own.probs[item * pairs + pair] = probs
            mixed = contract(probs.astype(low), text_values[texts, lanes], 0, 0)
            own.cross_attended[here, lanes] = joined(mixed).astype(low)
    loads[2].wait()
    after_cross = (
        own.after[...]
        + contract(own.cross_attended[...], own.cross_out[...], 1, 0)
        + small[2:3, :]
    )
    own.after[...] = after_cross
    normed, inverse_two = row_norm(after_cross)
    own.normed_two[...] = normed
    own.ff_normed[...] = (normed * small[5:6, :] + small[7:8, :]).astype(low)
    save(*"cross_normed cross_attended ff_normed".split())
    loads[3].wait()
    loads[4].wait()
    own.forward_sum[...] = jnp.zeros_like(own.forward_sum)
    own.backward_sum[...] = jnp.zeros_like(own.backward_sum)

    def tile(number, carry):
        here = pl.ds(pl.multiple_of(number * FF_TILE, FF_TILE), FF_TILE)
        pre = contract(own.ff_normed[...], own.ff_up[:, here], 1, 0) + up_bias[:, here]
        act_grad = contract(out_grad[...], own.ff_down[here, :], 1, 1)
        below = 0.5 + 0.5 * lax.erf(pre * (0.5**0.5))
        active = (pre * below).astype(low)
        slope = below + pre * (jnp.exp(-0.5 * pre * pre) * 0.3989422804014327)
        grad = (act_grad * slope).astype(low)
        own.activated[:, here] = active
        own.pre_grad[:, here] = grad
        up_sums[:, here] = total_rows(grad)
        own.forward_sum[...] += contract(active, own.ff_down[here, :], 1, 0)
        own.backward_sum[...] += contract(grad, own.ff_up[:, here], 1, 1)
        return carry

    lax.fori_loop(0, own.ff_up.shape[1] // FF_TILE, tile, 0)
    own.layer_output[...] = (own.after[...] + own.forward_sum[...] + small[3:4, :]).astype(low)
    save(*"layer_output activated pre_grad".split())
    grad = own.backward_sum[...]
    sums[0:1, :] = total_rows(out_grad[...])
    sums[5:6, :] = total_rows(grad * own.normed_two[...])
    sums[7:8, :] = total_rows(grad)
    cross_grad = out_grad[...].astype(jnp.float32) + row_norm_back(
        grad, own.normed_two[...], inverse_two, small[5:6, :]
    )
    own.after[...] = cross_grad
    own.cross_grad_low[...] = cross_grad.astype(low)
    sums[1:2, :] = total_rows(own.cross_grad_low[...])
    own.cross_att_grad[...] = contract(own.cross_grad_low[...], own.cross_out[...], 1, 1).astype(low)
    for item in range(items):
        for pair in range(pairs):
            here, texts, lanes = pair_parts(item, pair)
            grads = two_heads(own.cross_att_grad[here, lanes], low_half)
            queries = two_heads(own.cross_queries[here, lanes] * low(scale), low_half)
            probs = own.probs[item * pairs + pair]
            prob_grads = contract(text_values[texts, lanes], grads, 1, 1)
            score_grads = probs * (prob_grads - jnp.sum(probs * prob_grads, 0, keepdims=True))
            score_grads = score_grads.astype(low)
            own.text_key[texts, lanes] = contract(score_grads, queries, 1, 0).astype(low)
            own.text_value[texts, lanes] = contract(probs.astype(low), grads, 1, 0).astype(low)
            query_grads = scale * contract(score_grads, text_keys[texts, lanes], 0, 0)
            own.cross_q_grad[here, lanes] = joined(query_grads).astype(low)
    save(*"cross_grad_low cross_q_grad text_key text_value".split())
    grad = contract(own.cross_q_grad[...], own.cross_query[...], 1, 1)
    sums[2:3, :] = total_rows(own.cross_q_grad[...])
    sums[4:5, :] = total_rows(grad * own.normed_one[...])
    sums[6:7, :] = total_rows(grad)
    self_grad = own.after[...] + row_norm_back(
        grad, own.normed_one[...], inverse_one, small[4:5, :]
    )
    own.self_grad[...] = self_grad
    own.self_grad_low[...] = self_grad.astype(low)
    sums[3:4, :] = total_rows(own.self_grad_low[...])
    own.att_grad[...] = contract(own.self_grad_low[...], own.attn_out[...], 1, 1).astype(low)
    save(*"self_grad self_grad_low att_grad".split())
    for copy in saves:
        copy.wait()


def middle(lengths, hidden, attended, out_grad, text_keys, text_values, small, up_bias, weights):
    items, frames, width = hidden.shape
    text_count = text_keys.shape[1]
    rows = items * frames
    wide = weights[3].shape[1]
    low = jnp.bfloat16
    full = jnp.float32
    saved = [((rows, width), low)] * 4 + [((rows, wide), low)] * 2 + [((rows, width), low)] * 3
    saved += [((rows, width), full), ((rows, width), low)]
    saved += [((items * text_count, width), low)] * 2
    kept = [((rows, width), full)] * 5 + [((rows, width), low)] * 2
    kept += [((items * HEADS // 2, text_count, 2 * frames), full)]
    near = pl.BlockSpec(memory_space=pltpu.VMEM)
    far = pl.BlockSpec(memory_space=pl.ANY)
    outs = pl.pallas_call(
        partial(middle_kernel, items, width // HEADS),
        out_shape=[jax.ShapeDtypeStruct(shape, kind) for shape, kind in saved]
        + [jax.ShapeDtypeStruct((8, width), full), jax.ShapeDtypeStruct((1, wide), full)],
        in_specs=[pl.BlockSpec(memory_space=pltpu.SMEM)] + [near] * 7 + [far] * 5,
        out_specs=[far] * len(saved) + [near] * 2,
        scratch_shapes=[pltpu.VMEM(weight.shape, weight.dtype) for weight in weights]
        + [pltpu.VMEM(shape, kind) for shape, kind in saved + kept]
        + [pltpu.SemaphoreType.DMA((5,)), pltpu.SemaphoreType.DMA((len(saved),))],
        compiler_params=pltpu.CompilerParams(vmem_limit_bytes=62 * 1024 * 1024),
    )(
        lengths,
        hidden.reshape(rows, width),
        attended.reshape(rows, width),
        out_grad.reshape(rows, width),
        text_keys.reshape(-1, width),
        text_values.reshape(-1, width),
        small,
        up_bias,
        *weights,
    )
    shaped = [
        out.reshape(items, -1, out.shape[1]) for out in outs[: len(saved)]
    ]
    return shaped, outs[len(saved)], outs[len(saved) + 1]


def fast_device(
    hidden_in,
    text_states,
    frame_lengths,
    text_lengths,
    out_grad,
    attn_in,
    attn_in_bias,
    attn_out,
    attn_out_bias,
    cross_query,
    cross_query_bias,
    cross_kv,
    cross_v_bias,
    cross_out,
    cross_out_bias,
    ff_up,
    ff_up_bias,
    ff_down,
    ff_down_bias,
    norm_gain,
    norm_bias,
):
    seq_count, frames, width = hidden_in.shape
    blocks = lax.axis_size("blk")
    block_index = lax.axis_index("blk")
    length = frames * blocks
    gains = norm_gain.astype(jnp.float32)
    shifts = norm_bias.astype(jnp.float32)

    residual = hidden_in.astype(jnp.float32)
    attn_full, normed_zero, inverse_zero = normalize(residual, gains[0], shifts[0])
    attn_normed = attn_full.astype(jnp.bfloat16)
    qkv_bias = jnp.concatenate(
        [attn_in_bias[:width], jnp.zeros((width,), attn_in_bias.dtype), attn_in_bias[width:]]
    )
    projected = (apply_fwd(attn_normed, attn_in) + qkv_bias).astype(jnp.bfloat16)
    whole_shape = (seq_count, length, LANES)
    queries, keys, values = exchange(
        blocks,
        0,
        [projected] * 3,
        [whole_shape] * 3,
        [(column_block(part * width), row_block(frames)) for part in range(3)],
    )
    mixed, mixed_low, log_total = attention_call(
        attend_kernel,
        frame_lengths,
        [queries, keys, values],
        [jnp.float32, jnp.bfloat16, jnp.float32],
        0,
    )
    frame_shape = (seq_count, frames, width)
    (attended,) = exchange(
        blocks, 1, [mixed_low], [frame_shape], [(row_block(frames), column_block(0))]
    )
    text_proj = apply_fwd(text_states, cross_kv)
    text_keys = text_proj[..., :width].astype(jnp.bfloat16)
    text_values = (text_proj[..., width:] + cross_v_bias).astype(jnp.bfloat16)
    small = jnp.concatenate(
        [
            attn_out_bias[None],
            cross_query_bias[None],
            cross_out_bias[None],
            ff_down_bias[None],
            norm_gain[1:],
            norm_bias[1:],
        ]
    ).astype(jnp.float32)
    (
        layer_output,
        cross_normed,
        cross_attended,
        ff_normed,
        activated,
        pre_grad,
        cross_grad_low,
        cross_q_grad,
        self_grad_low,
        self_grad,
        att_grad,
        text_key_part,
        text_value_part,
    ), sums, up_sums = middle(
        text_lengths,
        hidden_in,
        attended,
        out_grad,
        text_keys,
        text_values,
        small,
        ff_up_bias.astype(jnp.float32)[None],
        [attn_out, cross_query, cross_out, ff_up, ff_down],
    )
    ff_down_grad = product(activated, out_grad)
    ff_up_grad = product(ff_normed, pre_grad)
    cross_out_grad = product(cross_attended, cross_grad_low)
    cross_query_grad = product(cross_normed, cross_q_grad)
    attn_out_grad = product(attended, self_grad_low)
    row_share = width // blocks
    text_slice = lax.dynamic_slice_in_dim(text_states, block_index * row_share, row_share, 2)
    (
        attn_out_grad,
        cross_query_grad,
        cross_out_grad,
        ff_up_grad,
        ff_down_grad,
        attn_in_grad,
    ), (qkv_grad, text_kv_low, cross_kv_sides) = backward(
        [attn_out_grad, cross_query_grad, cross_out_grad, ff_up_grad, ff_down_grad],
        attn_in.shape[1],
        blocks,
        2,
        frame_lengths,
        [att_grad, text_key_part, text_value_part],
        [queries, keys, values, mixed, log_total, attn_normed, text_slice],
    )
    cross_kv_grad = jnp.concatenate([cross_kv_sides[0], cross_kv_sides[1]], 1)
    back_zero, gain_zero, shift_zero = norm_back(
        apply_back(qkv_grad, attn_in), normed_zero, inverse_zero, gains[0]
    )
    hidden_grad = (self_grad + back_zero).astype(jnp.bfloat16)

    text_grad = jnp.einsum(
        "stf,df->std", text_kv_low, cross_kv, preferred_element_type=jnp.float32
    ).astype(jnp.bfloat16)
    value_slice = lax.dynamic_slice_in_dim(
        text_kv_low, width + block_index * row_share, row_share, 2
    )
    cross_v_bias_rows = column_sum(value_slice)
    qkv_sum = column_sum(qkv_grad)

    def by_block(vector):
        return vector.reshape(blocks, -1)

    own_slot = jnp.arange(blocks, dtype=jnp.int32)[:, None] == block_index
    pieces = [
        by_block(jnp.concatenate([qkv_sum[:width], qkv_sum[2 * width :]])),
        by_block(sums[3]),
        by_block(sums[2]),
        jnp.where(own_slot, cross_v_bias_rows[None, :], 0.0),
        by_block(sums[1]),
        by_block(up_sums),
        by_block(sums[0]),
        by_block(gain_zero),
        by_block(sums[4]),
        by_block(sums[5]),
        by_block(shift_zero),
        by_block(sums[6]),
        by_block(sums[7]),
    ]
    sizes = [piece.shape[1] for piece in pieces]
    packed = jnp.concatenate(pieces, 1)
    spare = -packed.shape[1] % (8 * LANES)
    packed = jnp.pad(packed, ((0, 0), (0, spare))).reshape(blocks, 8, -1)
    summed = vector_sum(packed, blocks, lax.axis_size("items"), 3).reshape(-1)
    vectors = []
    start = 0
    for size in sizes:
        vectors.append(summed[start : start + size])
        start += size
    return (
        layer_output,
        hidden_grad,
        text_grad,
        attn_in_grad,
        vectors[0],
        attn_out_grad,
        vectors[1],
        cross_query_grad,
        vectors[2],
        cross_kv_grad,
        vectors[3],
        cross_out_grad,
        vectors[4],
        ff_up_grad,
        vectors[5],
        ff_down_grad,
        vectors[6],
        jnp.stack(vectors[7:10]),
        jnp.stack(vectors[10:13]),
    )


def solution(mesh):
    fast = mesh.shape["items"] == 4 and mesh.shape["blk"] == 8
    placed = (
        P("items", "blk", None),
        P("items", None, None),
        P("items"),
        P("items"),
        P("items", "blk", None),
        P(),
        P(),
        P(),
        P(),
        P(),
        P(),
        P(),
        P(),
        P(),
        P(),
        P(),
        P(),
        P(),
        P(),
        P(),
        P(),
    )
    return jax.shard_map(
        fast_device if fast else general_device,
        mesh=mesh,
        in_specs=placed,
        out_specs=(
            P("items", "blk", None),
            P("items", "blk", None),
            P("items", None, None),
            P("blk", None),
            P("blk"),
            P("blk", None),
            P("blk"),
            P("blk", None),
            P("blk"),
            P("blk", None),
            P("blk"),
            P("blk", None),
            P("blk"),
            P("blk", None),
            P("blk"),
            P("blk", None),
            P("blk"),
            P(None, "blk"),
            P(None, "blk"),
        ),
        check_vma=False,
    )
```

```python
from functools import partial
from typing import NamedTuple

import jax
import jax.numpy as jnp
from jax import lax
from jax.experimental import pallas as pl
from jax.experimental.pallas import tpu as pltpu
from jax.sharding import PartitionSpec as P

HEADS = 16


NEG_FILL = -1e30


def normalize(values, gain, shift):
    centre = jnp.mean(values, -1, keepdims=True)
    spread = values - centre
    variance = jnp.mean(spread * spread, -1, keepdims=True)
    inverse = lax.rsqrt(variance + 1e-05)
    normed = spread * inverse
    return (normed * gain + shift, normed, inverse)


def norm_back(grad, normed, inverse, gain):
    scaled = grad * gain
    first_mean = jnp.mean(scaled, -1, keepdims=True)
    second_mean = jnp.mean(scaled * normed, -1, keepdims=True)
    return (
        inverse * (scaled - first_mean - normed * second_mean),
        jnp.sum(grad * normed, (0, 1)),
        jnp.sum(grad, (0, 1)),
    )


def outer_sum(left, right):
    return jnp.einsum("sfd,sfe->de", left, right, preferred_element_type=jnp.float32)


def apply_fwd(values, weight):
    return jnp.einsum("sfd,de->sfe", values, weight, preferred_element_type=jnp.float32)


def apply_back(grad, weight):
    return jnp.einsum("sfe,de->sfd", grad, weight, preferred_element_type=jnp.float32)


def column_sum(values):
    return jnp.sum(values.astype(jnp.float32), (0, 1))


def general_device(
    hidden_in,
    text_states,
    frame_lengths,
    text_lengths,
    out_grad,
    attn_in,
    attn_in_bias,
    attn_out,
    attn_out_bias,
    cross_query,
    cross_query_bias,
    cross_kv,
    cross_v_bias,
    cross_out,
    cross_out_bias,
    ff_up,
    ff_up_bias,
    ff_down,
    ff_down_bias,
    norm_gain,
    norm_bias,
):
    seq_count, frames, width = hidden_in.shape
    head_count = HEADS
    head_size = width // head_count
    scale = head_size ** (-0.5)
    text_count = text_states.shape[1]
    axis_count = lax.axis_size("blk")
    block_index = lax.axis_index("blk")
    first_frame = block_index * frames
    last_frame = first_frame + frames - 1
    my_pos = first_frame + jnp.arange(frames, dtype=jnp.int32)
    frame_limit = frame_lengths[:, None, None, None]
    gains = norm_gain.astype(jnp.float32)
    shifts = norm_bias.astype(jnp.float32)

    def visible(key_pos, query_pos):
        return (key_pos[None, None, None, :] <= query_pos[None, None, :, None]) & (
            key_pos[None, None, None, :] < frame_limit
        )

    def heads_of(values):
        return values.reshape(values.shape[0], values.shape[1], head_count, head_size)

    residual = hidden_in.astype(jnp.float32)
    attn_full, normed_zero, inverse_zero = normalize(residual, gains[0], shifts[0])
    attn_normed = attn_full.astype(jnp.bfloat16)
    projected = apply_fwd(attn_normed, attn_in)
    query_rows = (projected[..., :width] + attn_in_bias[:width]).astype(jnp.bfloat16)
    key_rows = projected[..., width : 2 * width].astype(jnp.bfloat16)
    value_rows = (projected[..., 2 * width :] + attn_in_bias[width:]).astype(jnp.bfloat16)
    query_heads = heads_of(query_rows)

    def keep_state(state):
        return state

    start_state = (
        jnp.full((seq_count, head_count, frames), NEG_FILL, jnp.float32),
        jnp.zeros((seq_count, head_count, frames), jnp.float32),
        jnp.zeros((seq_count, head_count, frames, head_size), jnp.float32),
    )
    key_piece = lax.all_gather(key_rows, "blk", axis=1, tiled=True)
    value_piece = lax.all_gather(value_rows, "blk", axis=1, tiled=True)
    span = key_piece.shape[1]

    def forward_compute(state):
        running_max, running_sum, accumulated = state
        key_pos = jnp.arange(span, dtype=jnp.int32)
        scores = (
            jnp.einsum(
                "sfhd,sphd->shfp",
                query_heads,
                heads_of(key_piece),
                preferred_element_type=jnp.float32,
            )
            * scale
        )
        mask = visible(key_pos, my_pos)
        scores = jnp.where(mask, scores, NEG_FILL)
        new_max = jnp.maximum(running_max, jnp.max(scores, -1))
        weights = jnp.where(mask, jnp.exp(scores - new_max[..., None]), 0.0)
        running_sum = jnp.sum(weights, -1)
        accumulated = jnp.einsum(
            "shfp,sphd->shfd",
            weights.astype(jnp.bfloat16),
            heads_of(value_piece),
            preferred_element_type=jnp.float32,
        )
        return (new_max, running_sum, accumulated)

    final_state = lax.cond(jnp.int32(0) > last_frame, keep_state, forward_compute, start_state)
    final_max, final_sum, final_acc = final_state
    log_total = final_max + jnp.log(final_sum)
    attended_full = final_acc / final_sum[..., None]
    attended = (
        jnp.transpose(attended_full, (0, 2, 1, 3))
        .reshape(seq_count, frames, width)
        .astype(jnp.bfloat16)
    )
    after_self = residual + apply_fwd(attended, attn_out) + attn_out_bias
    cross_full, normed_one, inverse_one = normalize(after_self, gains[1], shifts[1])
    cross_normed = cross_full.astype(jnp.bfloat16)
    cross_queries = (apply_fwd(cross_normed, cross_query) + cross_query_bias).astype(jnp.bfloat16)
    cross_attention_heads = heads_of(cross_queries)
    text_proj = apply_fwd(text_states, cross_kv)
    encoder_key_rows = heads_of(text_proj[..., :width].astype(jnp.bfloat16))
    encoder_value_rows = heads_of((text_proj[..., width:] + cross_v_bias).astype(jnp.bfloat16))
    cross_scores = (
        jnp.einsum(
            "qybj,qzbj->qbyz",
            cross_attention_heads,
            encoder_key_rows,
            preferred_element_type=jnp.float32,
        )
        * scale
    )
    text_mask = (
        jnp.arange(text_count, dtype=jnp.int32)[None, None, None, :]
        < text_lengths[:, None, None, None]
    )
    cross_scores = jnp.where(text_mask, cross_scores, NEG_FILL)
    cross_top = jnp.max(cross_scores, -1, keepdims=True)
    cross_raised = jnp.where(text_mask, jnp.exp(cross_scores - cross_top), 0.0)
    cross_probs = cross_raised / jnp.sum(cross_raised, -1, keepdims=True)
    cross_attention_weights = cross_probs.astype(jnp.bfloat16)
    cross_attended = (
        jnp.einsum(
            "oalx,oxak->olak",
            cross_attention_weights,
            encoder_value_rows,
            preferred_element_type=jnp.float32,
        )
        .reshape(seq_count, frames, width)
        .astype(jnp.bfloat16)
    )
    after_cross = after_self + apply_fwd(cross_attended, cross_out) + cross_out_bias
    ff_full, normed_two, inverse_two = normalize(after_cross, gains[2], shifts[2])
    ff_normed = ff_full.astype(jnp.bfloat16)
    pre_gelu = apply_fwd(ff_normed, ff_up) + ff_up_bias
    activated = jax.nn.gelu(pre_gelu, approximate=False).astype(jnp.bfloat16)
    layer_output = (after_cross + apply_fwd(activated, ff_down) + ff_down_bias).astype(jnp.bfloat16)
    ff_down_grad = outer_sum(activated, out_grad)
    ff_down_bias_grad = column_sum(out_grad)
    act_grad = apply_back(out_grad, ff_down)
    gelu_value, gelu_pull = jax.vjp(partial(jax.nn.gelu, approximate=False), pre_gelu)
    before_gelu_gradient = gelu_pull(act_grad)[0].astype(jnp.bfloat16)
    ff_up_grad = outer_sum(ff_normed, before_gelu_gradient)
    ff_up_bias_grad = column_sum(before_gelu_gradient)
    back_two, gain_two, shift_two = norm_back(
        apply_back(before_gelu_gradient, ff_up), normed_two, inverse_two, gains[2]
    )
    cross_grad = out_grad.astype(jnp.float32) + back_two
    cross_grad_low = cross_grad.astype(jnp.bfloat16)
    cross_out_grad = outer_sum(cross_attended, cross_grad_low)
    cross_out_bias_grad = column_sum(cross_grad_low)
    cross_attention_gradient = heads_of(apply_back(cross_grad_low, cross_out).astype(jnp.bfloat16))
    cross_dp = jnp.einsum(
        "qybj,qzbj->qbyz",
        cross_attention_gradient,
        encoder_value_rows,
        preferred_element_type=jnp.float32,
    )
    cross_logit_gradient = (
        cross_probs * (cross_dp - jnp.sum(cross_probs * cross_dp, -1, keepdims=True))
    ).astype(jnp.bfloat16)
    text_key_grad = scale * jnp.einsum(
        "wopc,wpou->wcou",
        cross_logit_gradient,
        cross_attention_heads,
        preferred_element_type=jnp.float32,
    ).reshape(seq_count, text_count, width)
    text_value_grad = jnp.einsum(
        "wopc,wpou->wcou",
        cross_attention_weights,
        cross_attention_gradient,
        preferred_element_type=jnp.float32,
    ).reshape(seq_count, text_count, width)
    text_key_grad, text_value_grad = lax.psum((text_key_grad, text_value_grad), "blk")
    text_kv_low = jnp.concatenate([text_key_grad, text_value_grad], -1).astype(jnp.bfloat16)
    text_grad = jnp.einsum(
        "stf,df->std", text_kv_low, cross_kv, preferred_element_type=jnp.float32
    ).astype(jnp.bfloat16)
    row_share = width // axis_count
    text_slice = lax.dynamic_slice_in_dim(text_states, block_index * row_share, row_share, 2)
    cross_kv_rows = jnp.einsum(
        "std,stf->df", text_slice, text_kv_low, preferred_element_type=jnp.float32
    )
    value_slice = lax.dynamic_slice_in_dim(
        text_kv_low, width + block_index * row_share, row_share, 2
    )
    cross_v_bias_rows = column_sum(value_slice)
    cross_q_grad = (
        (
            scale
            * jnp.einsum(
                "oalx,oxak->olak",
                cross_logit_gradient,
                encoder_key_rows,
                preferred_element_type=jnp.float32,
            )
        )
        .reshape(seq_count, frames, width)
        .astype(jnp.bfloat16)
    )
    cross_query_grad = outer_sum(cross_normed, cross_q_grad)
    cross_query_bias_grad = column_sum(cross_q_grad)
    back_one, gain_one, shift_one = norm_back(
        apply_back(cross_q_grad, cross_query), normed_one, inverse_one, gains[1]
    )
    self_grad = cross_grad + back_one
    self_grad_low = self_grad.astype(jnp.bfloat16)
    attn_out_grad = outer_sum(attended, self_grad_low)
    attn_out_bias_grad = column_sum(self_grad_low)
    att_grad = apply_back(self_grad_low, attn_out).astype(jnp.bfloat16)
    att_heads = heads_of(att_grad)
    delta = jnp.sum(jnp.transpose(att_heads.astype(jnp.float32), (0, 2, 1, 3)) * attended_full, -1)
    query_zero = jnp.zeros((seq_count, frames, head_count, head_size), jnp.float32)
    query_key_piece = lax.all_gather(key_rows, "blk", axis=1, tiled=True)
    query_value_piece = lax.all_gather(value_rows, "blk", axis=1, tiled=True)
    query_span = query_key_piece.shape[1]

    def query_compute(state):
        key_pos = jnp.arange(query_span, dtype=jnp.int32)
        piece_keys = heads_of(query_key_piece)
        scores = (
            jnp.einsum(
                "sfhd,sphd->shfp", query_heads, piece_keys, preferred_element_type=jnp.float32
            )
            * scale
        )
        mask = visible(key_pos, my_pos)
        probs = jnp.where(mask, jnp.exp(scores - log_total[..., None]), 0.0)
        prob_grad = jnp.einsum(
            "sfhd,sphd->shfp",
            att_heads,
            heads_of(query_value_piece),
            preferred_element_type=jnp.float32,
        )
        score_grad = (probs * (prob_grad - delta[..., None])).astype(jnp.bfloat16)
        return scale * jnp.einsum(
            "shfp,sphd->sfhd", score_grad, piece_keys, preferred_element_type=jnp.float32
        )

    query_grad = lax.cond(jnp.int32(0) > last_frame, keep_state, query_compute, query_zero)
    total_logs, total_deltas = (
        lax.all_gather(log_total, "blk", axis=2, tiled=True),
        lax.all_gather(delta, "blk", axis=2, tiled=True),
    )
    my_keys = heads_of(key_rows)
    my_values = heads_of(value_rows)
    query_piece_rows = lax.all_gather(query_rows, "blk", axis=1, tiled=True)
    grad_piece_rows = lax.all_gather(att_grad, "blk", axis=1, tiled=True)
    key_span = query_piece_rows.shape[1]

    def key_compute(state):
        query_pos = jnp.arange(key_span, dtype=jnp.int32)
        piece_queries = heads_of(query_piece_rows)
        piece_grads = heads_of(grad_piece_rows)
        scores = (
            jnp.einsum(
                "sphd,sfhd->shpf", piece_queries, my_keys, preferred_element_type=jnp.float32
            )
            * scale
        )
        mask = visible(my_pos, query_pos)
        probs = jnp.where(mask, jnp.exp(scores - total_logs[..., None]), 0.0)
        value_acc = jnp.einsum(
            "shpf,sphd->sfhd",
            probs.astype(jnp.bfloat16),
            piece_grads,
            preferred_element_type=jnp.float32,
        )
        prob_grad = jnp.einsum(
            "sphd,sfhd->shpf", piece_grads, my_values, preferred_element_type=jnp.float32
        )
        score_grad = (probs * (prob_grad - total_deltas[..., None])).astype(jnp.bfloat16)
        key_acc = scale * jnp.einsum(
            "shpf,sphd->sfhd", score_grad, piece_queries, preferred_element_type=jnp.float32
        )
        return (key_acc, value_acc)

    key_grad, value_grad = lax.cond(
        jnp.int32(0) + key_span - 1 < first_frame, keep_state, key_compute, (query_zero, query_zero)
    )
    query_low = query_grad.reshape(seq_count, frames, width).astype(jnp.bfloat16)
    value_low = value_grad.reshape(seq_count, frames, width).astype(jnp.bfloat16)
    qkv_grad = jnp.concatenate(
        [query_low, key_grad.reshape(seq_count, frames, width).astype(jnp.bfloat16), value_low], -1
    )
    attn_in_grad = outer_sum(attn_normed, qkv_grad)
    attn_in_bias_grad = jnp.concatenate([column_sum(query_low), column_sum(value_low)])
    back_zero, gain_zero, shift_zero = norm_back(
        apply_back(qkv_grad, attn_in), normed_zero, inverse_zero, gains[0]
    )
    hidden_grad = (self_grad + back_zero).astype(jnp.bfloat16)
    gain_grads = jnp.stack([gain_zero, gain_one, gain_two])
    shift_grads = jnp.stack([shift_zero, shift_one, shift_two])
    (
        ain_rows,
        ainb_rows,
        aout_rows,
        aoutb_rows,
        cq_rows,
        cqb_rows,
        cout_rows,
        coutb_rows,
        up_rows,
        up_bias_rows,
        down_rows,
        downb_rows,
        gain_rows,
        shift_rows,
    ) = (
        lax.psum_scatter(attn_in_grad, "blk", scatter_dimension=0, tiled=True),
        lax.psum_scatter(attn_in_bias_grad, "blk", scatter_dimension=0, tiled=True),
        lax.psum_scatter(attn_out_grad, "blk", scatter_dimension=0, tiled=True),
        lax.psum_scatter(attn_out_bias_grad, "blk", scatter_dimension=0, tiled=True),
        lax.psum_scatter(cross_query_grad, "blk", scatter_dimension=0, tiled=True),
        lax.psum_scatter(cross_query_bias_grad, "blk", scatter_dimension=0, tiled=True),
        lax.psum_scatter(cross_out_grad, "blk", scatter_dimension=0, tiled=True),
        lax.psum_scatter(cross_out_bias_grad, "blk", scatter_dimension=0, tiled=True),
        lax.psum_scatter(ff_up_grad, "blk", scatter_dimension=0, tiled=True),
        lax.psum_scatter(ff_up_bias_grad, "blk", scatter_dimension=0, tiled=True),
        lax.psum_scatter(ff_down_grad, "blk", scatter_dimension=0, tiled=True),
        lax.psum_scatter(ff_down_bias_grad, "blk", scatter_dimension=0, tiled=True),
        lax.psum_scatter(gain_grads, "blk", scatter_dimension=1, tiled=True),
        lax.psum_scatter(shift_grads, "blk", scatter_dimension=1, tiled=True),
    )
    summed = (
        lax.psum(ain_rows.astype(jnp.bfloat16), "items").astype(jnp.float32),
        lax.psum(ainb_rows.astype(jnp.bfloat16), "items").astype(jnp.float32),
        lax.psum(aout_rows.astype(jnp.bfloat16), "items").astype(jnp.float32),
        lax.psum(aoutb_rows.astype(jnp.bfloat16), "items").astype(jnp.float32),
        lax.psum(cq_rows.astype(jnp.bfloat16), "items").astype(jnp.float32),
        lax.psum(cqb_rows.astype(jnp.bfloat16), "items").astype(jnp.float32),
        lax.psum(cross_kv_rows.astype(jnp.bfloat16), "items").astype(jnp.float32),
        lax.psum(cross_v_bias_rows.astype(jnp.bfloat16), "items").astype(jnp.float32),
        lax.psum(cout_rows.astype(jnp.bfloat16), "items").astype(jnp.float32),
        lax.psum(coutb_rows.astype(jnp.bfloat16), "items").astype(jnp.float32),
        lax.psum(up_rows.astype(jnp.bfloat16), "items").astype(jnp.float32),
        lax.psum(up_bias_rows.astype(jnp.bfloat16), "items").astype(jnp.float32),
        lax.psum(down_rows.astype(jnp.bfloat16), "items").astype(jnp.float32),
        lax.psum(downb_rows.astype(jnp.bfloat16), "items").astype(jnp.float32),
        lax.psum(gain_rows.astype(jnp.bfloat16), "items").astype(jnp.float32),
        lax.psum(shift_rows.astype(jnp.bfloat16), "items").astype(jnp.float32),
    )
    return (
        layer_output,
        hidden_grad,
        text_grad,
        summed[0],
        summed[1],
        summed[2],
        summed[3],
        summed[4],
        summed[5],
        summed[6],
        summed[7],
        summed[8],
        summed[9],
        summed[10],
        summed[11],
        summed[12],
        summed[13],
        summed[14],
        summed[15],
    )


LANES = 128
MESH_ID = pl.DeviceIdType.MESH
VMEM_BYTES = 56 * 1024 * 1024


def contract(left, right, left_dim, right_dim):
    return lax.dot_general(
        left, right, (((left_dim,), (right_dim,)), ((), ())), preferred_element_type=jnp.float32
    )


def vector_kernel(blocks, groups, in_ref, out_ref, stage, second, send_sem, recv_sem):
    mine = lax.axis_index("blk")
    group = lax.axis_index("items")
    barrier = pltpu.get_barrier_semaphore()
    for step in range(1, blocks):
        pl.semaphore_signal(
            barrier, inc=1, device_id={"blk": lax.rem(mine + step, blocks)}, device_id_type=MESH_ID
        )
    for step in range(1, groups):
        pl.semaphore_signal(
            barrier,
            inc=1,
            device_id={"items": lax.rem(group + step, groups)},
            device_id_type=MESH_ID,
        )
    pl.semaphore_wait(barrier, blocks + groups - 2)
    copies = []
    for step in range(1, blocks):
        peer = lax.rem(mine + step, blocks)
        copy = pltpu.make_async_remote_copy(
            src_ref=in_ref.at[peer],
            dst_ref=stage.at[step],
            send_sem=send_sem.at[step],
            recv_sem=recv_sem.at[step],
            device_id={"blk": peer},
            device_id_type=MESH_ID,
        )
        copy.start()
        copies.append(copy)
    total = in_ref[mine]
    for step, copy in enumerate(copies):
        copy.wait()
        total = total + stage[step + 1]
    second[0] = total
    copies = []
    for step in range(1, groups):
        copy = pltpu.make_async_remote_copy(
            src_ref=second.at[0],
            dst_ref=second.at[step],
            send_sem=send_sem.at[blocks + step],
            recv_sem=recv_sem.at[blocks + step],
            device_id={"items": lax.rem(group + step, groups)},
            device_id_type=MESH_ID,
        )
        copy.start()
        copies.append(copy)
    for step, copy in enumerate(copies):
        copy.wait()
    out_ref[...] = (second[0] + second[1]) + (second[2] + second[3])


def vector_sum(values, blocks, groups, identity):
    _, rows, columns = values.shape
    return pl.pallas_call(
        partial(vector_kernel, blocks, groups),
        out_shape=jax.ShapeDtypeStruct((rows, columns), jnp.float32),
        in_specs=[pl.BlockSpec(memory_space=pltpu.VMEM)],
        out_specs=pl.BlockSpec(memory_space=pltpu.VMEM),
        scratch_shapes=[
            pltpu.VMEM((blocks, rows, columns), jnp.float32),
            pltpu.VMEM((groups, rows, columns), jnp.float32),
            pltpu.SemaphoreType.DMA((blocks + groups,)),
            pltpu.SemaphoreType.DMA((blocks + groups,)),
        ],
        compiler_params=pltpu.CompilerParams(collective_id=identity, has_side_effects=True),
    )(values)


def two_heads(values, low_half):
    none = jnp.zeros_like(values)
    return jnp.concatenate(
        [jnp.where(low_half, values, none), jnp.where(low_half, none, values)], 0
    )


LAGS = (0, 1, 2, 6, 12, 21, 25, 26, 28)
FLASH_TURN = 7
TEXT_TURN = 8
SEND_TURNS = (10, 13)
LAND_TURN = 32
EARLY = 32
LATE = 5
SECOND_TURN = 11
ROWS = 256


def added(*terms):
    total = terms[0].astype(jnp.float32)
    for term in terms[1:]:
        total = total + term.astype(jnp.float32)
    return total.astype(jnp.bfloat16)


class Lane(NamedTuple):
    own: object
    got: object
    left: object
    right: object
    one_got: object
    one_sum: object
    two_got: object
    two_sum: object
    z_got: object
    z_sum: object
    spread: object
    half: object
    back: object
    out: object
    made: object


class Slots(NamedTuple):
    mixed_grads: object
    query_grads: object
    key_grads: object
    value_grads: object
    key_sum: object
    value_sum: object
    landed: object
    turned: object
    text_parts: object
    text_sums: object
    text_low: object
    matrix: object
    matrix_got: object
    matrix_sum: object
    send_sem: object
    recv_sem: object
    load_sem: object
    store_sem: object
    out_send: object
    out_recv: object
    back_send: object
    back_recv: object
    text_send: object
    text_recv: object
    matrix_send: object
    matrix_recv: object
    save_sem: object


def lane_slots(half, rows_first, rows):
    low = jnp.bfloat16
    one = (4, 2, half, LANES) if rows_first else (4, LANES, LANES)
    return Lane(
        own=pltpu.VMEM((8, 4, 2, LANES, LANES), low),
        got=pltpu.VMEM((4, 4, 2, LANES, LANES), low),
        left=pltpu.VMEM((2, 4, 2, LANES, rows), low),
        right=pltpu.VMEM((2, rows, 2 * LANES), low),
        one_got=pltpu.VMEM((16,) + one, low),
        one_sum=pltpu.VMEM((10,) + one, low),
        two_got=pltpu.VMEM((18, 4, half, LANES), low),
        two_sum=pltpu.VMEM((12, 4, half, LANES), low),
        z_got=pltpu.VMEM((22, 3, half, LANES), low),
        z_sum=pltpu.VMEM((8, half, LANES), low),
        spread=pltpu.VMEM((12, half, LANES), low),
        half=pltpu.VMEM((4, LANES, LANES), low),
        back=pltpu.VMEM((4, LANES, LANES), low),
        out=pltpu.VMEM((4, 2, LANES, LANES), jnp.float32),
        made=pltpu.VMEM((4, 4, 2, LANES, LANES), low),
    )


def rings(text_shape, item_shape, frame_shape, blocks):
    items, length, lanes = item_shape
    low = jnp.bfloat16
    return Slots(
        mixed_grads=pltpu.VMEM(item_shape, low),
        query_grads=pltpu.VMEM(item_shape, low),
        key_grads=pltpu.VMEM(item_shape, low),
        value_grads=pltpu.VMEM(item_shape, low),
        key_sum=pltpu.VMEM((length, lanes), jnp.float32),
        value_sum=pltpu.VMEM((length, lanes), jnp.float32),
        landed=pltpu.VMEM(frame_shape, low),
        turned=pltpu.VMEM((frame_shape[0], frame_shape[2] // 3, frame_shape[1]), low),
        text_parts=pltpu.VMEM((2, blocks) + text_shape, low),
        text_sums=pltpu.VMEM((2,) + text_shape, low),
        text_low=pltpu.VMEM(text_shape[:2] + (2 * blocks * LANES,), low),
        matrix=pltpu.VMEM((2, LANES, blocks * LANES), low),
        matrix_got=pltpu.VMEM((3, LANES, blocks * LANES), low),
        matrix_sum=pltpu.VMEM((2, LANES, blocks * LANES), low),
        send_sem=pltpu.SemaphoreType.DMA((16, 22)),
        recv_sem=pltpu.SemaphoreType.DMA((16, 22)),
        load_sem=pltpu.SemaphoreType.DMA((2, 2, 2)),
        store_sem=pltpu.SemaphoreType.DMA((2, 2, 4)),
        out_send=pltpu.SemaphoreType.DMA((3, blocks)),
        out_recv=pltpu.SemaphoreType.DMA((3, blocks)),
        back_send=pltpu.SemaphoreType.DMA((items, 3, blocks)),
        back_recv=pltpu.SemaphoreType.DMA((items, 3, blocks)),
        text_send=pltpu.SemaphoreType.DMA((2, blocks)),
        text_recv=pltpu.SemaphoreType.DMA((2, blocks)),
        matrix_send=pltpu.SemaphoreType.DMA((3,)),
        matrix_recv=pltpu.SemaphoreType.DMA((3,)),
        save_sem=pltpu.SemaphoreType.DMA((2,)),
    )


def backward_kernel(plan, head, *refs):
    refs = list(refs)

    def take(count):
        taken = refs[:count]
        del refs[:count]
        return taken

    (limit_ref, att_grad, text_key, text_value) = take(4)
    (q_ref, k_ref, v_ref, o_ref, lse_ref, normed_ref, text_ref) = take(7)
    lefts = take(len(plan) - 1)
    rights = take(len(plan) - 1)
    outs = take(len(plan))
    qkv_out, text_out, matrix_out = take(3)
    lanes_of = [Lane(*take(len(Lane._fields))) for _ in range(2)]
    own = Slots(*refs)
    items, length, lanes = q_ref.shape
    frames = att_grad.shape[1]
    width = att_grad.shape[2]
    blocks = length // frames
    group = lax.axis_index("items")
    block = lax.axis_index("blk")
    y, core = group // 2, group % 2
    z, x = block // 2, block % 2
    to_core = {"items": y * 2 + (1 - core)}
    to_y = {"items": (1 - y) * 2 + core}
    to_x = {"blk": z * 2 + (1 - x)}
    z_places = [lax.rem(z + step, 4) for step in range(1, 4)]
    to_z = [{"blk": place * 2 + x} for place in z_places]
    places = [lax.rem(block + step, blocks) for step in range(blocks)]
    barrier = pltpu.get_barrier_semaphore()
    peers = [to_core, to_y] + [{"blk": place} for place in places[1:]]
    for peer in peers:
        pl.semaphore_signal(barrier, inc=1, device_id=peer, device_id_type=MESH_ID)
    pl.semaphore_wait(barrier, len(peers))

    def at(ring, index):
        return ring.at[lax.rem(index, ring.shape[0])]

    def half_rows(place):
        return pl.ds(pl.multiple_of(place * (LANES // 2), LANES // 2), LANES // 2)

    def lane_block(offset, place):
        return pl.ds(pl.multiple_of(offset + place * LANES, LANES), LANES)

    def frame_rows(place):
        return pl.ds(pl.multiple_of(place * frames, frames), frames)

    def copy_to(peer, source, target, send, recv):
        return pltpu.make_async_remote_copy(
            src_ref=source,
            dst_ref=target,
            send_sem=send,
            recv_sem=recv,
            device_id=peer,
            device_id_type=MESH_ID,
        )

    def remote(kind, got, index, source, peer):
        slot = lax.rem(index, got.shape[0])
        return copy_to(
            peer,
            source,
            got.at[slot],
            own.send_sem.at[kind, slot],
            own.recv_sem.at[kind, slot],
        )

    def target_view(tensor, local, half):
        parts = plan[tensor][2]
        return outs[tensor].at[local % parts, :, lane_block(half * LANES, 2 * (local // parts))]

    def with_tensor(piece, action):
        for tensor, (start, count, _) in enumerate(plan):

            @pl.when((piece >= start) & (piece < start + count))
            def _():
                action(tensor, piece - start)

    made_start = plan[-1][0]

    def lane_steps(number, lane, base, offset, rows_first):
        def loads(index, tensor, local):
            slot = lax.rem(index, lane.left.shape[0])
            parts = plan[tensor][2]
            columns = pl.ds(pl.multiple_of((local // parts) * 2 * LANES, LANES), 2 * LANES)
            return [
                pltpu.make_async_copy(
                    lefts[tensor].at[:, :, local % parts],
                    lane.left.at[slot],
                    own.load_sem.at[number, 0, slot],
                ),
                pltpu.make_async_copy(
                    rights[tensor].at[:, columns],
                    lane.right.at[slot],
                    own.load_sem.at[number, 1, slot],
                ),
            ]

        def fetch(index):
            def start(tensor, local):
                if tensor < len(plan) - 1:
                    for copy in loads(index, tensor, local):
                        copy.start()

            with_tensor(base + index, start)

        def send(kind, got, index, source, peer):
            return remote(8 * number + kind, got, index, source, peer)

        def split(index, product):
            product = product.reshape(4, 2, LANES, 2 * LANES).astype(jnp.bfloat16)
            sides = (product[..., :LANES], product[..., LANES:])
            at(lane.own, index)[...] = jnp.where(core == 0, sides[0], sides[1])
            at(lane.made, index)[...] = jnp.where(core == 0, sides[1], sides[0])

        def begin(index):
            @pl.when(base + index < made_start)
            def _():
                for copy in loads(index, 0, 0):
                    copy.wait()
                left = at(lane.left, index)[...].reshape(8 * LANES, -1)
                split(index, contract(left, at(lane.right, index)[...], 1, 0))

            @pl.when(base + index >= made_start)
            def _():
                local = base + index - made_start
                columns = pl.ds(pl.multiple_of(local * 2 * LANES, LANES), 2 * LANES)
                parts = [
                    contract(own.turned[item], own.landed[item, :, columns], 1, 0)
                    for item in range(items)
                ]
                split(index, sum(parts))

            send(0, lane.got, index, at(lane.made, index), to_core).start()

        def one_copy(index):
            if rows_first:
                source = at(lane.own, index).at[:, :, half_rows(1 - y), :]
                return send(1, lane.one_got, index, source, to_y)
            return send(1, lane.one_got, index, at(lane.own, index).at[:, 1 - x], to_x)

        def two_copy(index):
            if rows_first:
                return send(2, lane.two_got, index, at(lane.one_sum, index).at[:, 1 - x], to_x)
            source = at(lane.one_sum, index).at[:, half_rows(1 - y), :]
            return send(2, lane.two_got, index, source, to_y)

        def z_copies(index):
            slot = lax.rem(index, lane.z_got.shape[0])
            return [
                copy_to(
                    to_z[k],
                    at(lane.two_sum, index).at[z_places[k]],
                    lane.z_got.at[slot, k],
                    own.send_sem.at[8 * number + 3 + k, slot],
                    own.recv_sem.at[8 * number + 3 + k, slot],
                )
                for k in range(3)
            ]

        def spread_copy(index):
            return send(6, lane.spread, index, at(lane.z_sum, index), to_y)

        def back_copy(index):
            return send(7, lane.back, index, at(lane.half, index), to_core)

        def chip(index):
            send(0, lane.got, index, at(lane.made, index), to_core).wait()
            target = at(lane.own, index)
            target[...] = added(target[...], at(lane.got, index)[...])
            one_copy(index).start()

        def one(index):
            one_copy(index).wait()
            kept = at(lane.own, index)
            kept = kept[:, :, half_rows(y), :] if rows_first else kept[:, x]
            at(lane.one_sum, index)[...] = added(kept, at(lane.one_got, index)[...])
            two_copy(index).start()

        def two(index):
            two_copy(index).wait()
            kept = at(lane.one_sum, index)
            kept = kept[:, x] if rows_first else kept[:, half_rows(y), :]
            at(lane.two_sum, index)[...] = added(kept, at(lane.two_got, index)[...])
            for copy in z_copies(index):
                copy.start()

        def three(index):
            for copy in z_copies(index):
                copy.wait()
            terms = at(lane.z_got, index)
            at(lane.z_sum, index)[...] = added(
                at(lane.two_sum, index)[z], terms[0], terms[1], terms[2]
            )
            spread_copy(index).start()

        def four(index):
            spread_copy(index).wait()
            target = at(lane.half, index)
            target[half_rows(y), :] = at(lane.z_sum, index)[...]
            target[half_rows(1 - y), :] = at(lane.spread, index)[...]
            back_copy(index).start()

        def finish(index):
            back_copy(index).wait()
            slot = lax.rem(index, lane.out.shape[0])
            lane.out[slot, core] = at(lane.half, index)[...].astype(jnp.float32)
            lane.out[slot, 1 - core] = at(lane.back, index)[...].astype(jnp.float32)

            def start(tensor, local):
                for side in range(2):
                    pltpu.make_async_copy(
                        lane.out.at[slot, side],
                        target_view(tensor, local, side),
                        own.store_sem.at[number, side, slot],
                    ).start()

            with_tensor(base + index, start)

        def close(index):
            slot = lax.rem(index, lane.out.shape[0])
            for side in range(2):
                pltpu.make_async_copy(
                    lane.out.at[slot, side],
                    target_view(0, 0, side),
                    own.store_sem.at[number, side, slot],
                ).wait()

        return [
            lambda index, step=step: step(index + offset)
            for step in (fetch, begin, chip, one, two, three, four, finish, close)
        ]

    def out_copies():
        copies = []
        for step in range(1, blocks):
            ends = [
                (
                    att_grad.at[:, :, lane_block(0, places[step])],
                    own.mixed_grads.at[:, frame_rows(block), :],
                ),
                (
                    text_key.at[:, :, lane_block(0, places[step])],
                    own.text_parts.at[0, step],
                ),
                (
                    text_value.at[:, :, lane_block(0, places[step])],
                    own.text_parts.at[1, step],
                ),
            ]
            for kind, (source, target) in enumerate(ends):
                copies.append(
                    copy_to(
                        {"blk": places[step]},
                        source,
                        target,
                        own.out_send.at[kind, step],
                        own.out_recv.at[kind, step],
                    )
                )
        ends = [
            (att_grad.at[:, :, lane_block(0, block)], own.mixed_grads.at[:, frame_rows(block), :]),
            (text_key.at[:, :, lane_block(0, block)], own.text_parts.at[0, 0]),
            (text_value.at[:, :, lane_block(0, block)], own.text_parts.at[1, 0]),
        ]
        for kind, (source, target) in enumerate(ends):
            copies.append(pltpu.make_async_copy(source, target, own.out_recv.at[kind, 0]))
        return copies

    def out_start(_):
        for copy in out_copies():
            copy.start()

    def out_wait(_):
        for copy in out_copies():
            copy.wait()

    scale = head ** (-0.5)
    flash_blocks = length // ROWS

    def flash_unit(item, number):
        span = (number + 1) * ROWS
        here = slice(number * ROWS, span)
        low_half = lax.broadcasted_iota(jnp.int32, (ROWS, lanes), 1) < head
        queries = two_heads(q_ref[item, here, :] * jnp.bfloat16(scale), low_half)
        mixed_grad = own.mixed_grads[item, here, :]
        mixed_grads = two_heads(mixed_grad, low_half)
        logs = jnp.transpose(lse_ref[item, here, :])
        logs = jnp.concatenate([logs[0:1], logs[head : head + 1]], 1)
        products = jnp.transpose(mixed_grad.astype(jnp.float32) * o_ref[item, here, :])
        delta = jnp.concatenate(
            [
                jnp.sum(products[:head], 0, keepdims=True),
                jnp.sum(products[head:], 0, keepdims=True),
            ],
            1,
        )
        keys = k_ref[item, :span, :]
        scores = contract(keys, queries, 1, 1)
        key_pos = lax.broadcasted_iota(jnp.int32, (ROWS, 2 * ROWS), 0)
        query_pos = lax.broadcasted_iota(jnp.int32, (ROWS, 2 * ROWS), 1) % ROWS
        corner = jnp.where(key_pos <= query_pos, scores[span - ROWS :], NEG_FILL)
        scores = corner if number == 0 else jnp.concatenate([scores[: span - ROWS], corner], 0)
        if span > length // 2:
            valid = lax.broadcasted_iota(jnp.int32, (span, 1), 0) < limit_ref[item]
            scores = scores + jnp.where(valid, 0.0, NEG_FILL)
        probs = jnp.exp(scores - logs)
        prob_grads = contract(v_ref[item, :span, :], mixed_grads, 1, 1)
        score_grads = (probs * (prob_grads - delta)).astype(jnp.bfloat16)
        query_grads = scale * contract(score_grads, keys, 0, 0)
        own.query_grads[item, here, :] = jnp.where(
            low_half, query_grads[:ROWS], query_grads[ROWS:]
        ).astype(jnp.bfloat16)
        value_part = contract(probs.astype(jnp.bfloat16), mixed_grads, 1, 0)
        key_part = contract(score_grads, queries, 1, 0)
        if number == flash_blocks - 1:
            own.value_sum[...] = value_part
            own.key_sum[...] = key_part
        else:
            own.value_sum[:span] += value_part
            own.key_sum[:span] += key_part
        if number == flash_order[-1]:
            own.key_grads[item] = own.key_sum[...].astype(jnp.bfloat16)
            own.value_grads[item] = own.value_sum[...].astype(jnp.bfloat16)

    pairs = flash_blocks // 2
    flash_order = [flash_blocks - 1 - turn if side == 0 else turn for turn in range(pairs) for side in range(2)]

    def flash(index):
        for pair in range(pairs):

            @pl.when(lax.rem(index, pairs) == pair)
            def _():
                for number in flash_order[2 * pair : 2 * pair + 2]:
                    flash_unit(index // pairs, number)

    parts_of = (own.query_grads, own.key_grads, own.value_grads)

    def back_copy(item, part, step):
        place = lax.rem(block + step, blocks)
        return copy_to(
            {"blk": place},
            parts_of[part].at[item, frame_rows(place), :],
            own.landed.at[item, :, lane_block(part * width, block)],
            own.back_send.at[item, part, step],
            own.back_recv.at[item, part, step],
        )

    def back_own(item, part):
        return pltpu.make_async_copy(
            parts_of[part].at[item, frame_rows(block), :],
            own.landed.at[item, :, lane_block(part * width, block)],
            own.back_recv.at[item, part, 0],
        )

    def back_some(item):
        def run(index):
            @pl.when(index == 0)
            def _():
                for part in range(3):
                    back_own(item, part).start()

            for turn in range(2):

                @pl.when(lax.rem(index, 2) == turn)
                def _():
                    for part in range(turn, 1 + 2 * turn):
                        back_copy(item, part, 1 + index // 2).start()

        return run

    def save_copies():
        return [
            pltpu.make_async_copy(own.landed, qkv_out, own.save_sem.at[0]),
            pltpu.make_async_copy(own.text_low, text_out, own.save_sem.at[1]),
        ]

    def back_wait(_):
        for item in range(items):
            for part in range(3):
                back_own(item, part).wait()
                for step in range(1, blocks):
                    back_copy(item, part, step).wait()
            own.turned[item] = jnp.transpose(normed_ref[item])
        for copy in save_copies():
            copy.start()

    def text_copies():
        copies = []
        for part in range(2):
            target = own.text_low.at[:, :, lane_block(part * width, block)]
            source = own.text_sums.at[part]
            for step in range(1, blocks):
                copies.append(
                    copy_to(
                        {"blk": places[step]},
                        source,
                        target,
                        own.text_send.at[part, step],
                        own.text_recv.at[part, step],
                    )
                )
            copies.append(pltpu.make_async_copy(source, target, own.text_recv.at[part, 0]))
        return copies

    def text_sum(_):
        for part in range(2):
            own.text_sums[part] = added(*[own.text_parts[part, step] for step in range(blocks)])
        for copy in text_copies():
            copy.start()

    def matrix_copy(number):
        source = [own.matrix.at[1 - core], own.matrix_sum.at[0], own.matrix_sum.at[1]]
        return copy_to(
            [to_core, to_y, to_core][number],
            source[number],
            own.matrix_got.at[number],
            own.matrix_send.at[number],
            own.matrix_recv.at[number],
        )

    def text_product(_):
        for copy in text_copies():
            copy.wait()
        for side in range(2):
            columns = slice(side * width, (side + 1) * width)
            rows = sum(
                contract(text_ref[item], own.text_low[item, :, columns], 0, 0)
                for item in range(items)
            )
            own.matrix[side] = rows.astype(jnp.bfloat16)
        matrix_copy(0).start()

    def matrix_one(_):
        matrix_copy(0).wait()
        own.matrix_sum[0] = added(own.matrix[core], own.matrix_got[0])
        matrix_copy(1).start()

    def matrix_two(_):
        matrix_copy(1).wait()
        own.matrix_sum[1] = added(own.matrix_sum[0], own.matrix_got[1])
        matrix_copy(2).start()

    def matrix_three(_):
        matrix_copy(2).wait()
        matrix_out[core] = own.matrix_sum[1].astype(jnp.float32)
        matrix_out[1 - core] = own.matrix_got[2].astype(jnp.float32)

    stages = [(0, 1, out_start), (LAND_TURN, 1, back_wait)]
    late = plan[-1][1]
    segments = [
        (0, EARLY, 0, 0, 0),
        (1, made_start - EARLY, 0, EARLY, SECOND_TURN),
        (0, LATE, EARLY, made_start - EARLY, LAND_TURN),
        (1, late - LATE, made_start - EARLY, LATE + EARLY, LAND_TURN),
    ]
    for number, count, offset, base, turn_base in segments:
        steps = lane_steps(number, lanes_of[number], base, offset, number == 0)
        stages += [(turn_base + lag, count, step) for lag, step in zip(LAGS, steps)]
    stages += [
        (FLASH_TURN, 1, out_wait),
        (FLASH_TURN, items * pairs, flash),
        (TEXT_TURN, 1, text_sum),
        (TEXT_TURN + 6, 1, text_product),
        (TEXT_TURN + 8, 1, matrix_one),
        (TEXT_TURN + 16, 1, matrix_two),
        (TEXT_TURN + 18, 1, matrix_three),
    ]
    stages += [
        (turn, 2 * (blocks - 1), back_some(item)) for item, turn in enumerate(SEND_TURNS)
    ]

    def turn(time, carry):
        for lag, count, action in stages:

            @pl.when((time >= lag) & (time < lag + count))
            def _():
                action(time - lag)

        return carry

    lax.fori_loop(0, max(lag + count for lag, count, _ in stages), turn, 0)
    for copy in save_copies():
        copy.wait()


def backward(factors, last_columns, blocks, identity, limits, sent, kept):
    plan = []
    start = 0
    lefts = []
    rights = []
    shapes = []
    width = sent[0].shape[2]
    sizes = [(left.shape[0], right.shape[1]) for left, right in factors] + [(width, last_columns)]
    for rows, columns in sizes:
        parts = rows // blocks // LANES
        count = parts * columns // (2 * LANES)
        plan.append((start, count, parts))
        start += count
        shapes.append(jax.ShapeDtypeStruct((parts, LANES, columns), jnp.float32))
    for (left, right), (_, _, parts) in zip(factors, plan):
        lefts.append(left.reshape(blocks // 2, 2, parts, LANES, left.shape[1]))
        rights.append(right)
    items, frames, _ = sent[0].shape
    text_count = sent[1].shape[1]
    frame_shape = (items, frames, 3 * width)
    text_shape = (items, text_count, LANES)
    scratch = lane_slots(LANES // 2, True, items * frames)
    scratch += lane_slots(LANES // 2, False, items * frames)
    scratch += rings(text_shape, kept[0].shape, frame_shape, blocks)
    far = pl.BlockSpec(memory_space=pl.ANY)
    near = pl.BlockSpec(memory_space=pltpu.VMEM)
    small = pl.BlockSpec(memory_space=pltpu.SMEM)
    outs = pl.pallas_call(
        partial(
            backward_kernel,
            plan,
            width // HEADS,
        ),
        out_shape=shapes
        + [
            jax.ShapeDtypeStruct(frame_shape, jnp.bfloat16),
            jax.ShapeDtypeStruct((items, text_count, 2 * width), jnp.bfloat16),
            jax.ShapeDtypeStruct((2, LANES, width), jnp.float32),
        ],
        in_specs=[small] + [far] * len(sent) + [near] * len(kept) + [far] * 2 * len(lefts),
        out_specs=[far] * (len(shapes) + 2) + [near],
        scratch_shapes=list(scratch),
        compiler_params=pltpu.CompilerParams(
            collective_id=identity, has_side_effects=True, vmem_limit_bytes=VMEM_BYTES
        ),
    )(limits, *sent, *kept, *lefts, *rights)
    grads = [out.reshape(-1, out.shape[-1]) for out in outs[: len(shapes)]]
    return grads, outs[len(shapes) :]


FF_TILE = 512


class Middle(NamedTuple):
    attn_out: object
    cross_query: object
    cross_out: object
    ff_up: object
    ff_down: object
    layer_output: object
    attended_turned: object
    cross_normed_turned: object
    cross_attended_turned: object
    ff_normed_turned: object
    activated_turned: object
    pre_grad: object
    cross_grad_low: object
    cross_q_grad: object
    self_grad_low: object
    self_grad: object
    att_grad: object
    text_key: object
    text_value: object
    after: object
    normed_one: object
    normed_two: object
    forward_sum: object
    backward_sum: object
    cross_normed: object
    cross_attended: object
    ff_normed: object
    cross_queries: object
    cross_att_grad: object
    probs: object
    load_sem: object
    save_sem: object


def row_norm(values):
    centre = jnp.mean(values, -1, keepdims=True)
    spread = values - centre
    inverse = lax.rsqrt(jnp.mean(spread * spread, -1, keepdims=True) + 1e-05)
    return spread * inverse, inverse


def row_norm_back(grad, normed, inverse, gain):
    scaled = grad * gain
    first_mean = jnp.mean(scaled, -1, keepdims=True)
    second_mean = jnp.mean(scaled * normed, -1, keepdims=True)
    return inverse * (scaled - first_mean - normed * second_mean)


def total_rows(values):
    return jnp.sum(values.astype(jnp.float32), 0, keepdims=True)


def middle_kernel(items, head, *refs):
    refs = list(refs)
    length_ref, hidden, attended, out_grad, text_keys, text_values, small, up_bias = refs[:8]
    weights = refs[8:13]
    saved = refs[13:27]
    sums, up_sums = refs[27:29]
    own = Middle(*refs[29:])
    low = jnp.bfloat16
    rows = hidden.shape[0]
    width = hidden.shape[1]
    frames = rows // items
    text_count = text_keys.shape[0] // items
    pairs = width // (2 * head)
    scale = head ** (-0.5)
    loads = [
        pltpu.make_async_copy(weight, own[number], own.load_sem.at[number])
        for number, weight in enumerate(weights)
    ]
    for load in loads:
        load.start()
    saves = [
        pltpu.make_async_copy(own[5 + number], out, own.save_sem.at[number])
        for number, out in enumerate(saved)
    ]

    def save(*names):
        for name in names:
            saves[Middle._fields.index(name) - 5].start()

    own.attended_turned[...] = jnp.transpose(attended[...])
    loads[0].wait()
    after_self = (
        hidden[...].astype(jnp.float32)
        + contract(attended[...], own.attn_out[...], 1, 0)
        + small[0:1, :]
    )
    own.after[...] = after_self
    normed, inverse_one = row_norm(after_self)
    own.normed_one[...] = normed
    own.cross_normed[...] = (normed * small[4:5, :] + small[6:7, :]).astype(low)
    own.cross_normed_turned[...] = jnp.transpose(own.cross_normed[...])
    save(*"attended_turned cross_normed_turned".split())
    loads[1].wait()
    own.cross_queries[...] = (
        contract(own.cross_normed[...], own.cross_query[...], 1, 0) + small[1:2, :]
    ).astype(low)
    low_half = lax.broadcasted_iota(jnp.int32, (frames, 2 * head), 1) < head

    def pair_parts(item, pair):
        return (
            slice(item * frames, (item + 1) * frames),
            slice(item * text_count, (item + 1) * text_count),
            slice(pair * 2 * head, (pair + 1) * 2 * head),
        )

    def joined(values):
        return jnp.where(low_half, values[:frames], values[frames:])

    for item in range(items):
        seen = lax.broadcasted_iota(jnp.int32, (text_count, 1), 0) < length_ref[item]
        for pair in range(pairs):
            here, texts, lanes = pair_parts(item, pair)
            queries = two_heads(own.cross_queries[here, lanes] * low(scale), low_half)
            scores = contract(text_keys[texts, lanes], queries, 1, 1)
            scores = jnp.where(seen, scores, NEG_FILL)
            raised = jnp.exp(scores - jnp.max(scores, 0, keepdims=True))
            raised = jnp.where(seen, raised, 0.0)
            probs = raised / jnp.sum(raised, 0, keepdims=True)
            own.probs[item * pairs + pair] = probs
            mixed = contract(probs.astype(low), text_values[texts, lanes], 0, 0)
            own.cross_attended[here, lanes] = joined(mixed).astype(low)
    loads[2].wait()
    after_cross = (
        own.after[...]
        + contract(own.cross_attended[...], own.cross_out[...], 1, 0)
        + small[2:3, :]
    )
    own.after[...] = after_cross
    normed, inverse_two = row_norm(after_cross)
    own.normed_two[...] = normed
    own.ff_normed[...] = (normed * small[5:6, :] + small[7:8, :]).astype(low)
    own.cross_attended_turned[...] = jnp.transpose(own.cross_attended[...])
    own.ff_normed_turned[...] = jnp.transpose(own.ff_normed[...])
    save(*"cross_attended_turned ff_normed_turned".split())
    loads[3].wait()
    loads[4].wait()
    own.forward_sum[...] = jnp.zeros_like(own.forward_sum)
    own.backward_sum[...] = jnp.zeros_like(own.backward_sum)

    def tile(number, carry):
        here = pl.ds(pl.multiple_of(number * FF_TILE, FF_TILE), FF_TILE)
        pre = contract(own.ff_normed[...], own.ff_up[:, here], 1, 0) + up_bias[:, here]
        act_grad = contract(out_grad[...], own.ff_down[here, :], 1, 1)
        below = 0.5 + 0.5 * lax.erf(pre * (0.5**0.5))
        active = (pre * below).astype(low)
        slope = below + pre * (jnp.exp(-0.5 * pre * pre) * 0.3989422804014327)
        grad = (act_grad * slope).astype(low)
        own.activated_turned[here, :] = jnp.transpose(active)
        own.pre_grad[:, here] = grad
        up_sums[:, here] = total_rows(grad)
        own.forward_sum[...] += contract(active, own.ff_down[here, :], 1, 0)
        own.backward_sum[...] += contract(grad, own.ff_up[:, here], 1, 1)
        return carry

    lax.fori_loop(0, own.ff_up.shape[1] // FF_TILE, tile, 0)
    own.layer_output[...] = (own.after[...] + own.forward_sum[...] + small[3:4, :]).astype(low)
    save(*"layer_output activated_turned pre_grad".split())
    grad = own.backward_sum[...]
    sums[0:1, :] = total_rows(out_grad[...])
    sums[5:6, :] = total_rows(grad * own.normed_two[...])
    sums[7:8, :] = total_rows(grad)
    cross_grad = out_grad[...].astype(jnp.float32) + row_norm_back(
        grad, own.normed_two[...], inverse_two, small[5:6, :]
    )
    own.after[...] = cross_grad
    own.cross_grad_low[...] = cross_grad.astype(low)
    sums[1:2, :] = total_rows(own.cross_grad_low[...])
    own.cross_att_grad[...] = contract(own.cross_grad_low[...], own.cross_out[...], 1, 1).astype(low)
    for item in range(items):
        for pair in range(pairs):
            here, texts, lanes = pair_parts(item, pair)
            grads = two_heads(own.cross_att_grad[here, lanes], low_half)
            queries = two_heads(own.cross_queries[here, lanes] * low(scale), low_half)
            probs = own.probs[item * pairs + pair]
            prob_grads = contract(text_values[texts, lanes], grads, 1, 1)
            score_grads = probs * (prob_grads - jnp.sum(probs * prob_grads, 0, keepdims=True))
            score_grads = score_grads.astype(low)
            own.text_key[texts, lanes] = contract(score_grads, queries, 1, 0).astype(low)
            own.text_value[texts, lanes] = contract(probs.astype(low), grads, 1, 0).astype(low)
            query_grads = scale * contract(score_grads, text_keys[texts, lanes], 0, 0)
            own.cross_q_grad[here, lanes] = joined(query_grads).astype(low)
    save(*"cross_grad_low cross_q_grad text_key text_value".split())
    grad = contract(own.cross_q_grad[...], own.cross_query[...], 1, 1)
    sums[2:3, :] = total_rows(own.cross_q_grad[...])
    sums[4:5, :] = total_rows(grad * own.normed_one[...])
    sums[6:7, :] = total_rows(grad)
    self_grad = own.after[...] + row_norm_back(
        grad, own.normed_one[...], inverse_one, small[4:5, :]
    )
    own.self_grad[...] = self_grad
    own.self_grad_low[...] = self_grad.astype(low)
    sums[3:4, :] = total_rows(own.self_grad_low[...])
    own.att_grad[...] = contract(own.self_grad_low[...], own.attn_out[...], 1, 1).astype(low)
    save(*"self_grad self_grad_low att_grad".split())
    for copy in saves:
        copy.wait()


def middle(lengths, hidden, attended, out_grad, text_keys, text_values, small, up_bias, weights):
    items, frames, width = hidden.shape
    text_count = text_keys.shape[0] // items
    rows = items * frames
    wide = weights[3].shape[1]
    low = jnp.bfloat16
    full = jnp.float32
    saved = [((rows, width), low)] + [((width, rows), low)] * 4
    saved += [((wide, rows), low), ((rows, wide), low)] + [((rows, width), low)] * 3
    saved += [((rows, width), full), ((rows, width), low)]
    saved += [((items * text_count, width), low)] * 2
    kept = [((rows, width), full)] * 5 + [((rows, width), low)] * 5
    kept += [((items * HEADS // 2, text_count, 2 * frames), full)]
    near = pl.BlockSpec(memory_space=pltpu.VMEM)
    far = pl.BlockSpec(memory_space=pl.ANY)
    outs = pl.pallas_call(
        partial(middle_kernel, items, width // HEADS),
        out_shape=[jax.ShapeDtypeStruct(shape, kind) for shape, kind in saved]
        + [jax.ShapeDtypeStruct((8, width), full), jax.ShapeDtypeStruct((1, wide), full)],
        in_specs=[pl.BlockSpec(memory_space=pltpu.SMEM)] + [near] * 7 + [far] * 5,
        out_specs=[far] * len(saved) + [near] * 2,
        scratch_shapes=[pltpu.VMEM(weight.shape, weight.dtype) for weight in weights]
        + [pltpu.VMEM(shape, kind) for shape, kind in saved + kept]
        + [pltpu.SemaphoreType.DMA((5,)), pltpu.SemaphoreType.DMA((len(saved),))],
        compiler_params=pltpu.CompilerParams(vmem_limit_bytes=62 * 1024 * 1024),
    )(
        lengths,
        hidden.reshape(rows, width),
        attended.reshape(rows, width),
        out_grad.reshape(rows, width),
        text_keys,
        text_values,
        small,
        up_bias,
        *weights,
    )
    return outs[: len(saved)], outs[len(saved)], outs[len(saved) + 1]


class Forward(NamedTuple):
    attn_in: object
    cross_kv: object
    projected: object
    queries: object
    keys: object
    values: object
    mixed: object
    mixed_low: object
    log_total: object
    load_sem: object
    there_send: object
    there_recv: object
    back_send: object
    back_recv: object
    save_sem: object


def forward_kernel(head, *refs):
    refs = list(refs)
    limit_ref, hidden, gain, shift, bias, text, value_bias, attn_in, cross_kv = refs[:9]
    normed_out, text_keys, text_values = refs[9:12]
    attended, queries_out, keys_out, values_out, mixed_out, log_out = refs[12:18]
    own = Forward(*refs[18:])
    low = jnp.bfloat16
    items, length, lanes = own.queries.shape
    frames, width = hidden.shape[1:]
    blocks = length // frames
    block = lax.axis_index("blk")
    scale = head ** (-0.5)
    barrier = pltpu.get_barrier_semaphore()
    for step in range(1, blocks):
        pl.semaphore_signal(
            barrier, inc=1, device_id={"blk": lax.rem(block + step, blocks)}, device_id_type=MESH_ID
        )
    loads = [
        pltpu.make_async_copy(
            attn_in.at[:, part * width : (part + 1) * width],
            own.attn_in.at[:, part * width : (part + 1) * width],
            own.load_sem.at[part],
        )
        for part in range(3)
    ]
    loads.append(pltpu.make_async_copy(cross_kv, own.cross_kv, own.load_sem.at[3]))
    for load in loads:
        load.start()
    gains = gain[0:1, :].astype(jnp.float32)
    shifts = shift[0:1, :].astype(jnp.float32)
    for item in range(items):
        normed, _ = row_norm(hidden[item].astype(jnp.float32))
        normed_out[item] = (normed * gains + shifts).astype(low)
    landing = (own.queries, own.keys, own.values)

    def lane_block(offset, place):
        return pl.ds(pl.multiple_of(offset + place * LANES, LANES), LANES)

    def frame_rows(place):
        return pl.ds(pl.multiple_of(place * frames, frames), frames)

    def there(item, part, step):
        place = lax.rem(block + step, blocks)
        source = own.projected.at[item, :, lane_block(part * width, place)]
        target = landing[part].at[item, frame_rows(block), :]
        if step == 0:
            return pltpu.make_async_copy(source, target, own.there_recv.at[item, part, 0])
        return pltpu.make_async_remote_copy(
            src_ref=source,
            dst_ref=target,
            send_sem=own.there_send.at[item, part, step],
            recv_sem=own.there_recv.at[item, part, step],
            device_id={"blk": place},
            device_id_type=MESH_ID,
        )

    def back(item, step):
        place = lax.rem(block + step, blocks)
        source = own.mixed_low.at[item, frame_rows(place), :]
        target = attended.at[item, :, lane_block(0, block)]
        if step == 0:
            return pltpu.make_async_copy(source, target, own.back_recv.at[item, 0])
        return pltpu.make_async_remote_copy(
            src_ref=source,
            dst_ref=target,
            send_sem=own.back_send.at[item, step],
            recv_sem=own.back_recv.at[item, step],
            device_id={"blk": place},
            device_id_type=MESH_ID,
        )

    def save_copies(item):
        kept = (own.queries, own.keys, own.values, own.mixed, own.log_total)
        outs = (queries_out, keys_out, values_out, mixed_out, log_out)
        return [
            pltpu.make_async_copy(source.at[item], out.at[item], own.save_sem.at[item, number])
            for number, (source, out) in enumerate(zip(kept, outs))
        ]

    for item in range(items):
        for part in range(3):
            if item == 0:
                loads[part].wait()
            columns = slice(part * width, (part + 1) * width)
            rows = contract(normed_out[item], own.attn_in[:, columns], 1, 0)
            if part != 1:
                start = (part // 2) * width
                rows = rows + bias[0:1, start : start + width].astype(jnp.float32)
            own.projected[item, :, columns] = rows.astype(low)
            if item == 0 and part == 0:
                pl.semaphore_wait(barrier, blocks - 1)
            for step in range(blocks):
                there(item, part, step).start()
    loads[3].wait()
    text_keys[...] = contract(text[...], own.cross_kv[:, :width], 1, 0).astype(low)
    text_values[...] = (
        contract(text[...], own.cross_kv[:, width:], 1, 0) + value_bias[...].astype(jnp.float32)
    ).astype(low)
    low_half = lax.broadcasted_iota(jnp.int32, (ROWS, lanes), 1) < head

    def attend(item, carry):
        for part in range(3):
            for step in range(blocks):
                there(item, part, step).wait()
        for number in range(length // ROWS):
            span = (number + 1) * ROWS
            here = slice(number * ROWS, span)
            queries = two_heads(own.queries[item, here, :] * low(scale), low_half)
            scores = contract(queries, own.keys[item, :span, :], 1, 1)
            query_pos = lax.broadcasted_iota(jnp.int32, (2 * ROWS, ROWS), 0) % ROWS
            key_pos = lax.broadcasted_iota(jnp.int32, (2 * ROWS, ROWS), 1)
            corner = jnp.where(key_pos <= query_pos, scores[:, span - ROWS :], NEG_FILL)
            scores = corner if number == 0 else jnp.concatenate([scores[:, : span - ROWS], corner], 1)
            if span > length // 2:
                valid = lax.broadcasted_iota(jnp.int32, (1, span), 1) < limit_ref[item]
                scores = scores + jnp.where(valid, 0.0, NEG_FILL)
            top = jnp.max(scores, 1, keepdims=True)
            raised = jnp.exp(scores - top)
            total = jnp.sum(raised, 1, keepdims=True)
            mixed = contract(raised.astype(low), own.values[item, :span, :], 1, 0) / total
            mixed = jnp.where(low_half, mixed[:ROWS], mixed[ROWS:])
            own.mixed[item, here, :] = mixed
            own.mixed_low[item, here, :] = mixed.astype(low)
            log_total = top + jnp.log(total)
            own.log_total[item, here, :] = jnp.where(low_half, log_total[:ROWS], log_total[ROWS:])
        for step in range(blocks):
            back(item, step).start()
        for copy in save_copies(item):
            copy.start()
        return carry

    lax.fori_loop(0, items, attend, 0)
    for item in range(items):
        for step in range(blocks):
            back(item, step).wait()
        for copy in save_copies(item):
            copy.wait()


def forward(identity, blocks, limits, hidden, gain, shift, bias, text, value_bias, attn_in, cross_kv):
    items, frames, width = hidden.shape
    low = jnp.bfloat16
    full = jnp.float32
    whole_shape = (items, frames * blocks, LANES)
    near = pl.BlockSpec(memory_space=pltpu.VMEM)
    far = pl.BlockSpec(memory_space=pl.ANY)
    rows = text.reshape(-1, width)

    def shape(dims, kind):
        return jax.ShapeDtypeStruct(dims, kind)

    kinds = [low, low, low, full, low, full]
    return pl.pallas_call(
        partial(forward_kernel, width // HEADS),
        out_shape=[shape(hidden.shape, low), shape(rows.shape, low), shape(rows.shape, low)]
        + [shape(hidden.shape, low)]
        + [shape(whole_shape, kind) for kind in (low, low, low, full, full)],
        in_specs=[pl.BlockSpec(memory_space=pltpu.SMEM)] + [near] * 6 + [far] * 2,
        out_specs=[near] * 3 + [far] * 6,
        scratch_shapes=[
            pltpu.VMEM(attn_in.shape, low),
            pltpu.VMEM(cross_kv.shape, low),
            pltpu.VMEM((items, frames, 3 * width), low),
        ]
        + [pltpu.VMEM(whole_shape, kind) for kind in kinds]
        + [
            pltpu.SemaphoreType.DMA((4,)),
            pltpu.SemaphoreType.DMA((items, 3, blocks)),
            pltpu.SemaphoreType.DMA((items, 3, blocks)),
            pltpu.SemaphoreType.DMA((items, blocks)),
            pltpu.SemaphoreType.DMA((items, blocks)),
            pltpu.SemaphoreType.DMA((items, 5)),
        ],
        compiler_params=pltpu.CompilerParams(
            collective_id=identity, has_side_effects=True, vmem_limit_bytes=VMEM_BYTES
        ),
    )(limits, hidden, gain, shift, bias, rows, value_bias[None], attn_in, cross_kv)


def fast_device(
    hidden_in,
    text_states,
    frame_lengths,
    text_lengths,
    out_grad,
    attn_in,
    attn_in_bias,
    attn_out,
    attn_out_bias,
    cross_query,
    cross_query_bias,
    cross_kv,
    cross_v_bias,
    cross_out,
    cross_out_bias,
    ff_up,
    ff_up_bias,
    ff_down,
    ff_down_bias,
    norm_gain,
    norm_bias,
):
    seq_count, frames, width = hidden_in.shape
    blocks = lax.axis_size("blk")
    block_index = lax.axis_index("blk")
    gains = norm_gain.astype(jnp.float32)

    (
        attn_normed,
        text_keys,
        text_values,
        attended,
        queries,
        keys,
        values,
        mixed,
        log_total,
    ) = forward(
        0,
        blocks,
        frame_lengths,
        hidden_in,
        norm_gain,
        norm_bias,
        attn_in_bias[None],
        text_states,
        cross_v_bias,
        attn_in,
        cross_kv,
    )
    small = jnp.concatenate(
        [
            attn_out_bias[None],
            cross_query_bias[None],
            cross_out_bias[None],
            ff_down_bias[None],
            norm_gain[1:],
            norm_bias[1:],
        ]
    ).astype(jnp.float32)
    (
        layer_output,
        attended_turned,
        cross_normed_turned,
        cross_attended_turned,
        ff_normed_turned,
        activated_turned,
        pre_grad,
        cross_grad_low,
        cross_q_grad,
        self_grad_low,
        self_grad,
        att_grad,
        text_key_part,
        text_value_part,
    ), sums, up_sums = middle(
        text_lengths,
        hidden_in,
        attended,
        out_grad,
        text_keys,
        text_values,
        small,
        ff_up_bias.astype(jnp.float32)[None],
        [attn_out, cross_query, cross_out, ff_up, ff_down],
    )
    text_shape = text_states.shape
    layer_output = layer_output.reshape(hidden_in.shape)
    self_grad = self_grad.reshape(hidden_in.shape)
    row_share = width // blocks
    text_slice = lax.dynamic_slice_in_dim(text_states, block_index * row_share, row_share, 2)
    (
        attn_out_grad,
        cross_query_grad,
        cross_out_grad,
        ff_up_grad,
        ff_down_grad,
        attn_in_grad,
    ), (qkv_grad, text_kv_low, cross_kv_sides) = backward(
        [
            (attended_turned, self_grad_low),
            (cross_normed_turned, cross_q_grad),
            (cross_attended_turned, cross_grad_low),
            (ff_normed_turned, pre_grad),
            (activated_turned, out_grad.reshape(-1, width)),
        ],
        attn_in.shape[1],
        blocks,
        2,
        frame_lengths,
        [
            att_grad.reshape(hidden_in.shape),
            text_key_part.reshape(text_shape),
            text_value_part.reshape(text_shape),
        ],
        [queries, keys, values, mixed, log_total, attn_normed, text_slice],
    )
    cross_kv_grad = jnp.concatenate([cross_kv_sides[0], cross_kv_sides[1]], 1)
    _, normed_zero, inverse_zero = normalize(hidden_in.astype(jnp.float32), gains[0], 0.0)
    back_zero, gain_zero, shift_zero = norm_back(
        apply_back(qkv_grad, attn_in), normed_zero, inverse_zero, gains[0]
    )
    hidden_grad = (self_grad + back_zero).astype(jnp.bfloat16)

    text_grad = jnp.einsum(
        "stf,df->std", text_kv_low, cross_kv, preferred_element_type=jnp.float32
    ).astype(jnp.bfloat16)
    value_slice = lax.dynamic_slice_in_dim(
        text_kv_low, width + block_index * row_share, row_share, 2
    )
    cross_v_bias_rows = column_sum(value_slice)
    qkv_sum = column_sum(qkv_grad)

    def by_block(vector):
        return vector.reshape(blocks, -1)

    own_slot = jnp.arange(blocks, dtype=jnp.int32)[:, None] == block_index
    pieces = [
        by_block(jnp.concatenate([qkv_sum[:width], qkv_sum[2 * width :]])),
        by_block(sums[3]),
        by_block(sums[2]),
        jnp.where(own_slot, cross_v_bias_rows[None, :], 0.0),
        by_block(sums[1]),
        by_block(up_sums),
        by_block(sums[0]),
        by_block(gain_zero),
        by_block(sums[4]),
        by_block(sums[5]),
        by_block(shift_zero),
        by_block(sums[6]),
        by_block(sums[7]),
    ]
    sizes = [piece.shape[1] for piece in pieces]
    packed = jnp.concatenate(pieces, 1)
    spare = -packed.shape[1] % (8 * LANES)
    packed = jnp.pad(packed, ((0, 0), (0, spare))).reshape(blocks, 8, -1)
    summed = vector_sum(packed, blocks, lax.axis_size("items"), 3).reshape(-1)
    vectors = []
    start = 0
    for size in sizes:
        vectors.append(summed[start : start + size])
        start += size
    return (
        layer_output,
        hidden_grad,
        text_grad,
        attn_in_grad,
        vectors[0],
        attn_out_grad,
        vectors[1],
        cross_query_grad,
        vectors[2],
        cross_kv_grad,
        vectors[3],
        cross_out_grad,
        vectors[4],
        ff_up_grad,
        vectors[5],
        ff_down_grad,
        vectors[6],
        jnp.stack(vectors[7:10]),
        jnp.stack(vectors[10:13]),
    )


def solution(mesh):
    fast = mesh.shape["items"] == 4 and mesh.shape["blk"] == 8
    placed = (
        P("items", "blk", None),
        P("items", None, None),
        P("items"),
        P("items"),
        P("items", "blk", None),
        P(),
        P(),
        P(),
        P(),
        P(),
        P(),
        P(),
        P(),
        P(),
        P(),
        P(),
        P(),
        P(),
        P(),
        P(),
        P(),
    )
    return jax.shard_map(
        fast_device if fast else general_device,
        mesh=mesh,
        in_specs=placed,
        out_specs=(
            P("items", "blk", None),
            P("items", "blk", None),
            P("items", None, None),
            P("blk", None),
            P("blk"),
            P("blk", None),
            P("blk"),
            P("blk", None),
            P("blk"),
            P("blk", None),
            P("blk"),
            P("blk", None),
            P("blk"),
            P("blk", None),
            P("blk"),
            P("blk", None),
            P("blk"),
            P(None, "blk"),
            P(None, "blk"),
        ),
        check_vma=False,
    )
```

```python
from functools import partial
from typing import NamedTuple

import jax
import jax.numpy as jnp
from jax import lax
from jax.experimental import pallas as pl
from jax.experimental.pallas import tpu as pltpu
from jax.sharding import PartitionSpec as P

HEADS = 16


NEG_FILL = -1e30


def normalize(values, gain, shift):
    centre = jnp.mean(values, -1, keepdims=True)
    spread = values - centre
    variance = jnp.mean(spread * spread, -1, keepdims=True)
    inverse = lax.rsqrt(variance + 1e-05)
    normed = spread * inverse
    return (normed * gain + shift, normed, inverse)


def norm_back(grad, normed, inverse, gain):
    scaled = grad * gain
    first_mean = jnp.mean(scaled, -1, keepdims=True)
    second_mean = jnp.mean(scaled * normed, -1, keepdims=True)
    return (
        inverse * (scaled - first_mean - normed * second_mean),
        jnp.sum(grad * normed, (0, 1)),
        jnp.sum(grad, (0, 1)),
    )


def outer_sum(left, right):
    return jnp.einsum("sfd,sfe->de", left, right, preferred_element_type=jnp.float32)


def apply_fwd(values, weight):
    return jnp.einsum("sfd,de->sfe", values, weight, preferred_element_type=jnp.float32)


def apply_back(grad, weight):
    return jnp.einsum("sfe,de->sfd", grad, weight, preferred_element_type=jnp.float32)


def column_sum(values):
    return jnp.sum(values.astype(jnp.float32), (0, 1))


def general_device(
    hidden_in,
    text_states,
    frame_lengths,
    text_lengths,
    out_grad,
    attn_in,
    attn_in_bias,
    attn_out,
    attn_out_bias,
    cross_query,
    cross_query_bias,
    cross_kv,
    cross_v_bias,
    cross_out,
    cross_out_bias,
    ff_up,
    ff_up_bias,
    ff_down,
    ff_down_bias,
    norm_gain,
    norm_bias,
):
    seq_count, frames, width = hidden_in.shape
    head_count = HEADS
    head_size = width // head_count
    scale = head_size ** (-0.5)
    text_count = text_states.shape[1]
    axis_count = lax.axis_size("blk")
    block_index = lax.axis_index("blk")
    first_frame = block_index * frames
    last_frame = first_frame + frames - 1
    my_pos = first_frame + jnp.arange(frames, dtype=jnp.int32)
    frame_limit = frame_lengths[:, None, None, None]
    gains = norm_gain.astype(jnp.float32)
    shifts = norm_bias.astype(jnp.float32)

    def visible(key_pos, query_pos):
        return (key_pos[None, None, None, :] <= query_pos[None, None, :, None]) & (
            key_pos[None, None, None, :] < frame_limit
        )

    def heads_of(values):
        return values.reshape(values.shape[0], values.shape[1], head_count, head_size)

    residual = hidden_in.astype(jnp.float32)
    attn_full, normed_zero, inverse_zero = normalize(residual, gains[0], shifts[0])
    attn_normed = attn_full.astype(jnp.bfloat16)
    projected = apply_fwd(attn_normed, attn_in)
    query_rows = (projected[..., :width] + attn_in_bias[:width]).astype(jnp.bfloat16)
    key_rows = projected[..., width : 2 * width].astype(jnp.bfloat16)
    value_rows = (projected[..., 2 * width :] + attn_in_bias[width:]).astype(jnp.bfloat16)
    query_heads = heads_of(query_rows)

    def keep_state(state):
        return state

    start_state = (
        jnp.full((seq_count, head_count, frames), NEG_FILL, jnp.float32),
        jnp.zeros((seq_count, head_count, frames), jnp.float32),
        jnp.zeros((seq_count, head_count, frames, head_size), jnp.float32),
    )
    key_piece = lax.all_gather(key_rows, "blk", axis=1, tiled=True)
    value_piece = lax.all_gather(value_rows, "blk", axis=1, tiled=True)
    span = key_piece.shape[1]

    def forward_compute(state):
        running_max, running_sum, accumulated = state
        key_pos = jnp.arange(span, dtype=jnp.int32)
        scores = (
            jnp.einsum(
                "sfhd,sphd->shfp",
                query_heads,
                heads_of(key_piece),
                preferred_element_type=jnp.float32,
            )
            * scale
        )
        mask = visible(key_pos, my_pos)
        scores = jnp.where(mask, scores, NEG_FILL)
        new_max = jnp.maximum(running_max, jnp.max(scores, -1))
        weights = jnp.where(mask, jnp.exp(scores - new_max[..., None]), 0.0)
        running_sum = jnp.sum(weights, -1)
        accumulated = jnp.einsum(
            "shfp,sphd->shfd",
            weights.astype(jnp.bfloat16),
            heads_of(value_piece),
            preferred_element_type=jnp.float32,
        )
        return (new_max, running_sum, accumulated)

    final_state = lax.cond(jnp.int32(0) > last_frame, keep_state, forward_compute, start_state)
    final_max, final_sum, final_acc = final_state
    log_total = final_max + jnp.log(final_sum)
    attended_full = final_acc / final_sum[..., None]
    attended = (
        jnp.transpose(attended_full, (0, 2, 1, 3))
        .reshape(seq_count, frames, width)
        .astype(jnp.bfloat16)
    )
    after_self = residual + apply_fwd(attended, attn_out) + attn_out_bias
    cross_full, normed_one, inverse_one = normalize(after_self, gains[1], shifts[1])
    cross_normed = cross_full.astype(jnp.bfloat16)
    cross_queries = (apply_fwd(cross_normed, cross_query) + cross_query_bias).astype(jnp.bfloat16)
    cross_attention_heads = heads_of(cross_queries)
    text_proj = apply_fwd(text_states, cross_kv)
    encoder_key_rows = heads_of(text_proj[..., :width].astype(jnp.bfloat16))
    encoder_value_rows = heads_of((text_proj[..., width:] + cross_v_bias).astype(jnp.bfloat16))
    cross_scores = (
        jnp.einsum(
            "qybj,qzbj->qbyz",
            cross_attention_heads,
            encoder_key_rows,
            preferred_element_type=jnp.float32,
        )
        * scale
    )
    text_mask = (
        jnp.arange(text_count, dtype=jnp.int32)[None, None, None, :]
        < text_lengths[:, None, None, None]
    )
    cross_scores = jnp.where(text_mask, cross_scores, NEG_FILL)
    cross_top = jnp.max(cross_scores, -1, keepdims=True)
    cross_raised = jnp.where(text_mask, jnp.exp(cross_scores - cross_top), 0.0)
    cross_probs = cross_raised / jnp.sum(cross_raised, -1, keepdims=True)
    cross_attention_weights = cross_probs.astype(jnp.bfloat16)
    cross_attended = (
        jnp.einsum(
            "oalx,oxak->olak",
            cross_attention_weights,
            encoder_value_rows,
            preferred_element_type=jnp.float32,
        )
        .reshape(seq_count, frames, width)
        .astype(jnp.bfloat16)
    )
    after_cross = after_self + apply_fwd(cross_attended, cross_out) + cross_out_bias
    ff_full, normed_two, inverse_two = normalize(after_cross, gains[2], shifts[2])
    ff_normed = ff_full.astype(jnp.bfloat16)
    pre_gelu = apply_fwd(ff_normed, ff_up) + ff_up_bias
    activated = jax.nn.gelu(pre_gelu, approximate=False).astype(jnp.bfloat16)
    layer_output = (after_cross + apply_fwd(activated, ff_down) + ff_down_bias).astype(jnp.bfloat16)
    ff_down_grad = outer_sum(activated, out_grad)
    ff_down_bias_grad = column_sum(out_grad)
    act_grad = apply_back(out_grad, ff_down)
    gelu_value, gelu_pull = jax.vjp(partial(jax.nn.gelu, approximate=False), pre_gelu)
    before_gelu_gradient = gelu_pull(act_grad)[0].astype(jnp.bfloat16)
    ff_up_grad = outer_sum(ff_normed, before_gelu_gradient)
    ff_up_bias_grad = column_sum(before_gelu_gradient)
    back_two, gain_two, shift_two = norm_back(
        apply_back(before_gelu_gradient, ff_up), normed_two, inverse_two, gains[2]
    )
    cross_grad = out_grad.astype(jnp.float32) + back_two
    cross_grad_low = cross_grad.astype(jnp.bfloat16)
    cross_out_grad = outer_sum(cross_attended, cross_grad_low)
    cross_out_bias_grad = column_sum(cross_grad_low)
    cross_attention_gradient = heads_of(apply_back(cross_grad_low, cross_out).astype(jnp.bfloat16))
    cross_dp = jnp.einsum(
        "qybj,qzbj->qbyz",
        cross_attention_gradient,
        encoder_value_rows,
        preferred_element_type=jnp.float32,
    )
    cross_logit_gradient = (
        cross_probs * (cross_dp - jnp.sum(cross_probs * cross_dp, -1, keepdims=True))
    ).astype(jnp.bfloat16)
    text_key_grad = scale * jnp.einsum(
        "wopc,wpou->wcou",
        cross_logit_gradient,
        cross_attention_heads,
        preferred_element_type=jnp.float32,
    ).reshape(seq_count, text_count, width)
    text_value_grad = jnp.einsum(
        "wopc,wpou->wcou",
        cross_attention_weights,
        cross_attention_gradient,
        preferred_element_type=jnp.float32,
    ).reshape(seq_count, text_count, width)
    text_key_grad, text_value_grad = lax.psum((text_key_grad, text_value_grad), "blk")
    text_kv_low = jnp.concatenate([text_key_grad, text_value_grad], -1).astype(jnp.bfloat16)
    text_grad = jnp.einsum(
        "stf,df->std", text_kv_low, cross_kv, preferred_element_type=jnp.float32
    ).astype(jnp.bfloat16)
    row_share = width // axis_count
    text_slice = lax.dynamic_slice_in_dim(text_states, block_index * row_share, row_share, 2)
    cross_kv_rows = jnp.einsum(
        "std,stf->df", text_slice, text_kv_low, preferred_element_type=jnp.float32
    )
    value_slice = lax.dynamic_slice_in_dim(
        text_kv_low, width + block_index * row_share, row_share, 2
    )
    cross_v_bias_rows = column_sum(value_slice)
    cross_q_grad = (
        (
            scale
            * jnp.einsum(
                "oalx,oxak->olak",
                cross_logit_gradient,
                encoder_key_rows,
                preferred_element_type=jnp.float32,
            )
        )
        .reshape(seq_count, frames, width)
        .astype(jnp.bfloat16)
    )
    cross_query_grad = outer_sum(cross_normed, cross_q_grad)
    cross_query_bias_grad = column_sum(cross_q_grad)
    back_one, gain_one, shift_one = norm_back(
        apply_back(cross_q_grad, cross_query), normed_one, inverse_one, gains[1]
    )
    self_grad = cross_grad + back_one
    self_grad_low = self_grad.astype(jnp.bfloat16)
    attn_out_grad = outer_sum(attended, self_grad_low)
    attn_out_bias_grad = column_sum(self_grad_low)
    att_grad = apply_back(self_grad_low, attn_out).astype(jnp.bfloat16)
    att_heads = heads_of(att_grad)
    delta = jnp.sum(jnp.transpose(att_heads.astype(jnp.float32), (0, 2, 1, 3)) * attended_full, -1)
    query_zero = jnp.zeros((seq_count, frames, head_count, head_size), jnp.float32)
    query_key_piece = lax.all_gather(key_rows, "blk", axis=1, tiled=True)
    query_value_piece = lax.all_gather(value_rows, "blk", axis=1, tiled=True)
    query_span = query_key_piece.shape[1]

    def query_compute(state):
        key_pos = jnp.arange(query_span, dtype=jnp.int32)
        piece_keys = heads_of(query_key_piece)
        scores = (
            jnp.einsum(
                "sfhd,sphd->shfp", query_heads, piece_keys, preferred_element_type=jnp.float32
            )
            * scale
        )
        mask = visible(key_pos, my_pos)
        probs = jnp.where(mask, jnp.exp(scores - log_total[..., None]), 0.0)
        prob_grad = jnp.einsum(
            "sfhd,sphd->shfp",
            att_heads,
            heads_of(query_value_piece),
            preferred_element_type=jnp.float32,
        )
        score_grad = (probs * (prob_grad - delta[..., None])).astype(jnp.bfloat16)
        return scale * jnp.einsum(
            "shfp,sphd->sfhd", score_grad, piece_keys, preferred_element_type=jnp.float32
        )

    query_grad = lax.cond(jnp.int32(0) > last_frame, keep_state, query_compute, query_zero)
    total_logs, total_deltas = (
        lax.all_gather(log_total, "blk", axis=2, tiled=True),
        lax.all_gather(delta, "blk", axis=2, tiled=True),
    )
    my_keys = heads_of(key_rows)
    my_values = heads_of(value_rows)
    query_piece_rows = lax.all_gather(query_rows, "blk", axis=1, tiled=True)
    grad_piece_rows = lax.all_gather(att_grad, "blk", axis=1, tiled=True)
    key_span = query_piece_rows.shape[1]

    def key_compute(state):
        query_pos = jnp.arange(key_span, dtype=jnp.int32)
        piece_queries = heads_of(query_piece_rows)
        piece_grads = heads_of(grad_piece_rows)
        scores = (
            jnp.einsum(
                "sphd,sfhd->shpf", piece_queries, my_keys, preferred_element_type=jnp.float32
            )
            * scale
        )
        mask = visible(my_pos, query_pos)
        probs = jnp.where(mask, jnp.exp(scores - total_logs[..., None]), 0.0)
        value_acc = jnp.einsum(
            "shpf,sphd->sfhd",
            probs.astype(jnp.bfloat16),
            piece_grads,
            preferred_element_type=jnp.float32,
        )
        prob_grad = jnp.einsum(
            "sphd,sfhd->shpf", piece_grads, my_values, preferred_element_type=jnp.float32
        )
        score_grad = (probs * (prob_grad - total_deltas[..., None])).astype(jnp.bfloat16)
        key_acc = scale * jnp.einsum(
            "shpf,sphd->sfhd", score_grad, piece_queries, preferred_element_type=jnp.float32
        )
        return (key_acc, value_acc)

    key_grad, value_grad = lax.cond(
        jnp.int32(0) + key_span - 1 < first_frame, keep_state, key_compute, (query_zero, query_zero)
    )
    query_low = query_grad.reshape(seq_count, frames, width).astype(jnp.bfloat16)
    value_low = value_grad.reshape(seq_count, frames, width).astype(jnp.bfloat16)
    qkv_grad = jnp.concatenate(
        [query_low, key_grad.reshape(seq_count, frames, width).astype(jnp.bfloat16), value_low], -1
    )
    attn_in_grad = outer_sum(attn_normed, qkv_grad)
    attn_in_bias_grad = jnp.concatenate([column_sum(query_low), column_sum(value_low)])
    back_zero, gain_zero, shift_zero = norm_back(
        apply_back(qkv_grad, attn_in), normed_zero, inverse_zero, gains[0]
    )
    hidden_grad = (self_grad + back_zero).astype(jnp.bfloat16)
    gain_grads = jnp.stack([gain_zero, gain_one, gain_two])
    shift_grads = jnp.stack([shift_zero, shift_one, shift_two])
    (
        ain_rows,
        ainb_rows,
        aout_rows,
        aoutb_rows,
        cq_rows,
        cqb_rows,
        cout_rows,
        coutb_rows,
        up_rows,
        up_bias_rows,
        down_rows,
        downb_rows,
        gain_rows,
        shift_rows,
    ) = (
        lax.psum_scatter(attn_in_grad, "blk", scatter_dimension=0, tiled=True),
        lax.psum_scatter(attn_in_bias_grad, "blk", scatter_dimension=0, tiled=True),
        lax.psum_scatter(attn_out_grad, "blk", scatter_dimension=0, tiled=True),
        lax.psum_scatter(attn_out_bias_grad, "blk", scatter_dimension=0, tiled=True),
        lax.psum_scatter(cross_query_grad, "blk", scatter_dimension=0, tiled=True),
        lax.psum_scatter(cross_query_bias_grad, "blk", scatter_dimension=0, tiled=True),
        lax.psum_scatter(cross_out_grad, "blk", scatter_dimension=0, tiled=True),
        lax.psum_scatter(cross_out_bias_grad, "blk", scatter_dimension=0, tiled=True),
        lax.psum_scatter(ff_up_grad, "blk", scatter_dimension=0, tiled=True),
        lax.psum_scatter(ff_up_bias_grad, "blk", scatter_dimension=0, tiled=True),
        lax.psum_scatter(ff_down_grad, "blk", scatter_dimension=0, tiled=True),
        lax.psum_scatter(ff_down_bias_grad, "blk", scatter_dimension=0, tiled=True),
        lax.psum_scatter(gain_grads, "blk", scatter_dimension=1, tiled=True),
        lax.psum_scatter(shift_grads, "blk", scatter_dimension=1, tiled=True),
    )
    summed = (
        lax.psum(ain_rows.astype(jnp.bfloat16), "items").astype(jnp.float32),
        lax.psum(ainb_rows.astype(jnp.bfloat16), "items").astype(jnp.float32),
        lax.psum(aout_rows.astype(jnp.bfloat16), "items").astype(jnp.float32),
        lax.psum(aoutb_rows.astype(jnp.bfloat16), "items").astype(jnp.float32),
        lax.psum(cq_rows.astype(jnp.bfloat16), "items").astype(jnp.float32),
        lax.psum(cqb_rows.astype(jnp.bfloat16), "items").astype(jnp.float32),
        lax.psum(cross_kv_rows.astype(jnp.bfloat16), "items").astype(jnp.float32),
        lax.psum(cross_v_bias_rows.astype(jnp.bfloat16), "items").astype(jnp.float32),
        lax.psum(cout_rows.astype(jnp.bfloat16), "items").astype(jnp.float32),
        lax.psum(coutb_rows.astype(jnp.bfloat16), "items").astype(jnp.float32),
        lax.psum(up_rows.astype(jnp.bfloat16), "items").astype(jnp.float32),
        lax.psum(up_bias_rows.astype(jnp.bfloat16), "items").astype(jnp.float32),
        lax.psum(down_rows.astype(jnp.bfloat16), "items").astype(jnp.float32),
        lax.psum(downb_rows.astype(jnp.bfloat16), "items").astype(jnp.float32),
        lax.psum(gain_rows.astype(jnp.bfloat16), "items").astype(jnp.float32),
        lax.psum(shift_rows.astype(jnp.bfloat16), "items").astype(jnp.float32),
    )
    return (
        layer_output,
        hidden_grad,
        text_grad,
        summed[0],
        summed[1],
        summed[2],
        summed[3],
        summed[4],
        summed[5],
        summed[6],
        summed[7],
        summed[8],
        summed[9],
        summed[10],
        summed[11],
        summed[12],
        summed[13],
        summed[14],
        summed[15],
    )


LANES = 128
MESH_ID = pl.DeviceIdType.MESH
VMEM_BYTES = 56 * 1024 * 1024


def contract(left, right, left_dim, right_dim):
    return lax.dot_general(
        left, right, (((left_dim,), (right_dim,)), ((), ())), preferred_element_type=jnp.float32
    )


def two_heads(values, low_half):
    none = jnp.zeros_like(values)
    return jnp.concatenate(
        [jnp.where(low_half, values, none), jnp.where(low_half, none, values)], 0
    )


LAGS = (0, 1, 2, 6, 11, 16, 21, 25, 26, 28)
FLASH_TURN = 3
TEXT_TURN = 14
SEND_TURNS = (9, 16)
LAND_TURN = 27
EARLY = 27
LATE = 5
SECOND_TURN = 2
ROWS = 256
VECTOR_ROWS = 24
VECTORS = ((0, 2), (2, 1), (3, 1), (4, 1), (5, 1), (6, 4), (10, 1))


def added(*terms):
    total = terms[0].astype(jnp.float32)
    for term in terms[1:]:
        total = total + term.astype(jnp.float32)
    return total.astype(jnp.bfloat16)


class Lane(NamedTuple):
    own: object
    got: object
    left: object
    right: object
    one_got: object
    one_sum: object
    two_got: object
    two_sum: object
    z_got: object
    z_sums: object
    z_kept: object
    z_far: object
    z_sum: object
    spread: object
    half: object
    back: object
    out: object
    made: object


class Slots(NamedTuple):
    mixed_grads: object
    query_grads: object
    key_grads: object
    value_grads: object
    key_sum: object
    value_sum: object
    landed: object
    turned: object
    text_parts: object
    text_sums: object
    text_low: object
    matrix: object
    matrix_got: object
    matrix_sum: object
    send_sem: object
    recv_sem: object
    load_sem: object
    store_sem: object
    out_send: object
    out_recv: object
    back_send: object
    back_recv: object
    text_send: object
    text_recv: object
    matrix_send: object
    matrix_recv: object
    save_sem: object
    hidden_sum: object
    self_grad: object
    hidden: object
    vectors: object
    vector_got: object
    vector_items: object
    final_sem: object
    vector_send: object
    vector_recv: object
    inputs: object
    input_sem: object
    matrix_final: object
    hidden_final: object
    vector_final: object
    end_sem: object


def lane_slots(half, rows_first, rows):
    low = jnp.bfloat16
    one = (4, 2, half, LANES) if rows_first else (4, LANES, LANES)
    return Lane(
        own=pltpu.VMEM((8, 4, 2, LANES, LANES), low),
        got=pltpu.VMEM((4, 4, 2, LANES, LANES), low),
        left=pltpu.VMEM((2, 4, 2, LANES, rows), low),
        right=pltpu.VMEM((2, rows, 2 * LANES), low),
        one_got=pltpu.VMEM((16,) + one, low),
        one_sum=pltpu.VMEM((10,) + one, low),
        two_got=pltpu.VMEM((18, 4, half, LANES), low),
        two_sum=pltpu.VMEM((12, 4, half, LANES), low),
        z_got=pltpu.VMEM((14, 3, half, LANES), low),
        z_sums=pltpu.VMEM((8, 3, half, LANES), low),
        z_kept=pltpu.VMEM((8, half, LANES), low),
        z_far=pltpu.VMEM((20, half, LANES), low),
        z_sum=pltpu.VMEM((8, half, LANES), low),
        spread=pltpu.VMEM((12, half, LANES), low),
        half=pltpu.VMEM((4, LANES, LANES), low),
        back=pltpu.VMEM((4, LANES, LANES), low),
        out=pltpu.VMEM((4, 2, LANES, LANES), low),
        made=pltpu.VMEM((4, 4, 2, LANES, LANES), low),
    )


def rings(text_shape, item_shape, frame_shape, blocks, kept):
    items, length, lanes = item_shape
    _, frames, triple = frame_shape
    width = triple // 3
    low = jnp.bfloat16
    return Slots(
        mixed_grads=pltpu.VMEM(item_shape, low),
        query_grads=pltpu.VMEM(item_shape, low),
        key_grads=pltpu.VMEM(item_shape, low),
        value_grads=pltpu.VMEM(item_shape, low),
        key_sum=pltpu.VMEM((length, lanes), jnp.float32),
        value_sum=pltpu.VMEM((length, lanes), jnp.float32),
        landed=pltpu.VMEM(frame_shape, low),
        turned=pltpu.VMEM((frame_shape[0], frame_shape[2] // 3, frame_shape[1]), low),
        text_parts=pltpu.VMEM((2, blocks) + text_shape, low),
        text_sums=pltpu.VMEM((2,) + text_shape, low),
        text_low=pltpu.VMEM(text_shape[:2] + (2 * blocks * LANES,), low),
        matrix=pltpu.VMEM((2, LANES, blocks * LANES), low),
        matrix_got=pltpu.VMEM((3, LANES, blocks * LANES), low),
        matrix_sum=pltpu.VMEM((2, LANES, blocks * LANES), low),
        send_sem=pltpu.SemaphoreType.DMA((16, 22)),
        recv_sem=pltpu.SemaphoreType.DMA((16, 22)),
        load_sem=pltpu.SemaphoreType.DMA((2, 2, 2)),
        store_sem=pltpu.SemaphoreType.DMA((2, 2, 4)),
        out_send=pltpu.SemaphoreType.DMA((items + 2, blocks)),
        out_recv=pltpu.SemaphoreType.DMA((items + 2, blocks)),
        back_send=pltpu.SemaphoreType.DMA((items, 3, blocks)),
        back_recv=pltpu.SemaphoreType.DMA((items, 3, blocks)),
        text_send=pltpu.SemaphoreType.DMA((2, blocks)),
        text_recv=pltpu.SemaphoreType.DMA((2, blocks)),
        matrix_send=pltpu.SemaphoreType.DMA((3,)),
        matrix_recv=pltpu.SemaphoreType.DMA((3,)),
        save_sem=pltpu.SemaphoreType.DMA((2,)),
        hidden_sum=pltpu.VMEM((items, frames, width), jnp.float32),
        self_grad=pltpu.VMEM((items, frames, width), jnp.float32),
        hidden=pltpu.VMEM((items, frames, width), low),
        vectors=pltpu.VMEM((blocks, VECTOR_ROWS, LANES), jnp.float32),
        vector_got=pltpu.VMEM((blocks, VECTOR_ROWS, LANES), jnp.float32),
        vector_items=pltpu.VMEM((4, VECTOR_ROWS, LANES), jnp.float32),
        final_sem=pltpu.SemaphoreType.DMA((2,)),
        vector_send=pltpu.SemaphoreType.DMA((blocks + 3,)),
        vector_recv=pltpu.SemaphoreType.DMA((blocks + 3,)),
        inputs=tuple(pltpu.VMEM(array.shape, array.dtype) for array in kept),
        input_sem=pltpu.SemaphoreType.DMA((len(kept),)),
        matrix_final=pltpu.VMEM((2, LANES, width), jnp.float32),
        hidden_final=pltpu.VMEM((items, frames, width), low),
        vector_final=pltpu.VMEM((VECTOR_ROWS, LANES), jnp.float32),
        end_sem=pltpu.SemaphoreType.DMA((3,)),
    )


def backward_kernel(plan, head, *refs):
    refs = list(refs)

    def take(count):
        taken = refs[:count]
        del refs[:count]
        return taken

    (limit_ref, att_grad, text_key, text_value) = take(4)
    kept = take(10)
    hidden_ref, self_ref, weight_ref = take(3)
    lefts = take(len(plan) - 1)
    rights = take(len(plan) - 1)
    outs = take(len(plan))
    text_out, matrix_out, hidden_out = take(3)
    vector_out = take(1)[0]
    lanes_of = [Lane(*take(len(Lane._fields))) for _ in range(2)]
    own = Slots(*refs)
    q_ref, k_ref, v_ref, o_ref, lse_ref, normed_ref, text_ref, sums_ref, up_ref, gain_ref = own.inputs
    items, length, lanes = q_ref.shape
    frames = att_grad.shape[1]
    width = att_grad.shape[2]
    blocks = length // frames
    group = lax.axis_index("items")
    block = lax.axis_index("blk")
    y, core = group // 2, group % 2
    z, x = block // 2, block % 2
    to_core = {"items": y * 2 + (1 - core)}
    to_y = {"items": (1 - y) * 2 + core}
    to_x = {"blk": z * 2 + (1 - x)}
    is_inner = (z == 1) | (z == 2)
    to_neighbour = {"blk": (z + 1 - 2 * (z % 2)) * 2 + x}
    to_far_inner = {"blk": (2 - z // 2) * 2 + x}
    to_far_outer = {"blk": (3 - 3 * (z // 2)) * 2 + x}
    places = [lax.rem(block + step, blocks) for step in range(blocks)]
    inputs = [
        pltpu.make_async_copy(source, target, own.input_sem.at[number])
        for number, (source, target) in enumerate(zip(kept, own.inputs))
    ]
    for copy in inputs:
        copy.start()
    barrier = pltpu.get_barrier_semaphore()
    to_far = {"items": (1 - y) * 2 + (1 - core)}
    peers = [to_core, to_y, to_far] + [{"blk": place} for place in places[1:]]
    for peer in peers:
        pl.semaphore_signal(barrier, inc=1, device_id=peer, device_id_type=MESH_ID)
    pl.semaphore_wait(barrier, len(peers))

    def at(ring, index):
        return ring.at[lax.rem(index, ring.shape[0])]

    def half_rows(place):
        return pl.ds(pl.multiple_of(place * (LANES // 2), LANES // 2), LANES // 2)

    def lane_block(offset, place):
        return pl.ds(pl.multiple_of(offset + place * LANES, LANES), LANES)

    def frame_rows(place):
        return pl.ds(pl.multiple_of(place * frames, frames), frames)

    def copy_to(peer, source, target, send, recv):
        return pltpu.make_async_remote_copy(
            src_ref=source,
            dst_ref=target,
            send_sem=send,
            recv_sem=recv,
            device_id=peer,
            device_id_type=MESH_ID,
        )

    def remote(kind, got, index, source, peer):
        slot = lax.rem(index, got.shape[0])
        return copy_to(
            peer,
            source,
            got.at[slot],
            own.send_sem.at[kind, slot],
            own.recv_sem.at[kind, slot],
        )

    def target_view(tensor, local, half):
        parts = plan[tensor][2]
        return outs[tensor].at[local % parts, :, lane_block(half * LANES, 2 * (local // parts))]

    def with_tensor(piece, action):
        for tensor, (start, count, _) in enumerate(plan):

            @pl.when((piece >= start) & (piece < start + count))
            def _():
                action(tensor, piece - start)

    made_start = plan[-1][0]

    def lane_steps(number, lane, base, offset, rows_first):
        def loads(index, tensor, local):
            slot = lax.rem(index, lane.left.shape[0])
            parts = plan[tensor][2]
            columns = pl.ds(pl.multiple_of((local // parts) * 2 * LANES, LANES), 2 * LANES)
            return [
                pltpu.make_async_copy(
                    lefts[tensor].at[:, :, local % parts],
                    lane.left.at[slot],
                    own.load_sem.at[number, 0, slot],
                ),
                pltpu.make_async_copy(
                    rights[tensor].at[:, columns],
                    lane.right.at[slot],
                    own.load_sem.at[number, 1, slot],
                ),
            ]

        def weight_load(index, local):
            slot = lax.rem(index, lane.left.shape[0])
            columns = pl.ds(pl.multiple_of(local * 2 * LANES, LANES), 2 * LANES)
            return pltpu.make_async_copy(
                weight_ref.at[:, :, :, columns],
                lane.left.at[slot, :, :, :, 0 : 2 * LANES],
                own.load_sem.at[number, 0, slot],
            )

        def fetch(index):
            def start(tensor, local):
                if tensor < len(plan) - 1:
                    for copy in loads(index, tensor, local):
                        copy.start()
                else:
                    weight_load(index, local).start()

            with_tensor(base + index, start)

        def send(kind, got, index, source, peer):
            return remote(8 * number + kind, got, index, source, peer)

        def split(index, product):
            product = product.reshape(4, 2, LANES, 2 * LANES).astype(jnp.bfloat16)
            sides = (product[..., :LANES], product[..., LANES:])
            at(lane.own, index)[...] = jnp.where(core == 0, sides[0], sides[1])
            at(lane.made, index)[...] = jnp.where(core == 0, sides[1], sides[0])

        def begin(index):
            @pl.when(base + index < made_start)
            def _():
                for copy in loads(index, 0, 0):
                    copy.wait()
                left = at(lane.left, index)[...].reshape(8 * LANES, -1)
                split(index, contract(left, at(lane.right, index)[...], 1, 0))

            @pl.when(base + index >= made_start)
            def _():
                local = base + index - made_start
                columns = pl.ds(pl.multiple_of(local * 2 * LANES, LANES), 2 * LANES)
                parts = [
                    contract(own.turned[item], own.landed[item, :, columns], 1, 0)
                    for item in range(items)
                ]
                split(index, sum(parts))
                weight_load(index, local).wait()
                weight = at(lane.left, index)[:, :, :, 0 : 2 * LANES].reshape(width, 2 * LANES)
                for item in range(items):
                    own.hidden_sum[item] += contract(own.landed[item, :, columns], weight, 1, 1)

            send(0, lane.got, index, at(lane.made, index), to_core).start()

        def one_copy(index):
            if rows_first:
                source = at(lane.own, index).at[:, :, half_rows(1 - y), :]
                return send(1, lane.one_got, index, source, to_y)
            return send(1, lane.one_got, index, at(lane.own, index).at[:, 1 - x], to_x)

        def two_copy(index):
            if rows_first:
                return send(2, lane.two_got, index, at(lane.one_sum, index).at[:, 1 - x], to_x)
            source = at(lane.one_sum, index).at[:, half_rows(1 - y), :]
            return send(2, lane.two_got, index, source, to_y)

        def z_near(index, outward):
            slot = lax.rem(index, lane.z_got.shape[0])
            sums = at(lane.two_sum, index)
            if outward:
                source, target = sums.at[3 * (z // 2)], lane.z_got.at[slot, 0]
            else:
                source, target = sums.at[pl.ds(1 - z // 2, 3)], lane.z_got.at[slot]
            return copy_to(
                to_neighbour,
                source,
                target,
                own.send_sem.at[8 * number + 3, slot],
                own.recv_sem.at[8 * number + 3, slot],
            )

        def z_across(index, outer):
            slot = lax.rem(index, lane.z_far.shape[0])
            sums = at(lane.z_sums, index)
            return copy_to(
                to_far_outer if outer else to_far_inner,
                sums.at[2 * (1 - z // 2)] if outer else sums.at[1],
                lane.z_far.at[slot],
                own.send_sem.at[8 * number + 4 + outer, slot],
                own.recv_sem.at[8 * number + 4, slot],
            )

        def spread_copy(index):
            return send(6, lane.spread, index, at(lane.z_sum, index), to_y)

        def back_copy(index):
            return send(7, lane.back, index, at(lane.half, index), to_core)

        def chip(index):
            send(0, lane.got, index, at(lane.made, index), to_core).wait()
            target = at(lane.own, index)
            target[...] = added(target[...], at(lane.got, index)[...])
            one_copy(index).start()

        def one(index):
            one_copy(index).wait()
            kept = at(lane.own, index)
            kept = kept[:, :, half_rows(y), :] if rows_first else kept[:, x]
            at(lane.one_sum, index)[...] = added(kept, at(lane.one_got, index)[...])
            two_copy(index).start()

        def two(index):
            two_copy(index).wait()
            kept = at(lane.one_sum, index)
            kept = kept[:, x] if rows_first else kept[:, half_rows(y), :]
            at(lane.two_sum, index)[...] = added(kept, at(lane.two_got, index)[...])
            @pl.when(is_inner)
            def _():
                z_near(index, True).start()

            @pl.when(jnp.logical_not(is_inner))
            def _():
                z_near(index, False).start()

        def near(index):
            @pl.when(is_inner)
            def _():
                z_near(index, True).wait_send()
                z_near(index, False).wait_recv()
                first = 1 - z // 2
                sums = at(lane.z_sums, index)
                sums[...] = added(
                    at(lane.two_sum, index)[pl.ds(first, 3)], at(lane.z_got, index)[...]
                )
                at(lane.z_kept, index)[...] = sums[2 * (z // 2)]
                z_across(index, 0).start()
                z_across(index, 1).start()

            @pl.when(jnp.logical_not(is_inner))
            def _():
                z_near(index, False).wait_send()
                z_near(index, True).wait_recv()
                at(lane.z_kept, index)[...] = added(
                    at(lane.two_sum, index)[z], at(lane.z_got, index)[0]
                )

        def three(index):
            @pl.when(is_inner)
            def _():
                z_across(index, 0).wait_send()
                z_across(index, 1).wait_send()

            z_across(index, 0).wait_recv()
            at(lane.z_sum, index)[...] = added(
                at(lane.z_kept, index)[...], at(lane.z_far, index)[...]
            )
            spread_copy(index).start()

        def four(index):
            spread_copy(index).wait()
            target = at(lane.half, index)
            target[half_rows(y), :] = at(lane.z_sum, index)[...]
            target[half_rows(1 - y), :] = at(lane.spread, index)[...]
            back_copy(index).start()

        def finish(index):
            back_copy(index).wait()
            slot = lax.rem(index, lane.out.shape[0])
            lane.out[slot, core] = at(lane.half, index)[...]
            lane.out[slot, 1 - core] = at(lane.back, index)[...]

            def start(tensor, local):
                for side in range(2):
                    pltpu.make_async_copy(
                        lane.out.at[slot, side],
                        target_view(tensor, local, side),
                        own.store_sem.at[number, side, slot],
                    ).start()

            with_tensor(base + index, start)

        def close(index):
            slot = lax.rem(index, lane.out.shape[0])
            for side in range(2):
                pltpu.make_async_copy(
                    lane.out.at[slot, side],
                    target_view(0, 0, side),
                    own.store_sem.at[number, side, slot],
                ).wait()

        return [
            lambda index, step=step: step(index + offset)
            for step in (fetch, begin, chip, one, two, near, three, four, finish, close)
        ]

    def out_copies(item):
        copies = []
        for step in range(blocks):
            source = att_grad.at[item, :, lane_block(0, places[step])]
            target = own.mixed_grads.at[item, frame_rows(block), :]
            recv = own.out_recv.at[item, step]
            if step == 0:
                copies.append(pltpu.make_async_copy(source, target, recv))
            else:
                peer = {"blk": places[step]}
                copies.append(copy_to(peer, source, target, own.out_send.at[item, step], recv))
        return copies

    def text_out_copies():
        copies = []
        for part, text in enumerate((text_key, text_value)):
            for step in range(blocks):
                source = text.at[:, :, lane_block(0, places[step])]
                target = own.text_parts.at[part, step]
                recv = own.out_recv.at[items + part, step]
                if step == 0:
                    copies.append(pltpu.make_async_copy(source, target, recv))
                else:
                    peer = {"blk": places[step]}
                    send = own.out_send.at[items + part, step]
                    copies.append(copy_to(peer, source, target, send, recv))
        return copies

    def out_start(_):
        for item in range(items):
            for copy in out_copies(item):
                copy.start()
        for copy in text_out_copies():
            copy.start()

    def out_wait(item):
        def run(_):
            for copy in out_copies(item) + (inputs[:5] if item == 0 else []):
                copy.wait()

        return run

    scale = head ** (-0.5)
    flash_blocks = length // ROWS

    def flash_unit(item, number):
        span = (number + 1) * ROWS
        here = slice(number * ROWS, span)
        low_half = lax.broadcasted_iota(jnp.int32, (ROWS, lanes), 1) < head
        queries = two_heads(q_ref[item, here, :] * jnp.bfloat16(scale), low_half)
        mixed_grad = own.mixed_grads[item, here, :]
        mixed_grads = two_heads(mixed_grad, low_half)
        logs = jnp.transpose(lse_ref[item, here, :])
        logs = jnp.concatenate([logs[0:1], logs[head : head + 1]], 1)
        products = jnp.transpose(mixed_grad.astype(jnp.float32) * o_ref[item, here, :])
        delta = jnp.concatenate(
            [
                jnp.sum(products[:head], 0, keepdims=True),
                jnp.sum(products[head:], 0, keepdims=True),
            ],
            1,
        )
        keys = k_ref[item, :span, :]
        scores = contract(keys, queries, 1, 1)
        key_pos = lax.broadcasted_iota(jnp.int32, (ROWS, 2 * ROWS), 0)
        query_pos = lax.broadcasted_iota(jnp.int32, (ROWS, 2 * ROWS), 1) % ROWS
        corner = jnp.where(key_pos <= query_pos, scores[span - ROWS :], NEG_FILL)
        scores = corner if number == 0 else jnp.concatenate([scores[: span - ROWS], corner], 0)
        if span > length // 2:
            valid = lax.broadcasted_iota(jnp.int32, (span, 1), 0) < limit_ref[item]
            scores = scores + jnp.where(valid, 0.0, NEG_FILL)
        probs = jnp.exp(scores - logs)
        prob_grads = contract(v_ref[item, :span, :], mixed_grads, 1, 1)
        score_grads = (probs * (prob_grads - delta)).astype(jnp.bfloat16)
        query_grads = scale * contract(score_grads, keys, 0, 0)
        own.query_grads[item, here, :] = jnp.where(
            low_half, query_grads[:ROWS], query_grads[ROWS:]
        ).astype(jnp.bfloat16)
        value_part = contract(probs.astype(jnp.bfloat16), mixed_grads, 1, 0)
        key_part = contract(score_grads, queries, 1, 0)
        if number == flash_blocks - 1:
            own.value_sum[...] = value_part
            own.key_sum[...] = key_part
        else:
            own.value_sum[:span] += value_part
            own.key_sum[:span] += key_part
        if number == 0:
            own.key_grads[item] = own.key_sum[...].astype(jnp.bfloat16)
            own.value_grads[item] = own.value_sum[...].astype(jnp.bfloat16)

    def flash(index):
        for number in range(flash_blocks):

            @pl.when(lax.rem(index, flash_blocks) == flash_blocks - 1 - number)
            def _():
                flash_unit(index // flash_blocks, number)

    parts_of = (own.query_grads, own.key_grads, own.value_grads)

    def back_copy(item, part, step):
        place = lax.rem(block + step, blocks)
        return copy_to(
            {"blk": place},
            parts_of[part].at[item, frame_rows(place), :],
            own.landed.at[item, :, lane_block(part * width, block)],
            own.back_send.at[item, part, step],
            own.back_recv.at[item, part, step],
        )

    def back_own(item, part):
        return pltpu.make_async_copy(
            parts_of[part].at[item, frame_rows(block), :],
            own.landed.at[item, :, lane_block(part * width, block)],
            own.back_recv.at[item, part, 0],
        )

    def back_some(item):
        def run(index):
            @pl.when(index == 0)
            def _():
                for part in range(3):
                    back_own(item, part).start()

            for part in range(3):
                back_copy(item, part, 1 + index).start()

        return run

    def text_save():
        return pltpu.make_async_copy(own.text_low, text_out, own.save_sem.at[0])

    def final_loads():
        return [
            pltpu.make_async_copy(self_ref, own.self_grad, own.final_sem.at[0]),
            pltpu.make_async_copy(hidden_ref, own.hidden, own.final_sem.at[1]),
        ]

    def back_wait(_):
        for item in range(items):
            for part in range(3):
                back_own(item, part).wait()
                for step in range(1, blocks):
                    back_copy(item, part, step).wait()
            if item == 0:
                inputs[5].wait()
            own.turned[item] = jnp.transpose(normed_ref[item])
        own.hidden_sum[...] = jnp.zeros_like(own.hidden_sum)
        for copy in final_loads():
            copy.start()

    def vector_copy(kind, source, target, peer):
        return copy_to(
            peer, source, target, own.vector_send.at[kind], own.vector_recv.at[kind]
        )

    def vector_blocks():
        return [
            vector_copy(
                step, own.vectors.at[places[step]], own.vector_got.at[step], {"blk": places[step]}
            )
            for step in range(1, blocks)
        ]

    def vector_spread():
        return [
            vector_copy(
                blocks + number, own.vector_items.at[0], own.vector_items.at[1 + number], peer
            )
            for number, peer in enumerate([to_core, to_y, to_far])
        ]

    def final(_):
        for copy in final_loads() + inputs[7:]:
            copy.wait()
        gain_zero = 0.0
        shift_zero = 0.0
        query_bias = 0.0
        value_bias = 0.0
        gains = gain_ref[0:1, :].astype(jnp.float32)
        for item in range(items):
            normed, inverse = row_norm(own.hidden[item].astype(jnp.float32))
            grad = own.hidden_sum[item]
            gain_zero = gain_zero + total_rows(grad * normed)
            shift_zero = shift_zero + total_rows(grad)
            own.hidden_final[item] = (
                own.self_grad[item] + row_norm_back(grad, normed, inverse, gains)
            ).astype(jnp.bfloat16)
            query_bias = query_bias + total_rows(own.landed[item, :, :width])
            value_bias = value_bias + total_rows(own.landed[item, :, 2 * width :])
        singles = [
            (2, sums_ref[3:4, :]),
            (3, sums_ref[2:3, :]),
            (5, sums_ref[1:2, :]),
            (10, sums_ref[0:1, :]),
            (11, gain_zero),
            (12, sums_ref[4:5, :]),
            (13, sums_ref[5:6, :]),
            (14, shift_zero),
            (15, sums_ref[6:7, :]),
            (16, sums_ref[7:8, :]),
        ]
        own.vectors[...] = jnp.zeros_like(own.vectors)
        for place in range(blocks):
            for row, vector in singles:
                own.vectors[place, row : row + 1, :] = vector[:, place * LANES : (place + 1) * LANES]
            bias = query_bias if place < blocks // 2 else value_bias
            for half in range(2):
                start = (place % (blocks // 2)) * 2 * LANES + half * LANES
                own.vectors[place, half : half + 1, :] = bias[:, start : start + LANES]
            for part in range(4):
                start = (place * 4 + part) * LANES
                own.vectors[place, 6 + part : 7 + part, :] = up_ref[:, start : start + LANES]
        for copy in vector_blocks():
            copy.start()
        end_copies()[1].start()

    def vector_sum(_):
        total = own.vectors[block]
        for step, copy in enumerate(vector_blocks()):
            copy.wait()
            total = total + own.vector_got[step + 1]
        own.vector_items[0] = total
        columns = lane_block(width, block)
        value_bias = sum(total_rows(own.text_low[item, :, columns]) for item in range(items))
        own.vector_items[0, 4:5, :] = value_bias
        for copy in vector_spread():
            copy.start()

    def vector_finish(_):
        for copy in vector_spread():
            copy.wait()
        own.vector_final[...] = (own.vector_items[0] + own.vector_items[1]) + (
            own.vector_items[2] + own.vector_items[3]
        )
        end_copies()[2].start()

    def end_copies():
        ends = [
            (own.matrix_final, matrix_out),
            (own.hidden_final, hidden_out),
            (own.vector_final, vector_out),
        ]
        return [
            pltpu.make_async_copy(source, out, own.end_sem.at[number])
            for number, (source, out) in enumerate(ends)
        ]

    def text_copies():
        copies = []
        for part in range(2):
            target = own.text_low.at[:, :, lane_block(part * width, block)]
            source = own.text_sums.at[part]
            for step in range(1, blocks):
                copies.append(
                    copy_to(
                        {"blk": places[step]},
                        source,
                        target,
                        own.text_send.at[part, step],
                        own.text_recv.at[part, step],
                    )
                )
            copies.append(pltpu.make_async_copy(source, target, own.text_recv.at[part, 0]))
        return copies

    def text_sum(_):
        for copy in text_out_copies():
            copy.wait()
        for part in range(2):
            own.text_sums[part] = added(*[own.text_parts[part, step] for step in range(blocks)])
        for copy in text_copies():
            copy.start()

    def matrix_copy(number):
        source = [own.matrix.at[1 - core], own.matrix_sum.at[0], own.matrix_sum.at[1]]
        return copy_to(
            [to_core, to_y, to_core][number],
            source[number],
            own.matrix_got.at[number],
            own.matrix_send.at[number],
            own.matrix_recv.at[number],
        )

    def text_product(_):
        for copy in text_copies() + inputs[6:7]:
            copy.wait()
        for side in range(2):
            columns = slice(side * width, (side + 1) * width)
            rows = sum(
                contract(
                    text_ref[item, :, lane_block(0, block)], own.text_low[item, :, columns], 0, 0
                )
                for item in range(items)
            )
            own.matrix[side] = rows.astype(jnp.bfloat16)
        matrix_copy(0).start()
        text_save().start()

    def matrix_one(_):
        matrix_copy(0).wait()
        own.matrix_sum[0] = added(own.matrix[core], own.matrix_got[0])
        matrix_copy(1).start()

    def matrix_two(_):
        matrix_copy(1).wait()
        own.matrix_sum[1] = added(own.matrix_sum[0], own.matrix_got[1])
        matrix_copy(2).start()

    def matrix_three(_):
        matrix_copy(2).wait()
        own.matrix_final[core] = own.matrix_sum[1].astype(jnp.float32)
        own.matrix_final[1 - core] = own.matrix_got[2].astype(jnp.float32)
        end_copies()[0].start()

    stages = [(0, 1, out_start), (LAND_TURN, 1, back_wait)]
    late = plan[-1][1]
    final_turn = LAND_TURN + max(LATE, late - LATE) + 1
    segments = [
        (0, EARLY, 0, 0, 0),
        (1, made_start - EARLY, 0, EARLY, SECOND_TURN),
        (0, LATE, EARLY, made_start - EARLY, LAND_TURN),
        (1, late - LATE, made_start - EARLY, LATE + EARLY, LAND_TURN),
    ]
    for number, count, offset, base, turn_base in segments:
        steps = lane_steps(number, lanes_of[number], base, offset, number == 0)
        stages += [(turn_base + lag, count, step) for lag, step in zip(LAGS, steps)]
    stages += [
        (FLASH_TURN, 1, out_wait(0)),
        (FLASH_TURN + flash_blocks, 1, out_wait(1)),
        (FLASH_TURN, items * flash_blocks, flash),
        (TEXT_TURN, 1, text_sum),
        (LAND_TURN + 1, 1, text_product),
        (LAND_TURN + 3, 1, matrix_one),
        (LAND_TURN + 14, 1, matrix_two),
        (LAND_TURN + 18, 1, matrix_three),
    ]
    stages += [
        (turn, blocks - 1, back_some(item)) for item, turn in enumerate(SEND_TURNS)
    ]

    stages += [
        (final_turn, 1, final),
        (final_turn + 9, 1, vector_sum),
        (final_turn + 18, 1, vector_finish),
    ]

    def turn(time, carry):
        for lag, count, action in stages:

            @pl.when((time >= lag) & (time < lag + count))
            def _():
                action(time - lag)

        return carry

    lax.fori_loop(0, max(lag + count for lag, count, _ in stages), turn, 0)
    for copy in [text_save()] + end_copies():
        copy.wait()


def backward(factors, weight, blocks, identity, limits, sent, kept, more):
    plan = []
    start = 0
    lefts = []
    rights = []
    shapes = []
    width = sent[0].shape[2]
    sizes = [(left.shape[0], right.shape[1]) for left, right in factors] + [weight.shape]
    for rows, columns in sizes:
        parts = rows // blocks // LANES
        count = parts * columns // (2 * LANES)
        plan.append((start, count, parts))
        start += count
        shapes.append(jax.ShapeDtypeStruct((parts, LANES, columns), jnp.bfloat16))
    for (left, right), (_, _, parts) in zip(factors, plan):
        lefts.append(left.reshape(blocks // 2, 2, parts, LANES, left.shape[1]))
        rights.append(right)
    items, frames, _ = sent[0].shape
    text_count = sent[1].shape[1]
    frame_shape = (items, frames, 3 * width)
    text_shape = (items, text_count, LANES)
    scratch = lane_slots(LANES // 2, True, items * frames)
    scratch += lane_slots(LANES // 2, False, items * frames)
    scratch += rings(text_shape, kept[0].shape, frame_shape, blocks, kept)
    far = pl.BlockSpec(memory_space=pl.ANY)
    small = pl.BlockSpec(memory_space=pltpu.SMEM)
    outs = pl.pallas_call(
        partial(
            backward_kernel,
            plan,
            width // HEADS,
        ),
        out_shape=shapes
        + [
            jax.ShapeDtypeStruct((items, text_count, 2 * width), jnp.bfloat16),
            jax.ShapeDtypeStruct((2, LANES, width), jnp.float32),
            jax.ShapeDtypeStruct((items, frames, width), jnp.bfloat16),
        ]
        + [jax.ShapeDtypeStruct((VECTOR_ROWS, LANES), jnp.float32)],
        in_specs=[small] + [far] * (len(sent) + len(kept) + 3 + 2 * len(lefts)),
        out_specs=[far] * (len(shapes) + 4),
        scratch_shapes=list(scratch),
        compiler_params=pltpu.CompilerParams(
            collective_id=identity, has_side_effects=True, vmem_limit_bytes=62 * 1024 * 1024
        ),
    )(
        limits,
        *sent,
        *kept,
        *more,
        weight.reshape(blocks // 2, 2, LANES, weight.shape[1]),
        *lefts,
        *rights,
    )
    grads = [out.reshape(-1, out.shape[-1]) for out in outs[: len(shapes)]]
    return grads, outs[len(shapes) :]


FF_TILE = 512


class Middle(NamedTuple):
    attn_out: object
    cross_query: object
    cross_out: object
    ff_up: object
    ff_down: object
    layer_output: object
    attended_turned: object
    cross_normed_turned: object
    cross_attended_turned: object
    ff_normed_turned: object
    activated_turned: object
    pre_grad: object
    cross_grad_low: object
    cross_q_grad: object
    self_grad_low: object
    self_grad: object
    att_grad: object
    text_key: object
    text_value: object
    after: object
    normed_one: object
    normed_two: object
    forward_sum: object
    backward_sum: object
    cross_normed: object
    cross_attended: object
    ff_normed: object
    cross_queries: object
    cross_att_grad: object
    probs: object
    load_sem: object
    save_sem: object


def row_norm(values):
    centre = jnp.mean(values, -1, keepdims=True)
    spread = values - centre
    inverse = lax.rsqrt(jnp.mean(spread * spread, -1, keepdims=True) + 1e-05)
    return spread * inverse, inverse


def row_norm_back(grad, normed, inverse, gain):
    scaled = grad * gain
    first_mean = jnp.mean(scaled, -1, keepdims=True)
    second_mean = jnp.mean(scaled * normed, -1, keepdims=True)
    return inverse * (scaled - first_mean - normed * second_mean)


def total_rows(values):
    return jnp.sum(values.astype(jnp.float32), 0, keepdims=True)


def middle_kernel(items, head, *refs):
    refs = list(refs)
    length_ref, hidden, attended, out_grad, text_keys, text_values, gain, shift, bias = refs[:9]
    weights = refs[9:14]
    saved = refs[14:28]
    sums, up_sums = refs[28:30]
    own = Middle(*refs[30:])
    low = jnp.bfloat16
    rows = hidden.shape[0]
    width = hidden.shape[1]
    frames = rows // items
    text_count = text_keys.shape[0] // items
    pairs = width // (2 * head)
    scale = head ** (-0.5)
    gains = gain[...].astype(jnp.float32)
    shifts = shift[...].astype(jnp.float32)

    def bias_of(number):
        return bias[:, (3 + number) * width : (4 + number) * width]

    loads = [
        pltpu.make_async_copy(weight, own[number], own.load_sem.at[number])
        for number, weight in enumerate(weights)
    ]
    for load in loads:
        load.start()
    saves = [
        pltpu.make_async_copy(own[5 + number], out, own.save_sem.at[number])
        for number, out in enumerate(saved)
    ]

    def save(*names):
        for name in names:
            saves[Middle._fields.index(name) - 5].start()

    own.attended_turned[...] = jnp.transpose(attended[...])
    loads[0].wait()
    after_self = (
        hidden[...].astype(jnp.float32)
        + contract(attended[...], own.attn_out[...], 1, 0)
        + bias_of(0)
    )
    own.after[...] = after_self
    normed, inverse_one = row_norm(after_self)
    own.normed_one[...] = normed
    own.cross_normed[...] = (normed * gains[1:2] + shifts[1:2]).astype(low)
    own.cross_normed_turned[...] = jnp.transpose(own.cross_normed[...])
    save(*"attended_turned cross_normed_turned".split())
    loads[1].wait()
    own.cross_queries[...] = (
        contract(own.cross_normed[...], own.cross_query[...], 1, 0) + bias_of(1)
    ).astype(low)
    low_half = lax.broadcasted_iota(jnp.int32, (frames, 2 * head), 1) < head

    def pair_parts(item, pair):
        return (
            slice(item * frames, (item + 1) * frames),
            slice(item * text_count, (item + 1) * text_count),
            slice(pair * 2 * head, (pair + 1) * 2 * head),
        )

    def joined(values):
        return jnp.where(low_half, values[:frames], values[frames:])

    for item in range(items):
        seen = lax.broadcasted_iota(jnp.int32, (text_count, 1), 0) < length_ref[item]
        for pair in range(pairs):
            here, texts, lanes = pair_parts(item, pair)
            queries = two_heads(own.cross_queries[here, lanes] * low(scale), low_half)
            scores = contract(text_keys[texts, lanes], queries, 1, 1)
            scores = jnp.where(seen, scores, NEG_FILL)
            raised = jnp.exp(scores - jnp.max(scores, 0, keepdims=True))
            raised = jnp.where(seen, raised, 0.0)
            probs = raised / jnp.sum(raised, 0, keepdims=True)
            own.probs[item * pairs + pair] = probs
            mixed = contract(probs.astype(low), text_values[texts, lanes], 0, 0)
            own.cross_attended[here, lanes] = joined(mixed).astype(low)
    loads[2].wait()
    after_cross = (
        own.after[...]
        + contract(own.cross_attended[...], own.cross_out[...], 1, 0)
        + bias_of(2)
    )
    own.after[...] = after_cross
    normed, inverse_two = row_norm(after_cross)
    own.normed_two[...] = normed
    own.ff_normed[...] = (normed * gains[2:3] + shifts[2:3]).astype(low)
    own.cross_attended_turned[...] = jnp.transpose(own.cross_attended[...])
    own.ff_normed_turned[...] = jnp.transpose(own.ff_normed[...])
    save(*"cross_attended_turned ff_normed_turned".split())
    loads[3].wait()
    loads[4].wait()
    own.forward_sum[...] = jnp.zeros_like(own.forward_sum)
    own.backward_sum[...] = jnp.zeros_like(own.backward_sum)

    def tile(number, carry):
        here = pl.ds(pl.multiple_of(number * FF_TILE, FF_TILE), FF_TILE)
        pre = contract(own.ff_normed[...], own.ff_up[:, here], 1, 0) + bias[:, pl.ds(pl.multiple_of(7 * width + number * FF_TILE, FF_TILE), FF_TILE)]
        act_grad = contract(out_grad[...], own.ff_down[here, :], 1, 1)
        below = 0.5 + 0.5 * lax.erf(pre * (0.5**0.5))
        active = (pre * below).astype(low)
        slope = below + pre * (jnp.exp(-0.5 * pre * pre) * 0.3989422804014327)
        grad = (act_grad * slope).astype(low)
        own.activated_turned[here, :] = jnp.transpose(active)
        own.pre_grad[:, here] = grad
        up_sums[:, here] = total_rows(grad)
        own.forward_sum[...] += contract(active, own.ff_down[here, :], 1, 0)
        own.backward_sum[...] += contract(grad, own.ff_up[:, here], 1, 1)
        return carry

    lax.fori_loop(0, own.ff_up.shape[1] // FF_TILE, tile, 0)
    own.layer_output[...] = (own.after[...] + own.forward_sum[...] + bias_of(3)).astype(low)
    save(*"layer_output activated_turned pre_grad".split())
    grad = own.backward_sum[...]
    sums[0:1, :] = total_rows(out_grad[...])
    sums[5:6, :] = total_rows(grad * own.normed_two[...])
    sums[7:8, :] = total_rows(grad)
    cross_grad = out_grad[...].astype(jnp.float32) + row_norm_back(
        grad, own.normed_two[...], inverse_two, gains[2:3]
    )
    own.after[...] = cross_grad
    own.cross_grad_low[...] = cross_grad.astype(low)
    sums[1:2, :] = total_rows(own.cross_grad_low[...])
    own.cross_att_grad[...] = contract(own.cross_grad_low[...], own.cross_out[...], 1, 1).astype(low)
    for item in range(items):
        for pair in range(pairs):
            here, texts, lanes = pair_parts(item, pair)
            grads = two_heads(own.cross_att_grad[here, lanes], low_half)
            queries = two_heads(own.cross_queries[here, lanes] * low(scale), low_half)
            probs = own.probs[item * pairs + pair]
            prob_grads = contract(text_values[texts, lanes], grads, 1, 1)
            score_grads = probs * (prob_grads - jnp.sum(probs * prob_grads, 0, keepdims=True))
            score_grads = score_grads.astype(low)
            own.text_key[texts, lanes] = contract(score_grads, queries, 1, 0).astype(low)
            own.text_value[texts, lanes] = contract(probs.astype(low), grads, 1, 0).astype(low)
            query_grads = scale * contract(score_grads, text_keys[texts, lanes], 0, 0)
            own.cross_q_grad[here, lanes] = joined(query_grads).astype(low)
    save(*"cross_grad_low cross_q_grad text_key text_value".split())
    grad = contract(own.cross_q_grad[...], own.cross_query[...], 1, 1)
    sums[2:3, :] = total_rows(own.cross_q_grad[...])
    sums[4:5, :] = total_rows(grad * own.normed_one[...])
    sums[6:7, :] = total_rows(grad)
    self_grad = own.after[...] + row_norm_back(
        grad, own.normed_one[...], inverse_one, gains[1:2]
    )
    own.self_grad[...] = self_grad
    own.self_grad_low[...] = self_grad.astype(low)
    sums[3:4, :] = total_rows(own.self_grad_low[...])
    own.att_grad[...] = contract(own.self_grad_low[...], own.attn_out[...], 1, 1).astype(low)
    save(*"self_grad self_grad_low att_grad".split())
    for copy in saves:
        copy.wait()


def middle(lengths, hidden, attended, out_grad, text_keys, text_values, gain, shift, bias, weights):
    items, frames, width = hidden.shape
    text_count = text_keys.shape[0] // items
    rows = items * frames
    wide = weights[3].shape[1]
    low = jnp.bfloat16
    full = jnp.float32
    saved = [((rows, width), low)] + [((width, rows), low)] * 4
    saved += [((wide, rows), low), ((rows, wide), low)] + [((rows, width), low)] * 3
    saved += [((rows, width), full), ((rows, width), low)]
    saved += [((items * text_count, width), low)] * 2
    kept = [((rows, width), full)] * 5 + [((rows, width), low)] * 5
    kept += [((items * HEADS // 2, text_count, 2 * frames), full)]
    near = pl.BlockSpec(memory_space=pltpu.VMEM)
    far = pl.BlockSpec(memory_space=pl.ANY)
    outs = pl.pallas_call(
        partial(middle_kernel, items, width // HEADS),
        out_shape=[jax.ShapeDtypeStruct(shape, kind) for shape, kind in saved]
        + [jax.ShapeDtypeStruct((8, width), full), jax.ShapeDtypeStruct((1, wide), full)],
        in_specs=[pl.BlockSpec(memory_space=pltpu.SMEM)] + [near] * 8 + [far] * 5,
        out_specs=[far] * len(saved) + [near] * 2,
        scratch_shapes=[pltpu.VMEM(weight.shape, weight.dtype) for weight in weights]
        + [pltpu.VMEM(shape, kind) for shape, kind in saved + kept]
        + [pltpu.SemaphoreType.DMA((5,)), pltpu.SemaphoreType.DMA((len(saved),))],
        compiler_params=pltpu.CompilerParams(vmem_limit_bytes=62 * 1024 * 1024),
    )(
        lengths,
        hidden.reshape(rows, width),
        attended.reshape(rows, width),
        out_grad.reshape(rows, width),
        text_keys,
        text_values,
        gain,
        shift,
        bias,
        *weights,
    )
    return outs[: len(saved)], outs[len(saved)], outs[len(saved) + 1]


class Forward(NamedTuple):
    attn_in: object
    cross_kv: object
    projected: object
    queries: object
    keys: object
    values: object
    mixed: object
    mixed_low: object
    log_total: object
    load_sem: object
    there_send: object
    there_recv: object
    back_send: object
    back_recv: object
    save_sem: object


def forward_kernel(head, *refs):
    refs = list(refs)
    limit_ref, hidden, gain, shift, bias, text, attn_in, cross_kv = refs[:8]
    normed_out, text_keys, text_values = refs[8:11]
    attended, queries_out, keys_out, values_out, mixed_out, log_out = refs[11:17]
    own = Forward(*refs[17:])
    low = jnp.bfloat16
    items, length, lanes = own.queries.shape
    frames, width = hidden.shape[1:]
    blocks = length // frames
    block = lax.axis_index("blk")
    scale = head ** (-0.5)
    barrier = pltpu.get_barrier_semaphore()
    for step in range(1, blocks):
        pl.semaphore_signal(
            barrier, inc=1, device_id={"blk": lax.rem(block + step, blocks)}, device_id_type=MESH_ID
        )
    loads = [
        pltpu.make_async_copy(
            attn_in.at[:, part * width : (part + 1) * width],
            own.attn_in.at[:, part * width : (part + 1) * width],
            own.load_sem.at[part],
        )
        for part in range(3)
    ]
    loads.append(pltpu.make_async_copy(cross_kv, own.cross_kv, own.load_sem.at[3]))
    for load in loads:
        load.start()
    gains = gain[0:1, :].astype(jnp.float32)
    shifts = shift[0:1, :].astype(jnp.float32)
    for item in range(items):
        normed, _ = row_norm(hidden[item].astype(jnp.float32))
        normed_out[item] = (normed * gains + shifts).astype(low)
    landing = (own.queries, own.keys, own.values)

    def lane_block(offset, place):
        return pl.ds(pl.multiple_of(offset + place * LANES, LANES), LANES)

    def frame_rows(place):
        return pl.ds(pl.multiple_of(place * frames, frames), frames)

    def there(item, part, step):
        place = lax.rem(block + step, blocks)
        source = own.projected.at[item, :, lane_block(part * width, place)]
        target = landing[part].at[item, frame_rows(block), :]
        if step == 0:
            return pltpu.make_async_copy(source, target, own.there_recv.at[item, part, 0])
        return pltpu.make_async_remote_copy(
            src_ref=source,
            dst_ref=target,
            send_sem=own.there_send.at[item, part, step],
            recv_sem=own.there_recv.at[item, part, step],
            device_id={"blk": place},
            device_id_type=MESH_ID,
        )

    def back(item, step):
        place = lax.rem(block + step, blocks)
        source = own.mixed_low.at[item, frame_rows(place), :]
        target = attended.at[item, :, lane_block(0, block)]
        if step == 0:
            return pltpu.make_async_copy(source, target, own.back_recv.at[item, 0])
        return pltpu.make_async_remote_copy(
            src_ref=source,
            dst_ref=target,
            send_sem=own.back_send.at[item, step],
            recv_sem=own.back_recv.at[item, step],
            device_id={"blk": place},
            device_id_type=MESH_ID,
        )

    def save_copies(item):
        kept = (own.queries, own.keys, own.values, own.mixed, own.log_total)
        outs = (queries_out, keys_out, values_out, mixed_out, log_out)
        return [
            pltpu.make_async_copy(source.at[item], out.at[item], own.save_sem.at[item, number])
            for number, (source, out) in enumerate(zip(kept, outs))
        ]

    for item in range(items):
        for part in range(3):
            if item == 0:
                loads[part].wait()
            columns = slice(part * width, (part + 1) * width)
            rows = contract(normed_out[item], own.attn_in[:, columns], 1, 0)
            if part != 1:
                start = (part // 2) * width
                rows = rows + bias[:, start : start + width]
            own.projected[item, :, columns] = rows.astype(low)
            if item == 0 and part == 0:
                pl.semaphore_wait(barrier, blocks - 1)
            for step in range(blocks):
                there(item, part, step).start()
    loads[3].wait()
    text_keys[...] = contract(text[...], own.cross_kv[:, :width], 1, 0).astype(low)
    text_values[...] = (
        contract(text[...], own.cross_kv[:, width:], 1, 0) + bias[:, 2 * width : 3 * width]
    ).astype(low)
    low_half = lax.broadcasted_iota(jnp.int32, (ROWS, lanes), 1) < head

    def attend(item, carry):
        for part in range(3):
            for step in range(blocks):
                there(item, part, step).wait()
        for number in range(length // ROWS):
            span = (number + 1) * ROWS
            here = slice(number * ROWS, span)
            queries = two_heads(own.queries[item, here, :] * low(scale), low_half)
            scores = contract(queries, own.keys[item, :span, :], 1, 1)
            query_pos = lax.broadcasted_iota(jnp.int32, (2 * ROWS, ROWS), 0) % ROWS
            key_pos = lax.broadcasted_iota(jnp.int32, (2 * ROWS, ROWS), 1)
            corner = jnp.where(key_pos <= query_pos, scores[:, span - ROWS :], NEG_FILL)
            scores = corner if number == 0 else jnp.concatenate([scores[:, : span - ROWS], corner], 1)
            if span > length // 2:
                valid = lax.broadcasted_iota(jnp.int32, (1, span), 1) < limit_ref[item]
                scores = scores + jnp.where(valid, 0.0, NEG_FILL)
            top = jnp.max(scores, 1, keepdims=True)
            raised = jnp.exp(scores - top)
            total = jnp.sum(raised, 1, keepdims=True)
            mixed = contract(raised.astype(low), own.values[item, :span, :], 1, 0) / total
            mixed = jnp.where(low_half, mixed[:ROWS], mixed[ROWS:])
            own.mixed[item, here, :] = mixed
            own.mixed_low[item, here, :] = mixed.astype(low)
            log_total = top + jnp.log(total)
            own.log_total[item, here, :] = jnp.where(low_half, log_total[:ROWS], log_total[ROWS:])
        for step in range(blocks):
            back(item, step).start()
        for copy in save_copies(item):
            copy.start()
        return carry

    lax.fori_loop(0, items, attend, 0)
    for item in range(items):
        for step in range(blocks):
            back(item, step).wait()
        for copy in save_copies(item):
            copy.wait()


def forward(identity, blocks, limits, hidden, gain, shift, bias, text, attn_in, cross_kv):
    items, frames, width = hidden.shape
    low = jnp.bfloat16
    full = jnp.float32
    whole_shape = (items, frames * blocks, LANES)
    near = pl.BlockSpec(memory_space=pltpu.VMEM)
    far = pl.BlockSpec(memory_space=pl.ANY)
    rows = text.reshape(-1, width)

    def shape(dims, kind):
        return jax.ShapeDtypeStruct(dims, kind)

    kinds = [low, low, low, full, low, full]
    return pl.pallas_call(
        partial(forward_kernel, width // HEADS),
        out_shape=[shape(hidden.shape, low), shape(rows.shape, low), shape(rows.shape, low)]
        + [shape(hidden.shape, low)]
        + [shape(whole_shape, kind) for kind in (low, low, low, full, full)],
        in_specs=[pl.BlockSpec(memory_space=pltpu.SMEM)] + [near] * 5 + [far] * 2,
        out_specs=[near] * 3 + [far] * 6,
        scratch_shapes=[
            pltpu.VMEM(attn_in.shape, low),
            pltpu.VMEM(cross_kv.shape, low),
            pltpu.VMEM((items, frames, 3 * width), low),
        ]
        + [pltpu.VMEM(whole_shape, kind) for kind in kinds]
        + [
            pltpu.SemaphoreType.DMA((4,)),
            pltpu.SemaphoreType.DMA((items, 3, blocks)),
            pltpu.SemaphoreType.DMA((items, 3, blocks)),
            pltpu.SemaphoreType.DMA((items, blocks)),
            pltpu.SemaphoreType.DMA((items, blocks)),
            pltpu.SemaphoreType.DMA((items, 5)),
        ],
        compiler_params=pltpu.CompilerParams(
            collective_id=identity, has_side_effects=True, vmem_limit_bytes=VMEM_BYTES
        ),
    )(limits, hidden, gain, shift, bias, rows, attn_in, cross_kv)


def finish_kernel(count, *refs):
    refs = list(refs)
    grads = refs[:count]
    text_low, weight, sides, vectors = refs[count : count + 4]
    outs = refs[count + 4 : 2 * count + 4]
    text_out, matrix_out = refs[2 * count + 4 : 2 * count + 6]
    vector_outs = refs[2 * count + 6 : 2 * count + 15]
    scratch = refs[2 * count + 15 :]
    low = scratch[:count]
    text_near, weight_near, vector_near, sides_near = scratch[count : count + 4]
    full = scratch[count + 4 : 2 * count + 4]
    text_grad, load_sem, save_sem = scratch[2 * count + 4 :]
    pairs = list(zip(grads, low)) + [(text_low, text_near), (weight, weight_near)]
    pairs += [(vectors, vector_near), (sides, sides_near)]
    loads = [
        pltpu.make_async_copy(source, target, load_sem.at[number])
        for number, (source, target) in enumerate(pairs)
    ]
    for load in loads:
        load.start()
    saves = []

    def save(source, target):
        copy = pltpu.make_async_copy(source, target, save_sem.at[len(saves)])
        copy.start()
        saves.append(copy)

    width = sides.shape[2]
    loads[count + 2].wait()
    for out, (row, rows) in zip(vector_outs, VECTORS):
        for part in range(rows):
            save(
                vector_near.at[row + part : row + part + 1, :],
                out.at[:, part * LANES : (part + 1) * LANES],
            )
    for number in range(2):
        for part in range(3):
            row = 11 + 3 * number + part
            save(vector_near.at[row : row + 1, :], vector_outs[7 + number].at[part : part + 1, :])
    for number in range(count):
        loads[number].wait()
        full[number][...] = low[number][...].astype(jnp.float32)
        save(full[number], outs[number])
    loads[count + 3].wait()
    for side in range(2):
        save(sides_near.at[side], matrix_out.at[:, side * width : (side + 1) * width])
    loads[count].wait()
    loads[count + 1].wait()
    for item in range(text_low.shape[0]):
        text_grad[item] = contract(text_near[item], weight_near[...], 1, 1).astype(jnp.bfloat16)
    save(text_grad, text_out)
    for copy in saves:
        copy.wait()


def finish(grads, text_low, weight, sides, vectors):
    count = len(grads)
    full = jnp.float32
    items, texts, _ = text_low.shape
    width = weight.shape[0]

    def shape(*dims, kind=full):
        return jax.ShapeDtypeStruct(dims, kind)

    far = pl.BlockSpec(memory_space=pl.ANY)
    near_low = [pltpu.VMEM(array.shape, array.dtype) for array in grads]
    near_low += [pltpu.VMEM(array.shape, array.dtype) for array in (text_low, weight, vectors, sides)]
    outs = [shape(*grad.shape) for grad in grads]
    outs += [shape(items, texts, width, kind=jnp.bfloat16), shape(LANES, 2 * width)]
    outs += [shape(1, rows * LANES) for _, rows in VECTORS] + [shape(3, LANES)] * 2
    return pl.pallas_call(
        partial(finish_kernel, count),
        out_shape=outs,
        in_specs=[far] * (count + 4),
        out_specs=[far] * len(outs),
        scratch_shapes=near_low
        + [pltpu.VMEM(grad.shape, full) for grad in grads]
        + [
            pltpu.VMEM((items, texts, width), jnp.bfloat16),
            pltpu.SemaphoreType.DMA((count + 4,)),
            pltpu.SemaphoreType.DMA((count + 32,)),
        ],
        compiler_params=pltpu.CompilerParams(vmem_limit_bytes=VMEM_BYTES),
    )(*grads, text_low, weight, sides, vectors)


def fast_device(
    hidden_in,
    text_states,
    frame_lengths,
    text_lengths,
    out_grad,
    attn_in,
    attn_in_bias,
    attn_out,
    attn_out_bias,
    cross_query,
    cross_query_bias,
    cross_kv,
    cross_v_bias,
    cross_out,
    cross_out_bias,
    ff_up,
    ff_up_bias,
    ff_down,
    ff_down_bias,
    norm_gain,
    norm_bias,
):
    seq_count, frames, width = hidden_in.shape
    blocks = lax.axis_size("blk")
    block_index = lax.axis_index("blk")

    biases = [attn_in_bias, cross_v_bias, attn_out_bias, cross_query_bias, cross_out_bias]
    biases += [ff_down_bias, ff_up_bias]
    size = sum(bias.shape[0] for bias in biases)
    start = 0
    packed = 0.0
    for bias in biases:
        rest = size - start - bias.shape[0]
        packed = packed + jnp.pad(bias.astype(jnp.float32), (start, rest))
        start += bias.shape[0]
    biases = packed.reshape(1, -1)
    (
        attn_normed,
        text_keys,
        text_values,
        attended,
        queries,
        keys,
        values,
        mixed,
        log_total,
    ) = forward(
        0,
        blocks,
        frame_lengths,
        hidden_in,
        norm_gain,
        norm_bias,
        biases,
        text_states,
        attn_in,
        cross_kv,
    )
    (
        layer_output,
        attended_turned,
        cross_normed_turned,
        cross_attended_turned,
        ff_normed_turned,
        activated_turned,
        pre_grad,
        cross_grad_low,
        cross_q_grad,
        self_grad_low,
        self_grad,
        att_grad,
        text_key_part,
        text_value_part,
    ), sums, up_sums = middle(
        text_lengths,
        hidden_in,
        attended,
        out_grad,
        text_keys,
        text_values,
        norm_gain,
        norm_bias,
        biases,
        [attn_out, cross_query, cross_out, ff_up, ff_down],
    )
    text_shape = text_states.shape
    layer_output = layer_output.reshape(hidden_in.shape)
    grads, (text_kv_low, cross_kv_sides, hidden_grad, summed) = backward(
        [
            (attended_turned, self_grad_low),
            (cross_normed_turned, cross_q_grad),
            (cross_attended_turned, cross_grad_low),
            (ff_normed_turned, pre_grad),
            (activated_turned, out_grad.reshape(-1, width)),
        ],
        attn_in,
        blocks,
        2,
        frame_lengths,
        [
            att_grad.reshape(hidden_in.shape),
            text_key_part.reshape(text_shape),
            text_value_part.reshape(text_shape),
        ],
        [
            queries,
            keys,
            values,
            mixed,
            log_total,
            attn_normed,
            text_states,
            sums,
            up_sums,
            norm_gain,
        ],
        [hidden_in, self_grad.reshape(hidden_in.shape)],
    )
    outs = finish(grads, text_kv_low, cross_kv, cross_kv_sides, summed)
    attn_out_grad, cross_query_grad, cross_out_grad, ff_up_grad, ff_down_grad, attn_in_grad = outs[:6]
    text_grad, cross_kv_grad = outs[6:8]
    vectors = [vector.reshape(-1) for vector in outs[8:15]] + list(outs[15:17])
    return (
        layer_output,
        hidden_grad,
        text_grad,
        attn_in_grad,
        vectors[0],
        attn_out_grad,
        vectors[1],
        cross_query_grad,
        vectors[2],
        cross_kv_grad,
        vectors[3],
        cross_out_grad,
        vectors[4],
        ff_up_grad,
        vectors[5],
        ff_down_grad,
        vectors[6],
        vectors[7],
        vectors[8],
    )


def solution(mesh):
    fast = mesh.shape["items"] == 4 and mesh.shape["blk"] == 8
    placed = (
        P("items", "blk", None),
        P("items", None, None),
        P("items"),
        P("items"),
        P("items", "blk", None),
        P(),
        P(),
        P(),
        P(),
        P(),
        P(),
        P(),
        P(),
        P(),
        P(),
        P(),
        P(),
        P(),
        P(),
        P(),
        P(),
    )
    return jax.shard_map(
        fast_device if fast else general_device,
        mesh=mesh,
        in_specs=placed,
        out_specs=(
            P("items", "blk", None),
            P("items", "blk", None),
            P("items", None, None),
            P("blk", None),
            P("blk"),
            P("blk", None),
            P("blk"),
            P("blk", None),
            P("blk"),
            P("blk", None),
            P("blk"),
            P("blk", None),
            P("blk"),
            P("blk", None),
            P("blk"),
            P("blk", None),
            P("blk"),
            P(None, "blk"),
            P(None, "blk"),
        ),
        check_vma=False,
    )
```

```python
from functools import partial
from typing import NamedTuple

import jax
import jax.numpy as jnp
from jax import lax
from jax.experimental import pallas as pl
from jax.experimental.pallas import tpu as pltpu
from jax.sharding import PartitionSpec as P

HEADS = 16


NEG_FILL = -1e30


def normalize(values, gain, shift):
    centre = jnp.mean(values, -1, keepdims=True)
    spread = values - centre
    variance = jnp.mean(spread * spread, -1, keepdims=True)
    inverse = lax.rsqrt(variance + 1e-05)
    normed = spread * inverse
    return (normed * gain + shift, normed, inverse)


def norm_back(grad, normed, inverse, gain):
    scaled = grad * gain
    first_mean = jnp.mean(scaled, -1, keepdims=True)
    second_mean = jnp.mean(scaled * normed, -1, keepdims=True)
    return (
        inverse * (scaled - first_mean - normed * second_mean),
        jnp.sum(grad * normed, (0, 1)),
        jnp.sum(grad, (0, 1)),
    )


def outer_sum(left, right):
    return jnp.einsum("sfd,sfe->de", left, right, preferred_element_type=jnp.float32)


def apply_fwd(values, weight):
    return jnp.einsum("sfd,de->sfe", values, weight, preferred_element_type=jnp.float32)


def apply_back(grad, weight):
    return jnp.einsum("sfe,de->sfd", grad, weight, preferred_element_type=jnp.float32)


def column_sum(values):
    return jnp.sum(values.astype(jnp.float32), (0, 1))


def general_device(
    hidden_in,
    text_states,
    frame_lengths,
    text_lengths,
    out_grad,
    attn_in,
    attn_in_bias,
    attn_out,
    attn_out_bias,
    cross_query,
    cross_query_bias,
    cross_kv,
    cross_v_bias,
    cross_out,
    cross_out_bias,
    ff_up,
    ff_up_bias,
    ff_down,
    ff_down_bias,
    norm_gain,
    norm_bias,
):
    seq_count, frames, width = hidden_in.shape
    head_count = HEADS
    head_size = width // head_count
    scale = head_size ** (-0.5)
    text_count = text_states.shape[1]
    axis_count = lax.axis_size("blk")
    block_index = lax.axis_index("blk")
    first_frame = block_index * frames
    last_frame = first_frame + frames - 1
    my_pos = first_frame + jnp.arange(frames, dtype=jnp.int32)
    frame_limit = frame_lengths[:, None, None, None]
    gains = norm_gain.astype(jnp.float32)
    shifts = norm_bias.astype(jnp.float32)

    def visible(key_pos, query_pos):
        return (key_pos[None, None, None, :] <= query_pos[None, None, :, None]) & (
            key_pos[None, None, None, :] < frame_limit
        )

    def heads_of(values):
        return values.reshape(values.shape[0], values.shape[1], head_count, head_size)

    residual = hidden_in.astype(jnp.float32)
    attn_full, normed_zero, inverse_zero = normalize(residual, gains[0], shifts[0])
    attn_normed = attn_full.astype(jnp.bfloat16)
    projected = apply_fwd(attn_normed, attn_in)
    query_rows = (projected[..., :width] + attn_in_bias[:width]).astype(jnp.bfloat16)
    key_rows = projected[..., width : 2 * width].astype(jnp.bfloat16)
    value_rows = (projected[..., 2 * width :] + attn_in_bias[width:]).astype(jnp.bfloat16)
    query_heads = heads_of(query_rows)

    def keep_state(state):
        return state

    start_state = (
        jnp.full((seq_count, head_count, frames), NEG_FILL, jnp.float32),
        jnp.zeros((seq_count, head_count, frames), jnp.float32),
        jnp.zeros((seq_count, head_count, frames, head_size), jnp.float32),
    )
    key_piece = lax.all_gather(key_rows, "blk", axis=1, tiled=True)
    value_piece = lax.all_gather(value_rows, "blk", axis=1, tiled=True)
    span = key_piece.shape[1]

    def forward_compute(state):
        running_max, running_sum, accumulated = state
        key_pos = jnp.arange(span, dtype=jnp.int32)
        scores = (
            jnp.einsum(
                "sfhd,sphd->shfp",
                query_heads,
                heads_of(key_piece),
                preferred_element_type=jnp.float32,
            )
            * scale
        )
        mask = visible(key_pos, my_pos)
        scores = jnp.where(mask, scores, NEG_FILL)
        new_max = jnp.maximum(running_max, jnp.max(scores, -1))
        weights = jnp.where(mask, jnp.exp(scores - new_max[..., None]), 0.0)
        running_sum = jnp.sum(weights, -1)
        accumulated = jnp.einsum(
            "shfp,sphd->shfd",
            weights.astype(jnp.bfloat16),
            heads_of(value_piece),
            preferred_element_type=jnp.float32,
        )
        return (new_max, running_sum, accumulated)

    final_state = lax.cond(jnp.int32(0) > last_frame, keep_state, forward_compute, start_state)
    final_max, final_sum, final_acc = final_state
    log_total = final_max + jnp.log(final_sum)
    attended_full = final_acc / final_sum[..., None]
    attended = (
        jnp.transpose(attended_full, (0, 2, 1, 3))
        .reshape(seq_count, frames, width)
        .astype(jnp.bfloat16)
    )
    after_self = residual + apply_fwd(attended, attn_out) + attn_out_bias
    cross_full, normed_one, inverse_one = normalize(after_self, gains[1], shifts[1])
    cross_normed = cross_full.astype(jnp.bfloat16)
    cross_queries = (apply_fwd(cross_normed, cross_query) + cross_query_bias).astype(jnp.bfloat16)
    cross_attention_heads = heads_of(cross_queries)
    text_proj = apply_fwd(text_states, cross_kv)
    encoder_key_rows = heads_of(text_proj[..., :width].astype(jnp.bfloat16))
    encoder_value_rows = heads_of((text_proj[..., width:] + cross_v_bias).astype(jnp.bfloat16))
    cross_scores = (
        jnp.einsum(
            "qybj,qzbj->qbyz",
            cross_attention_heads,
            encoder_key_rows,
            preferred_element_type=jnp.float32,
        )
        * scale
    )
    text_mask = (
        jnp.arange(text_count, dtype=jnp.int32)[None, None, None, :]
        < text_lengths[:, None, None, None]
    )
    cross_scores = jnp.where(text_mask, cross_scores, NEG_FILL)
    cross_top = jnp.max(cross_scores, -1, keepdims=True)
    cross_raised = jnp.where(text_mask, jnp.exp(cross_scores - cross_top), 0.0)
    cross_probs = cross_raised / jnp.sum(cross_raised, -1, keepdims=True)
    cross_attention_weights = cross_probs.astype(jnp.bfloat16)
    cross_attended = (
        jnp.einsum(
            "oalx,oxak->olak",
            cross_attention_weights,
            encoder_value_rows,
            preferred_element_type=jnp.float32,
        )
        .reshape(seq_count, frames, width)
        .astype(jnp.bfloat16)
    )
    after_cross = after_self + apply_fwd(cross_attended, cross_out) + cross_out_bias
    ff_full, normed_two, inverse_two = normalize(after_cross, gains[2], shifts[2])
    ff_normed = ff_full.astype(jnp.bfloat16)
    pre_gelu = apply_fwd(ff_normed, ff_up) + ff_up_bias
    activated = jax.nn.gelu(pre_gelu, approximate=False).astype(jnp.bfloat16)
    layer_output = (after_cross + apply_fwd(activated, ff_down) + ff_down_bias).astype(jnp.bfloat16)
    ff_down_grad = outer_sum(activated, out_grad)
    ff_down_bias_grad = column_sum(out_grad)
    act_grad = apply_back(out_grad, ff_down)
    gelu_value, gelu_pull = jax.vjp(partial(jax.nn.gelu, approximate=False), pre_gelu)
    before_gelu_gradient = gelu_pull(act_grad)[0].astype(jnp.bfloat16)
    ff_up_grad = outer_sum(ff_normed, before_gelu_gradient)
    ff_up_bias_grad = column_sum(before_gelu_gradient)
    back_two, gain_two, shift_two = norm_back(
        apply_back(before_gelu_gradient, ff_up), normed_two, inverse_two, gains[2]
    )
    cross_grad = out_grad.astype(jnp.float32) + back_two
    cross_grad_low = cross_grad.astype(jnp.bfloat16)
    cross_out_grad = outer_sum(cross_attended, cross_grad_low)
    cross_out_bias_grad = column_sum(cross_grad_low)
    cross_attention_gradient = heads_of(apply_back(cross_grad_low, cross_out).astype(jnp.bfloat16))
    cross_dp = jnp.einsum(
        "qybj,qzbj->qbyz",
        cross_attention_gradient,
        encoder_value_rows,
        preferred_element_type=jnp.float32,
    )
    cross_logit_gradient = (
        cross_probs * (cross_dp - jnp.sum(cross_probs * cross_dp, -1, keepdims=True))
    ).astype(jnp.bfloat16)
    text_key_grad = scale * jnp.einsum(
        "wopc,wpou->wcou",
        cross_logit_gradient,
        cross_attention_heads,
        preferred_element_type=jnp.float32,
    ).reshape(seq_count, text_count, width)
    text_value_grad = jnp.einsum(
        "wopc,wpou->wcou",
        cross_attention_weights,
        cross_attention_gradient,
        preferred_element_type=jnp.float32,
    ).reshape(seq_count, text_count, width)
    text_key_grad, text_value_grad = lax.psum((text_key_grad, text_value_grad), "blk")
    text_kv_low = jnp.concatenate([text_key_grad, text_value_grad], -1).astype(jnp.bfloat16)
    text_grad = jnp.einsum(
        "stf,df->std", text_kv_low, cross_kv, preferred_element_type=jnp.float32
    ).astype(jnp.bfloat16)
    row_share = width // axis_count
    text_slice = lax.dynamic_slice_in_dim(text_states, block_index * row_share, row_share, 2)
    cross_kv_rows = jnp.einsum(
        "std,stf->df", text_slice, text_kv_low, preferred_element_type=jnp.float32
    )
    value_slice = lax.dynamic_slice_in_dim(
        text_kv_low, width + block_index * row_share, row_share, 2
    )
    cross_v_bias_rows = column_sum(value_slice)
    cross_q_grad = (
        (
            scale
            * jnp.einsum(
                "oalx,oxak->olak",
                cross_logit_gradient,
                encoder_key_rows,
                preferred_element_type=jnp.float32,
            )
        )
        .reshape(seq_count, frames, width)
        .astype(jnp.bfloat16)
    )
    cross_query_grad = outer_sum(cross_normed, cross_q_grad)
    cross_query_bias_grad = column_sum(cross_q_grad)
    back_one, gain_one, shift_one = norm_back(
        apply_back(cross_q_grad, cross_query), normed_one, inverse_one, gains[1]
    )
    self_grad = cross_grad + back_one
    self_grad_low = self_grad.astype(jnp.bfloat16)
    attn_out_grad = outer_sum(attended, self_grad_low)
    attn_out_bias_grad = column_sum(self_grad_low)
    att_grad = apply_back(self_grad_low, attn_out).astype(jnp.bfloat16)
    att_heads = heads_of(att_grad)
    delta = jnp.sum(jnp.transpose(att_heads.astype(jnp.float32), (0, 2, 1, 3)) * attended_full, -1)
    query_zero = jnp.zeros((seq_count, frames, head_count, head_size), jnp.float32)
    query_key_piece = lax.all_gather(key_rows, "blk", axis=1, tiled=True)
    query_value_piece = lax.all_gather(value_rows, "blk", axis=1, tiled=True)
    query_span = query_key_piece.shape[1]

    def query_compute(state):
        key_pos = jnp.arange(query_span, dtype=jnp.int32)
        piece_keys = heads_of(query_key_piece)
        scores = (
            jnp.einsum(
                "sfhd,sphd->shfp", query_heads, piece_keys, preferred_element_type=jnp.float32
            )
            * scale
        )
        mask = visible(key_pos, my_pos)
        probs = jnp.where(mask, jnp.exp(scores - log_total[..., None]), 0.0)
        prob_grad = jnp.einsum(
            "sfhd,sphd->shfp",
            att_heads,
            heads_of(query_value_piece),
            preferred_element_type=jnp.float32,
        )
        score_grad = (probs * (prob_grad - delta[..., None])).astype(jnp.bfloat16)
        return scale * jnp.einsum(
            "shfp,sphd->sfhd", score_grad, piece_keys, preferred_element_type=jnp.float32
        )

    query_grad = lax.cond(jnp.int32(0) > last_frame, keep_state, query_compute, query_zero)
    total_logs, total_deltas = (
        lax.all_gather(log_total, "blk", axis=2, tiled=True),
        lax.all_gather(delta, "blk", axis=2, tiled=True),
    )
    my_keys = heads_of(key_rows)
    my_values = heads_of(value_rows)
    query_piece_rows = lax.all_gather(query_rows, "blk", axis=1, tiled=True)
    grad_piece_rows = lax.all_gather(att_grad, "blk", axis=1, tiled=True)
    key_span = query_piece_rows.shape[1]

    def key_compute(state):
        query_pos = jnp.arange(key_span, dtype=jnp.int32)
        piece_queries = heads_of(query_piece_rows)
        piece_grads = heads_of(grad_piece_rows)
        scores = (
            jnp.einsum(
                "sphd,sfhd->shpf", piece_queries, my_keys, preferred_element_type=jnp.float32
            )
            * scale
        )
        mask = visible(my_pos, query_pos)
        probs = jnp.where(mask, jnp.exp(scores - total_logs[..., None]), 0.0)
        value_acc = jnp.einsum(
            "shpf,sphd->sfhd",
            probs.astype(jnp.bfloat16),
            piece_grads,
            preferred_element_type=jnp.float32,
        )
        prob_grad = jnp.einsum(
            "sphd,sfhd->shpf", piece_grads, my_values, preferred_element_type=jnp.float32
        )
        score_grad = (probs * (prob_grad - total_deltas[..., None])).astype(jnp.bfloat16)
        key_acc = scale * jnp.einsum(
            "shpf,sphd->sfhd", score_grad, piece_queries, preferred_element_type=jnp.float32
        )
        return (key_acc, value_acc)

    key_grad, value_grad = lax.cond(
        jnp.int32(0) + key_span - 1 < first_frame, keep_state, key_compute, (query_zero, query_zero)
    )
    query_low = query_grad.reshape(seq_count, frames, width).astype(jnp.bfloat16)
    value_low = value_grad.reshape(seq_count, frames, width).astype(jnp.bfloat16)
    qkv_grad = jnp.concatenate(
        [query_low, key_grad.reshape(seq_count, frames, width).astype(jnp.bfloat16), value_low], -1
    )
    attn_in_grad = outer_sum(attn_normed, qkv_grad)
    attn_in_bias_grad = jnp.concatenate([column_sum(query_low), column_sum(value_low)])
    back_zero, gain_zero, shift_zero = norm_back(
        apply_back(qkv_grad, attn_in), normed_zero, inverse_zero, gains[0]
    )
    hidden_grad = (self_grad + back_zero).astype(jnp.bfloat16)
    gain_grads = jnp.stack([gain_zero, gain_one, gain_two])
    shift_grads = jnp.stack([shift_zero, shift_one, shift_two])
    (
        ain_rows,
        ainb_rows,
        aout_rows,
        aoutb_rows,
        cq_rows,
        cqb_rows,
        cout_rows,
        coutb_rows,
        up_rows,
        up_bias_rows,
        down_rows,
        downb_rows,
        gain_rows,
        shift_rows,
    ) = (
        lax.psum_scatter(attn_in_grad, "blk", scatter_dimension=0, tiled=True),
        lax.psum_scatter(attn_in_bias_grad, "blk", scatter_dimension=0, tiled=True),
        lax.psum_scatter(attn_out_grad, "blk", scatter_dimension=0, tiled=True),
        lax.psum_scatter(attn_out_bias_grad, "blk", scatter_dimension=0, tiled=True),
        lax.psum_scatter(cross_query_grad, "blk", scatter_dimension=0, tiled=True),
        lax.psum_scatter(cross_query_bias_grad, "blk", scatter_dimension=0, tiled=True),
        lax.psum_scatter(cross_out_grad, "blk", scatter_dimension=0, tiled=True),
        lax.psum_scatter(cross_out_bias_grad, "blk", scatter_dimension=0, tiled=True),
        lax.psum_scatter(ff_up_grad, "blk", scatter_dimension=0, tiled=True),
        lax.psum_scatter(ff_up_bias_grad, "blk", scatter_dimension=0, tiled=True),
        lax.psum_scatter(ff_down_grad, "blk", scatter_dimension=0, tiled=True),
        lax.psum_scatter(ff_down_bias_grad, "blk", scatter_dimension=0, tiled=True),
        lax.psum_scatter(gain_grads, "blk", scatter_dimension=1, tiled=True),
        lax.psum_scatter(shift_grads, "blk", scatter_dimension=1, tiled=True),
    )
    summed = (
        lax.psum(ain_rows.astype(jnp.bfloat16), "items").astype(jnp.float32),
        lax.psum(ainb_rows.astype(jnp.bfloat16), "items").astype(jnp.float32),
        lax.psum(aout_rows.astype(jnp.bfloat16), "items").astype(jnp.float32),
        lax.psum(aoutb_rows.astype(jnp.bfloat16), "items").astype(jnp.float32),
        lax.psum(cq_rows.astype(jnp.bfloat16), "items").astype(jnp.float32),
        lax.psum(cqb_rows.astype(jnp.bfloat16), "items").astype(jnp.float32),
        lax.psum(cross_kv_rows.astype(jnp.bfloat16), "items").astype(jnp.float32),
        lax.psum(cross_v_bias_rows.astype(jnp.bfloat16), "items").astype(jnp.float32),
        lax.psum(cout_rows.astype(jnp.bfloat16), "items").astype(jnp.float32),
        lax.psum(coutb_rows.astype(jnp.bfloat16), "items").astype(jnp.float32),
        lax.psum(up_rows.astype(jnp.bfloat16), "items").astype(jnp.float32),
        lax.psum(up_bias_rows.astype(jnp.bfloat16), "items").astype(jnp.float32),
        lax.psum(down_rows.astype(jnp.bfloat16), "items").astype(jnp.float32),
        lax.psum(downb_rows.astype(jnp.bfloat16), "items").astype(jnp.float32),
        lax.psum(gain_rows.astype(jnp.bfloat16), "items").astype(jnp.float32),
        lax.psum(shift_rows.astype(jnp.bfloat16), "items").astype(jnp.float32),
    )
    return (
        layer_output,
        hidden_grad,
        text_grad,
        summed[0],
        summed[1],
        summed[2],
        summed[3],
        summed[4],
        summed[5],
        summed[6],
        summed[7],
        summed[8],
        summed[9],
        summed[10],
        summed[11],
        summed[12],
        summed[13],
        summed[14],
        summed[15],
    )


LANES = 128
MESH_ID = pl.DeviceIdType.MESH
VMEM_BYTES = 56 * 1024 * 1024


def contract(left, right, left_dim, right_dim):
    return lax.dot_general(
        left, right, (((left_dim,), (right_dim,)), ((), ())), preferred_element_type=jnp.float32
    )


def two_heads(values, low_half):
    none = jnp.zeros_like(values)
    return jnp.concatenate(
        [jnp.where(low_half, values, none), jnp.where(low_half, none, values)], 0
    )


LAGS = (0, 1, 2, 7, 13, 18, 23, 27, 28, 30)
FLASH_TURN = 3
TEXT_TURN = 14
SEND_TURNS = (9, 16)
LAND_TURN = 30
EARLY = 30
LATE = 4
SECOND_TURN = 0
ROWS = 256
VECTOR_ROWS = 24
VECTORS = ((0, 2), (2, 1), (3, 1), (4, 1), (5, 1), (6, 4), (10, 1))


def added(*terms):
    total = terms[0].astype(jnp.float32)
    for term in terms[1:]:
        total = total + term.astype(jnp.float32)
    return total.astype(jnp.bfloat16)


class Lane(NamedTuple):
    own: object
    got: object
    left: object
    right: object
    one_got: object
    one_sum: object
    two_got: object
    two_sum: object
    z_got: object
    z_sums: object
    z_kept: object
    z_far: object
    z_sum: object
    spread: object
    half: object
    back: object
    out: object
    made: object


class Slots(NamedTuple):
    mixed_grads: object
    query_grads: object
    key_grads: object
    value_grads: object
    key_sum: object
    value_sum: object
    landed: object
    turned: object
    text_parts: object
    text_sums: object
    text_low: object
    matrix: object
    matrix_got: object
    matrix_sum: object
    send_sem: object
    recv_sem: object
    load_sem: object
    store_sem: object
    out_send: object
    out_recv: object
    back_send: object
    back_recv: object
    text_send: object
    text_recv: object
    matrix_send: object
    matrix_recv: object
    save_sem: object
    hidden_sum: object
    self_grad: object
    hidden: object
    vectors: object
    vector_got: object
    vector_items: object
    final_sem: object
    vector_send: object
    vector_recv: object
    inputs: object
    input_sem: object
    matrix_final: object
    hidden_final: object
    vector_final: object
    end_sem: object


def lane_slots(half, rows_first, rows):
    low = jnp.bfloat16
    one = (4, 2, half, LANES) if rows_first else (4, LANES, LANES)
    return Lane(
        own=pltpu.VMEM((8, 4, 2, LANES, LANES), low),
        got=pltpu.VMEM((4, 4, 2, LANES, LANES), low),
        left=pltpu.VMEM((2, 4, 2, LANES, rows), low),
        right=pltpu.VMEM((2, rows, 2 * LANES), low),
        one_got=pltpu.VMEM((16,) + one, low),
        one_sum=pltpu.VMEM((10,) + one, low),
        two_got=pltpu.VMEM((18, 4, half, LANES), low),
        two_sum=pltpu.VMEM((12, 4, half, LANES), low),
        z_got=pltpu.VMEM((14, 3, half, LANES), low),
        z_sums=pltpu.VMEM((8, 3, half, LANES), low),
        z_kept=pltpu.VMEM((8, half, LANES), low),
        z_far=pltpu.VMEM((20, half, LANES), low),
        z_sum=pltpu.VMEM((8, half, LANES), low),
        spread=pltpu.VMEM((12, half, LANES), low),
        half=pltpu.VMEM((4, LANES, LANES), low),
        back=pltpu.VMEM((4, LANES, LANES), low),
        out=pltpu.VMEM((4, 2, LANES, LANES), low),
        made=pltpu.VMEM((4, 4, 2, LANES, LANES), low),
    )


def rings(text_shape, item_shape, frame_shape, blocks, kept):
    items, length, lanes = item_shape
    _, frames, triple = frame_shape
    width = triple // 3
    low = jnp.bfloat16
    return Slots(
        mixed_grads=pltpu.VMEM(item_shape, low),
        query_grads=pltpu.VMEM(item_shape, low),
        key_grads=pltpu.VMEM(item_shape, low),
        value_grads=pltpu.VMEM(item_shape, low),
        key_sum=pltpu.VMEM((length, lanes), jnp.float32),
        value_sum=pltpu.VMEM((length, lanes), jnp.float32),
        landed=pltpu.VMEM(frame_shape, low),
        turned=pltpu.VMEM((frame_shape[0], frame_shape[2] // 3, frame_shape[1]), low),
        text_parts=pltpu.VMEM((2, blocks) + text_shape, low),
        text_sums=pltpu.VMEM((2,) + text_shape, low),
        text_low=pltpu.VMEM(text_shape[:2] + (2 * blocks * LANES,), low),
        matrix=pltpu.VMEM((2, LANES, blocks * LANES), low),
        matrix_got=pltpu.VMEM((3, LANES, blocks * LANES), low),
        matrix_sum=pltpu.VMEM((2, LANES, blocks * LANES), low),
        send_sem=pltpu.SemaphoreType.DMA((16, 22)),
        recv_sem=pltpu.SemaphoreType.DMA((16, 22)),
        load_sem=pltpu.SemaphoreType.DMA((2, 2, 2)),
        store_sem=pltpu.SemaphoreType.DMA((2, 2, 4)),
        out_send=pltpu.SemaphoreType.DMA((items + 2, blocks)),
        out_recv=pltpu.SemaphoreType.DMA((items + 2, blocks)),
        back_send=pltpu.SemaphoreType.DMA((items, 3, blocks)),
        back_recv=pltpu.SemaphoreType.DMA((items, 3, blocks)),
        text_send=pltpu.SemaphoreType.DMA((2, blocks)),
        text_recv=pltpu.SemaphoreType.DMA((2, blocks)),
        matrix_send=pltpu.SemaphoreType.DMA((3,)),
        matrix_recv=pltpu.SemaphoreType.DMA((3,)),
        save_sem=pltpu.SemaphoreType.DMA((2,)),
        hidden_sum=pltpu.VMEM((items, frames, width), jnp.float32),
        self_grad=pltpu.VMEM((items, frames, width), jnp.float32),
        hidden=pltpu.VMEM((items, frames, width), low),
        vectors=pltpu.VMEM((blocks, VECTOR_ROWS, LANES), jnp.float32),
        vector_got=pltpu.VMEM((blocks, VECTOR_ROWS, LANES), jnp.float32),
        vector_items=pltpu.VMEM((4, VECTOR_ROWS, LANES), jnp.float32),
        final_sem=pltpu.SemaphoreType.DMA((2,)),
        vector_send=pltpu.SemaphoreType.DMA((blocks + 3,)),
        vector_recv=pltpu.SemaphoreType.DMA((blocks + 3,)),
        inputs=tuple(pltpu.VMEM(array.shape, array.dtype) for array in kept),
        input_sem=pltpu.SemaphoreType.DMA((len(kept),)),
        matrix_final=pltpu.VMEM((2, LANES, width), jnp.float32),
        hidden_final=pltpu.VMEM((items, frames, width), low),
        vector_final=pltpu.VMEM((VECTOR_ROWS, LANES), jnp.float32),
        end_sem=pltpu.SemaphoreType.DMA((3,)),
    )


def backward_kernel(plan, head, *refs):
    refs = list(refs)

    def take(count):
        taken = refs[:count]
        del refs[:count]
        return taken

    (limit_ref, att_grad, text_key, text_value) = take(4)
    kept = take(10)
    hidden_ref, self_ref, weight_ref = take(3)
    lefts = take(len(plan) - 1)
    rights = take(len(plan) - 1)
    outs = take(len(plan))
    text_out, matrix_out, hidden_out = take(3)
    vector_out = take(1)[0]
    lanes_of = [Lane(*take(len(Lane._fields))) for _ in range(2)]
    own = Slots(*refs)
    q_ref, k_ref, v_ref, o_ref, lse_ref, normed_ref, text_ref, sums_ref, up_ref, gain_ref = own.inputs
    items, length, lanes = q_ref.shape
    frames = att_grad.shape[1]
    width = att_grad.shape[2]
    blocks = length // frames
    group = lax.axis_index("items")
    block = lax.axis_index("blk")
    y, core = group // 2, group % 2
    z, x = block // 2, block % 2
    to_core = {"items": y * 2 + (1 - core)}
    to_y = {"items": (1 - y) * 2 + core}
    to_x = {"blk": z * 2 + (1 - x)}
    is_inner = (z == 1) | (z == 2)
    to_neighbour = {"blk": (z + 1 - 2 * (z % 2)) * 2 + x}
    to_far_inner = {"blk": (2 - z // 2) * 2 + x}
    to_far_outer = {"blk": (3 - 3 * (z // 2)) * 2 + x}
    places = [lax.rem(block + step, blocks) for step in range(blocks)]
    inputs = [
        pltpu.make_async_copy(source, target, own.input_sem.at[number])
        for number, (source, target) in enumerate(zip(kept, own.inputs))
    ]
    for copy in inputs:
        copy.start()
    barrier = pltpu.get_barrier_semaphore()
    to_far = {"items": (1 - y) * 2 + (1 - core)}
    peers = [to_core, to_y, to_far] + [{"blk": place} for place in places[1:]]
    for peer in peers:
        pl.semaphore_signal(barrier, inc=1, device_id=peer, device_id_type=MESH_ID)
    pl.semaphore_wait(barrier, len(peers))

    def at(ring, index):
        return ring.at[lax.rem(index, ring.shape[0])]

    def half_rows(place):
        return pl.ds(pl.multiple_of(place * (LANES // 2), LANES // 2), LANES // 2)

    def lane_block(offset, place):
        return pl.ds(pl.multiple_of(offset + place * LANES, LANES), LANES)

    def frame_rows(place):
        return pl.ds(pl.multiple_of(place * frames, frames), frames)

    def copy_to(peer, source, target, send, recv):
        return pltpu.make_async_remote_copy(
            src_ref=source,
            dst_ref=target,
            send_sem=send,
            recv_sem=recv,
            device_id=peer,
            device_id_type=MESH_ID,
        )

    def remote(kind, got, index, source, peer):
        slot = lax.rem(index, got.shape[0])
        return copy_to(
            peer,
            source,
            got.at[slot],
            own.send_sem.at[kind, slot],
            own.recv_sem.at[kind, slot],
        )

    def target_view(tensor, local, half):
        parts = plan[tensor][2]
        return outs[tensor].at[local % parts, :, lane_block(half * LANES, 2 * (local // parts))]

    def with_tensor(piece, action):
        for tensor, (start, count, _) in enumerate(plan):

            @pl.when((piece >= start) & (piece < start + count))
            def _():
                action(tensor, piece - start)

    made_start = plan[-1][0]

    def lane_steps(number, lane, base, offset, rows_first):
        def loads(index, tensor, local):
            slot = lax.rem(index, lane.left.shape[0])
            parts = plan[tensor][2]
            columns = pl.ds(pl.multiple_of((local // parts) * 2 * LANES, LANES), 2 * LANES)
            return [
                pltpu.make_async_copy(
                    lefts[tensor].at[:, :, local % parts],
                    lane.left.at[slot],
                    own.load_sem.at[number, 0, slot],
                ),
                pltpu.make_async_copy(
                    rights[tensor].at[:, columns],
                    lane.right.at[slot],
                    own.load_sem.at[number, 1, slot],
                ),
            ]

        def weight_load(index, local):
            slot = lax.rem(index, lane.left.shape[0])
            columns = pl.ds(pl.multiple_of(local * 2 * LANES, LANES), 2 * LANES)
            return pltpu.make_async_copy(
                weight_ref.at[:, :, :, columns],
                lane.left.at[slot, :, :, :, 0 : 2 * LANES],
                own.load_sem.at[number, 0, slot],
            )

        def fetch(index):
            def start(tensor, local):
                if tensor < len(plan) - 1:
                    for copy in loads(index, tensor, local):
                        copy.start()
                else:
                    weight_load(index, local).start()

            with_tensor(base + index, start)

        def send(kind, got, index, source, peer):
            return remote(8 * number + kind, got, index, source, peer)

        def split(index, product):
            product = product.reshape(4, 2, LANES, 2 * LANES).astype(jnp.bfloat16)
            sides = (product[..., :LANES], product[..., LANES:])
            at(lane.own, index)[...] = jnp.where(core == 0, sides[0], sides[1])
            at(lane.made, index)[...] = jnp.where(core == 0, sides[1], sides[0])

        def begin(index):
            @pl.when(base + index < made_start)
            def _():
                for copy in loads(index, 0, 0):
                    copy.wait()
                left = at(lane.left, index)[...].reshape(8 * LANES, -1)
                split(index, contract(left, at(lane.right, index)[...], 1, 0))

            @pl.when(base + index >= made_start)
            def _():
                local = base + index - made_start
                columns = pl.ds(pl.multiple_of(local * 2 * LANES, LANES), 2 * LANES)
                parts = [
                    contract(own.turned[item], own.landed[item, :, columns], 1, 0)
                    for item in range(items)
                ]
                split(index, sum(parts))
                weight_load(index, local).wait()
                weight = at(lane.left, index)[:, :, :, 0 : 2 * LANES].reshape(width, 2 * LANES)
                for item in range(items):
                    own.hidden_sum[item] += contract(own.landed[item, :, columns], weight, 1, 1)

            send(0, lane.got, index, at(lane.made, index), to_core).start()

        def one_copy(index):
            if rows_first:
                source = at(lane.own, index).at[:, :, half_rows(1 - y), :]
                return send(1, lane.one_got, index, source, to_y)
            return send(1, lane.one_got, index, at(lane.own, index).at[:, 1 - x], to_x)

        def two_copy(index):
            if rows_first:
                return send(2, lane.two_got, index, at(lane.one_sum, index).at[:, 1 - x], to_x)
            source = at(lane.one_sum, index).at[:, half_rows(1 - y), :]
            return send(2, lane.two_got, index, source, to_y)

        def z_near(index, outward):
            slot = lax.rem(index, lane.z_got.shape[0])
            sums = at(lane.two_sum, index)
            if outward:
                source, target = sums.at[3 * (z // 2)], lane.z_got.at[slot, 0]
            else:
                source, target = sums.at[pl.ds(1 - z // 2, 3)], lane.z_got.at[slot]
            return copy_to(
                to_neighbour,
                source,
                target,
                own.send_sem.at[8 * number + 3, slot],
                own.recv_sem.at[8 * number + 3, slot],
            )

        def z_across(index, outer):
            slot = lax.rem(index, lane.z_far.shape[0])
            sums = at(lane.z_sums, index)
            return copy_to(
                to_far_outer if outer else to_far_inner,
                sums.at[2 * (1 - z // 2)] if outer else sums.at[1],
                lane.z_far.at[slot],
                own.send_sem.at[8 * number + 4 + outer, slot],
                own.recv_sem.at[8 * number + 4, slot],
            )

        def spread_copy(index):
            return send(6, lane.spread, index, at(lane.z_sum, index), to_y)

        def back_copy(index):
            return send(7, lane.back, index, at(lane.half, index), to_core)

        def chip(index):
            send(0, lane.got, index, at(lane.made, index), to_core).wait()
            target = at(lane.own, index)
            target[...] = added(target[...], at(lane.got, index)[...])
            one_copy(index).start()

        def one(index):
            one_copy(index).wait()
            kept = at(lane.own, index)
            kept = kept[:, :, half_rows(y), :] if rows_first else kept[:, x]
            at(lane.one_sum, index)[...] = added(kept, at(lane.one_got, index)[...])
            two_copy(index).start()

        def two(index):
            two_copy(index).wait()
            kept = at(lane.one_sum, index)
            kept = kept[:, x] if rows_first else kept[:, half_rows(y), :]
            at(lane.two_sum, index)[...] = added(kept, at(lane.two_got, index)[...])
            @pl.when(is_inner)
            def _():
                z_near(index, True).start()

            @pl.when(jnp.logical_not(is_inner))
            def _():
                z_near(index, False).start()

        def near(index):
            @pl.when(is_inner)
            def _():
                z_near(index, True).wait_send()
                z_near(index, False).wait_recv()
                first = 1 - z // 2
                sums = at(lane.z_sums, index)
                sums[...] = added(
                    at(lane.two_sum, index)[pl.ds(first, 3)], at(lane.z_got, index)[...]
                )
                at(lane.z_kept, index)[...] = sums[2 * (z // 2)]
                z_across(index, 0).start()
                z_across(index, 1).start()

            @pl.when(jnp.logical_not(is_inner))
            def _():
                z_near(index, False).wait_send()
                z_near(index, True).wait_recv()
                at(lane.z_kept, index)[...] = added(
                    at(lane.two_sum, index)[z], at(lane.z_got, index)[0]
                )

        def three(index):
            @pl.when(is_inner)
            def _():
                z_across(index, 0).wait_send()
                z_across(index, 1).wait_send()

            z_across(index, 0).wait_recv()
            at(lane.z_sum, index)[...] = added(
                at(lane.z_kept, index)[...], at(lane.z_far, index)[...]
            )
            spread_copy(index).start()

        def four(index):
            spread_copy(index).wait()
            target = at(lane.half, index)
            target[half_rows(y), :] = at(lane.z_sum, index)[...]
            target[half_rows(1 - y), :] = at(lane.spread, index)[...]
            back_copy(index).start()

        def finish(index):
            back_copy(index).wait()
            slot = lax.rem(index, lane.out.shape[0])
            lane.out[slot, core] = at(lane.half, index)[...]
            lane.out[slot, 1 - core] = at(lane.back, index)[...]

            def start(tensor, local):
                for side in range(2):
                    pltpu.make_async_copy(
                        lane.out.at[slot, side],
                        target_view(tensor, local, side),
                        own.store_sem.at[number, side, slot],
                    ).start()

            with_tensor(base + index, start)

        def close(index):
            slot = lax.rem(index, lane.out.shape[0])
            for side in range(2):
                pltpu.make_async_copy(
                    lane.out.at[slot, side],
                    target_view(0, 0, side),
                    own.store_sem.at[number, side, slot],
                ).wait()

        return [
            lambda index, step=step: step(index + offset)
            for step in (fetch, begin, chip, one, two, near, three, four, finish, close)
        ]

    def out_copies(item):
        copies = []
        for step in range(blocks):
            source = att_grad.at[item, :, lane_block(0, places[step])]
            target = own.mixed_grads.at[item, frame_rows(block), :]
            recv = own.out_recv.at[item, step]
            if step == 0:
                copies.append(pltpu.make_async_copy(source, target, recv))
            else:
                peer = {"blk": places[step]}
                copies.append(copy_to(peer, source, target, own.out_send.at[item, step], recv))
        return copies

    def text_out_copies():
        copies = []
        for part, text in enumerate((text_key, text_value)):
            for step in range(blocks):
                source = text.at[:, :, lane_block(0, places[step])]
                target = own.text_parts.at[part, step]
                recv = own.out_recv.at[items + part, step]
                if step == 0:
                    copies.append(pltpu.make_async_copy(source, target, recv))
                else:
                    peer = {"blk": places[step]}
                    send = own.out_send.at[items + part, step]
                    copies.append(copy_to(peer, source, target, send, recv))
        return copies

    def out_start(_):
        for item in range(items):
            for copy in out_copies(item):
                copy.start()
        for copy in text_out_copies():
            copy.start()

    def out_wait(item):
        def run(_):
            for copy in out_copies(item) + (inputs[:5] if item == 0 else []):
                copy.wait()

        return run

    scale = head ** (-0.5)
    flash_blocks = length // ROWS

    def flash_unit(item, number):
        span = (number + 1) * ROWS
        here = slice(number * ROWS, span)
        low_half = lax.broadcasted_iota(jnp.int32, (ROWS, lanes), 1) < head
        queries = two_heads(q_ref[item, here, :] * jnp.bfloat16(scale), low_half)
        mixed_grad = own.mixed_grads[item, here, :]
        mixed_grads = two_heads(mixed_grad, low_half)
        logs = jnp.transpose(lse_ref[item, here, :])
        logs = jnp.concatenate([logs[0:1], logs[head : head + 1]], 1)
        products = jnp.transpose(mixed_grad.astype(jnp.float32) * o_ref[item, here, :])
        delta = jnp.concatenate(
            [
                jnp.sum(products[:head], 0, keepdims=True),
                jnp.sum(products[head:], 0, keepdims=True),
            ],
            1,
        )
        keys = k_ref[item, :span, :]
        scores = contract(keys, queries, 1, 1)
        key_pos = lax.broadcasted_iota(jnp.int32, (ROWS, 2 * ROWS), 0)
        query_pos = lax.broadcasted_iota(jnp.int32, (ROWS, 2 * ROWS), 1) % ROWS
        corner = jnp.where(key_pos <= query_pos, scores[span - ROWS :], NEG_FILL)
        scores = corner if number == 0 else jnp.concatenate([scores[: span - ROWS], corner], 0)
        if span > length // 2:
            valid = lax.broadcasted_iota(jnp.int32, (span, 1), 0) < limit_ref[item]
            scores = scores + jnp.where(valid, 0.0, NEG_FILL)
        probs = jnp.exp(scores - logs)
        prob_grads = contract(v_ref[item, :span, :], mixed_grads, 1, 1)
        score_grads = (probs * (prob_grads - delta)).astype(jnp.bfloat16)
        query_grads = scale * contract(score_grads, keys, 0, 0)
        own.query_grads[item, here, :] = jnp.where(
            low_half, query_grads[:ROWS], query_grads[ROWS:]
        ).astype(jnp.bfloat16)
        value_part = contract(probs.astype(jnp.bfloat16), mixed_grads, 1, 0)
        key_part = contract(score_grads, queries, 1, 0)
        if number == flash_blocks - 1:
            own.value_sum[...] = value_part
            own.key_sum[...] = key_part
        else:
            own.value_sum[:span] += value_part
            own.key_sum[:span] += key_part
        if number == 0:
            own.key_grads[item] = own.key_sum[...].astype(jnp.bfloat16)
            own.value_grads[item] = own.value_sum[...].astype(jnp.bfloat16)

    def flash(index):
        for number in range(flash_blocks):

            @pl.when(lax.rem(index, flash_blocks) == flash_blocks - 1 - number)
            def _():
                flash_unit(index // flash_blocks, number)

    parts_of = (own.query_grads, own.key_grads, own.value_grads)

    def back_copy(item, part, step):
        place = lax.rem(block + step, blocks)
        return copy_to(
            {"blk": place},
            parts_of[part].at[item, frame_rows(place), :],
            own.landed.at[item, :, lane_block(part * width, block)],
            own.back_send.at[item, part, step],
            own.back_recv.at[item, part, step],
        )

    def back_own(item, part):
        return pltpu.make_async_copy(
            parts_of[part].at[item, frame_rows(block), :],
            own.landed.at[item, :, lane_block(part * width, block)],
            own.back_recv.at[item, part, 0],
        )

    def back_some(item):
        def run(index):
            @pl.when(index == 0)
            def _():
                for part in range(3):
                    back_own(item, part).start()

            for part in range(3):
                back_copy(item, part, 1 + index).start()

        return run

    def text_save():
        return pltpu.make_async_copy(own.text_low, text_out, own.save_sem.at[0])

    def final_loads():
        return [
            pltpu.make_async_copy(self_ref, own.self_grad, own.final_sem.at[0]),
            pltpu.make_async_copy(hidden_ref, own.hidden, own.final_sem.at[1]),
        ]

    def back_wait(_):
        for item in range(items):
            for part in range(3):
                back_own(item, part).wait()
                for step in range(1, blocks):
                    back_copy(item, part, step).wait()
            if item == 0:
                inputs[5].wait()
            own.turned[item] = jnp.transpose(normed_ref[item])
        own.hidden_sum[...] = jnp.zeros_like(own.hidden_sum)
        for copy in final_loads():
            copy.start()

    def vector_copy(kind, source, target, peer):
        return copy_to(
            peer, source, target, own.vector_send.at[kind], own.vector_recv.at[kind]
        )

    def vector_blocks():
        return [
            vector_copy(
                step, own.vectors.at[places[step]], own.vector_got.at[step], {"blk": places[step]}
            )
            for step in range(1, blocks)
        ]

    def vector_spread():
        return [
            vector_copy(
                blocks + number, own.vector_items.at[0], own.vector_items.at[1 + number], peer
            )
            for number, peer in enumerate([to_core, to_y, to_far])
        ]

    def final(_):
        for copy in final_loads() + inputs[7:]:
            copy.wait()
        gain_zero = 0.0
        shift_zero = 0.0
        query_bias = 0.0
        value_bias = 0.0
        gains = gain_ref[0:1, :].astype(jnp.float32)
        for item in range(items):
            normed, inverse = row_norm(own.hidden[item].astype(jnp.float32))
            grad = own.hidden_sum[item]
            gain_zero = gain_zero + total_rows(grad * normed)
            shift_zero = shift_zero + total_rows(grad)
            own.hidden_final[item] = (
                own.self_grad[item] + row_norm_back(grad, normed, inverse, gains)
            ).astype(jnp.bfloat16)
            query_bias = query_bias + total_rows(own.landed[item, :, :width])
            value_bias = value_bias + total_rows(own.landed[item, :, 2 * width :])
        singles = [
            (2, sums_ref[3:4, :]),
            (3, sums_ref[2:3, :]),
            (5, sums_ref[1:2, :]),
            (10, sums_ref[0:1, :]),
            (11, gain_zero),
            (12, sums_ref[4:5, :]),
            (13, sums_ref[5:6, :]),
            (14, shift_zero),
            (15, sums_ref[6:7, :]),
            (16, sums_ref[7:8, :]),
        ]
        own.vectors[...] = jnp.zeros_like(own.vectors)
        for place in range(blocks):
            for row, vector in singles:
                own.vectors[place, row : row + 1, :] = vector[:, place * LANES : (place + 1) * LANES]
            bias = query_bias if place < blocks // 2 else value_bias
            for half in range(2):
                start = (place % (blocks // 2)) * 2 * LANES + half * LANES
                own.vectors[place, half : half + 1, :] = bias[:, start : start + LANES]
            for part in range(4):
                start = (place * 4 + part) * LANES
                own.vectors[place, 6 + part : 7 + part, :] = up_ref[:, start : start + LANES]
        for copy in vector_blocks():
            copy.start()
        end_copies()[1].start()

    def vector_sum(_):
        total = own.vectors[block]
        for step, copy in enumerate(vector_blocks()):
            copy.wait()
            total = total + own.vector_got[step + 1]
        own.vector_items[0] = total
        columns = lane_block(width, block)
        value_bias = sum(total_rows(own.text_low[item, :, columns]) for item in range(items))
        own.vector_items[0, 4:5, :] = value_bias
        for copy in vector_spread():
            copy.start()

    def vector_finish(_):
        for copy in vector_spread():
            copy.wait()
        own.vector_final[...] = (own.vector_items[0] + own.vector_items[1]) + (
            own.vector_items[2] + own.vector_items[3]
        )
        end_copies()[2].start()

    def end_copies():
        ends = [
            (own.matrix_final, matrix_out),
            (own.hidden_final, hidden_out),
            (own.vector_final, vector_out),
        ]
        return [
            pltpu.make_async_copy(source, out, own.end_sem.at[number])
            for number, (source, out) in enumerate(ends)
        ]

    def text_copies():
        copies = []
        for part in range(2):
            target = own.text_low.at[:, :, lane_block(part * width, block)]
            source = own.text_sums.at[part]
            for step in range(1, blocks):
                copies.append(
                    copy_to(
                        {"blk": places[step]},
                        source,
                        target,
                        own.text_send.at[part, step],
                        own.text_recv.at[part, step],
                    )
                )
            copies.append(pltpu.make_async_copy(source, target, own.text_recv.at[part, 0]))
        return copies

    def text_sum(_):
        for copy in text_out_copies():
            copy.wait()
        for part in range(2):
            own.text_sums[part] = added(*[own.text_parts[part, step] for step in range(blocks)])
        for copy in text_copies():
            copy.start()

    def matrix_copy(number):
        source = [own.matrix.at[1 - core], own.matrix_sum.at[0], own.matrix_sum.at[1]]
        return copy_to(
            [to_core, to_y, to_core][number],
            source[number],
            own.matrix_got.at[number],
            own.matrix_send.at[number],
            own.matrix_recv.at[number],
        )

    def text_product(_):
        for copy in text_copies() + inputs[6:7]:
            copy.wait()
        for side in range(2):
            columns = slice(side * width, (side + 1) * width)
            rows = sum(
                contract(
                    text_ref[item, :, lane_block(0, block)], own.text_low[item, :, columns], 0, 0
                )
                for item in range(items)
            )
            own.matrix[side] = rows.astype(jnp.bfloat16)
        matrix_copy(0).start()
        text_save().start()

    def matrix_one(_):
        matrix_copy(0).wait()
        own.matrix_sum[0] = added(own.matrix[core], own.matrix_got[0])
        matrix_copy(1).start()

    def matrix_two(_):
        matrix_copy(1).wait()
        own.matrix_sum[1] = added(own.matrix_sum[0], own.matrix_got[1])
        matrix_copy(2).start()

    def matrix_three(_):
        matrix_copy(2).wait()
        own.matrix_final[core] = own.matrix_sum[1].astype(jnp.float32)
        own.matrix_final[1 - core] = own.matrix_got[2].astype(jnp.float32)
        end_copies()[0].start()

    stages = [(0, 1, out_start), (LAND_TURN, 1, back_wait)]
    late = plan[-1][1]
    final_turn = LAND_TURN + max(LATE, late - LATE) + 1
    segments = [
        (0, EARLY, 0, 0, 0),
        (1, made_start - EARLY, 0, EARLY, SECOND_TURN),
        (0, LATE, EARLY, made_start - EARLY, LAND_TURN),
        (1, late - LATE, made_start - EARLY, LATE + EARLY, LAND_TURN),
    ]
    for number, count, offset, base, turn_base in segments:
        steps = lane_steps(number, lanes_of[number], base, offset, number == 0)
        stages += [(turn_base + lag, count, step) for lag, step in zip(LAGS, steps)]
    stages += [
        (FLASH_TURN, 1, out_wait(0)),
        (FLASH_TURN + flash_blocks, 1, out_wait(1)),
        (FLASH_TURN, items * flash_blocks, flash),
        (TEXT_TURN, 1, text_sum),
        (LAND_TURN + 1, 1, text_product),
        (LAND_TURN + 3, 1, matrix_one),
        (LAND_TURN + 14, 1, matrix_two),
        (LAND_TURN + 18, 1, matrix_three),
    ]
    stages += [
        (turn, blocks - 1, back_some(item)) for item, turn in enumerate(SEND_TURNS)
    ]

    stages += [
        (final_turn, 1, final),
        (final_turn + 9, 1, vector_sum),
        (final_turn + 18, 1, vector_finish),
    ]

    def turn(time, carry):
        for lag, count, action in stages:

            @pl.when((time >= lag) & (time < lag + count))
            def _():
                action(time - lag)

        return carry

    lax.fori_loop(0, max(lag + count for lag, count, _ in stages), turn, 0)
    for copy in [text_save()] + end_copies():
        copy.wait()


def backward(factors, weight, blocks, identity, limits, sent, kept, more):
    plan = []
    start = 0
    lefts = []
    rights = []
    shapes = []
    width = sent[0].shape[2]
    sizes = [(left.shape[0], right.shape[1]) for left, right in factors] + [weight.shape]
    for rows, columns in sizes:
        parts = rows // blocks // LANES
        count = parts * columns // (2 * LANES)
        plan.append((start, count, parts))
        start += count
        shapes.append(jax.ShapeDtypeStruct((parts, LANES, columns), jnp.bfloat16))
    for (left, right), (_, _, parts) in zip(factors, plan):
        lefts.append(left.reshape(blocks // 2, 2, parts, LANES, left.shape[1]))
        rights.append(right)
    items, frames, _ = sent[0].shape
    text_count = sent[1].shape[1]
    frame_shape = (items, frames, 3 * width)
    text_shape = (items, text_count, LANES)
    scratch = lane_slots(LANES // 2, True, items * frames)
    scratch += lane_slots(LANES // 2, False, items * frames)
    scratch += rings(text_shape, kept[0].shape, frame_shape, blocks, kept)
    far = pl.BlockSpec(memory_space=pl.ANY)
    small = pl.BlockSpec(memory_space=pltpu.SMEM)
    outs = pl.pallas_call(
        partial(
            backward_kernel,
            plan,
            width // HEADS,
        ),
        out_shape=shapes
        + [
            jax.ShapeDtypeStruct((items, text_count, 2 * width), jnp.bfloat16),
            jax.ShapeDtypeStruct((2, LANES, width), jnp.float32),
            jax.ShapeDtypeStruct((items, frames, width), jnp.bfloat16),
        ]
        + [jax.ShapeDtypeStruct((VECTOR_ROWS, LANES), jnp.float32)],
        in_specs=[small] + [far] * (len(sent) + len(kept) + 3 + 2 * len(lefts)),
        out_specs=[far] * (len(shapes) + 4),
        scratch_shapes=list(scratch),
        compiler_params=pltpu.CompilerParams(
            collective_id=identity, has_side_effects=True, vmem_limit_bytes=62 * 1024 * 1024
        ),
    )(
        limits,
        *sent,
        *kept,
        *more,
        weight.reshape(blocks // 2, 2, LANES, weight.shape[1]),
        *lefts,
        *rights,
    )
    grads = [out.reshape(-1, out.shape[-1]) for out in outs[: len(shapes)]]
    return grads, outs[len(shapes) :]


FF_TILE = 1024


class Middle(NamedTuple):
    attn_out: object
    cross_query: object
    cross_out: object
    ff_up: object
    ff_down: object
    layer_output: object
    attended_turned: object
    cross_normed_turned: object
    cross_attended_turned: object
    ff_normed_turned: object
    activated_turned: object
    pre_grad: object
    cross_grad_low: object
    cross_q_grad: object
    self_grad_low: object
    self_grad: object
    att_grad: object
    text_key: object
    text_value: object
    after: object
    normed_one: object
    normed_two: object
    forward_sum: object
    backward_sum: object
    cross_normed: object
    cross_attended: object
    ff_normed: object
    cross_queries: object
    cross_att_grad: object
    probs: object
    load_sem: object
    save_sem: object


def row_norm(values):
    centre = jnp.mean(values, -1, keepdims=True)
    spread = values - centre
    inverse = lax.rsqrt(jnp.mean(spread * spread, -1, keepdims=True) + 1e-05)
    return spread * inverse, inverse


def row_norm_back(grad, normed, inverse, gain):
    scaled = grad * gain
    first_mean = jnp.mean(scaled, -1, keepdims=True)
    second_mean = jnp.mean(scaled * normed, -1, keepdims=True)
    return inverse * (scaled - first_mean - normed * second_mean)


def total_rows(values):
    return jnp.sum(values.astype(jnp.float32), 0, keepdims=True)


def middle_kernel(items, head, *refs):
    refs = list(refs)
    length_ref, hidden, attended, out_grad, text_keys, text_values, gain, shift, bias = refs[:9]
    weights = refs[9:14]
    saved = refs[14:28]
    sums, up_sums = refs[28:30]
    own = Middle(*refs[30:])
    low = jnp.bfloat16
    rows = hidden.shape[0]
    width = hidden.shape[1]
    frames = rows // items
    text_count = text_keys.shape[0] // items
    pairs = width // (2 * head)
    scale = head ** (-0.5)
    gains = gain[...].astype(jnp.float32)
    shifts = shift[...].astype(jnp.float32)

    def bias_of(number):
        return bias[:, (3 + number) * width : (4 + number) * width]

    loads = [
        pltpu.make_async_copy(weight, own[number], own.load_sem.at[number])
        for number, weight in enumerate(weights)
    ]
    for load in loads:
        load.start()
    saves = [
        pltpu.make_async_copy(own[5 + number], out, own.save_sem.at[number])
        for number, out in enumerate(saved)
    ]

    def save(*names):
        for name in names:
            saves[Middle._fields.index(name) - 5].start()

    own.attended_turned[...] = jnp.transpose(attended[...])
    loads[0].wait()
    after_self = (
        hidden[...].astype(jnp.float32)
        + contract(attended[...], own.attn_out[...], 1, 0)
        + bias_of(0)
    )
    own.after[...] = after_self
    normed, inverse_one = row_norm(after_self)
    own.normed_one[...] = normed
    own.cross_normed[...] = (normed * gains[1:2] + shifts[1:2]).astype(low)
    own.cross_normed_turned[...] = jnp.transpose(own.cross_normed[...])
    save(*"attended_turned cross_normed_turned".split())
    loads[1].wait()
    own.cross_queries[...] = (
        contract(own.cross_normed[...], own.cross_query[...], 1, 0) + bias_of(1)
    ).astype(low)
    low_half = lax.broadcasted_iota(jnp.int32, (frames, 2 * head), 1) < head

    def pair_parts(item, pair):
        return (
            slice(item * frames, (item + 1) * frames),
            slice(item * text_count, (item + 1) * text_count),
            slice(pair * 2 * head, (pair + 1) * 2 * head),
        )

    def joined(values):
        return jnp.where(low_half, values[:frames], values[frames:])

    for item in range(items):
        seen = lax.broadcasted_iota(jnp.int32, (text_count, 1), 0) < length_ref[item]
        for pair in range(pairs):
            here, texts, lanes = pair_parts(item, pair)
            queries = two_heads(own.cross_queries[here, lanes] * low(scale), low_half)
            scores = contract(text_keys[texts, lanes], queries, 1, 1)
            scores = jnp.where(seen, scores, NEG_FILL)
            raised = jnp.exp(scores - jnp.max(scores, 0, keepdims=True))
            raised = jnp.where(seen, raised, 0.0)
            probs = raised / jnp.sum(raised, 0, keepdims=True)
            own.probs[item * pairs + pair] = probs
            mixed = contract(probs.astype(low), text_values[texts, lanes], 0, 0)
            own.cross_attended[here, lanes] = joined(mixed).astype(low)
    loads[2].wait()
    after_cross = (
        own.after[...]
        + contract(own.cross_attended[...], own.cross_out[...], 1, 0)
        + bias_of(2)
    )
    own.after[...] = after_cross
    normed, inverse_two = row_norm(after_cross)
    own.normed_two[...] = normed
    own.ff_normed[...] = (normed * gains[2:3] + shifts[2:3]).astype(low)
    own.cross_attended_turned[...] = jnp.transpose(own.cross_attended[...])
    own.ff_normed_turned[...] = jnp.transpose(own.ff_normed[...])
    save(*"cross_attended_turned ff_normed_turned".split())
    loads[3].wait()
    loads[4].wait()
    own.forward_sum[...] = jnp.zeros_like(own.forward_sum)
    own.backward_sum[...] = jnp.zeros_like(own.backward_sum)

    def tile(number, carry):
        here = pl.ds(pl.multiple_of(number * FF_TILE, FF_TILE), FF_TILE)
        pre = contract(own.ff_normed[...], own.ff_up[:, here], 1, 0) + bias[:, pl.ds(pl.multiple_of(7 * width + number * FF_TILE, FF_TILE), FF_TILE)]
        act_grad = contract(out_grad[...], own.ff_down[here, :], 1, 1)
        below = 0.5 + 0.5 * lax.erf(pre * (0.5**0.5))
        active = (pre * below).astype(low)
        slope = below + pre * (jnp.exp(-0.5 * pre * pre) * 0.3989422804014327)
        grad = (act_grad * slope).astype(low)
        own.activated_turned[here, :] = jnp.transpose(active)
        own.pre_grad[:, here] = grad
        up_sums[:, here] = total_rows(grad)
        own.forward_sum[...] += contract(active, own.ff_down[here, :], 1, 0)
        own.backward_sum[...] += contract(grad, own.ff_up[:, here], 1, 1)
        return carry

    lax.fori_loop(0, own.ff_up.shape[1] // FF_TILE, tile, 0)
    own.layer_output[...] = (own.after[...] + own.forward_sum[...] + bias_of(3)).astype(low)
    save(*"layer_output activated_turned pre_grad".split())
    grad = own.backward_sum[...]
    sums[0:1, :] = total_rows(out_grad[...])
    sums[5:6, :] = total_rows(grad * own.normed_two[...])
    sums[7:8, :] = total_rows(grad)
    cross_grad = out_grad[...].astype(jnp.float32) + row_norm_back(
        grad, own.normed_two[...], inverse_two, gains[2:3]
    )
    own.after[...] = cross_grad
    own.cross_grad_low[...] = cross_grad.astype(low)
    sums[1:2, :] = total_rows(own.cross_grad_low[...])
    own.cross_att_grad[...] = contract(own.cross_grad_low[...], own.cross_out[...], 1, 1).astype(low)
    for item in range(items):
        for pair in range(pairs):
            here, texts, lanes = pair_parts(item, pair)
            grads = two_heads(own.cross_att_grad[here, lanes], low_half)
            queries = two_heads(own.cross_queries[here, lanes] * low(scale), low_half)
            probs = own.probs[item * pairs + pair]
            prob_grads = contract(text_values[texts, lanes], grads, 1, 1)
            score_grads = probs * (prob_grads - jnp.sum(probs * prob_grads, 0, keepdims=True))
            score_grads = score_grads.astype(low)
            own.text_key[texts, lanes] = contract(score_grads, queries, 1, 0).astype(low)
            own.text_value[texts, lanes] = contract(probs.astype(low), grads, 1, 0).astype(low)
            query_grads = scale * contract(score_grads, text_keys[texts, lanes], 0, 0)
            own.cross_q_grad[here, lanes] = joined(query_grads).astype(low)
    save(*"cross_grad_low cross_q_grad text_key text_value".split())
    grad = contract(own.cross_q_grad[...], own.cross_query[...], 1, 1)
    sums[2:3, :] = total_rows(own.cross_q_grad[...])
    sums[4:5, :] = total_rows(grad * own.normed_one[...])
    sums[6:7, :] = total_rows(grad)
    self_grad = own.after[...] + row_norm_back(
        grad, own.normed_one[...], inverse_one, gains[1:2]
    )
    own.self_grad[...] = self_grad
    own.self_grad_low[...] = self_grad.astype(low)
    sums[3:4, :] = total_rows(own.self_grad_low[...])
    own.att_grad[...] = contract(own.self_grad_low[...], own.attn_out[...], 1, 1).astype(low)
    save(*"self_grad self_grad_low att_grad".split())
    for copy in saves:
        copy.wait()


def middle(lengths, hidden, attended, out_grad, text_keys, text_values, gain, shift, bias, weights):
    items, frames, width = hidden.shape
    text_count = text_keys.shape[0] // items
    rows = items * frames
    wide = weights[3].shape[1]
    low = jnp.bfloat16
    full = jnp.float32
    saved = [((rows, width), low)] + [((width, rows), low)] * 4
    saved += [((wide, rows), low), ((rows, wide), low)] + [((rows, width), low)] * 3
    saved += [((rows, width), full), ((rows, width), low)]
    saved += [((items * text_count, width), low)] * 2
    kept = [((rows, width), full)] * 5 + [((rows, width), low)] * 5
    kept += [((items * HEADS // 2, text_count, 2 * frames), full)]
    near = pl.BlockSpec(memory_space=pltpu.VMEM)
    far = pl.BlockSpec(memory_space=pl.ANY)
    outs = pl.pallas_call(
        partial(middle_kernel, items, width // HEADS),
        out_shape=[jax.ShapeDtypeStruct(shape, kind) for shape, kind in saved]
        + [jax.ShapeDtypeStruct((8, width), full), jax.ShapeDtypeStruct((1, wide), full)],
        in_specs=[pl.BlockSpec(memory_space=pltpu.SMEM)] + [near] * 8 + [far] * 5,
        out_specs=[far] * len(saved) + [near] * 2,
        scratch_shapes=[pltpu.VMEM(weight.shape, weight.dtype) for weight in weights]
        + [pltpu.VMEM(shape, kind) for shape, kind in saved + kept]
        + [pltpu.SemaphoreType.DMA((5,)), pltpu.SemaphoreType.DMA((len(saved),))],
        compiler_params=pltpu.CompilerParams(vmem_limit_bytes=62 * 1024 * 1024),
    )(
        lengths,
        hidden.reshape(rows, width),
        attended.reshape(rows, width),
        out_grad.reshape(rows, width),
        text_keys,
        text_values,
        gain,
        shift,
        bias,
        *weights,
    )
    return outs[: len(saved)], outs[len(saved)], outs[len(saved) + 1]


class Forward(NamedTuple):
    attn_in: object
    cross_kv: object
    projected: object
    queries: object
    keys: object
    values: object
    mixed: object
    mixed_low: object
    log_total: object
    load_sem: object
    there_send: object
    there_recv: object
    back_send: object
    back_recv: object
    save_sem: object


def forward_kernel(head, *refs):
    refs = list(refs)
    limit_ref, hidden, gain, shift, bias, text, attn_in, cross_kv = refs[:8]
    normed_out, text_keys, text_values = refs[8:11]
    attended, queries_out, keys_out, values_out, mixed_out, log_out = refs[11:17]
    own = Forward(*refs[17:])
    low = jnp.bfloat16
    items, length, lanes = own.queries.shape
    frames, width = hidden.shape[1:]
    blocks = length // frames
    block = lax.axis_index("blk")
    scale = head ** (-0.5)
    barrier = pltpu.get_barrier_semaphore()
    for step in range(1, blocks):
        pl.semaphore_signal(
            barrier, inc=1, device_id={"blk": lax.rem(block + step, blocks)}, device_id_type=MESH_ID
        )
    loads = [
        pltpu.make_async_copy(
            attn_in.at[:, part * width : (part + 1) * width],
            own.attn_in.at[:, part * width : (part + 1) * width],
            own.load_sem.at[part],
        )
        for part in range(3)
    ]
    loads.append(pltpu.make_async_copy(cross_kv, own.cross_kv, own.load_sem.at[3]))
    for load in loads:
        load.start()
    gains = gain[0:1, :].astype(jnp.float32)
    shifts = shift[0:1, :].astype(jnp.float32)
    for item in range(items):
        normed, _ = row_norm(hidden[item].astype(jnp.float32))
        normed_out[item] = (normed * gains + shifts).astype(low)
    landing = (own.queries, own.keys, own.values)

    def lane_block(offset, place):
        return pl.ds(pl.multiple_of(offset + place * LANES, LANES), LANES)

    def frame_rows(place):
        return pl.ds(pl.multiple_of(place * frames, frames), frames)

    def there(item, part, step):
        place = lax.rem(block + step, blocks)
        source = own.projected.at[item, :, lane_block(part * width, place)]
        target = landing[part].at[item, frame_rows(block), :]
        if step == 0:
            return pltpu.make_async_copy(source, target, own.there_recv.at[item, part, 0])
        return pltpu.make_async_remote_copy(
            src_ref=source,
            dst_ref=target,
            send_sem=own.there_send.at[item, part, step],
            recv_sem=own.there_recv.at[item, part, step],
            device_id={"blk": place},
            device_id_type=MESH_ID,
        )

    def back(item, step):
        place = lax.rem(block + step, blocks)
        source = own.mixed_low.at[item, frame_rows(place), :]
        target = attended.at[item, :, lane_block(0, block)]
        if step == 0:
            return pltpu.make_async_copy(source, target, own.back_recv.at[item, 0])
        return pltpu.make_async_remote_copy(
            src_ref=source,
            dst_ref=target,
            send_sem=own.back_send.at[item, step],
            recv_sem=own.back_recv.at[item, step],
            device_id={"blk": place},
            device_id_type=MESH_ID,
        )

    def save_copies(item):
        kept = (own.queries, own.keys, own.values, own.mixed, own.log_total)
        outs = (queries_out, keys_out, values_out, mixed_out, log_out)
        return [
            pltpu.make_async_copy(source.at[item], out.at[item], own.save_sem.at[item, number])
            for number, (source, out) in enumerate(zip(kept, outs))
        ]

    for item in range(items):
        for part in range(3):
            if item == 0:
                loads[part].wait()
            columns = slice(part * width, (part + 1) * width)
            rows = contract(normed_out[item], own.attn_in[:, columns], 1, 0)
            if part != 1:
                start = (part // 2) * width
                rows = rows + bias[:, start : start + width]
            own.projected[item, :, columns] = rows.astype(low)
            if item == 0 and part == 0:
                pl.semaphore_wait(barrier, blocks - 1)
            for step in range(blocks):
                there(item, part, step).start()
    loads[3].wait()
    text_keys[...] = contract(text[...], own.cross_kv[:, :width], 1, 0).astype(low)
    text_values[...] = (
        contract(text[...], own.cross_kv[:, width:], 1, 0) + bias[:, 2 * width : 3 * width]
    ).astype(low)
    low_half = lax.broadcasted_iota(jnp.int32, (ROWS, lanes), 1) < head

    def attend(item, carry):
        for part in range(3):
            for step in range(blocks):
                there(item, part, step).wait()
        for number in range(length // ROWS):
            span = (number + 1) * ROWS
            here = slice(number * ROWS, span)
            queries = two_heads(own.queries[item, here, :] * low(scale), low_half)
            scores = contract(queries, own.keys[item, :span, :], 1, 1)
            query_pos = lax.broadcasted_iota(jnp.int32, (2 * ROWS, ROWS), 0) % ROWS
            key_pos = lax.broadcasted_iota(jnp.int32, (2 * ROWS, ROWS), 1)
            corner = jnp.where(key_pos <= query_pos, scores[:, span - ROWS :], NEG_FILL)
            scores = corner if number == 0 else jnp.concatenate([scores[:, : span - ROWS], corner], 1)
            if span > length // 2:
                valid = lax.broadcasted_iota(jnp.int32, (1, span), 1) < limit_ref[item]
                scores = scores + jnp.where(valid, 0.0, NEG_FILL)
            top = jnp.max(scores, 1, keepdims=True)
            raised = jnp.exp(scores - top)
            total = jnp.sum(raised, 1, keepdims=True)
            mixed = contract(raised.astype(low), own.values[item, :span, :], 1, 0) / total
            mixed = jnp.where(low_half, mixed[:ROWS], mixed[ROWS:])
            own.mixed[item, here, :] = mixed
            own.mixed_low[item, here, :] = mixed.astype(low)
            log_total = top + jnp.log(total)
            own.log_total[item, here, :] = jnp.where(low_half, log_total[:ROWS], log_total[ROWS:])
        for step in range(blocks):
            back(item, step).start()
        for copy in save_copies(item):
            copy.start()
        return carry

    lax.fori_loop(0, items, attend, 0)
    for item in range(items):
        for step in range(blocks):
            back(item, step).wait()
        for copy in save_copies(item):
            copy.wait()


def forward(identity, blocks, limits, hidden, gain, shift, bias, text, attn_in, cross_kv):
    items, frames, width = hidden.shape
    low = jnp.bfloat16
    full = jnp.float32
    whole_shape = (items, frames * blocks, LANES)
    near = pl.BlockSpec(memory_space=pltpu.VMEM)
    far = pl.BlockSpec(memory_space=pl.ANY)
    rows = text.reshape(-1, width)

    def shape(dims, kind):
        return jax.ShapeDtypeStruct(dims, kind)

    kinds = [low, low, low, full, low, full]
    return pl.pallas_call(
        partial(forward_kernel, width // HEADS),
        out_shape=[shape(hidden.shape, low), shape(rows.shape, low), shape(rows.shape, low)]
        + [shape(hidden.shape, low)]
        + [shape(whole_shape, kind) for kind in (low, low, low, full, full)],
        in_specs=[pl.BlockSpec(memory_space=pltpu.SMEM)] + [near] * 5 + [far] * 2,
        out_specs=[near] * 3 + [far] * 6,
        scratch_shapes=[
            pltpu.VMEM(attn_in.shape, low),
            pltpu.VMEM(cross_kv.shape, low),
            pltpu.VMEM((items, frames, 3 * width), low),
        ]
        + [pltpu.VMEM(whole_shape, kind) for kind in kinds]
        + [
            pltpu.SemaphoreType.DMA((4,)),
            pltpu.SemaphoreType.DMA((items, 3, blocks)),
            pltpu.SemaphoreType.DMA((items, 3, blocks)),
            pltpu.SemaphoreType.DMA((items, blocks)),
            pltpu.SemaphoreType.DMA((items, blocks)),
            pltpu.SemaphoreType.DMA((items, 5)),
        ],
        compiler_params=pltpu.CompilerParams(
            collective_id=identity, has_side_effects=True, vmem_limit_bytes=VMEM_BYTES
        ),
    )(limits, hidden, gain, shift, bias, rows, attn_in, cross_kv)


def finish_kernel(count, *refs):
    refs = list(refs)
    grads = refs[:count]
    text_low, weight, sides, vectors = refs[count : count + 4]
    outs = refs[count + 4 : 2 * count + 4]
    text_out, matrix_out = refs[2 * count + 4 : 2 * count + 6]
    vector_outs = refs[2 * count + 6 : 2 * count + 15]
    scratch = refs[2 * count + 15 :]
    low = scratch[:count]
    text_near, weight_near, vector_near, sides_near = scratch[count : count + 4]
    full = scratch[count + 4 : 2 * count + 4]
    text_grad, load_sem, save_sem = scratch[2 * count + 4 :]
    pairs = list(zip(grads, low)) + [(text_low, text_near), (weight, weight_near)]
    pairs += [(vectors, vector_near), (sides, sides_near)]
    loads = [
        pltpu.make_async_copy(source, target, load_sem.at[number])
        for number, (source, target) in enumerate(pairs)
    ]
    for load in loads:
        load.start()
    saves = []

    def save(source, target):
        copy = pltpu.make_async_copy(source, target, save_sem.at[len(saves)])
        copy.start()
        saves.append(copy)

    width = sides.shape[2]
    loads[count + 2].wait()
    for out, (row, rows) in zip(vector_outs, VECTORS):
        for part in range(rows):
            save(
                vector_near.at[row + part : row + part + 1, :],
                out.at[:, part * LANES : (part + 1) * LANES],
            )
    for number in range(2):
        for part in range(3):
            row = 11 + 3 * number + part
            save(vector_near.at[row : row + 1, :], vector_outs[7 + number].at[part : part + 1, :])
    for number in range(count):
        loads[number].wait()
        full[number][...] = low[number][...].astype(jnp.float32)
        save(full[number], outs[number])
    loads[count + 3].wait()
    for side in range(2):
        save(sides_near.at[side], matrix_out.at[:, side * width : (side + 1) * width])
    loads[count].wait()
    loads[count + 1].wait()
    for item in range(text_low.shape[0]):
        text_grad[item] = contract(text_near[item], weight_near[...], 1, 1).astype(jnp.bfloat16)
    save(text_grad, text_out)
    for copy in saves:
        copy.wait()


def finish(grads, text_low, weight, sides, vectors):
    count = len(grads)
    full = jnp.float32
    items, texts, _ = text_low.shape
    width = weight.shape[0]

    def shape(*dims, kind=full):
        return jax.ShapeDtypeStruct(dims, kind)

    far = pl.BlockSpec(memory_space=pl.ANY)
    near_low = [pltpu.VMEM(array.shape, array.dtype) for array in grads]
    near_low += [pltpu.VMEM(array.shape, array.dtype) for array in (text_low, weight, vectors, sides)]
    outs = [shape(*grad.shape) for grad in grads]
    outs += [shape(items, texts, width, kind=jnp.bfloat16), shape(LANES, 2 * width)]
    outs += [shape(1, rows * LANES) for _, rows in VECTORS] + [shape(3, LANES)] * 2
    return pl.pallas_call(
        partial(finish_kernel, count),
        out_shape=outs,
        in_specs=[far] * (count + 4),
        out_specs=[far] * len(outs),
        scratch_shapes=near_low
        + [pltpu.VMEM(grad.shape, full) for grad in grads]
        + [
            pltpu.VMEM((items, texts, width), jnp.bfloat16),
            pltpu.SemaphoreType.DMA((count + 4,)),
            pltpu.SemaphoreType.DMA((count + 32,)),
        ],
        compiler_params=pltpu.CompilerParams(vmem_limit_bytes=VMEM_BYTES),
    )(*grads, text_low, weight, sides, vectors)


def fast_device(
    hidden_in,
    text_states,
    frame_lengths,
    text_lengths,
    out_grad,
    attn_in,
    attn_in_bias,
    attn_out,
    attn_out_bias,
    cross_query,
    cross_query_bias,
    cross_kv,
    cross_v_bias,
    cross_out,
    cross_out_bias,
    ff_up,
    ff_up_bias,
    ff_down,
    ff_down_bias,
    norm_gain,
    norm_bias,
):
    seq_count, frames, width = hidden_in.shape
    blocks = lax.axis_size("blk")
    block_index = lax.axis_index("blk")

    biases = [attn_in_bias, cross_v_bias, attn_out_bias, cross_query_bias, cross_out_bias]
    biases += [ff_down_bias, ff_up_bias]
    size = sum(bias.shape[0] for bias in biases)
    start = 0
    packed = 0.0
    for bias in biases:
        rest = size - start - bias.shape[0]
        packed = packed + jnp.pad(bias.astype(jnp.float32), (start, rest))
        start += bias.shape[0]
    biases = packed.reshape(1, -1)
    (
        attn_normed,
        text_keys,
        text_values,
        attended,
        queries,
        keys,
        values,
        mixed,
        log_total,
    ) = forward(
        0,
        blocks,
        frame_lengths,
        hidden_in,
        norm_gain,
        norm_bias,
        biases,
        text_states,
        attn_in,
        cross_kv,
    )
    (
        layer_output,
        attended_turned,
        cross_normed_turned,
        cross_attended_turned,
        ff_normed_turned,
        activated_turned,
        pre_grad,
        cross_grad_low,
        cross_q_grad,
        self_grad_low,
        self_grad,
        att_grad,
        text_key_part,
        text_value_part,
    ), sums, up_sums = middle(
        text_lengths,
        hidden_in,
        attended,
        out_grad,
        text_keys,
        text_values,
        norm_gain,
        norm_bias,
        biases,
        [attn_out, cross_query, cross_out, ff_up, ff_down],
    )
    text_shape = text_states.shape
    layer_output = layer_output.reshape(hidden_in.shape)
    grads, (text_kv_low, cross_kv_sides, hidden_grad, summed) = backward(
        [
            (attended_turned, self_grad_low),
            (cross_normed_turned, cross_q_grad),
            (cross_attended_turned, cross_grad_low),
            (ff_normed_turned, pre_grad),
            (activated_turned, out_grad.reshape(-1, width)),
        ],
        attn_in,
        blocks,
        2,
        frame_lengths,
        [
            att_grad.reshape(hidden_in.shape),
            text_key_part.reshape(text_shape),
            text_value_part.reshape(text_shape),
        ],
        [
            queries,
            keys,
            values,
            mixed,
            log_total,
            attn_normed,
            text_states,
            sums,
            up_sums,
            norm_gain,
        ],
        [hidden_in, self_grad.reshape(hidden_in.shape)],
    )
    outs = finish(grads, text_kv_low, cross_kv, cross_kv_sides, summed)
    attn_out_grad, cross_query_grad, cross_out_grad, ff_up_grad, ff_down_grad, attn_in_grad = outs[:6]
    text_grad, cross_kv_grad = outs[6:8]
    vectors = [vector.reshape(-1) for vector in outs[8:15]] + list(outs[15:17])
    return (
        layer_output,
        hidden_grad,
        text_grad,
        attn_in_grad,
        vectors[0],
        attn_out_grad,
        vectors[1],
        cross_query_grad,
        vectors[2],
        cross_kv_grad,
        vectors[3],
        cross_out_grad,
        vectors[4],
        ff_up_grad,
        vectors[5],
        ff_down_grad,
        vectors[6],
        vectors[7],
        vectors[8],
    )


def solution(mesh):
    fast = mesh.shape["items"] == 4 and mesh.shape["blk"] == 8
    placed = (
        P("items", "blk", None),
        P("items", None, None),
        P("items"),
        P("items"),
        P("items", "blk", None),
        P(),
        P(),
        P(),
        P(),
        P(),
        P(),
        P(),
        P(),
        P(),
        P(),
        P(),
        P(),
        P(),
        P(),
        P(),
        P(),
    )
    return jax.shard_map(
        fast_device if fast else general_device,
        mesh=mesh,
        in_specs=placed,
        out_specs=(
            P("items", "blk", None),
            P("items", "blk", None),
            P("items", None, None),
            P("blk", None),
            P("blk"),
            P("blk", None),
            P("blk"),
            P("blk", None),
            P("blk"),
            P("blk", None),
            P("blk"),
            P("blk", None),
            P("blk"),
            P("blk", None),
            P("blk"),
            P("blk", None),
            P("blk"),
            P(None, "blk"),
            P(None, "blk"),
        ),
        check_vma=False,
    )
```
